32 devices in a mesh: copy: 16 (over z, y, core), tok: 2 (over x).
Axes of the slice: x: 2, y: 2, z: 4, core: 2. Of those that a mesh axis runs over, the one named last changes fastest.
Arguments:
- noisy: bfloat16 [16, 256, 768], P('copy', 'tok'), may hold values from -6 to 6
- single: bfloat16 [256, 768], P('tok'), may hold values from -6 to 6
- pair: bfloat16 [256, 256, 128], P('tok', 'copy'), may hold values from -6 to 6
- restype: int32 [256], P('tok'), may hold values from 0 to 31
- chain: int32 [256], replicated, may hold values from 0 to 5, never falling along the last dimension, each value on 1 to 128 neighbouring positions
- keymask: int32 [256], replicated, may hold values from 0 to 1, as said below
- restype_table: bfloat16 [32, 768], replicated, may hold values from -3 to 3
- norm_gain: float32 [768], replicated, may hold values from 0.25 to 1.75
- pair_gain: float32 [128], replicated, may hold values from 0.25 to 1.75
- trans_gain: float32 [768], replicated, may hold values from 0.25 to 1.75
- w_query: bfloat16 [768, 768], replicated, may hold values from -0.21875 to 0.21875
- w_key: bfloat16 [768, 768], replicated, may hold values from -0.21875 to 0.21875
- w_value: bfloat16 [768, 768], replicated, may hold values from -0.21875 to 0.21875
- w_out: bfloat16 [768, 768], replicated, may hold values from -0.21875 to 0.21875
- w_pair: bfloat16 [128, 8], replicated, may hold values from -0.5 to 0.5
- chain_weight: float32 [6, 8], replicated, may hold values from -80 to 240
- w_hidden_gate: bfloat16 [768, 1536], replicated, may hold values from -0.21875 to 0.21875
- w_hidden_up: bfloat16 [768, 1536], replicated, may hold values from -0.21875 to 0.21875
- w_down: bfloat16 [1536, 768], replicated, may hold values from -0.15625 to 0.15625
- cotangent: bfloat16 [16, 256, 768], P('copy', 'tok'), may hold values from -6 to 6
Outputs:
- grad_noisy: bfloat16 [16, 256, 768], P('copy', 'tok')
- grad_single: float32 [256, 768], P('tok', 'copy')
- grad_pair: bfloat16 [256, 256, 128], P('tok', 'copy')
- grad_query: float32 [768, 768], P('tok', 'copy')
- grad_key: float32 [768, 768], P('tok', 'copy')
- grad_value: float32 [768, 768], P('tok', 'copy')
- grad_out: float32 [768, 768], P('tok', 'copy')
- grad_pair_weight: float32 [128, 8], replicated
The draws below stay inside these ranges and needn't reach their ends.
Inputs may be any that keep to these rules, and one draw needn't show every extreme that they name: `keymask`: 1 on the first positions of the crop and 0 after them, with at least 128 ones. chain numbers never fall along the crop.
All inputs are finite; a program needn't handle non-finite values.
Results may differ from the reference program's by a relative error of at most 0.03.
Values may be sent and summed in bfloat16 or wider, within the bound.
No kernel may reach another device: no remote copies, remote signals or barrier semaphores. Data moves between devices by JAX's collectives and lax.ppermute only.
A program may use at most 128 MiB of HBM per device.

```python
import math
import jax
import jax.numpy as jnp
import numpy as np
from jax import lax

D = 768
H = 8
HD = 96
CZ = 128
FF = 1536
RES_TYPES = 32
CHAINS = 6
N = 256
COPIES = 16


def draw_keymask(key, part):
    length = jax.random.randint(key, (), N // 2, N + 1)
    return (jnp.arange(N, dtype=jnp.int32) < length).astype(jnp.int32)


def draw_chain_weight(key, part):
    return jax.random.uniform(key, (CHAINS, H), jnp.float32, -2.0, 2.0)


def place_ends(drawn, stream_key, smallest, high):
    index_at = [jax.random.randint(jax.random.fold_in(stream_key, axis), (), 0, length) for axis, length in enumerate(drawn.shape)]
    widest = drawn.shape.index(max(drawn.shape))
    neighbour = index_at[:widest] + [(index_at[widest] + 1) % drawn.shape[widest]] + index_at[widest + 1:]
    return drawn.at[tuple(index_at)].set(smallest).at[tuple(neighbour)].set(high)


def block_levels(key, extent, split, low, largest):
    level, own = 1.0, jax.random.fold_in(key, 6)
    for dim, blocks in split:
        heights = jnp.exp(jax.random.uniform(jax.random.fold_in(own, dim), (blocks,), jnp.float32, low / len(split), largest / len(split)))
        level = level * jnp.repeat(heights, extent[dim] // blocks).reshape([-1 if axis == dim else 1 for axis in range(len(extent))])
    return level


def split_up(number_of, total, reach, skew):
    loads = [(1 << 20) // math.isqrt(rank ** skew) + 1 for rank in range(2, number_of + 1)]
    rest, given = total - reach - (number_of - 1), [1] * (number_of - 1)
    while rest > 0:
        candidates = [i for i in range(number_of - 1) if given[i] < reach]
        mass, budget = sum([loads[i] for i in candidates]), rest
        for i in candidates:
            more = min(reach - given[i], max(1, budget * loads[i] // mass), rest)
            given[i] = given[i] + more
            rest = rest - more
    return np.array([reach] + given)


def uneven(key, number_of, total, most, lean):
    if number_of == 2:
        one = jax.random.randint(key, (), max(1, total - most), min(most, total - 1) + 1)
        return jnp.stack([one, total - one])
    tallies = jnp.asarray(split_up(number_of, total, most, lean), jnp.int32)
    twos = (number_of - 1) // 2
    source_of, taker = tallies[1:1 + 2 * twos:2], tallies[2:2 + 2 * twos:2]
    room = jnp.minimum(source_of - 1, most - taker)
    moved = jax.random.randint(jax.random.fold_in(key, 1), (twos,), 0, 1 << 20) % (room + 1)
    tallies = tallies.at[1:1 + 2 * twos:2].set(source_of - moved).at[2:2 + 2 * twos:2].set(taker + moved)
    return tallies[jax.random.permutation(jax.random.fold_in(key, 2), number_of)]


def scatter_about(key, extent, spread, reach, split=(), kind=jnp.bfloat16):
    level = block_levels(key, extent, split, -0.22, 0.18) if split else 1.0
    drawn = jax.random.normal(key, extent, jnp.float32) * spread * level
    return jnp.minimum(jnp.maximum(drawn, -reach), reach).astype(kind)


def setup_inputs(seed: int = 0) -> dict:
    key_list = jax.random.split(jax.random.key(seed), 21)
    return {
        "noisy": scatter_about(key_list[0], (COPIES, N, D), 1.0, 6.0, ((0, 16), (1, 2))),
        "single": scatter_about(key_list[1], (N, D), 1.0, 6.0, ((0, 2),)),
        "pair": scatter_about(key_list[2], (N, N, CZ), 1.0, 6.0, ((0, 2), (1, 16))),
        "restype": place_ends(jax.random.randint(key_list[3], (N,), 0, RES_TYPES), jax.random.fold_in(key_list[3], 1), 0, RES_TYPES - 1).astype(jnp.int32),
        "chain": jnp.searchsorted(jnp.cumsum(uneven(key_list[4], CHAINS, N, N // 2, 0)), jnp.arange(N), side="right").astype(jnp.int32),
        "keymask": draw_keymask(jax.random.fold_in(key_list[20], 71), 0),
        "restype_table": scatter_about(key_list[6], (RES_TYPES, D), 0.5, 3.0),
        "norm_gain": jnp.clip(1.0 + 0.15 * jax.random.normal(key_list[7], (D,), jnp.float32), 0.25, 1.75),
        "pair_gain": jnp.clip(1.0 + 0.15 * jax.random.normal(key_list[8], (CZ,), jnp.float32), 0.25, 1.75),
        "trans_gain": jnp.clip(1.0 + 0.15 * jax.random.normal(key_list[9], (D,), jnp.float32), 0.25, 1.75),
        "w_query": scatter_about(key_list[10], (D, D), D ** -0.5, 0.21875),
        "w_key": scatter_about(key_list[11], (D, D), D ** -0.5, 0.21875),
        "w_value": scatter_about(key_list[12], (D, D), D ** -0.5, 0.21875),
        "w_out": scatter_about(key_list[13], (D, D), D ** -0.5, 0.21875),
        "w_pair": scatter_about(key_list[14], (CZ, H), CZ ** -0.5, 0.5),
        "chain_weight": draw_chain_weight(jax.random.fold_in(key_list[20], 71), 0),
        "w_hidden_gate": scatter_about(key_list[16], (D, FF), D ** -0.5, 0.21875),
        "w_hidden_up": scatter_about(key_list[17], (D, FF), D ** -0.5, 0.21875),
        "w_down": scatter_about(key_list[18], (FF, D), FF ** -0.5, 0.15625),
        "cotangent": scatter_about(key_list[19], (COPIES, N, D), 1.0, 6.0, ((0, 16), (1, 2))),
    }


epsilon = 1e-05
highest_precision = lax.Precision.HIGHEST

def layer_forward(values, scales):
    average = lax.optimization_barrier(jnp.mean(values, axis=-1, keepdims=True))
    centred = values - average
    inverse = lax.rsqrt(lax.optimization_barrier(jnp.mean(centred * centred, axis=-1, keepdims=True)) + epsilon)
    normed = centred * inverse
    return (normed * scales, normed, inverse)

def layer_backward(upstream, scales, normed, inverse):
    scaled = upstream * scales
    first_moment = lax.optimization_barrier(jnp.mean(scaled, axis=-1, keepdims=True))
    second_moment = lax.optimization_barrier(jnp.mean(scaled * normed, axis=-1, keepdims=True))
    return inverse * (scaled - first_moment - normed * second_moment)

def widen(values):
    return lax.optimization_barrier(values).astype(jnp.float32)

def matmul(left, right):
    return jnp.dot(left, right, preferred_element_type=jnp.float32)

def reference(noisy, single, pair, restype, chain, keymask, restype_table, norm_gain, pair_gain, trans_gain, w_query, w_key, w_value, w_out, w_pair, chain_weight, w_hidden_gate, w_hidden_up, w_down, cotangent):
    scale = HD ** (-0.5)
    res_onehot = (restype[:, None] == jnp.arange(RES_TYPES, dtype=jnp.int32)[None, :]).astype(jnp.bfloat16)
    condition = single.astype(jnp.float32) + matmul(res_onehot, restype_table)
    pair_scaled, pair_hat, pair_inverse = layer_forward(pair.astype(jnp.float32), pair_gain)
    pair_rounded = widen(pair_scaled.astype(jnp.bfloat16))
    bias = jnp.einsum('ijc,ch->hij', pair_rounded, w_pair.astype(jnp.float32), precision=highest_precision).astype(jnp.bfloat16)
    chain_onehot = (chain[:, None] == jnp.arange(CHAINS, dtype=jnp.int32)[None, :]).astype(jnp.float32)
    key_weight = jnp.dot(chain_onehot, chain_weight, precision=highest_precision)
    same_chain = (chain[:, None] == chain[None, :]).astype(jnp.float32)
    extra = widen(bias) + same_chain[None, :, :] * key_weight.T[:, None, :]
    valid = (keymask > 0)[None, None, :]

    def one_copy(carry, pieces):
        single_sum, bias_sum, query_sum, key_sum, value_sum, out_sum = carry
        noisy_copy, upstream = pieces
        noisy_f = noisy_copy.astype(jnp.float32)
        normed_scaled, noisy_hat, noisy_inverse = layer_forward(noisy_f, norm_gain)
        inputs_x = (normed_scaled + condition).astype(jnp.bfloat16)
        query = matmul(inputs_x, w_query).astype(jnp.bfloat16)
        keys = matmul(inputs_x, w_key).astype(jnp.bfloat16)
        values = matmul(inputs_x, w_value).astype(jnp.bfloat16)
        query_heads = widen(query).reshape(N, H, HD)
        key_heads = widen(keys).reshape(N, H, HD)
        value_heads = widen(values).reshape(N, H, HD)
        logits = jnp.einsum('ihd,jhd->hij', query_heads, key_heads, precision=highest_precision) * scale + extra
        logits = jnp.where(valid, logits, -1e+30)
        highest = lax.optimization_barrier(jnp.max(logits, axis=-1, keepdims=True))
        exponent = jnp.exp(logits - highest)
        weights = exponent / lax.optimization_barrier(jnp.sum(exponent, axis=-1, keepdims=True))
        weights_b = widen(weights.astype(jnp.bfloat16))
        attended = jnp.einsum('hij,jhd->ihd', weights_b, value_heads, precision=highest_precision).reshape(N, D).astype(jnp.bfloat16)
        residual = noisy_f + matmul(attended, w_out)
        trans_scaled, trans_hat, trans_inverse = layer_forward(residual, trans_gain)
        trans_in = trans_scaled.astype(jnp.bfloat16)
        gate = matmul(trans_in, w_hidden_gate)
        up_part = matmul(trans_in, w_hidden_up)
        sigmoid_gate = jax.nn.sigmoid(gate)
        d_hidden = matmul(upstream, w_down.T)
        d_gate = (d_hidden * up_part * sigmoid_gate * (1.0 + gate * (1.0 - sigmoid_gate))).astype(jnp.bfloat16)
        d_up = (d_hidden * gate * sigmoid_gate).astype(jnp.bfloat16)
        d_trans = matmul(d_gate, w_hidden_gate.T) + matmul(d_up, w_hidden_up.T)
        d_res = upstream.astype(jnp.float32) + layer_backward(d_trans, trans_gain, trans_hat, trans_inverse)
        d_res_b = d_res.astype(jnp.bfloat16)
        out_term = matmul(attended.T, d_res_b)
        d_att = matmul(d_res_b, w_out.T).astype(jnp.bfloat16)
        d_att_heads = widen(d_att).reshape(N, H, HD)
        d_weights = jnp.einsum('ihd,jhd->hij', d_att_heads, value_heads, precision=highest_precision)
        delta = lax.optimization_barrier(jnp.sum(weights * d_weights, axis=-1, keepdims=True))
        d_logits = weights * (d_weights - delta)
        d_logits_b = widen(d_logits.astype(jnp.bfloat16))
        d_query = (jnp.einsum('hij,jhd->ihd', d_logits_b, key_heads, precision=highest_precision) * scale).reshape(N, D).astype(jnp.bfloat16)
        d_key = (jnp.einsum('hij,ihd->jhd', d_logits_b, query_heads, precision=highest_precision) * scale).reshape(N, D).astype(jnp.bfloat16)
        d_value = jnp.einsum('hij,ihd->jhd', weights_b, d_att_heads, precision=highest_precision).reshape(N, D).astype(jnp.bfloat16)
        d_inputs = matmul(d_query, w_query.T) + matmul(d_key, w_key.T) + matmul(d_value, w_value.T)
        grad_copy = (d_res + layer_backward(d_inputs, norm_gain, noisy_hat, noisy_inverse)).astype(jnp.bfloat16)
        carry = (single_sum + d_inputs, bias_sum + d_logits, query_sum + matmul(inputs_x.T, d_query), key_sum + matmul(inputs_x.T, d_key), value_sum + matmul(inputs_x.T, d_value), out_sum + out_term)
        return (carry, grad_copy)
    start = (jnp.zeros((N, D), jnp.float32), jnp.zeros((H, N, N), jnp.float32), jnp.zeros((D, D), jnp.float32), jnp.zeros((D, D), jnp.float32), jnp.zeros((D, D), jnp.float32), jnp.zeros((D, D), jnp.float32))
    carry, grad_noisy = lax.scan(one_copy, start, (noisy, cotangent))
    grad_single, bias_grad, grad_query, grad_key, grad_value, grad_out = carry
    d_pair_scaled = jnp.einsum('hij,ch->ijc', bias_grad, w_pair.astype(jnp.float32), precision=highest_precision)
    grad_pair = layer_backward(d_pair_scaled, pair_gain, pair_hat, pair_inverse).astype(jnp.bfloat16)
    grad_pair_weight = jnp.einsum('ijc,hij->ch', pair_rounded, bias_grad, precision=highest_precision)
    return (grad_noisy, grad_single, grad_pair, grad_query, grad_key, grad_value, grad_out, grad_pair_weight)
```

```python
import jax
import jax.numpy as jnp
from jax import lax
from jax.sharding import PartitionSpec as P

epsilon = 1e-05
f32 = jnp.float32
bf16 = jnp.bfloat16


def layer_forward(values, scales):
    average = jnp.mean(values, axis=-1, keepdims=True)
    centred = values - average
    inverse = lax.rsqrt(jnp.mean(centred * centred, axis=-1, keepdims=True) + epsilon)
    normed = centred * inverse
    return (normed * scales, normed, inverse)


def layer_backward(upstream, scales, normed, inverse):
    scaled = upstream * scales
    first_moment = jnp.mean(scaled, axis=-1, keepdims=True)
    second_moment = jnp.mean(scaled * normed, axis=-1, keepdims=True)
    return inverse * (scaled - first_moment - normed * second_moment)


def mm(left, right, dims=((1,), (0,))):
    return lax.dot_general(left, right, (dims, ((), ())), preferred_element_type=f32)


def swap(value, axis, mask):
    size = lax.axis_size(axis)
    return lax.ppermute(value, axis, [(i, i ^ mask) for i in range(size)])


def gather_tok(value):
    size = lax.axis_size("tok")
    return jnp.stack([value] + [swap(value, "tok", r) for r in range(1, size)])


def scatter_copy(parts):
    size = lax.axis_size("copy")
    me = lax.axis_index("copy")
    mask = 1
    while mask < size:
        bit = (me // mask) % 2
        pairs = parts.reshape((parts.shape[0] // 2, 2) + parts.shape[1:])
        kept = lax.dynamic_index_in_dim(pairs, bit, 1, keepdims=False)
        sent = lax.dynamic_index_in_dim(pairs, 1 - bit, 1, keepdims=False)
        got = swap(sent, "copy", mask)
        parts = (kept.astype(f32) + got.astype(f32)).astype(bf16)
        mask *= 2
    return parts[0]


def gather_copy(value):
    size = lax.axis_size("copy")
    me = lax.axis_index("copy")
    held = value[None]
    mask = size // 2
    while mask:
        got = swap(held, "copy", mask)
        bit = (me // mask) % 2
        held = jnp.where(
            bit == 0, jnp.stack([held, got], axis=1), jnp.stack([got, held], axis=1)
        )
        held = held.reshape((-1,) + value.shape)
        mask //= 2
    return held


def per_device(
    noisy,
    single,
    pair,
    restype,
    chain,
    keymask,
    restype_table,
    norm_gain,
    pair_gain,
    trans_gain,
    w_query,
    w_key,
    w_value,
    w_out,
    w_pair,
    chain_weight,
    w_hidden_gate,
    w_hidden_up,
    w_down,
    cotangent,
):
    copies = lax.axis_size("copy")
    toks = lax.axis_size("tok")
    me_tok = lax.axis_index("tok")
    _, rows, width = noisy.shape
    cols = pair.shape[1]
    channels = pair.shape[2]
    heads = w_pair.shape[1]
    head_width = width // heads
    own_heads = heads // toks
    own_width = own_heads * head_width
    tokens = rows * toks
    scale = head_width ** (-0.5)
    blocks = [me_tok ^ r for r in range(toks)]

    pair_scaled, pair_hat, pair_inverse = layer_forward(pair.astype(f32), pair_gain)
    pair_rounded = pair_scaled.astype(bf16)
    bias_local = jnp.einsum(
        "ijc,ch->hji", pair_rounded, w_pair, preferred_element_type=f32
    ).astype(bf16)
    bias_split = bias_local.reshape(toks, own_heads, cols, rows)
    bias_parts = []
    for r in range(toks):
        piece = lax.dynamic_index_in_dim(bias_split, blocks[r], 0, keepdims=False)
        bias_parts.append(piece if r == 0 else swap(piece, "tok", r))
    bias_mine = jnp.concatenate(bias_parts, axis=-1)
    bias_all = gather_copy(bias_mine)
    bias = jnp.transpose(bias_all, (1, 0, 2, 3)).reshape(own_heads, tokens, tokens)

    res_onehot = (
        restype[:, None] == jnp.arange(restype_table.shape[0], dtype=jnp.int32)[None, :]
    ).astype(bf16)
    condition = single.astype(f32) + mm(res_onehot, restype_table)
    noisy_f = noisy[0].astype(f32)
    normed_scaled, noisy_hat, noisy_inverse = layer_forward(noisy_f, norm_gain)
    x_own = (normed_scaled + condition).astype(bf16)
    x = gather_tok(x_own).reshape(tokens, width)

    def columns(weight):
        return lax.dynamic_slice_in_dim(weight, me_tok * own_width, own_width, axis=1)

    wq, wk, wv = columns(w_query), columns(w_key), columns(w_value)
    query = mm(wq, x, ((0,), (1,))).astype(bf16).reshape(own_heads, head_width, tokens)
    key = mm(wk, x, ((0,), (1,))).astype(bf16).reshape(own_heads, head_width, tokens)
    value = mm(wv, x, ((0,), (1,))).astype(bf16).reshape(own_heads, head_width, tokens)

    def token_order(array, axis):
        return jnp.concatenate(
            [
                lax.dynamic_slice_in_dim(array, b * rows, rows, axis=axis)
                for b in blocks
            ],
            axis=axis,
        )

    chain_rel = token_order(chain, 0)
    mask_rel = token_order(keymask, 0)
    chain_onehot = (
        chain_rel[:, None] == jnp.arange(chain_weight.shape[0], dtype=jnp.int32)[None, :]
    ).astype(f32)
    key_weight = jnp.dot(
        chain_onehot,
        lax.dynamic_slice_in_dim(chain_weight, me_tok * own_heads, own_heads, axis=1),
        precision=lax.Precision.HIGHEST,
    )
    same_chain = (chain_rel[:, None] == chain_rel[None, :]).astype(f32)
    extra = (
        token_order(bias, 1).astype(f32)
        + same_chain[None] * key_weight.T[:, :, None]
    )
    logits = (
        jnp.einsum("hdj,hdi->hji", key, query, preferred_element_type=f32) * scale + extra
    )
    logits = jnp.where((mask_rel > 0)[None, :, None], logits, -1e30)
    highest = jnp.max(logits, axis=1, keepdims=True)
    exponent = jnp.exp(logits - highest)
    weights = exponent / jnp.sum(exponent, axis=1, keepdims=True)
    weights_b = weights.astype(bf16)
    att = jnp.einsum("hdj,hji->hdi", value, weights_b, preferred_element_type=f32).astype(
        bf16
    )
    att = att.reshape(own_width, toks, rows)
    attended = []
    for r in range(toks):
        piece = att[:, r]
        attended.append(piece if r == 0 else swap(piece, "tok", r))

    projected = 0.0
    for r in range(toks):
        w_rows = lax.dynamic_slice_in_dim(w_out, blocks[r] * own_width, own_width, axis=0)
        projected = projected + mm(attended[r], w_rows, ((0,), (0,)))
    residual = noisy_f + projected
    trans_scaled, trans_hat, trans_inverse = layer_forward(residual, trans_gain)
    trans_in = trans_scaled.astype(bf16)
    gate = mm(trans_in, w_hidden_gate)
    up_part = mm(trans_in, w_hidden_up)
    sigmoid_gate = jax.nn.sigmoid(gate)
    upstream = cotangent[0]
    d_hidden = mm(upstream, w_down, ((1,), (1,)))
    d_gate = (
        d_hidden * up_part * sigmoid_gate * (1.0 + gate * (1.0 - sigmoid_gate))
    ).astype(bf16)
    d_up = (d_hidden * gate * sigmoid_gate).astype(bf16)
    d_trans = mm(d_gate, w_hidden_gate, ((1,), (1,))) + mm(
        d_up, w_hidden_up, ((1,), (1,))
    )
    d_res = upstream.astype(f32) + layer_backward(
        d_trans, trans_gain, trans_hat, trans_inverse
    )
    d_res_all = gather_tok(d_res.astype(bf16)).reshape(tokens, width)

    w_out_rows = lax.dynamic_slice_in_dim(w_out, me_tok * own_width, own_width, axis=0)
    d_att = mm(w_out_rows, d_res_all, ((1,), (1,))).astype(bf16)
    out_grad = mm(d_res_all, att.reshape(own_width, tokens), ((0,), (1,)))
    d_att = d_att.reshape(own_heads, head_width, tokens)
    d_weights = jnp.einsum("hdj,hdi->hji", value, d_att, preferred_element_type=f32)
    delta = jnp.sum(weights * d_weights, axis=1, keepdims=True)
    d_logits = weights * (d_weights - delta)
    d_logits_b = d_logits.astype(bf16)
    d_query = (
        jnp.einsum("hdj,hji->hdi", key, d_logits_b, preferred_element_type=f32) * scale
    )
    d_key = (
        jnp.einsum("hdi,hji->hdj", query, d_logits_b, preferred_element_type=f32) * scale
    )
    d_value = jnp.einsum("hdi,hji->hdj", d_att, weights_b, preferred_element_type=f32)
    d_query, d_key, d_value = [
        part.astype(bf16).reshape(own_width, tokens) for part in (d_query, d_key, d_value)
    ]

    d_bias = token_order(d_logits_b, 1).reshape(own_heads, copies, cols, tokens)
    bias_grad_mine = scatter_copy(jnp.transpose(d_bias, (1, 0, 2, 3)))
    bias_grad_mine = bias_grad_mine.reshape(own_heads, cols, toks, rows)
    received = []
    for r in range(toks):
        piece = bias_grad_mine[:, :, r]
        received.append(piece if r == 0 else swap(piece, "tok", r))
    received = jnp.stack(received)
    bias_grad = jnp.concatenate(
        [lax.dynamic_index_in_dim(received, me_tok ^ a, 0, keepdims=False) for a in range(toks)]
    )
    d_pair_scaled = jnp.einsum("hji,ch->ijc", bias_grad, w_pair, preferred_element_type=f32)
    grad_pair = layer_backward(d_pair_scaled, pair_gain, pair_hat, pair_inverse).astype(bf16)
    pair_weight_term = jnp.einsum(
        "ijc,hji->ch", pair_rounded, bias_grad, preferred_element_type=f32
    )
    mask = 1
    while mask < copies:
        pair_weight_term = pair_weight_term + swap(pair_weight_term, "copy", mask)
        mask *= 2
    mask = 1
    while mask < toks:
        pair_weight_term = pair_weight_term + swap(pair_weight_term, "tok", mask)
        mask *= 2

    d_inputs = mm(wq, d_query) + mm(wk, d_key) + mm(wv, d_value)
    d_inputs = d_inputs.reshape(width, toks, rows)
    total = d_inputs[:, 0]
    for r in range(1, toks):
        total = total + swap(d_inputs[:, r].astype(bf16), "tok", r).astype(f32)
    grad_noisy = (
        d_res + layer_backward(total.T, norm_gain, noisy_hat, noisy_inverse)
    ).astype(bf16)[None]
    grad_single = scatter_copy(total.astype(bf16).reshape(copies, width // copies, rows))
    grad_single = grad_single.T.astype(f32)

    group = copies // toks
    piece_cols = width // copies
    piece_rows = width // toks
    wide = jnp.stack([mm(part, x) for part in (d_query, d_key, d_value)]).astype(bf16)
    wide = wide.reshape(3, group, piece_cols, toks, piece_rows)
    wide = jnp.transpose(wide, (3, 1, 0, 2, 4)).reshape(copies, 3, piece_cols, piece_rows)
    narrow = out_grad.astype(bf16).reshape(copies, 1, piece_cols, own_width)
    mine = scatter_copy(jnp.concatenate([wide, narrow], axis=1))
    pairs = []
    for c in range(copies):
        for t in range(toks):
            pairs.append((c * toks + t, (t * group + c % group) * toks + c // group))
    moved = lax.ppermute(mine[:3], ("copy", "tok"), pairs)
    finals = [jnp.transpose(part).astype(f32) for part in (moved[0], moved[1], moved[2], mine[3])]
    return (
        grad_noisy,
        grad_single,
        grad_pair,
        finals[0],
        finals[1],
        finals[2],
        finals[3],
        pair_weight_term,
    )


def solution(mesh):
    placed = (
        P("copy", "tok", None),
        P("tok", None),
        P("tok", "copy", None),
        P("tok"),
    ) + (P(),) * 15 + (P("copy", "tok", None),)
    return jax.shard_map(
        per_device,
        mesh=mesh,
        in_specs=placed,
        out_specs=(
            P("copy", "tok", None),
            P("tok", "copy"),
            P("tok", "copy", None),
            P("tok", "copy"),
            P("tok", "copy"),
            P("tok", "copy"),
            P("tok", "copy"),
            P(),
        ),
        check_vma=False,
    )
```

```python
import functools

import jax
import jax.numpy as jnp
from jax import lax
from jax.experimental import pallas as pl
from jax.experimental.pallas import tpu as pltpu
from jax.sharding import PartitionSpec as P

epsilon = 1e-05
f32 = jnp.float32
bf16 = jnp.bfloat16
VMEM, SMEM, ANY = pltpu.VMEM, pltpu.SMEM, pl.ANY
MIB = 1 << 20


def layer_forward(values, scales):
    average = jnp.mean(values, axis=-1, keepdims=True)
    centred = values - average
    inverse = lax.rsqrt(jnp.mean(centred * centred, axis=-1, keepdims=True) + epsilon)
    normed = centred * inverse
    return (normed * scales, normed, inverse)


def layer_backward(upstream, scales, normed, inverse):
    scaled = upstream * scales
    first_moment = jnp.mean(scaled, axis=-1, keepdims=True)
    second_moment = jnp.mean(scaled * normed, axis=-1, keepdims=True)
    return inverse * (scaled - first_moment - normed * second_moment)


NN = ((1,), (0,))
NT = ((1,), (1,))
TN = ((0,), (0,))


def mm(left, right, dims=NN):
    return lax.dot_general(left, right, (dims, ((), ())), preferred_element_type=f32)


def call(body, name, inputs, outs, scratch=(), flops=0, limit=32):
    arrays, specs, moved = [], [], 0
    for item in inputs:
        array, space = item if isinstance(item, tuple) else (item, VMEM)
        arrays.append(array)
        specs.append(pl.BlockSpec(memory_space=space))
        moved += array.size * array.dtype.itemsize
    for shape, kind in outs:
        size = jnp.dtype(kind).itemsize
        for extent in shape:
            size *= extent
        moved += size
    results = pl.pallas_call(
        body,
        name=name,
        out_shape=[jax.ShapeDtypeStruct(shape, kind) for shape, kind in outs],
        in_specs=specs,
        out_specs=[pl.BlockSpec(memory_space=VMEM)] * len(outs),
        scratch_shapes=list(scratch),
        compiler_params=pltpu.CompilerParams(vmem_limit_bytes=limit * MIB),
        cost_estimate=pl.CostEstimate(flops=flops, bytes_accessed=moved, transcendentals=0),
    )(*arrays)
    return results


def low_bits(index, size):
    return jnp.bitwise_and(index, size - 1)


def pair_weight_rows(w_pair, head_count, cols):
    rows = head_count * cols
    shift = cols.bit_length() - 1
    head = lax.shift_right_logical(
        lax.broadcasted_iota(jnp.int32, (rows, head_count), 0), jnp.int32(shift)
    )
    pick = (head == lax.broadcasted_iota(jnp.int32, (rows, head_count), 1)).astype(f32)
    spread = mm(pick.astype(bf16), w_pair, NT)
    row_col = low_bits(lax.broadcasted_iota(jnp.int32, spread.shape, 0), cols)
    return spread, row_col


def enter_kernel(toks, cols, ids, noisy, single, restype, table, gain, pair, pair_gain, w_pair, *rest):
    x_out, bias_outs = rest[0], rest[1 : 1 + toks]
    rounded, bias = rest[1 + toks :]
    t = ids[0]
    rows = noisy.shape[0]
    pair_scaled, _, _ = layer_forward(pair[...].astype(f32), pair_gain[...])
    rounded[...] = pair_scaled.astype(bf16).astype(f32)
    head_count = w_pair.shape[1]
    spread, row_col = pair_weight_rows(w_pair[...], head_count, cols)
    total = jnp.zeros((head_count * cols, rows), f32)
    for j in range(cols):
        column = rounded[pl.ds(j, rows, stride=cols), :].astype(bf16)
        total = total + mm(jnp.where(row_col == j, spread, 0.0).astype(bf16), column, NT)
    bias[...] = total
    part = head_count // toks * cols
    for r in range(toks):
        start = pl.multiple_of(jnp.bitwise_xor(t, r) * part, part)
        bias_outs[r][...] = bias[pl.ds(start, part), :].astype(bf16)

    normed_scaled, _, _ = layer_forward(noisy[...].astype(f32), gain[...])
    types = table.shape[0]
    onehot = (lax.broadcasted_iota(jnp.int32, (types, rows), 0) == restype[...]).astype(f32)
    condition = single[...].astype(f32) + mm(onehot.astype(bf16), table[...], TN)
    x_out[...] = (normed_scaled + condition).astype(bf16)


def own_slice(weight, t, own_width):
    if weight.shape[1] == own_width:
        return weight
    return weight.at[:, pl.ds(pl.multiple_of(t * own_width, own_width), own_width)]


def project_kernel(toks, own_width, ids, *rest):
    parts = rest[:toks]
    weights = rest[toks : toks + 3]
    x_out, outs = rest[toks + 3], rest[toks + 4 : toks + 7]
    held, sem = rest[toks + 7 :]
    t = ids[0]
    copies = []
    for k in range(3):
        copy = pltpu.make_async_copy(
            own_slice(weights[k], t, own_width), held.at[k], sem.at[k]
        )
        copy.start()
        copies.append(copy)
    rows = parts[0].shape[0]
    for r in range(toks):
        start = pl.multiple_of(jnp.bitwise_xor(t, r) * rows, rows)
        x_out[pl.ds(start, rows), :] = parts[r][...]
    x = x_out[...]
    for k in range(3):
        copies[k].wait()
        outs[k][...] = jnp.transpose(mm(x, held[k])).astype(bf16)


def attention_kernel(copies, toks, near, cols, head_width, ids, query, key, value, *rest):
    biases = rest[:near]
    chain, keymask, chain_weight = rest[near : near + 3]
    weights_out, att_out = rest[near + 3 : near + 5]
    pieces = rest[near + 5 : near + 5 + toks]
    bias = rest[near + 5 + toks]
    t, c = ids[0], ids[1]
    far = copies // near
    z, yc = c // near, low_bits(c, near)
    own_heads = weights_out.shape[0]
    tokens = query.shape[1]
    rows = tokens // toks
    for m in range(near):
        for rz in range(far):
            start = (jnp.bitwise_xor(z, rz) * near + jnp.bitwise_xor(yc, m)) * cols
            start = pl.multiple_of(start, cols)
            for rt in range(toks):
                a = jnp.bitwise_xor(t, rt)
                for h in range(own_heads):
                    bias[h, a, pl.ds(start, cols), :] = biases[m][
                        rz * toks + rt, h * cols : (h + 1) * cols, :
                    ]
    chain_row = chain[...]
    keep_row = keymask[...].astype(f32)
    line = lax.broadcasted_iota(jnp.int32, (128, tokens), 0)
    facts = jnp.where(line == 0, chain_row.astype(f32), 0.0) + jnp.where(line == 1, keep_row, 0.0)
    for h in range(own_heads):
        weight_row = jnp.zeros((1, tokens), f32)
        for m in range(chain_weight.shape[0]):
            weight_row = jnp.where(chain_row == m, chain_weight[m, t * own_heads + h], weight_row)
        facts = jnp.where(line == 2 + h, weight_row, facts)
    facts = jnp.transpose(facts)
    same = facts[:, 0:1] == chain_row.astype(f32)
    keep = facts[:, 1:2] > 0.0
    scale = head_width ** (-0.5)
    attended = []
    for h in range(own_heads):
        span = slice(h * head_width, (h + 1) * head_width)
        logits = mm(key[span, :], query[span, :], TN) * scale
        extra = jnp.concatenate([bias[h, a] for a in range(toks)], axis=1).astype(f32)
        logits = logits + (extra + jnp.where(same, facts[:, 2 + h : 3 + h], 0.0))
        logits = jnp.where(keep, logits, -1e30)
        exponent = jnp.exp(logits - jnp.max(logits, axis=0, keepdims=True))
        weights = exponent / jnp.sum(exponent, axis=0, keepdims=True)
        weights_b = weights.astype(bf16)
        weights_out[h] = weights_b
        attended.append(mm(value[span, :], weights_b))
    att_out[...] = jnp.transpose(jnp.concatenate(attended, axis=0)).astype(bf16)
    for r in range(toks):
        start = pl.multiple_of(jnp.bitwise_xor(t, r) * rows, rows)
        pieces[r][...] = att_out[pl.ds(start, rows), :]


def down_kernel(upstream, w_down, d_hidden):
    d_hidden[...] = mm(upstream[...], w_down[...], NT)


def hidden_kernel(toks, chunk, ids, noisy, upstream, d_hidden, gain, *rest):
    parts = rest[:toks]
    w_out, w_gate, w_up = rest[toks : toks + 3]
    d_res_out, d_res_b_out = rest[toks + 3 : toks + 5]
    held_out, held_gate, held_up, sem = rest[toks + 5 :]
    t = ids[0]
    hidden = w_gate.shape[1]
    first = pltpu.make_async_copy(w_out, held_out, sem.at[0])
    first.start()
    copies = []
    for k in range(hidden // chunk):
        span = pl.ds(k * chunk, chunk)
        pair = [
            pltpu.make_async_copy(w.at[:, span], held.at[:, span], sem.at[1 + 2 * k + n])
            for n, (w, held) in enumerate(((w_gate, held_gate), (w_up, held_up)))
        ]
        for copy in pair:
            copy.start()
        copies.append(pair)
    residual = noisy[...].astype(f32)
    first.wait()
    own_width = parts[0].shape[1]
    for r in range(toks):
        start = pl.multiple_of(jnp.bitwise_xor(t, r) * own_width, own_width)
        residual = residual + mm(parts[r][...], held_out[pl.ds(start, own_width), :])
    trans_scaled, trans_hat, trans_inverse = layer_forward(residual, gain[...])
    trans_in = trans_scaled.astype(bf16)
    d_trans = jnp.zeros(residual.shape, f32)
    for k in range(hidden // chunk):
        for copy in copies[k]:
            copy.wait()
        span = slice(k * chunk, (k + 1) * chunk)
        gate = mm(trans_in, held_gate[:, span])
        up = mm(trans_in, held_up[:, span])
        incoming = d_hidden[:, span]
        sigmoid = jax.nn.sigmoid(gate)
        d_up = (incoming * gate * sigmoid).astype(bf16)
        d_gate = (incoming * up * sigmoid * (1.0 + gate * (1.0 - sigmoid))).astype(bf16)
        d_trans = d_trans + mm(d_gate, held_gate[:, span], NT) + mm(d_up, held_up[:, span], NT)
    d_res = upstream[...].astype(f32) + layer_backward(
        d_trans, gain[...], trans_hat, trans_inverse
    )
    d_res_out[...] = d_res
    d_res_b_out[...] = d_res.astype(bf16)


def backward_kernel(copies, toks, near, cols, head_width, ids, query, key, value, weights, *rest):
    parts = rest[:toks]
    w_out = rest[toks]
    d_res_out, d_query, d_key, d_value = rest[toks + 1 : toks + 5]
    d_bias = rest[toks + 5 : toks + 5 + near]
    d_logits, held, sem = rest[toks + 5 + near :]
    t, c = ids[0], ids[1]
    far = copies // near
    yc = low_bits(c, near)
    own_width, tokens = query.shape
    rows = tokens // toks
    start = pl.multiple_of(t * own_width, own_width)
    copy = pltpu.make_async_copy(w_out.at[pl.ds(start, own_width), :], held, sem.at[0])
    copy.start()
    for r in range(toks):
        start = pl.multiple_of(jnp.bitwise_xor(t, r) * rows, rows)
        d_res_out[pl.ds(start, rows), :] = parts[r][...]
    copy.wait()
    d_att = mm(held[...], d_res_out[...], NT).astype(bf16)
    scale = head_width ** (-0.5)
    for h in range(weights.shape[0]):
        span = slice(h * head_width, (h + 1) * head_width)
        d_att_h = d_att[span, :]
        weights_b = weights[h]
        d_weights = mm(value[span, :], d_att_h, TN)
        weights_f = weights_b.astype(f32)
        delta = jnp.sum(weights_f * d_weights, axis=0, keepdims=True)
        d_logits_b = (weights_f * (d_weights - delta)).astype(bf16)
        d_logits[h] = d_logits_b
        d_query[span, :] = (mm(key[span, :], d_logits_b) * scale).astype(bf16)
        d_key[span, :] = (mm(query[span, :], d_logits_b, NT) * scale).astype(bf16)
        d_value[span, :] = mm(d_att_h, weights_b, NT).astype(bf16)
    for m in range(near):
        for z in range(far):
            start = pl.multiple_of((z * near + jnp.bitwise_xor(yc, m)) * cols, cols)
            for h in range(weights.shape[0]):
                d_bias[m][z, h * cols : (h + 1) * cols, :] = d_logits[h, pl.ds(start, cols), :]


def gradient_kernel(copies, toks, ids, x, att, d_res, d_query, d_key, d_value, *rest):
    weights = rest[:3]
    kept, sent, d_own = rest[3:6]
    d_others = rest[6 : 5 + toks]
    wide, narrow, d_inputs, held, sem = rest[5 + toks :]
    t, c = ids[0], ids[1]
    own_width, tokens = d_query.shape
    rows = tokens // toks
    width = x.shape[1]
    group = copies // toks
    transfers = []
    for k in range(3):
        copy = pltpu.make_async_copy(
            own_slice(weights[k], t, own_width), held.at[k], sem.at[k]
        )
        copy.start()
        transfers.append(copy)
    for k, part in enumerate((d_query, d_key, d_value)):
        wide[k] = mm(part[...], x[...])
    narrow[...] = mm(d_res[...], att[...], TN)
    cut, depth = width // copies, width // toks
    near = low_bits(c, 2)
    for side, out in ((near, kept), (1 - near, sent)):
        for q in range(copies // 2):
            h = 2 * q // group
            first = pl.multiple_of((2 * q - h * group + side) * cut, 8)
            for k in range(3):
                out[q, k] = wide[k, pl.ds(first, cut), h * depth : (h + 1) * depth].astype(bf16)
            first = pl.multiple_of((2 * q + side) * cut, 8)
            out[q, 3] = narrow[pl.ds(first, cut), :].astype(bf16)
    total = None
    for k, part in enumerate((d_query, d_key, d_value)):
        transfers[k].wait()
        term = mm(held[k], part[...])
        total = term if total is None else total + term
    for a in range(toks):
        d_inputs[a] = total[:, a * rows : (a + 1) * rows]
    d_own[...] = d_inputs[t]
    for r in range(1, toks):
        d_others[r - 1][...] = d_inputs[jnp.bitwise_xor(t, r)].astype(bf16)


def halve_kernel(divide, ids, kept, got, kept_out, sent_out):
    bit = low_bits(ids[1] // divide, 2)
    for q in range(kept_out.shape[0]):
        for side, out in ((bit, kept_out), (1 - bit, sent_out)):
            out[q] = (kept[2 * q + side].astype(f32) + got[2 * q + side].astype(f32)).astype(bf16)


def spread_kernel(near, ids, kept, got, *outs):
    z = ids[1] // near
    for r, out in enumerate(outs):
        k = jnp.bitwise_xor(z, r)
        out[...] = (kept[k].astype(f32) + got[k].astype(f32)).astype(bf16)


def collect_kernel(count, *refs):
    parts, (moved, final, flat) = refs[:count], refs[count:]
    for k in range(4):
        total = parts[0][k].astype(f32)
        for part in parts[1:]:
            total = total + part[k].astype(f32)
        if k < 3:
            moved[k] = total.astype(bf16)
        else:
            flat[...] = jnp.zeros(flat.shape, f32)
            flat[: total.shape[0], : total.shape[1]] = total
            final[...] = jnp.transpose(flat[...])[: total.shape[1], : total.shape[0]]


def finish_kernel(moved, kept_single, got_single, first, second, third, single, flat):
    cut = moved.shape[1]
    flat[...] = jnp.zeros(flat.shape, f32)
    for k, out in enumerate((first, second, third)):
        flat[:cut, : moved.shape[2]] = moved[k].astype(f32)
        out[...] = jnp.transpose(flat[...])[: moved.shape[2], :cut]
    rows = single.shape[0]
    flat[:cut, :rows] = kept_single[...].astype(f32) + got_single[...].astype(f32)
    single[...] = jnp.transpose(flat[...])[:rows, :cut]


def exit_kernel(copies, toks, ids, noisy, gain, d_res, d_own, *rest):
    others = rest[: toks - 1]
    grad_noisy, kept, sent, total_ref = rest[toks - 1 :]
    total = d_own[...]
    for part in others:
        total = total + part[...].astype(f32)
    total_ref[...] = total
    _, noisy_hat, noisy_inverse = layer_forward(noisy[...].astype(f32), gain[...])
    grad_noisy[...] = (
        d_res[...] + layer_backward(jnp.transpose(total), gain[...], noisy_hat, noisy_inverse)
    ).astype(bf16)
    cut = total.shape[0] // copies
    bit = low_bits(ids[1] // 2, 2)
    for q in range(copies // 4):
        for low in range(2):
            for side, out in ((bit, kept), (1 - bit, sent)):
                start = pl.multiple_of((q * 4 + side * 2 + low) * cut, 8)
                out[q, low] = total_ref[pl.ds(start, cut), :].astype(bf16)


def single_spread_kernel(near, ids, kept, got, *outs):
    z = ids[1] // near
    for r, out in enumerate(outs):
        k = jnp.bitwise_xor(z, r)
        out[...] = (kept[k].astype(f32) + got[k].astype(f32)).astype(bf16)


def single_collect_kernel(count, ids, *refs):
    parts, (kept, sent) = refs[:count], refs[count:]
    bit = low_bits(ids[1], 2)
    for side, out in ((bit, kept), (1 - bit, sent)):
        total = parts[0][side].astype(f32)
        for part in parts[1:]:
            total = total + part[side].astype(f32)
        out[...] = total.astype(bf16)


def bias_sum_kernel(near, toks, ids, *refs):
    parts, outs, total = refs[:near], refs[near:-1], refs[-1]
    t, z = ids[0], ids[1] // near
    rows = outs[0].shape[1]
    for k in range(parts[0].shape[0]):
        whole = parts[0][k].astype(f32)
        for part in parts[1:]:
            whole = whole + part[k].astype(f32)
        for a in range(toks):
            total[k, a] = whole[:, a * rows : (a + 1) * rows].astype(bf16)
    for n, out in enumerate(outs):
        rz, rt = n // toks, n % toks
        out[...] = total[jnp.bitwise_xor(z, rz), jnp.bitwise_xor(t, rt)]


def pair_kernel(toks, cols, count, ids, pair, gain, w_pair, *refs):
    parts = refs[:count]
    grad_pair, weight_grad, rounded, grads, spread_out = refs[count:]
    t = ids[0]
    head_count = w_pair.shape[1]
    part_rows = parts[0].shape[0]
    rows = parts[0].shape[1]
    for rt in range(toks):
        total = parts[rt][...].astype(f32)
        for rz in range(1, count // toks):
            total = total + parts[rz * toks + rt][...].astype(f32)
        start = pl.multiple_of(jnp.bitwise_xor(t, rt) * part_rows, part_rows)
        grads[pl.ds(start, part_rows), :] = total
    pair_scaled, pair_hat, pair_inverse = layer_forward(pair[...].astype(f32), gain[...])
    rounded[...] = pair_scaled.astype(bf16).astype(f32)
    spread, row_col = pair_weight_rows(w_pair[...], head_count, cols)
    grad = grads[...]
    grad_b = grad.astype(bf16)
    turned = jnp.transpose(grad).astype(bf16)
    sums = jnp.zeros(spread.shape, f32)
    for j in range(cols):
        here = row_col == j
        column = rounded[pl.ds(j, rows, stride=cols), :].astype(bf16)
        sums = sums + jnp.where(here, mm(grad_b, column), 0.0)
        spread_out[pl.ds(j, rows, stride=cols), :] = mm(
            turned, jnp.where(here, spread, 0.0).astype(bf16)
        )
    grad_pair[...] = layer_backward(
        spread_out[...], gain[...], pair_hat, pair_inverse
    ).astype(bf16)
    for h in range(head_count):
        weight_grad[h : h + 1, :] = jnp.sum(
            sums[h * cols : (h + 1) * cols, :], axis=0, keepdims=True
        )


def xor_tree(parts):
    while len(parts) > 1:
        parts = [parts[k] + parts[k + 1] for k in range(0, len(parts), 2)]
    return parts[0]


def swap_copy(value, mask):
    size = lax.axis_size("copy")
    return lax.ppermute(value, "copy", [(i, i ^ mask) for i in range(size)])


def swap_tok(value, mask):
    size = lax.axis_size("tok")
    return lax.ppermute(value, "tok", [(i, i ^ mask) for i in range(size)])


def swap_both(value, mask_copy, mask_tok):
    size, toks = lax.axis_size("copy"), lax.axis_size("tok")
    pairs = [
        (c * toks + t, (c ^ mask_copy) * toks + (t ^ mask_tok))
        for c in range(size)
        for t in range(toks)
    ]
    return lax.ppermute(value, ("copy", "tok"), pairs)


def per_device(
    noisy,
    single,
    pair,
    restype,
    chain,
    keymask,
    restype_table,
    norm_gain,
    pair_gain,
    trans_gain,
    w_query,
    w_key,
    w_value,
    w_out,
    w_pair,
    chain_weight,
    w_hidden_gate,
    w_hidden_up,
    w_down,
    cotangent,
):
    copies = lax.axis_size("copy")
    toks = lax.axis_size("tok")
    _, rows, width = noisy.shape
    cols = pair.shape[1]
    channels = pair.shape[2]
    heads = w_pair.shape[1]
    head_width = width // heads
    own_heads = heads // toks
    own_width = own_heads * head_width
    tokens = rows * toks
    hidden = w_down.shape[0]
    near = 4
    far = copies // near
    cut = width // copies
    ids = jnp.stack([lax.axis_index("tok"), lax.axis_index("copy")]).astype(jnp.int32)
    where_am_i = (ids, SMEM)
    noisy2 = noisy.reshape(rows, width)
    upstream = cotangent.reshape(rows, width)
    pair2 = pair.reshape(rows * cols, channels)
    norm_gain2 = norm_gain.reshape(1, width)
    trans_gain2 = trans_gain.reshape(1, width)
    pair_gain2 = pair_gain.reshape(1, channels)

    entered = call(
        functools.partial(enter_kernel, toks, cols),
        "enter",
        [where_am_i, noisy2, single, restype.reshape(1, rows), restype_table, norm_gain2]
        + [pair2, pair_gain2, w_pair],
        [((rows, width), bf16)] + [((own_heads * cols, rows), bf16)] * toks,
        [VMEM((rows * cols, channels), f32), VMEM((heads * cols, rows), f32)],
        flops=2 * heads * cols * rows * channels * cols,
    )
    x_own, bias_parts = entered[0], entered[1:]
    first = []
    for rz in range(far):
        for rt in range(toks):
            part = bias_parts[rt]
            first.append(part if rz + rt == 0 else swap_both(part, rz * near, rt))
    x_parts = [x_own] + [swap_tok(x_own, r) for r in range(1, toks)]
    bias_first = jnp.stack(first)
    biases = [bias_first] + [swap_copy(bias_first, m) for m in range(1, near)]

    weights3 = [w_query, w_key, w_value]
    if own_width % 128:
        weights3 = [
            lax.dynamic_slice_in_dim(w, ids[0] * own_width, own_width, axis=1) for w in weights3
        ]
    weights3 = [(w, ANY) for w in weights3]
    x, query, key, value = call(
        functools.partial(project_kernel, toks, own_width),
        "project",
        [where_am_i] + x_parts + weights3,
        [((tokens, width), bf16)] + [((own_width, tokens), bf16)] * 3,
        [VMEM((3, width, own_width), bf16), pltpu.SemaphoreType.DMA((3,))],
        flops=6 * tokens * width * own_width,
    )
    done = call(
        functools.partial(attention_kernel, copies, toks, near, cols, head_width),
        "attention",
        [where_am_i, query, key, value]
        + biases
        + [chain.reshape(1, tokens), keymask.reshape(1, tokens), (chain_weight, SMEM)],
        [((own_heads, tokens, tokens), bf16), ((tokens, own_width), bf16)]
        + [((rows, own_width), bf16)] * toks,
        [VMEM((own_heads, toks, tokens, rows), bf16)],
        flops=4 * tokens * tokens * own_width,
    )
    weights, att, pieces = done[0], done[1], done[2:]
    att_parts = [pieces[0]] + [swap_tok(pieces[r], r) for r in range(1, toks)]

    (d_hidden,) = call(
        down_kernel,
        "down",
        [upstream, w_down],
        [((rows, hidden), f32)],
        flops=2 * rows * hidden * width,
    )
    chunk = hidden // 3
    d_res, d_res_b = call(
        functools.partial(hidden_kernel, toks, chunk),
        "hidden",
        [where_am_i, noisy2, upstream, d_hidden, trans_gain2]
        + att_parts
        + [(w_out, ANY), (w_hidden_gate, ANY), (w_hidden_up, ANY)],
        [((rows, width), f32), ((rows, width), bf16)],
        [
            VMEM((width, width), bf16),
            VMEM((width, hidden), bf16),
            VMEM((width, hidden), bf16),
            pltpu.SemaphoreType.DMA((7,)),
        ],
        flops=2 * rows * width * (width + 4 * hidden),
    )
    d_res_parts = [d_res_b] + [swap_tok(d_res_b, r) for r in range(1, toks)]

    back = call(
        functools.partial(backward_kernel, copies, toks, near, cols, head_width),
        "backward",
        [where_am_i, query, key, value, weights] + d_res_parts + [(w_out, ANY)],
        [((tokens, width), bf16)]
        + [((own_width, tokens), bf16)] * 3
        + [((far, own_heads * cols, tokens), bf16)] * near,
        [
            VMEM((own_heads, tokens, tokens), bf16),
            VMEM((own_width, width), bf16),
            pltpu.SemaphoreType.DMA((1,)),
        ],
        flops=8 * tokens * tokens * own_width + 2 * tokens * width * own_width,
    )
    d_res_all, d_query, d_key, d_value = back[:4]
    d_bias = [back[4]] + [swap_copy(back[4 + m], m) for m in range(1, near)]

    found = call(
        functools.partial(gradient_kernel, copies, toks),
        "gradient",
        [where_am_i, x, att, d_res_all, d_query, d_key, d_value] + weights3,
        [((copies // 2, 4, cut, own_width), bf16)] * 2
        + [((width, rows), f32)]
        + [((width, rows), bf16)] * (toks - 1),
        [
            VMEM((3, own_width, width), f32),
            VMEM((width, own_width), f32),
            VMEM((toks, width, rows), f32),
            VMEM((3, width, own_width), bf16),
            pltpu.SemaphoreType.DMA((3,)),
        ],
        flops=14 * tokens * width * own_width,
    )
    kept, sent, d_own = found[:3]
    d_others = [swap_tok(found[2 + r], r) for r in range(1, toks)]
    got = swap_copy(sent, 1)

    bias_out = call(
        functools.partial(bias_sum_kernel, near, toks),
        "bias_sum",
        [where_am_i] + d_bias,
        [((own_heads * cols, rows), bf16)] * (far * toks),
        [VMEM((far, toks, own_heads * cols, rows), bf16)],
    )
    bias_in = []
    for rz in range(far):
        for rt in range(toks):
            part = bias_out[rz * toks + rt]
            bias_in.append(part if rz + rt == 0 else swap_both(part, rz * near, rt))

    kept2, sent2 = call(
        functools.partial(halve_kernel, 2),
        "halve",
        [where_am_i, kept, got],
        [((copies // 4, 4, cut, own_width), bf16)] * 2,
    )
    got2 = swap_copy(sent2, 2)
    grad_noisy, kept_s, sent_s = call(
        functools.partial(exit_kernel, copies, toks),
        "exit",
        [where_am_i, noisy2, norm_gain2, d_res, d_own] + d_others,
        [((rows, width), bf16)] + [((far, 2, cut, rows), bf16)] * 2,
        [VMEM((width, rows), f32)],
    )
    got_s = swap_copy(sent_s, 2)
    grad_pair, weight_grad = call(
        functools.partial(pair_kernel, toks, cols, far * toks),
        "pair",
        [where_am_i, pair2, pair_gain2, w_pair] + bias_in,
        [((rows * cols, channels), bf16), ((heads, channels), f32)],
        [
            VMEM((rows * cols, channels), f32),
            VMEM((heads * cols, rows), f32),
            VMEM((rows * cols, channels), f32),
        ],
        flops=4 * heads * cols * rows * channels * cols,
    )
    terms = []
    for rz in range(far):
        for rt in range(toks):
            terms.append(
                weight_grad if rz + rt == 0 else swap_both(weight_grad, rz * near, rt)
            )
    far_sum = xor_tree(terms)

    spread = call(
        functools.partial(spread_kernel, near),
        "spread",
        [where_am_i, kept2, got2],
        [((4, cut, own_width), bf16)] * far,
    )
    arrived = [spread[0]] + [swap_copy(spread[r], r * near) for r in range(1, far)]
    spread_s = call(
        functools.partial(single_spread_kernel, near),
        "single_spread",
        [where_am_i, kept_s, got_s],
        [((2, cut, rows), bf16)] * far,
    )
    arrived_s = [spread_s[0]] + [swap_copy(spread_s[r], r * near) for r in range(1, far)]
    whole_sum = xor_tree([far_sum] + [swap_copy(far_sum, m) for m in range(1, near)])

    moved, grad_out = call(
        functools.partial(collect_kernel, far),
        "collect",
        arrived,
        [((3, cut, own_width), bf16), ((own_width, cut), f32)],
        [VMEM((128, max(own_width, 128)), f32)],
    )
    last_kept, last_sent = call(
        functools.partial(single_collect_kernel, far),
        "single_collect",
        [where_am_i] + arrived_s,
        [((cut, rows), bf16)] * 2,
    )
    last_got = swap_copy(last_sent, 1)
    group = copies // toks
    pairs = []
    for c in range(copies):
        for t in range(toks):
            pairs.append((c * toks + t, (t * group + c % group) * toks + c // group))
    moved = lax.ppermute(moved, ("copy", "tok"), pairs)
    grad_query, grad_key, grad_value, grad_single = call(
        finish_kernel,
        "finish",
        [moved, last_kept, last_got],
        [((own_width, cut), f32)] * 3 + [((rows, cut), f32)],
        [VMEM((128, max(own_width, rows, 128)), f32)],
    )
    return (
        grad_noisy[None],
        grad_single,
        grad_pair.reshape(rows, cols, channels),
        grad_query,
        grad_key,
        grad_value,
        grad_out,
        whole_sum.T,
    )


def solution(mesh):
    placed = (
        P("copy", "tok", None),
        P("tok", None),
        P("tok", "copy", None),
        P("tok"),
    ) + (P(),) * 15 + (P("copy", "tok", None),)
    return jax.shard_map(
        per_device,
        mesh=mesh,
        in_specs=placed,
        out_specs=(
            P("copy", "tok", None),
            P("tok", "copy"),
            P("tok", "copy", None),
            P("tok", "copy"),
            P("tok", "copy"),
            P("tok", "copy"),
            P("tok", "copy"),
            P(),
        ),
        check_vma=False,
    )
```

```python
import functools

import jax
import jax.numpy as jnp
from jax import lax
from jax.experimental import pallas as pl
from jax.experimental.pallas import tpu as pltpu
from jax.sharding import PartitionSpec as P

epsilon = 1e-05
f32 = jnp.float32
bf16 = jnp.bfloat16
VMEM, SMEM, ANY = pltpu.VMEM, pltpu.SMEM, pl.ANY
MIB = 1 << 20


def layer_forward(values, scales):
    average = jnp.mean(values, axis=-1, keepdims=True)
    centred = values - average
    inverse = lax.rsqrt(jnp.mean(centred * centred, axis=-1, keepdims=True) + epsilon)
    normed = centred * inverse
    return (normed * scales, normed, inverse)


def layer_backward(upstream, scales, normed, inverse):
    scaled = upstream * scales
    first_moment = jnp.mean(scaled, axis=-1, keepdims=True)
    second_moment = jnp.mean(scaled * normed, axis=-1, keepdims=True)
    return inverse * (scaled - first_moment - normed * second_moment)


NN = ((1,), (0,))
NT = ((1,), (1,))
TN = ((0,), (0,))


def mm(left, right, dims=NN):
    return lax.dot_general(left, right, (dims, ((), ())), preferred_element_type=f32)


def call(body, name, inputs, outs, scratch=(), flops=0, limit=32):
    arrays, specs, moved, fetched = [], [], 0, []
    for item in inputs:
        array, space = item if isinstance(item, tuple) else (item, VMEM)
        if space == "fetch":
            fetched.append(len(arrays))
            space = pltpu.HBM
        arrays.append(array)
        specs.append(pl.BlockSpec(memory_space=space))
        moved += array.size * array.dtype.itemsize
    for shape, kind in outs:
        size = jnp.dtype(kind).itemsize
        for extent in shape:
            size *= extent
        moved += size
    extra = [VMEM(arrays[k].shape, arrays[k].dtype) for k in fetched]
    if fetched:
        extra.append(pltpu.SemaphoreType.DMA((len(fetched),)))

    def whole(*refs):
        refs = list(refs)
        if fetched:
            held, sem = refs[-1 - len(fetched) : -1], refs[-1]
            refs = refs[: -1 - len(fetched)]
            transfers = []
            for n, k in enumerate(fetched):
                transfer = pltpu.make_async_copy(refs[k], held[n], sem.at[n])
                transfer.start()
                transfers.append(transfer)
                refs[k] = held[n]
            for transfer in transfers:
                transfer.wait()
        body(*refs)

    return pl.pallas_call(
        whole,
        name=name,
        out_shape=[jax.ShapeDtypeStruct(shape, kind) for shape, kind in outs],
        in_specs=specs,
        out_specs=[pl.BlockSpec(memory_space=VMEM)] * len(outs),
        scratch_shapes=list(scratch) + extra,
        compiler_params=pltpu.CompilerParams(vmem_limit_bytes=limit * MIB),
        cost_estimate=pl.CostEstimate(flops=flops, bytes_accessed=moved, transcendentals=0),
    )(*arrays)


def low_bits(index, size):
    return jnp.bitwise_and(index, size - 1)


def pair_weight_rows(w_pair, head_count, cols):
    rows = head_count * cols
    shift = cols.bit_length() - 1
    head = lax.shift_right_logical(
        lax.broadcasted_iota(jnp.int32, (rows, head_count), 0), jnp.int32(shift)
    )
    pick = (head == lax.broadcasted_iota(jnp.int32, (rows, head_count), 1)).astype(f32)
    spread = mm(pick.astype(bf16), w_pair)
    row_col = low_bits(lax.broadcasted_iota(jnp.int32, spread.shape, 0), cols)
    return spread, row_col


def enter_kernel(toks, cols, noisy, single, restype, table, gain, pair, pair_gain, w_pair, *rest):
    x_out, bias_out, rounded = rest
    rows = noisy.shape[0]
    pair_scaled, _, _ = layer_forward(pair[...].astype(f32), pair_gain[...])
    rounded[...] = pair_scaled.astype(bf16).astype(f32)
    head_count = w_pair.shape[0]
    spread, row_col = pair_weight_rows(w_pair[...], head_count, cols)
    total = jnp.zeros((head_count * cols, rows), f32)
    for j in range(cols):
        column = rounded[pl.ds(j, rows, stride=cols), :].astype(bf16)
        total = total + mm(jnp.where(row_col == j, spread, 0.0).astype(bf16), column, NT)
    bias = total.astype(bf16)
    part = bias_out.shape[1]
    for n in range(bias_out.shape[0]):
        t = n % toks
        bias_out[n] = bias[t * part : (t + 1) * part, :]

    normed_scaled, _, _ = layer_forward(noisy[...].astype(f32), gain[...])
    types = table.shape[0]
    onehot = (lax.broadcasted_iota(jnp.int32, (types, rows), 0) == restype[...]).astype(f32)
    condition = single[...].astype(f32) + mm(onehot.astype(bf16), table[...], TN)
    x_out[...] = (normed_scaled + condition).astype(bf16)


def own_slice(weight, t, own_width):
    if weight.shape[1] == own_width:
        return weight
    return weight.at[:, pl.ds(pl.multiple_of(t * own_width, own_width), own_width)]


def project_kernel(toks, own_width, ids, *rest):
    parts = rest[:toks]
    weights = rest[toks : toks + 3]
    x_out, outs = rest[toks + 3], rest[toks + 4 : toks + 7]
    held, sem = rest[toks + 7 :]
    t = ids[0]
    copies = []
    for k in range(3):
        copy = pltpu.make_async_copy(
            own_slice(weights[k], t, own_width), held.at[k], sem.at[k]
        )
        copy.start()
        copies.append(copy)
    rows = parts[0].shape[0]
    for r in range(toks):
        start = pl.multiple_of(jnp.bitwise_xor(t, r) * rows, rows)
        x_out[pl.ds(start, rows), :] = parts[r][...]
    x = x_out[...]
    for k in range(3):
        copies[k].wait()
        outs[k][...] = jnp.transpose(mm(x, held[k])).astype(bf16)


def attention_kernel(copies, toks, cols, head_width, ids, query, key, value, bias, *rest):
    chain, keymask, chain_weight, weights_out, att_out = rest[:5]
    pieces = rest[5 : 5 + toks]
    t = ids[0]
    own_heads = weights_out.shape[0]
    tokens = query.shape[1]
    rows = tokens // toks
    chain_row = chain[...]
    keep_row = keymask[...].astype(f32)
    line = lax.broadcasted_iota(jnp.int32, (128, tokens), 0)
    facts = jnp.where(line == 0, chain_row.astype(f32), 0.0) + jnp.where(line == 1, keep_row, 0.0)
    for h in range(own_heads):
        weight_row = jnp.zeros((1, tokens), f32)
        for m in range(chain_weight.shape[0]):
            weight_row = jnp.where(chain_row == m, chain_weight[m, t * own_heads + h], weight_row)
        facts = jnp.where(line == 2 + h, weight_row, facts)
    facts = jnp.transpose(facts)
    same = facts[:, 0:1] == chain_row.astype(f32)
    keep = facts[:, 1:2] > 0.0
    scale = head_width ** (-0.5)
    attended = []
    for h in range(own_heads):
        span = slice(h * head_width, (h + 1) * head_width)
        logits = mm(key[span, :], query[span, :], TN) * scale
        line = slice(h * cols, (h + 1) * cols)
        extra = jnp.concatenate(
            [
                jnp.concatenate([bias[c * toks + a, line, :] for c in range(copies)], axis=0)
                for a in range(toks)
            ],
            axis=1,
        ).astype(f32)
        logits = logits + (extra + jnp.where(same, facts[:, 2 + h : 3 + h], 0.0))
        logits = jnp.where(keep, logits, -1e30)
        exponent = jnp.exp(logits - jnp.max(logits, axis=0, keepdims=True))
        weights = exponent / jnp.sum(exponent, axis=0, keepdims=True)
        weights_b = weights.astype(bf16)
        weights_out[h] = weights_b
        attended.append(mm(value[span, :], weights_b))
    att_out[...] = jnp.transpose(jnp.concatenate(attended, axis=0)).astype(bf16)
    for r in range(toks):
        start = pl.multiple_of(jnp.bitwise_xor(t, r) * rows, rows)
        pieces[r][...] = att_out[pl.ds(start, rows), :]


def down_kernel(upstream, w_down, d_hidden):
    d_hidden[...] = mm(upstream[...], w_down[...], NT)


def hidden_kernel(toks, chunk, ids, noisy, upstream, d_hidden, gain, *rest):
    parts = rest[:toks]
    w_out, w_gate, w_up = rest[toks : toks + 3]
    d_res_out, d_res_b_out = rest[toks + 3 : toks + 5]
    d_att_outs = rest[toks + 5 : 2 * toks + 5]
    held_out, held_gate, held_up, sem = rest[2 * toks + 5 :]
    t = ids[0]
    hidden = w_gate.shape[1]
    first = pltpu.make_async_copy(w_out, held_out, sem.at[0])
    first.start()
    copies = []
    for k in range(hidden // chunk):
        span = pl.ds(k * chunk, chunk)
        pair = [
            pltpu.make_async_copy(w.at[:, span], held.at[:, span], sem.at[1 + 2 * k + n])
            for n, (w, held) in enumerate(((w_gate, held_gate), (w_up, held_up)))
        ]
        for copy in pair:
            copy.start()
        copies.append(pair)
    residual = noisy[...].astype(f32)
    first.wait()
    own_width = parts[0].shape[1]
    for r in range(toks):
        start = pl.multiple_of(jnp.bitwise_xor(t, r) * own_width, own_width)
        residual = residual + mm(parts[r][...], held_out[pl.ds(start, own_width), :])
    trans_scaled, trans_hat, trans_inverse = layer_forward(residual, gain[...])
    trans_in = trans_scaled.astype(bf16)
    d_trans = jnp.zeros(residual.shape, f32)
    for k in range(hidden // chunk):
        for copy in copies[k]:
            copy.wait()
        span = slice(k * chunk, (k + 1) * chunk)
        gate = mm(trans_in, held_gate[:, span])
        up = mm(trans_in, held_up[:, span])
        incoming = d_hidden[:, span]
        sigmoid = jax.nn.sigmoid(gate)
        d_up = (incoming * gate * sigmoid).astype(bf16)
        d_gate = (incoming * up * sigmoid * (1.0 + gate * (1.0 - sigmoid))).astype(bf16)
        d_trans = d_trans + mm(d_gate, held_gate[:, span], NT) + mm(d_up, held_up[:, span], NT)
    d_res = upstream[...].astype(f32) + layer_backward(
        d_trans, gain[...], trans_hat, trans_inverse
    )
    d_res_out[...] = d_res
    d_res_b = d_res.astype(bf16)
    d_res_b_out[...] = d_res_b
    for r in range(toks):
        start = pl.multiple_of(jnp.bitwise_xor(t, r) * own_width, own_width)
        d_att_outs[r][...] = mm(held_out[pl.ds(start, own_width), :], d_res_b, NT).astype(bf16)


def backward_kernel(copies, toks, cols, head_width, ids, query, key, value, weights, *rest):
    parts = rest[:toks]
    d_query, d_key, d_value, d_bias, blocks = rest[toks:]
    t = ids[0]
    rows = query.shape[1] // toks
    for r in range(toks):
        blocks[jnp.bitwise_xor(t, r)] = parts[r][...]
    d_att = jnp.concatenate([blocks[a] for a in range(toks)], axis=1)
    scale = head_width ** (-0.5)
    for h in range(weights.shape[0]):
        span = slice(h * head_width, (h + 1) * head_width)
        d_att_h = d_att[span, :]
        weights_b = weights[h]
        d_weights = mm(value[span, :], d_att_h, TN)
        weights_f = weights_b.astype(f32)
        delta = jnp.sum(weights_f * d_weights, axis=0, keepdims=True)
        d_logits_b = (weights_f * (d_weights - delta)).astype(bf16)
        for c in range(copies):
            for a in range(toks):
                d_bias[c * toks + a, h * cols : (h + 1) * cols, :] = d_logits_b[
                    c * cols : (c + 1) * cols, a * rows : (a + 1) * rows
                ]
        d_query[span, :] = (mm(key[span, :], d_logits_b) * scale).astype(bf16)
        d_key[span, :] = (mm(query[span, :], d_logits_b, NT) * scale).astype(bf16)
        d_value[span, :] = mm(d_att_h, weights_b, NT).astype(bf16)


def gradient_kernel(copies, toks, ids, x, att, d_query, d_key, d_value, *rest):
    d_res_parts = rest[:toks]
    weights = rest[toks : toks + 3]
    kept, sent, d_own = rest[toks + 3 : toks + 6]
    d_others = rest[toks + 6 : 2 * toks + 5]
    d_res, wide, narrow, d_inputs, held, sem = rest[2 * toks + 5 :]
    t, c = ids[0], ids[1]
    own_width, tokens = d_query.shape
    rows = tokens // toks
    width = x.shape[1]
    group = copies // toks
    transfers = []
    for k in range(3):
        copy = pltpu.make_async_copy(
            own_slice(weights[k], t, own_width), held.at[k], sem.at[k]
        )
        copy.start()
        transfers.append(copy)
    for r in range(toks):
        start = pl.multiple_of(jnp.bitwise_xor(t, r) * rows, rows)
        d_res[pl.ds(start, rows), :] = d_res_parts[r][...]
    for k, part in enumerate((d_query, d_key, d_value)):
        wide[k] = mm(part[...], x[...])
    narrow[...] = mm(d_res[...], att[...], TN)
    cut, depth = width // copies, width // toks
    near = low_bits(c, 2)
    for side, out in ((near, kept), (1 - near, sent)):
        for q in range(copies // 2):
            h = 2 * q // group
            first = pl.multiple_of((2 * q - h * group + side) * cut, 8)
            for k in range(3):
                out[q, k, :, :depth] = wide[
                    k, pl.ds(first, cut), h * depth : (h + 1) * depth
                ].astype(bf16)
            first = pl.multiple_of((2 * q + side) * cut, 8)
            out[q, 3, :, :own_width] = narrow[pl.ds(first, cut), :].astype(bf16)
            if out.shape[3] > own_width:
                out[q, :, :, own_width:] = jnp.zeros(
                    (4, cut, out.shape[3] - own_width), bf16
                )
    total = None
    for k, part in enumerate((d_query, d_key, d_value)):
        transfers[k].wait()
        term = mm(held[k], part[...])
        total = term if total is None else total + term
    for a in range(toks):
        d_inputs[a] = total[:, a * rows : (a + 1) * rows]
    d_own[...] = d_inputs[t]
    for r in range(1, toks):
        d_others[r - 1][...] = d_inputs[jnp.bitwise_xor(t, r)].astype(bf16)


def halve_kernel(toks, copies, ids, kept, got, d_own, *rest):
    others = rest[: toks - 1]
    kept_out, sent_out, total_ref = rest[toks - 1 :]
    total = d_own[...]
    for part in others:
        total = total + part[...].astype(f32)
    total_ref[...] = total
    bit = low_bits(ids[1] // 2, 2)
    rows = total.shape[1]
    cut = total.shape[0] // copies
    per = kept_out.shape[3] // rows
    for q in range(kept_out.shape[0]):
        for side, out in ((bit, kept_out), (1 - bit, sent_out)):
            k = 2 * q + side
            out[q, :4] = (kept[k].astype(f32) + got[k].astype(f32)).astype(bf16)
            if per > 2:
                out[q, 4, :, 2 * rows :] = jnp.zeros((cut, out.shape[3] - 2 * rows), bf16)
            for low in range(2):
                start = pl.multiple_of((q * 4 + side * 2 + low) * cut, 8)
                lane = low % per * rows
                out[q, 4 + low // per, :, lane : lane + rows] = total_ref[
                    pl.ds(start, cut), :
                ].astype(bf16)


def spread_kernel(near, ids, kept, got, *outs):
    z = ids[1] // near
    for r, out in enumerate(outs):
        k = jnp.bitwise_xor(z, r)
        out[...] = (kept[k].astype(f32) + got[k].astype(f32)).astype(bf16)


def collect_kernel(count, ids, *refs):
    parts, (moved, final, kept, sent, halves) = refs[:count], refs[count:]

    def total(k):
        whole = parts[0][k].astype(f32)
        for part in parts[1:]:
            whole = whole + part[k].astype(f32)
        return whole

    for k in range(3):
        moved[k] = total(k).astype(bf16)
    final[...] = total(3)[:, : final.shape[1]]
    rows = kept.shape[1]
    per = parts[0].shape[2] // rows
    for low in range(2):
        lane = low % per * rows
        halves[low] = total(4 + low // per)[:, lane : lane + rows].astype(bf16)
    bit = low_bits(ids[1], 2)
    kept[...] = halves[bit]
    sent[...] = halves[1 - bit]


def finish_kernel(moved, kept_single, got_single, first, second, third, single):
    for k, out in enumerate((first, second, third)):
        out[...] = moved[k][:, : out.shape[1]].astype(f32)
    single[...] = kept_single[...].astype(f32) + got_single[...].astype(f32)


def exit_kernel(toks, noisy, gain, d_res, d_own, *rest):
    others, (grad_noisy,) = rest[: toks - 1], rest[toks - 1 :]
    total = d_own[...]
    for part in others:
        total = total + part[...].astype(f32)
    _, noisy_hat, noisy_inverse = layer_forward(noisy[...].astype(f32), gain[...])
    grad_noisy[...] = (
        d_res[...] + layer_backward(jnp.transpose(total), gain[...], noisy_hat, noisy_inverse)
    ).astype(bf16)


def pair_kernel(toks, cols, pair, gain, w_pair, parts, grad_pair, weight_grad, *scratch):
    rounded, spread_out = scratch
    head_count = w_pair.shape[0]
    rows = parts.shape[2]
    sums = []
    for t in range(toks):
        total = parts[t].astype(f32)
        for n in range(t + toks, parts.shape[0], toks):
            total = total + parts[n].astype(f32)
        sums.append(total)
    grad = jnp.concatenate(sums, axis=0)
    pair_scaled, pair_hat, pair_inverse = layer_forward(pair[...].astype(f32), gain[...])
    rounded[...] = pair_scaled.astype(bf16).astype(f32)
    spread, row_col = pair_weight_rows(w_pair[...], head_count, cols)
    grad_b = grad.astype(bf16)
    turned = jnp.transpose(grad).astype(bf16)
    sums = jnp.zeros(spread.shape, f32)
    for j in range(cols):
        here = row_col == j
        column = rounded[pl.ds(j, rows, stride=cols), :].astype(bf16)
        sums = sums + jnp.where(here, mm(grad_b, column), 0.0)
        spread_out[pl.ds(j, rows, stride=cols), :] = mm(
            turned, jnp.where(here, spread, 0.0).astype(bf16)
        )
    grad_pair[...] = layer_backward(
        spread_out[...], gain[...], pair_hat, pair_inverse
    ).astype(bf16)
    for h in range(head_count):
        line = jnp.sum(sums[h * cols : (h + 1) * cols, :], axis=0, keepdims=True)
        for n in range(weight_grad.shape[0]):
            weight_grad[n, h : h + 1, :] = line


def swap_copy(value, mask):
    size = lax.axis_size("copy")
    return lax.ppermute(value, "copy", [(i, i ^ mask) for i in range(size)])


def swap_tok(value, mask):
    size = lax.axis_size("tok")
    return lax.ppermute(value, "tok", [(i, i ^ mask) for i in range(size)])


def exchange(value):
    return lax.all_to_all(value, ("copy", "tok"), 0, 0)


def per_device(
    noisy,
    single,
    pair,
    restype,
    chain,
    keymask,
    restype_table,
    norm_gain,
    pair_gain,
    trans_gain,
    w_query,
    w_key,
    w_value,
    w_out,
    w_pair,
    chain_weight,
    w_hidden_gate,
    w_hidden_up,
    w_down,
    cotangent,
):
    copies = lax.axis_size("copy")
    toks = lax.axis_size("tok")
    _, rows, width = noisy.shape
    cols = pair.shape[1]
    channels = pair.shape[2]
    heads = w_pair.shape[1]
    head_width = width // heads
    own_heads = heads // toks
    own_width = own_heads * head_width
    tokens = rows * toks
    hidden = w_down.shape[0]
    near = 4
    far = copies // near
    cut = width // copies
    lanes = max(own_width, rows)
    devices = copies * toks
    ids = jnp.stack([lax.axis_index("tok"), lax.axis_index("copy")]).astype(jnp.int32)
    where_am_i = (ids, SMEM)
    noisy2 = (noisy.reshape(rows, width), "fetch")
    upstream = (cotangent.reshape(rows, width), "fetch")
    pair2 = (pair.reshape(rows * cols, channels), "fetch")
    norm_gain2 = (norm_gain.reshape(1, width), "fetch")
    trans_gain2 = (trans_gain.reshape(1, width), "fetch")
    pair_gain2 = (pair_gain.reshape(1, channels), "fetch")
    w_pair2 = (w_pair.T, "fetch")

    x_own, bias_out = call(
        functools.partial(enter_kernel, toks, cols),
        "enter",
        [noisy2, (single, "fetch"), (restype.reshape(1, rows), "fetch"), (restype_table, "fetch")]
        + [norm_gain2, pair2, pair_gain2, w_pair2],
        [((rows, width), bf16), ((devices, own_heads * cols, rows), bf16)],
        [VMEM((rows * cols, channels), f32)],
        flops=2 * heads * cols * rows * channels * cols,
    )
    x_parts = [x_own] + [swap_tok(x_own, r) for r in range(1, toks)]
    bias = exchange(bias_out)

    weights3 = [w_query, w_key, w_value]
    if own_width % 128:
        weights3 = [
            lax.dynamic_slice_in_dim(w, ids[0] * own_width, own_width, axis=1) for w in weights3
        ]
    x, query, key, value = call(
        functools.partial(project_kernel, toks, own_width),
        "project",
        [where_am_i] + x_parts + [(w, pltpu.HBM) for w in weights3],
        [((tokens, width), bf16)] + [((own_width, tokens), bf16)] * 3,
        [VMEM((3, width, own_width), bf16), pltpu.SemaphoreType.DMA((3,))],
        flops=6 * tokens * width * own_width,
    )
    done = call(
        functools.partial(attention_kernel, copies, toks, cols, head_width),
        "attention",
        [where_am_i, query, key, value, bias]
        + [(chain.reshape(1, tokens), "fetch"), (keymask.reshape(1, tokens), "fetch")]
        + [(chain_weight, SMEM)],
        [((own_heads, tokens, tokens), bf16), ((tokens, own_width), bf16)]
        + [((rows, own_width), bf16)] * toks,
        flops=4 * tokens * tokens * own_width,
    )
    weights, att, pieces = done[0], done[1], done[2:]
    att_parts = [pieces[0]] + [swap_tok(pieces[r], r) for r in range(1, toks)]

    (d_hidden,) = call(
        down_kernel,
        "down",
        [upstream, (w_down, "fetch")],
        [((rows, hidden), f32)],
        flops=2 * rows * hidden * width,
    )
    chunk = hidden // 3
    after = call(
        functools.partial(hidden_kernel, toks, chunk),
        "hidden",
        [where_am_i, noisy2, upstream, d_hidden, trans_gain2]
        + att_parts
        + [(w_out, ANY), (w_hidden_gate, ANY), (w_hidden_up, ANY)],
        [((rows, width), f32), ((rows, width), bf16)] + [((own_width, rows), bf16)] * toks,
        [
            VMEM((width, width), bf16),
            VMEM((width, hidden), bf16),
            VMEM((width, hidden), bf16),
            pltpu.SemaphoreType.DMA((7,)),
        ],
        flops=2 * rows * width * (2 * width + 4 * hidden),
    )
    d_res, d_res_b, d_att = after[0], after[1], after[2:]
    d_att_parts = [d_att[0]] + [swap_tok(d_att[r], r) for r in range(1, toks)]
    d_res_parts = [d_res_b] + [swap_tok(d_res_b, r) for r in range(1, toks)]

    d_query, d_key, d_value, d_bias = call(
        functools.partial(backward_kernel, copies, toks, cols, head_width),
        "backward",
        [where_am_i, query, key, value, weights] + d_att_parts,
        [((own_width, tokens), bf16)] * 3 + [((devices, own_heads * cols, rows), bf16)],
        [VMEM((toks, own_width, rows), bf16)],
        flops=8 * tokens * tokens * own_width,
    )
    found = call(
        functools.partial(gradient_kernel, copies, toks),
        "gradient",
        [where_am_i, x, att, d_query, d_key, d_value]
        + d_res_parts
        + [(w, ANY) for w in weights3],
        [((copies // 2, 4, cut, lanes), bf16)] * 2
        + [((width, rows), f32)]
        + [((width, rows), bf16)] * (toks - 1),
        [
            VMEM((tokens, width), bf16),
            VMEM((3, own_width, width), f32),
            VMEM((width, own_width), f32),
            VMEM((toks, width, rows), f32),
            VMEM((3, width, own_width), bf16),
            pltpu.SemaphoreType.DMA((3,)),
        ],
        flops=14 * tokens * width * own_width,
    )
    kept, sent, d_own = found[:3]
    d_others = [swap_tok(found[2 + r], r) for r in range(1, toks)]
    got = swap_copy(sent, 1)

    slots = 4 + (1 if lanes >= 2 * rows else 2)
    kept, sent = call(
        functools.partial(halve_kernel, toks, copies),
        "halve",
        [where_am_i, kept, got, d_own] + d_others,
        [((far, slots, cut, lanes), bf16)] * 2,
        [VMEM((width, rows), f32)],
    )
    got = swap_copy(sent, 2)
    d_bias = exchange(d_bias)
    (grad_noisy,) = call(
        functools.partial(exit_kernel, toks),
        "exit",
        [noisy2, norm_gain2, d_res, d_own] + d_others,
        [((rows, width), bf16)],
    )
    grad_pair, weight_grad = call(
        functools.partial(pair_kernel, toks, cols),
        "pair",
        [pair2, pair_gain2, w_pair2, d_bias],
        [((rows * cols, channels), bf16), ((devices, heads, channels), f32)],
        [VMEM((rows * cols, channels), f32)] * 2,
        flops=4 * heads * cols * rows * channels * cols,
    )
    weight_grad = jnp.sum(exchange(weight_grad), axis=0)

    spread = call(
        functools.partial(spread_kernel, near),
        "spread",
        [where_am_i, kept, got],
        [((slots, cut, lanes), bf16)] * far,
    )
    arrived = [spread[0]] + [swap_copy(spread[r], r * near) for r in range(1, far)]
    moved, grad_out, last_kept, last_sent = call(
        functools.partial(collect_kernel, far),
        "collect",
        [where_am_i] + arrived,
        [((3, cut, lanes), bf16), ((cut, own_width), f32)] + [((cut, rows), bf16)] * 2,
        [VMEM((2, cut, rows), bf16)],
    )
    last_got = swap_copy(last_sent, 1)
    group = copies // toks
    pairs = []
    for c in range(copies):
        for t in range(toks):
            pairs.append((c * toks + t, (t * group + c % group) * toks + c // group))
    moved = lax.ppermute(moved, ("copy", "tok"), pairs)
    grad_query, grad_key, grad_value, grad_single = call(
        finish_kernel,
        "finish",
        [moved, last_kept, last_got],
        [((cut, own_width), f32)] * 3 + [((cut, rows), f32)],
    )
    return (
        grad_noisy[None],
        grad_single.T,
        grad_pair.reshape(rows, cols, channels),
        grad_query.T,
        grad_key.T,
        grad_value.T,
        grad_out.T,
        weight_grad.T,
    )


def solution(mesh):
    placed = (
        P("copy", "tok", None),
        P("tok", None),
        P("tok", "copy", None),
        P("tok"),
    ) + (P(),) * 15 + (P("copy", "tok", None),)
    return jax.shard_map(
        per_device,
        mesh=mesh,
        in_specs=placed,
        out_specs=(
            P("copy", "tok", None),
            P("tok", "copy"),
            P("tok", "copy", None),
            P("tok", "copy"),
            P("tok", "copy"),
            P("tok", "copy"),
            P("tok", "copy"),
            P(),
        ),
        check_vma=False,
    )
```

```python
import functools

import jax
import jax.numpy as jnp
from jax import lax
from jax.experimental import pallas as pl
from jax.experimental.pallas import tpu as pltpu
from jax.sharding import PartitionSpec as P

epsilon = 1e-05
f32 = jnp.float32
bf16 = jnp.bfloat16
VMEM, SMEM, ANY = pltpu.VMEM, pltpu.SMEM, pl.ANY
MIB = 1 << 20


def layer_forward(values, scales):
    average = jnp.mean(values, axis=-1, keepdims=True)
    centred = values - average
    inverse = lax.rsqrt(jnp.mean(centred * centred, axis=-1, keepdims=True) + epsilon)
    normed = centred * inverse
    return (normed * scales, normed, inverse)


def layer_backward(upstream, scales, normed, inverse):
    scaled = upstream * scales
    first_moment = jnp.mean(scaled, axis=-1, keepdims=True)
    second_moment = jnp.mean(scaled * normed, axis=-1, keepdims=True)
    return inverse * (scaled - first_moment - normed * second_moment)


NN = ((1,), (0,))
NT = ((1,), (1,))
TN = ((0,), (0,))


def mm(left, right, dims=NN):
    return lax.dot_general(left, right, (dims, ((), ())), preferred_element_type=f32)


def call(body, name, inputs, outs, scratch=(), flops=0, limit=16):
    arrays, specs, moved, fetched = [], [], 0, []
    for item in inputs:
        array, space = item if isinstance(item, tuple) else (item, VMEM)
        if space == "fetch":
            fetched.append(len(arrays))
            space = pltpu.HBM
        arrays.append(array)
        specs.append(pl.BlockSpec(memory_space=space))
        moved += array.size * array.dtype.itemsize
    for shape, kind in outs:
        size = jnp.dtype(kind).itemsize
        for extent in shape:
            size *= extent
        moved += size
    extra = [VMEM(arrays[k].shape, arrays[k].dtype) for k in fetched]
    if fetched:
        extra.append(pltpu.SemaphoreType.DMA((len(fetched),)))

    def whole(*refs):
        refs = list(refs)
        if fetched:
            held, sem = refs[-1 - len(fetched) : -1], refs[-1]
            refs = refs[: -1 - len(fetched)]
            transfers = []
            for n, k in enumerate(fetched):
                transfer = pltpu.make_async_copy(refs[k], held[n], sem.at[n])
                transfer.start()
                transfers.append(transfer)
                refs[k] = held[n]
            for transfer in transfers:
                transfer.wait()
        body(*refs)

    return pl.pallas_call(
        whole,
        name=name,
        out_shape=[jax.ShapeDtypeStruct(shape, kind) for shape, kind in outs],
        in_specs=specs,
        out_specs=[pl.BlockSpec(memory_space=VMEM)] * len(outs),
        scratch_shapes=list(scratch) + extra,
        compiler_params=pltpu.CompilerParams(vmem_limit_bytes=limit * MIB),
        cost_estimate=pl.CostEstimate(flops=flops, bytes_accessed=moved, transcendentals=0),
    )(*arrays)


def low_bits(index, size):
    return jnp.bitwise_and(index, size - 1)


def pair_weight_rows(w_pair, head_count, cols):
    rows = head_count * cols
    shift = cols.bit_length() - 1
    head = lax.shift_right_logical(
        lax.broadcasted_iota(jnp.int32, (rows, head_count), 0), jnp.int32(shift)
    )
    pick = (head == lax.broadcasted_iota(jnp.int32, (rows, head_count), 1)).astype(f32)
    spread = mm(pick.astype(bf16), w_pair)
    row_col = low_bits(lax.broadcasted_iota(jnp.int32, spread.shape, 0), cols)
    return spread, row_col


def enter_kernel(noisy, single, restype, table, gain, x_out):
    rows = noisy.shape[0]
    normed_scaled, _, _ = layer_forward(noisy[...].astype(f32), gain[...])
    types = table.shape[0]
    onehot = (lax.broadcasted_iota(jnp.int32, (types, rows), 0) == restype[...]).astype(f32)
    condition = single[...].astype(f32) + mm(onehot.astype(bf16), table[...], TN)
    x_out[...] = (normed_scaled + condition).astype(bf16)


def bias_kernel(toks, cols, pair, pair_gain, w_pair, bias_out, rounded):
    rows = bias_out.shape[2]
    pair_scaled, _, _ = layer_forward(pair[...].astype(f32), pair_gain[...])
    rounded[...] = pair_scaled.astype(bf16).astype(f32)
    head_count = w_pair.shape[0]
    spread, row_col = pair_weight_rows(w_pair[...], head_count, cols)
    total = jnp.zeros((head_count * cols, rows), f32)
    for j in range(cols):
        column = rounded[pl.ds(j, rows, stride=cols), :].astype(bf16)
        total = total + mm(jnp.where(row_col == j, spread, 0.0).astype(bf16), column, NT)
    bias = total.astype(bf16)
    part = bias_out.shape[1]
    for n in range(bias_out.shape[0]):
        t = n % toks
        bias_out[n] = bias[t * part : (t + 1) * part, :]


def own_slice(weight, t, own_width):
    if weight.shape[1] == own_width:
        return weight
    return weight.at[:, pl.ds(pl.multiple_of(t * own_width, own_width), own_width)]


def stage_kernel(own_heads, ids, chain, keymask, chain_weight, *rest):
    weights, (slices, facts_out, chain_out, sem) = rest[:3], rest[3:]
    t = ids[0]
    own_width = slices.shape[2]
    transfers = []
    for k in range(3):
        transfer = pltpu.make_async_copy(
            own_slice(weights[k], t, own_width), slices.at[k], sem.at[k]
        )
        transfer.start()
        transfers.append(transfer)
    chain_row = chain[...]
    tokens = chain_row.shape[1]
    keep_row = keymask[...].astype(f32)
    line = lax.broadcasted_iota(jnp.int32, (128, tokens), 0)
    facts = jnp.where(line == 0, chain_row.astype(f32), 0.0) + jnp.where(line == 1, keep_row, 0.0)
    for h in range(own_heads):
        weight_row = jnp.zeros((1, tokens), f32)
        for m in range(chain_weight.shape[0]):
            weight_row = jnp.where(chain_row == m, chain_weight[m, t * own_heads + h], weight_row)
        facts = jnp.where(line == 2 + h, weight_row, facts)
    facts_out[...] = jnp.transpose(facts)
    chain_out[...] = chain_row.astype(f32)
    for transfer in transfers:
        transfer.wait()


def project_kernel(toks, ids, slices, *rest):
    parts = rest[:toks]
    x_out, outs = rest[toks], rest[toks + 1 :]
    t = ids[0]
    rows = parts[0].shape[0]
    for r in range(toks):
        start = pl.multiple_of(jnp.bitwise_xor(t, r) * rows, rows)
        x_out[pl.ds(start, rows), :] = parts[r][...]
    x = x_out[...]
    for k in range(3):
        outs[k][...] = jnp.transpose(mm(x, slices[k])).astype(bf16)


def attention_kernel(copies, toks, cols, head_width, ids, query, key, value, own, other, *rest):
    facts, chain, weights_out, att_out = rest[:4]
    pieces, bias = rest[4 : 4 + toks], rest[4 + toks]
    t = ids[0]
    core = low_bits(ids[1], 2)
    bias[core] = own[...]
    bias[1 - core] = other[...]
    own_heads = weights_out.shape[0]
    tokens = query.shape[1]
    rows = tokens // toks
    same = facts[:, 0:1] == chain[...]
    keep = facts[:, 1:2] > 0.0
    scale = head_width ** (-0.5)
    attended = []
    for h in range(own_heads):
        span = slice(h * head_width, (h + 1) * head_width)
        logits = mm(key[span, :], query[span, :], TN) * scale
        line = slice(h * cols, (h + 1) * cols)
        extra = jnp.concatenate(
            [
                jnp.concatenate(
                    [bias[c % 2, c // 2 * toks + a, line, :] for c in range(copies)], axis=0
                )
                for a in range(toks)
            ],
            axis=1,
        ).astype(f32)
        logits = logits + (extra + jnp.where(same, facts[:, 2 + h : 3 + h], 0.0))
        logits = jnp.where(keep, logits, -1e30)
        exponent = jnp.exp(logits - jnp.max(logits, axis=0, keepdims=True))
        weights = exponent / jnp.sum(exponent, axis=0, keepdims=True)
        weights_b = weights.astype(bf16)
        weights_out[h] = weights_b
        attended.append(mm(value[span, :], weights_b))
    att_out[...] = jnp.transpose(jnp.concatenate(attended, axis=0)).astype(bf16)
    for r in range(toks):
        start = pl.multiple_of(jnp.bitwise_xor(t, r) * rows, rows)
        pieces[r][...] = att_out[pl.ds(start, rows), :]


def down_kernel(upstream, w_down, noisy, gain, d_hidden, upstream_out, noisy_out, gain_out):
    d_hidden[...] = mm(upstream[...], w_down[...], NT)
    upstream_out[...] = upstream[...]
    noisy_out[...] = noisy[...]
    gain_out[...] = gain[...]


def hidden_kernel(toks, chunk, ids, noisy, upstream, d_hidden, gain, *rest):
    parts = rest[:toks]
    w_out, w_gate, w_up = rest[toks : toks + 3]
    d_res_out, d_res_b_out = rest[toks + 3 : toks + 5]
    d_att_outs = rest[toks + 5 : 2 * toks + 5]
    held_out, held_gate, held_up, sem = rest[2 * toks + 5 :]
    t = ids[0]
    hidden = w_gate.shape[1]
    first = pltpu.make_async_copy(w_out, held_out, sem.at[0])
    first.start()
    copies = []
    for k in range(hidden // chunk):
        span = pl.ds(k * chunk, chunk)
        pair = [
            pltpu.make_async_copy(w.at[:, span], held.at[:, span], sem.at[1 + 2 * k + n])
            for n, (w, held) in enumerate(((w_gate, held_gate), (w_up, held_up)))
        ]
        for copy in pair:
            copy.start()
        copies.append(pair)
    residual = noisy[...].astype(f32)
    first.wait()
    own_width = parts[0].shape[1]
    for r in range(toks):
        start = pl.multiple_of(jnp.bitwise_xor(t, r) * own_width, own_width)
        residual = residual + mm(parts[r][...], held_out[pl.ds(start, own_width), :])
    trans_scaled, trans_hat, trans_inverse = layer_forward(residual, gain[...])
    trans_in = trans_scaled.astype(bf16)
    d_trans = jnp.zeros(residual.shape, f32)
    for k in range(hidden // chunk):
        for copy in copies[k]:
            copy.wait()
        span = slice(k * chunk, (k + 1) * chunk)
        gate = mm(trans_in, held_gate[:, span])
        up = mm(trans_in, held_up[:, span])
        incoming = d_hidden[:, span]
        sigmoid = jax.nn.sigmoid(gate)
        d_up = (incoming * gate * sigmoid).astype(bf16)
        d_gate = (incoming * up * sigmoid * (1.0 + gate * (1.0 - sigmoid))).astype(bf16)
        d_trans = d_trans + mm(d_gate, held_gate[:, span], NT) + mm(d_up, held_up[:, span], NT)
    d_res = upstream[...].astype(f32) + layer_backward(
        d_trans, gain[...], trans_hat, trans_inverse
    )
    d_res_out[...] = d_res
    d_res_b = d_res.astype(bf16)
    d_res_b_out[...] = d_res_b
    for r in range(toks):
        start = pl.multiple_of(jnp.bitwise_xor(t, r) * own_width, own_width)
        d_att_outs[r][...] = mm(held_out[pl.ds(start, own_width), :], d_res_b, NT).astype(bf16)


def backward_kernel(copies, toks, cols, head_width, ids, query, key, value, weights, *rest):
    parts = rest[:toks]
    d_query, d_key, d_value, bias_kept, bias_sent, blocks, d_logits = rest[toks:]
    t = ids[0]
    core = low_bits(ids[1], 2)
    for r in range(toks):
        blocks[jnp.bitwise_xor(t, r)] = parts[r][...]
    d_att = jnp.concatenate([blocks[a] for a in range(toks)], axis=1)
    scale = head_width ** (-0.5)
    for h in range(weights.shape[0]):
        span = slice(h * head_width, (h + 1) * head_width)
        d_att_h = d_att[span, :]
        weights_b = weights[h]
        d_weights = mm(value[span, :], d_att_h, TN)
        weights_f = weights_b.astype(f32)
        delta = jnp.sum(weights_f * d_weights, axis=0, keepdims=True)
        d_logits_b = (weights_f * (d_weights - delta)).astype(bf16)
        d_logits[...] = d_logits_b
        for q in range(copies // 2):
            for side, out in ((core, bias_kept), (1 - core, bias_sent)):
                start = pl.multiple_of((2 * q + side) * cols, cols)
                out[q, h * cols : (h + 1) * cols, :] = d_logits[pl.ds(start, cols), :]
        d_query[span, :] = (mm(key[span, :], d_logits_b) * scale).astype(bf16)
        d_key[span, :] = (mm(query[span, :], d_logits_b, NT) * scale).astype(bf16)
        d_value[span, :] = mm(d_att_h, weights_b, NT).astype(bf16)


def cut_wide(copies, toks, core, slot, grad, kept, sent):
    group = copies // toks
    cut, depth = grad.shape[1] // copies, grad.shape[1] // toks
    for side, out in ((core, kept), (1 - core, sent)):
        for q in range(copies // 2):
            h = 2 * q // group
            first = pl.multiple_of((2 * q - h * group + side) * cut, 8)
            out[q, slot] = grad[pl.ds(first, cut), h * depth : (h + 1) * depth].astype(bf16)


def first_kernel(copies, toks, ids, x, att, d_value, *rest):
    d_res_parts, (kept, sent, d_res, wide, narrow) = rest[:toks], rest[toks:]
    t, core = ids[0], low_bits(ids[1], 2)
    rows = d_res_parts[0].shape[0]
    for r in range(toks):
        start = pl.multiple_of(jnp.bitwise_xor(t, r) * rows, rows)
        d_res[pl.ds(start, rows), :] = d_res_parts[r][...]
    wide[...] = mm(d_value[...], x[...])
    cut_wide(copies, toks, core, 0, wide, kept, sent)
    narrow[...] = mm(d_res[...], att[...], TN)
    cut = narrow.shape[0] // copies
    for side, out in ((core, kept), (1 - core, sent)):
        for q in range(copies // 2):
            first = pl.multiple_of((2 * q + side) * cut, 8)
            out[q, 1] = narrow[pl.ds(first, cut), :].astype(bf16)


def second_kernel(copies, toks, ids, slices, x, d_query, d_key, d_value, *rest):
    kept, sent, d_own = rest[:3]
    d_others, (wide, d_inputs) = rest[3 : 2 + toks], rest[2 + toks :]
    t, core = ids[0], low_bits(ids[1], 2)
    rows = d_own.shape[1]
    for k, part in enumerate((d_query, d_key)):
        wide[...] = mm(part[...], x[...])
        cut_wide(copies, toks, core, k, wide, kept, sent)
    total = mm(slices[0], d_query[...]) + mm(slices[1], d_key[...])
    total = total + mm(slices[2], d_value[...])
    for a in range(toks):
        d_inputs[a] = total[:, a * rows : (a + 1) * rows]
    d_own[...] = d_inputs[t]
    for r in range(1, toks):
        d_others[r - 1][...] = d_inputs[jnp.bitwise_xor(t, r)].astype(bf16)


def halve_kernel(divide, count, ids, *refs):
    ins, outs = refs[: 2 * count], refs[2 * count :]
    bit = low_bits(ids[1] // divide, 2)
    for n in range(count):
        kept, got = ins[2 * n : 2 * n + 2]
        for q in range(kept.shape[0] // 2):
            for side, out in ((bit, outs[2 * n]), (1 - bit, outs[2 * n + 1])):
                k = 2 * q + side
                out[q] = (kept[k].astype(f32) + got[k].astype(f32)).astype(bf16)


def halve_single_kernel(toks, copies, ids, kept, got, d_own, *rest):
    others = rest[: toks - 1]
    kept_out, sent_out, single_kept, single_sent, total_ref = rest[toks - 1 :]
    total = d_own[...]
    for part in others:
        total = total + part[...].astype(f32)
    total_ref[...] = total
    bit = low_bits(ids[1] // 2, 2)
    cut = total.shape[0] // copies
    for q in range(kept_out.shape[0]):
        for side, out, single in ((bit, kept_out, single_kept), (1 - bit, sent_out, single_sent)):
            k = 2 * q + side
            out[q] = (kept[k].astype(f32) + got[k].astype(f32)).astype(bf16)
            for low in range(2):
                start = pl.multiple_of((q * 4 + side * 2 + low) * cut, 8)
                single[q, low] = total_ref[pl.ds(start, cut), :].astype(bf16)


def last_first_kernel(toks, ids, kept, got, bias_kept, bias_got, moved, final, *rest):
    pieces, blocks = rest[:toks], rest[toks]
    moved[...] = (kept[0, 0].astype(f32) + got[0, 0].astype(f32)).astype(bf16)
    final[...] = kept[0, 1].astype(f32) + got[0, 1].astype(f32)
    total = bias_kept[0].astype(f32) + bias_got[0].astype(f32)
    rows = blocks.shape[2]
    for a in range(toks):
        blocks[a] = total[:, a * rows : (a + 1) * rows].astype(bf16)
    for r in range(toks):
        pieces[r][...] = blocks[jnp.bitwise_xor(ids[0], r)]


def last_second_kernel(ids, kept, got, single_kept, single_got, moved, kept_out, sent_out, halves):
    moved[...] = (kept[0].astype(f32) + got[0].astype(f32)).astype(bf16)
    halves[...] = (single_kept[0].astype(f32) + single_got[0].astype(f32)).astype(bf16)
    core = low_bits(ids[1], 2)
    kept_out[...] = halves[core]
    sent_out[...] = halves[1 - core]


def finish_kernel(moved_a, moved_b, kept_single, got_single, first, second, third, single):
    first[...] = moved_b[0].astype(f32)
    second[...] = moved_b[1].astype(f32)
    third[...] = moved_a[...].astype(f32)
    single[...] = kept_single[...].astype(f32) + got_single[...].astype(f32)


def exit_kernel(toks, noisy, gain, d_res, d_own, *rest):
    others, (grad_noisy,) = rest[: toks - 1], rest[toks - 1 :]
    total = d_own[...]
    for part in others:
        total = total + part[...].astype(f32)
    _, noisy_hat, noisy_inverse = layer_forward(noisy[...].astype(f32), gain[...])
    grad_noisy[...] = (
        d_res[...] + layer_backward(jnp.transpose(total), gain[...], noisy_hat, noisy_inverse)
    ).astype(bf16)


def pair_kernel(toks, cols, ids, pair, gain, w_pair, *rest):
    parts, (grad_pair, weight_grad, rounded, spread_out, grads) = rest[:toks], rest[toks:]
    head_count = w_pair.shape[0]
    part_rows, rows = parts[0].shape
    for r in range(toks):
        start = pl.multiple_of(jnp.bitwise_xor(ids[0], r) * part_rows, part_rows)
        grads[pl.ds(start, part_rows), :] = parts[r][...].astype(f32)
    grad = grads[...]
    pair_scaled, pair_hat, pair_inverse = layer_forward(pair[...].astype(f32), gain[...])
    rounded[...] = pair_scaled.astype(bf16).astype(f32)
    spread, row_col = pair_weight_rows(w_pair[...], head_count, cols)
    grad_b = grad.astype(bf16)
    turned = jnp.transpose(grad).astype(bf16)
    sums = jnp.zeros(spread.shape, f32)
    for j in range(cols):
        here = row_col == j
        column = rounded[pl.ds(j, rows, stride=cols), :].astype(bf16)
        sums = sums + jnp.where(here, mm(grad_b, column), 0.0)
        spread_out[pl.ds(j, rows, stride=cols), :] = mm(
            turned, jnp.where(here, spread, 0.0).astype(bf16)
        )
    grad_pair[...] = layer_backward(
        spread_out[...], gain[...], pair_hat, pair_inverse
    ).astype(bf16)
    for h in range(head_count):
        line = jnp.sum(sums[h * cols : (h + 1) * cols, :], axis=0, keepdims=True)
        for n in range(weight_grad.shape[0]):
            weight_grad[n, h : h + 1, :] = line


def swap_copy(value, mask):
    size = lax.axis_size("copy")
    return lax.ppermute(value, "copy", [(i, i ^ mask) for i in range(size)])


def swap_tok(value, mask):
    size = lax.axis_size("tok")
    return lax.ppermute(value, "tok", [(i, i ^ mask) for i in range(size)])


def exchange(value, groups=None):
    return lax.all_to_all(value, ("copy", "tok"), 0, 0, axis_index_groups=groups)


def after(value, *earlier):
    return lax.optimization_barrier((value,) + earlier)[0]


def per_device(
    noisy,
    single,
    pair,
    restype,
    chain,
    keymask,
    restype_table,
    norm_gain,
    pair_gain,
    trans_gain,
    w_query,
    w_key,
    w_value,
    w_out,
    w_pair,
    chain_weight,
    w_hidden_gate,
    w_hidden_up,
    w_down,
    cotangent,
):
    copies = lax.axis_size("copy")
    toks = lax.axis_size("tok")
    _, rows, width = noisy.shape
    cols = pair.shape[1]
    channels = pair.shape[2]
    heads = w_pair.shape[1]
    head_width = width // heads
    own_heads = heads // toks
    own_width = own_heads * head_width
    tokens = rows * toks
    hidden = w_down.shape[0]
    cut = width // copies
    devices = copies * toks
    ids = jnp.stack([lax.axis_index("tok"), lax.axis_index("copy")]).astype(jnp.int32)
    where_am_i = (ids, SMEM)
    noisy2 = noisy.reshape(rows, width)
    pair2 = pair.reshape(rows * cols, channels)
    pair_gain2 = pair_gain.reshape(1, channels)
    norm_gain2 = norm_gain.reshape(1, width)

    (x_own,) = call(
        enter_kernel,
        "enter",
        [(array, "fetch") for array in (noisy2, single, restype.reshape(1, rows), restype_table)]
        + [(norm_gain2, "fetch")],
        [((rows, width), bf16)],
        limit=60,
    )
    x_parts = [x_own] + [swap_tok(x_own, r) for r in range(1, toks)]
    (bias_out,) = call(
        functools.partial(bias_kernel, toks, cols),
        "bias",
        [(pair2, "fetch"), (pair_gain2, "fetch"), (w_pair.T, "fetch")],
        [((devices // 2, own_heads * cols, rows), bf16)],
        [VMEM((rows * cols, channels), f32)],
        flops=2 * heads * cols * rows * channels * cols,
        limit=60,
    )
    groups = [
        [(2 * k + core) * toks + t for k in range(copies // 2) for t in range(toks)]
        for core in range(2)
    ]
    bias_own = exchange(after(bias_out, *x_parts[1:]), groups)
    bias_other = swap_copy(bias_own, 1)

    weights3 = [w_query, w_key, w_value]
    if own_width % 128:
        weights3 = [
            lax.dynamic_slice_in_dim(w, ids[0] * own_width, own_width, axis=1) for w in weights3
        ]
    slices, facts, chain_row = call(
        functools.partial(stage_kernel, own_heads),
        "stage",
        [where_am_i, chain.reshape(1, tokens), keymask.reshape(1, tokens), (chain_weight, SMEM)]
        + [(w, ANY) for w in weights3],
        [((3, width, own_width), bf16), ((tokens, 128), f32), ((1, tokens), f32)],
        [pltpu.SemaphoreType.DMA((3,))],
    )
    x, query, key, value = call(
        functools.partial(project_kernel, toks),
        "project",
        [where_am_i, slices] + x_parts,
        [((tokens, width), bf16)] + [((own_width, tokens), bf16)] * 3,
        flops=6 * tokens * width * own_width,
    )
    done = call(
        functools.partial(attention_kernel, copies, toks, cols, head_width),
        "attention",
        [where_am_i, query, key, value, bias_own, bias_other, facts, chain_row],
        [((own_heads, tokens, tokens), bf16), ((tokens, own_width), bf16)]
        + [((rows, own_width), bf16)] * toks,
        [VMEM((2, devices // 2, own_heads * cols, rows), bf16)],
        flops=4 * tokens * tokens * own_width,
        limit=32,
    )
    weights, att, pieces = done[0], done[1], done[2:]
    att_parts = [pieces[0]] + [swap_tok(pieces[r], r) for r in range(1, toks)]

    d_hidden, upstream, noisy3, trans_gain2 = call(
        down_kernel,
        "down",
        [cotangent.reshape(rows, width), w_down, noisy2, trans_gain.reshape(1, width)],
        [((rows, hidden), f32), ((rows, width), bf16), ((rows, width), bf16), ((1, width), f32)],
        flops=2 * rows * hidden * width,
    )
    chunk = hidden // 3
    results = call(
        functools.partial(hidden_kernel, toks, chunk),
        "hidden",
        [where_am_i, noisy3, upstream, d_hidden, trans_gain2]
        + att_parts
        + [(w_out, ANY), (w_hidden_gate, ANY), (w_hidden_up, ANY)],
        [((rows, width), f32), ((rows, width), bf16)] + [((own_width, rows), bf16)] * toks,
        [
            VMEM((width, width), bf16),
            VMEM((width, hidden), bf16),
            VMEM((width, hidden), bf16),
            pltpu.SemaphoreType.DMA((7,)),
        ],
        flops=2 * rows * width * (2 * width + 4 * hidden),
    )
    d_res, d_res_b, d_att = results[0], results[1], results[2:]
    d_att_parts = [d_att[0]] + [swap_tok(d_att[r], r) for r in range(1, toks)]
    d_res_b = after(d_res_b, *d_att_parts[1:])
    d_res_parts = [d_res_b] + [swap_tok(d_res_b, r) for r in range(1, toks)]

    bias_shape = (copies // 2, own_heads * cols, tokens)
    d_query, d_key, d_value, bias_kept, bias_sent = call(
        functools.partial(backward_kernel, copies, toks, cols, head_width),
        "backward",
        [where_am_i, query, key, value, weights] + d_att_parts,
        [((own_width, tokens), bf16)] * 3 + [(bias_shape, bf16)] * 2,
        [VMEM((toks, own_width, rows), bf16), VMEM((tokens, tokens), bf16)],
        flops=8 * tokens * tokens * own_width,
        limit=32,
    )
    bias_got = swap_copy(bias_sent, 1)

    part_shape = (copies // 2, 2, cut, own_width)
    kept, sent = call(
        functools.partial(first_kernel, copies, toks),
        "first",
        [where_am_i, x, att, d_value] + d_res_parts,
        [(part_shape, bf16)] * 2,
        [
            VMEM((tokens, width), bf16),
            VMEM((own_width, width), f32),
            VMEM((width, own_width), f32),
        ],
        flops=4 * tokens * width * own_width,
    )
    got = swap_copy(sent, 1)

    found = call(
        functools.partial(second_kernel, copies, toks),
        "second",
        [where_am_i, slices, x, d_query, d_key, d_value],
        [(part_shape, bf16)] * 2
        + [((width, rows), f32)]
        + [((width, rows), bf16)] * (toks - 1),
        [VMEM((own_width, width), f32), VMEM((toks, width, rows), f32)],
        flops=10 * tokens * width * own_width,
    )
    kept_b, sent_b, d_own = found[:3]
    d_others = [swap_tok(found[2 + r], r) for r in range(1, toks)]
    got_b = swap_copy(sent_b, 1)

    def halve(name, mask, pairs):
        outs = []
        for pair_kept, _ in pairs:
            outs += [((pair_kept.shape[0] // 2,) + pair_kept.shape[1:], bf16)] * 2
        flat = [array for one in pairs for array in one]
        results = call(
            functools.partial(halve_kernel, mask, len(pairs)), name, [where_am_i] + flat, outs
        )
        return [
            (results[2 * n], swap_copy(results[2 * n + 1], mask)) for n in range(len(pairs))
        ]

    chain_a = halve("halve_a2", 2, [(kept, got), (bias_kept, bias_got)])
    part_shape = (copies // 4, 2, cut, own_width)
    single_shape = (copies // 4, 2, cut, rows)
    kept_b, sent_b, single_kept, single_sent = call(
        functools.partial(halve_single_kernel, toks, copies),
        "halve_b2",
        [where_am_i, kept_b, got_b, d_own] + d_others,
        [(part_shape, bf16)] * 2 + [(single_shape, bf16)] * 2,
        [VMEM((width, rows), f32)],
    )
    chain_b = [(kept_b, swap_copy(sent_b, 2)), (single_kept, swap_copy(single_sent, 2))]
    (grad_noisy,) = call(
        functools.partial(exit_kernel, toks),
        "exit",
        [noisy3, norm_gain2, d_res, d_own] + d_others,
        [((rows, width), bf16)],
    )
    mask = 4
    while mask < copies:
        chain_a = halve("halve_a%d" % mask, mask, chain_a)
        chain_b = halve("halve_b%d" % mask, mask, chain_b)
        mask *= 2

    group = copies // toks
    swaps = []
    for c in range(copies):
        for t in range(toks):
            swaps.append((c * toks + t, (t * group + c % group) * toks + c // group))

    done = call(
        functools.partial(last_first_kernel, toks),
        "last_a",
        [where_am_i] + [array for one in chain_a for array in one],
        [((cut, own_width), bf16), ((cut, own_width), f32)]
        + [((own_heads * cols, rows), bf16)] * toks,
        [VMEM((toks, own_heads * cols, rows), bf16)],
    )
    moved_a, grad_out, bias_parts = done[0], done[1], done[2:]
    bias_parts = [bias_parts[0]] + [swap_tok(bias_parts[r], r) for r in range(1, toks)]
    moved_a = lax.ppermute(moved_a, ("copy", "tok"), swaps)
    grad_pair, weight_grad = call(
        functools.partial(pair_kernel, toks, cols),
        "pair",
        [where_am_i, pair2, pair_gain2, w_pair.T] + bias_parts,
        [((rows * cols, channels), bf16), ((devices, heads, channels), f32)],
        [VMEM((rows * cols, channels), f32)] * 2 + [VMEM((heads * cols, rows), f32)],
        flops=4 * heads * cols * rows * channels * cols,
    )
    weight_grad = jnp.sum(exchange(weight_grad), axis=0)

    moved_b, last_kept, last_sent = call(
        last_second_kernel,
        "last_b",
        [where_am_i] + [array for one in chain_b for array in one],
        [((2, cut, own_width), bf16)] + [((cut, rows), bf16)] * 2,
        [VMEM((2, cut, rows), bf16)],
    )
    last_got = swap_copy(last_sent, 1)
    moved_b = lax.ppermute(moved_b, ("copy", "tok"), swaps)
    grad_query, grad_key, grad_value, grad_single = call(
        finish_kernel,
        "finish",
        [moved_a, moved_b, last_kept, last_got],
        [((cut, own_width), f32)] * 3 + [((cut, rows), f32)],
    )
    return (
        grad_noisy[None],
        grad_single.T,
        grad_pair.reshape(rows, cols, channels),
        grad_query.T,
        grad_key.T,
        grad_value.T,
        grad_out.T,
        weight_grad.T,
    )


def solution(mesh):
    placed = (
        P("copy", "tok", None),
        P("tok", None),
        P("tok", "copy", None),
        P("tok"),
    ) + (P(),) * 15 + (P("copy", "tok", None),)
    return jax.shard_map(
        per_device,
        mesh=mesh,
        in_specs=placed,
        out_specs=(
            P("copy", "tok", None),
            P("tok", "copy"),
            P("tok", "copy", None),
            P("tok", "copy"),
            P("tok", "copy"),
            P("tok", "copy"),
            P("tok", "copy"),
            P(),
        ),
        check_vma=False,
    )
```

```python
import functools

import jax
import jax.numpy as jnp
from jax import lax
from jax.experimental import pallas as pl
from jax.experimental.pallas import tpu as pltpu
from jax.sharding import PartitionSpec as P

epsilon = 1e-05
f32 = jnp.float32
bf16 = jnp.bfloat16
VMEM, SMEM, ANY = pltpu.VMEM, pltpu.SMEM, pl.ANY
MIB = 1 << 20


def layer_forward(values, scales):
    average = jnp.mean(values, axis=-1, keepdims=True)
    centred = values - average
    inverse = lax.rsqrt(jnp.mean(centred * centred, axis=-1, keepdims=True) + epsilon)
    normed = centred * inverse
    return (normed * scales, normed, inverse)


def layer_backward(upstream, scales, normed, inverse):
    scaled = upstream * scales
    first_moment = jnp.mean(scaled, axis=-1, keepdims=True)
    second_moment = jnp.mean(scaled * normed, axis=-1, keepdims=True)
    return inverse * (scaled - first_moment - normed * second_moment)


NN = ((1,), (0,))
NT = ((1,), (1,))
TN = ((0,), (0,))


def mm(left, right, dims=NN):
    return lax.dot_general(left, right, (dims, ((), ())), preferred_element_type=f32)


def call(body, name, inputs, outs, scratch=(), flops=0, limit=16):
    arrays, specs, moved, fetched = [], [], 0, []
    for item in inputs:
        array, space = item if isinstance(item, tuple) else (item, VMEM)
        if space == "fetch":
            fetched.append(len(arrays))
            space = pltpu.HBM
        arrays.append(array)
        specs.append(pl.BlockSpec(memory_space=space))
        moved += array.size * array.dtype.itemsize
    for shape, kind in outs:
        size = jnp.dtype(kind).itemsize
        for extent in shape:
            size *= extent
        moved += size
    extra = [VMEM(arrays[k].shape, arrays[k].dtype) for k in fetched]
    if fetched:
        extra.append(pltpu.SemaphoreType.DMA((len(fetched),)))

    def whole(*refs):
        refs = list(refs)
        if fetched:
            held, sem = refs[-1 - len(fetched) : -1], refs[-1]
            refs = refs[: -1 - len(fetched)]
            transfers = []
            for n, k in enumerate(fetched):
                transfer = pltpu.make_async_copy(refs[k], held[n], sem.at[n])
                transfer.start()
                transfers.append(transfer)
                refs[k] = held[n]
            for transfer in transfers:
                transfer.wait()
        body(*refs)

    return pl.pallas_call(
        whole,
        name=name,
        out_shape=[jax.ShapeDtypeStruct(shape, kind) for shape, kind in outs],
        in_specs=specs,
        out_specs=[pl.BlockSpec(memory_space=VMEM)] * len(outs),
        scratch_shapes=list(scratch) + extra,
        compiler_params=pltpu.CompilerParams(vmem_limit_bytes=limit * MIB),
        cost_estimate=pl.CostEstimate(flops=flops, bytes_accessed=moved, transcendentals=0),
    )(*arrays)


def low_bits(index, size):
    return jnp.bitwise_and(index, size - 1)


def pair_weight_rows(w_pair, head_count, cols):
    rows = head_count * cols
    shift = cols.bit_length() - 1
    head = lax.shift_right_logical(
        lax.broadcasted_iota(jnp.int32, (rows, head_count), 0), jnp.int32(shift)
    )
    pick = (head == lax.broadcasted_iota(jnp.int32, (rows, head_count), 1)).astype(f32)
    spread = mm(pick.astype(bf16), w_pair)
    row_col = low_bits(lax.broadcasted_iota(jnp.int32, spread.shape, 0), cols)
    return spread, row_col


def enter_kernel(toks, cols, ids, noisy, single, restype, table, gain, pair, pair_gain, *rest):
    w_pair, x_out, bias_outs = rest[0], rest[1], rest[2 : 2 + toks]
    rounded, bias = rest[2 + toks :]
    rows = noisy.shape[0]
    pair_scaled, _, _ = layer_forward(pair[...].astype(f32), pair_gain[...])
    rounded[...] = pair_scaled.astype(bf16).astype(f32)
    head_count = w_pair.shape[0]
    spread, row_col = pair_weight_rows(w_pair[...], head_count, cols)
    total = jnp.zeros((head_count * cols, rows), f32)
    for j in range(cols):
        column = rounded[pl.ds(j, rows, stride=cols), :].astype(bf16)
        total = total + mm(jnp.where(row_col == j, spread, 0.0).astype(bf16), column, NT)
    bias[...] = total
    part = bias_outs[0].shape[0]
    for r in range(toks):
        start = pl.multiple_of(jnp.bitwise_xor(ids[0], r) * part, part)
        bias_outs[r][...] = bias[pl.ds(start, part), :].astype(bf16)
    normed_scaled, _, _ = layer_forward(noisy[...].astype(f32), gain[...])
    types = table.shape[0]
    onehot = (lax.broadcasted_iota(jnp.int32, (types, rows), 0) == restype[...]).astype(f32)
    condition = single[...].astype(f32) + mm(onehot.astype(bf16), table[...], TN)
    x_out[...] = (normed_scaled + condition).astype(bf16)


def own_slice(weight, t, own_width):
    if weight.shape[1] == own_width:
        return weight
    return weight.at[:, pl.ds(pl.multiple_of(t * own_width, own_width), own_width)]


def stage_kernel(own_heads, ids, chain, keymask, chain_weight, *rest):
    weights, (slices, facts_out, chain_out, sem) = rest[:3], rest[3:]
    t = ids[0]
    own_width = slices.shape[2]
    transfers = []
    for k in range(3):
        transfer = pltpu.make_async_copy(
            own_slice(weights[k], t, own_width), slices.at[k], sem.at[k]
        )
        transfer.start()
        transfers.append(transfer)
    chain_row = chain[...]
    tokens = chain_row.shape[1]
    keep_row = keymask[...].astype(f32)
    line = lax.broadcasted_iota(jnp.int32, (128, tokens), 0)
    facts = jnp.where(line == 0, chain_row.astype(f32), 0.0) + jnp.where(line == 1, keep_row, 0.0)
    for h in range(own_heads):
        weight_row = jnp.zeros((1, tokens), f32)
        for m in range(chain_weight.shape[0]):
            weight_row = jnp.where(chain_row == m, chain_weight[m, t * own_heads + h], weight_row)
        facts = jnp.where(line == 2 + h, weight_row, facts)
    facts_out[...] = jnp.transpose(facts)
    chain_out[...] = chain_row.astype(f32)
    for transfer in transfers:
        transfer.wait()


def project_kernel(toks, ids, slices, *rest):
    parts = rest[:toks]
    x_out, outs = rest[toks], rest[toks + 1 :]
    t = ids[0]
    rows = parts[0].shape[0]
    for r in range(toks):
        start = pl.multiple_of(jnp.bitwise_xor(t, r) * rows, rows)
        x_out[pl.ds(start, rows), :] = parts[r][...]
    x = x_out[...]
    for k in range(3):
        outs[k][...] = jnp.transpose(mm(x, slices[k])).astype(bf16)


def attention_kernel(copies, toks, cols, head_width, ids, query, key, value, own, other, *rest):
    facts, chain, weights_out, att_out = rest[:4]
    pieces, bias = rest[4 : 4 + toks], rest[4 + toks]
    t = ids[0]
    core, pair_index = low_bits(ids[1], 2), ids[1] // 2
    half = copies // 2
    for p in range(half):
        k = 0
        for b in range(half.bit_length() - 1):
            k += (p >> b & 1) * (half >> 1 >> b)
        k = jnp.bitwise_xor(pair_index, k)
        for r in range(toks):
            a = jnp.bitwise_xor(t, r)
            bias[core, k, a] = own[p * toks + r]
            bias[1 - core, k, a] = other[p * toks + r]
    own_heads = weights_out.shape[0]
    tokens = query.shape[1]
    rows = tokens // toks
    same = facts[:, 0:1] == chain[...]
    keep = facts[:, 1:2] > 0.0
    scale = head_width ** (-0.5)
    attended = []
    for h in range(own_heads):
        span = slice(h * head_width, (h + 1) * head_width)
        logits = mm(key[span, :], query[span, :], TN) * scale
        line = slice(h * cols, (h + 1) * cols)
        extra = jnp.concatenate(
            [
                jnp.concatenate(
                    [bias[c % 2, c // 2, a, line, :] for c in range(copies)], axis=0
                )
                for a in range(toks)
            ],
            axis=1,
        ).astype(f32)
        logits = logits + (extra + jnp.where(same, facts[:, 2 + h : 3 + h], 0.0))
        logits = jnp.where(keep, logits, -1e30)
        exponent = jnp.exp(logits - jnp.max(logits, axis=0, keepdims=True))
        weights = exponent / jnp.sum(exponent, axis=0, keepdims=True)
        weights_b = weights.astype(bf16)
        weights_out[h] = weights_b
        attended.append(mm(value[span, :], weights_b))
    att_out[...] = jnp.transpose(jnp.concatenate(attended, axis=0)).astype(bf16)
    for r in range(toks):
        start = pl.multiple_of(jnp.bitwise_xor(t, r) * rows, rows)
        pieces[r][...] = att_out[pl.ds(start, rows), :]


def down_kernel(upstream, w_down, noisy, gain, d_hidden, upstream_out, noisy_out, gain_out):
    d_hidden[...] = mm(upstream[...], w_down[...], NT)
    upstream_out[...] = upstream[...]
    noisy_out[...] = noisy[...]
    gain_out[...] = gain[...]


def hidden_kernel(toks, chunk, ids, noisy, upstream, d_hidden, gain, *rest):
    parts = rest[:toks]
    held_out, held_gate, held_up = rest[toks : toks + 3]
    d_res_out, d_res_b_out = rest[toks + 3 : toks + 5]
    d_att_outs = rest[toks + 5 :]
    t = ids[0]
    hidden = held_gate.shape[1]
    residual = noisy[...].astype(f32)
    own_width = parts[0].shape[1]
    for r in range(toks):
        start = pl.multiple_of(jnp.bitwise_xor(t, r) * own_width, own_width)
        residual = residual + mm(parts[r][...], held_out[pl.ds(start, own_width), :])
    trans_scaled, trans_hat, trans_inverse = layer_forward(residual, gain[...])
    trans_in = trans_scaled.astype(bf16)
    d_trans = jnp.zeros(residual.shape, f32)
    for k in range(hidden // chunk):
        span = slice(k * chunk, (k + 1) * chunk)
        gate = mm(trans_in, held_gate[:, span])
        up = mm(trans_in, held_up[:, span])
        incoming = d_hidden[:, span]
        sigmoid = jax.nn.sigmoid(gate)
        d_up = (incoming * gate * sigmoid).astype(bf16)
        d_gate = (incoming * up * sigmoid * (1.0 + gate * (1.0 - sigmoid))).astype(bf16)
        d_trans = d_trans + mm(d_gate, held_gate[:, span], NT) + mm(d_up, held_up[:, span], NT)
    d_res = upstream[...].astype(f32) + layer_backward(
        d_trans, gain[...], trans_hat, trans_inverse
    )
    d_res_out[...] = d_res
    d_res_b = d_res.astype(bf16)
    d_res_b_out[...] = d_res_b
    for r in range(toks):
        start = pl.multiple_of(jnp.bitwise_xor(t, r) * own_width, own_width)
        d_att_outs[r][...] = mm(held_out[pl.ds(start, own_width), :], d_res_b, NT).astype(bf16)


def backward_kernel(copies, toks, cols, head_width, ids, query, key, value, weights, *rest):
    parts = rest[:toks]
    d_query, d_key, d_value, bias_kept, bias_sent, blocks, d_logits = rest[toks:]
    t = ids[0]
    core = low_bits(ids[1], 2)
    for r in range(toks):
        blocks[jnp.bitwise_xor(t, r)] = parts[r][...]
    d_att = jnp.concatenate([blocks[a] for a in range(toks)], axis=1)
    scale = head_width ** (-0.5)
    for h in range(weights.shape[0]):
        span = slice(h * head_width, (h + 1) * head_width)
        d_att_h = d_att[span, :]
        weights_b = weights[h]
        d_weights = mm(value[span, :], d_att_h, TN)
        weights_f = weights_b.astype(f32)
        delta = jnp.sum(weights_f * d_weights, axis=0, keepdims=True)
        d_logits_b = (weights_f * (d_weights - delta)).astype(bf16)
        d_logits[...] = d_logits_b
        for q in range(copies // 2):
            for side, out in ((core, bias_kept), (1 - core, bias_sent)):
                start = pl.multiple_of((2 * q + side) * cols, cols)
                out[q, h * cols : (h + 1) * cols, :] = d_logits[pl.ds(start, cols), :]
        d_query[span, :] = (mm(key[span, :], d_logits_b) * scale).astype(bf16)
        d_key[span, :] = (mm(query[span, :], d_logits_b, NT) * scale).astype(bf16)
        d_value[span, :] = mm(d_att_h, weights_b, NT).astype(bf16)


def tile_count(rows, lanes):
    return -(-rows // 16) * -(-lanes // 128)


def put(out, q, base, value):
    rows, lanes = value.shape
    for i in range(0, rows, 16):
        for j in range(0, lanes, 128):
            part = value[i : i + 16, j : j + 128]
            if part.shape != (16, 128):
                out[q, base] = jnp.zeros((16, 128), out.dtype)
            out[q, base, : part.shape[0], : part.shape[1]] = part
            base += 1


def take(tiles, base, rows, lanes):
    across = -(-lanes // 128)
    lines = []
    for i in range(-(-rows // 16)):
        line = [tiles[base + i * across + j] for j in range(across)]
        lines.append(jnp.concatenate(line, axis=1) if across > 1 else line[0])
    whole = jnp.concatenate(lines, axis=0) if len(lines) > 1 else lines[0]
    return whole[:rows, :lanes]


def cut_wide(copies, toks, core, base, grad, kept, sent):
    group = copies // toks
    cut, depth = grad.shape[1] // copies, grad.shape[1] // toks
    for side, out in ((core, kept), (1 - core, sent)):
        for q in range(copies // 2):
            h = 2 * q // group
            first = pl.multiple_of((2 * q - h * group + side) * cut, 8)
            part = grad[pl.ds(first, cut), h * depth : (h + 1) * depth]
            put(out, q, base, part.astype(bf16))


def first_kernel(copies, toks, ids, slices, x, d_query, d_key, d_value, *rest):
    kept, sent, d_own = rest[:3]
    d_others, (wide, d_inputs, total_ref) = rest[3 : 2 + toks], rest[2 + toks :]
    t, core = ids[0], low_bits(ids[1], 2)
    rows = d_own.shape[1]
    cut = x.shape[1] // copies
    count = tile_count(cut, d_query.shape[0])
    for k, part in enumerate((d_query, d_key)):
        wide[...] = mm(part[...], x[...])
        cut_wide(copies, toks, core, k * count, wide, kept, sent)
    total = mm(slices[0], d_query[...]) + mm(slices[1], d_key[...])
    total = total + mm(slices[2], d_value[...])
    total_ref[...] = total
    for side, out in ((core, kept), (1 - core, sent)):
        for q in range(copies // 2):
            start = pl.multiple_of((2 * q + side) * cut, 8)
            put(out, q, 2 * count, total_ref[pl.ds(start, cut), :].astype(bf16))
    for a in range(toks):
        d_inputs[a] = total[:, a * rows : (a + 1) * rows]
    d_own[...] = d_inputs[t]
    for r in range(1, toks):
        d_others[r - 1][...] = d_inputs[jnp.bitwise_xor(t, r)].astype(bf16)


def second_kernel(copies, toks, ids, x, att, d_value, *rest):
    d_res_parts, (kept, sent, d_res, wide, narrow) = rest[:toks], rest[toks:]
    t, core = ids[0], low_bits(ids[1], 2)
    rows = d_res_parts[0].shape[0]
    wide[...] = mm(d_value[...], x[...])
    cut_wide(copies, toks, core, 0, wide, kept, sent)
    for r in range(toks):
        start = pl.multiple_of(jnp.bitwise_xor(t, r) * rows, rows)
        d_res[pl.ds(start, rows), :] = d_res_parts[r][...]
    narrow[...] = mm(d_res[...], att[...], TN)
    cut = narrow.shape[0] // copies
    count = tile_count(cut, narrow.shape[1])
    for side, out in ((core, kept), (1 - core, sent)):
        for q in range(copies // 2):
            first = pl.multiple_of((2 * q + side) * cut, 8)
            put(out, q, count, narrow[pl.ds(first, cut), :].astype(bf16))


def halve_kernel(mask, inner, ids, kept, got, kept_out, sent_out):
    bit = low_bits(ids[1] // mask, 2)
    for q in range(kept_out.shape[0]):
        for side, out in ((bit, kept_out), (1 - bit, sent_out)):
            k = q // inner * 2 * inner + side * inner + q % inner
            out[q] = (kept[k].astype(f32) + got[k].astype(f32)).astype(bf16)


def last_bias_kernel(toks, ids, kept, got, *rest):
    pieces, blocks = rest[:toks], rest[toks]
    total = kept[0].astype(f32) + got[0].astype(f32)
    rows = blocks.shape[2]
    for a in range(toks):
        blocks[a] = total[:, a * rows : (a + 1) * rows].astype(bf16)
    for r in range(toks):
        pieces[r][...] = blocks[jnp.bitwise_xor(ids[0], r)]


def last_first_kernel(toks, ids, kept, got, moved, *rest):
    pieces, blocks = rest[:toks], rest[toks]
    total = kept[0].astype(f32) + got[0].astype(f32)
    _, cut, own_width = moved.shape
    count = tile_count(cut, own_width)
    for k in range(2):
        moved[k] = take(total, k * count, cut, own_width).astype(bf16)
    rows = blocks.shape[2]
    single = take(total, 2 * count, cut, rows * toks)
    for a in range(toks):
        blocks[a] = single[:, a * rows : (a + 1) * rows]
    for r in range(toks):
        pieces[r][...] = blocks[jnp.bitwise_xor(ids[0], r)].astype(bf16)


def last_second_kernel(kept, got, moved, final):
    total = kept[0].astype(f32) + got[0].astype(f32)
    cut, own_width = moved.shape
    moved[...] = take(total, 0, cut, own_width).astype(bf16)
    final[...] = take(total, tile_count(cut, own_width), cut, own_width)


def finish_kernel(moved_first, moved_second, *rest):
    parts, (first, second, third, single) = rest[:-4], rest[-4:]
    first[...] = moved_first[0].astype(f32)
    second[...] = moved_first[1].astype(f32)
    third[...] = moved_second[...].astype(f32)
    total = parts[0][...].astype(f32)
    for part in parts[1:]:
        total = total + part[...].astype(f32)
    single[...] = total


def exit_kernel(toks, noisy, gain, d_res, d_own, *rest):
    others, (grad_noisy,) = rest[: toks - 1], rest[toks - 1 :]
    total = d_own[...]
    for part in others:
        total = total + part[...].astype(f32)
    _, noisy_hat, noisy_inverse = layer_forward(noisy[...].astype(f32), gain[...])
    grad_noisy[...] = (
        d_res[...] + layer_backward(jnp.transpose(total), gain[...], noisy_hat, noisy_inverse)
    ).astype(bf16)


def pair_kernel(toks, cols, ids, pair, gain, w_pair, *rest):
    parts, (grad_pair, weight_grad, rounded, spread_out, grads) = rest[:toks], rest[toks:]
    head_count = w_pair.shape[0]
    part_rows, rows = parts[0].shape
    for r in range(toks):
        start = pl.multiple_of(jnp.bitwise_xor(ids[0], r) * part_rows, part_rows)
        grads[pl.ds(start, part_rows), :] = parts[r][...].astype(f32)
    grad = grads[...]
    pair_scaled, pair_hat, pair_inverse = layer_forward(pair[...].astype(f32), gain[...])
    rounded[...] = pair_scaled.astype(bf16).astype(f32)
    spread, row_col = pair_weight_rows(w_pair[...], head_count, cols)
    grad_b = grad.astype(bf16)
    turned = jnp.transpose(grad).astype(bf16)
    sums = jnp.zeros(spread.shape, f32)
    for j in range(cols):
        here = row_col == j
        column = rounded[pl.ds(j, rows, stride=cols), :].astype(bf16)
        sums = sums + jnp.where(here, mm(grad_b, column), 0.0)
        spread_out[pl.ds(j, rows, stride=cols), :] = mm(
            turned, jnp.where(here, spread, 0.0).astype(bf16)
        )
    grad_pair[...] = layer_backward(
        spread_out[...], gain[...], pair_hat, pair_inverse
    ).astype(bf16)
    for h in range(head_count):
        line = jnp.sum(sums[h * cols : (h + 1) * cols, :], axis=0, keepdims=True)
        for n in range(weight_grad.shape[0]):
            weight_grad[n, h : h + 1, :] = line


def swap_copy(value, mask):
    size = lax.axis_size("copy")
    return lax.ppermute(value, "copy", [(i, i ^ mask) for i in range(size)])


def swap_tok(value, mask):
    size = lax.axis_size("tok")
    return lax.ppermute(value, "tok", [(i, i ^ mask) for i in range(size)])


def exchange(value):
    return lax.all_to_all(value, ("copy", "tok"), 0, 0)


def after(value, *earlier):
    return lax.optimization_barrier((value,) + earlier)[0]


def per_device(
    noisy,
    single,
    pair,
    restype,
    chain,
    keymask,
    restype_table,
    norm_gain,
    pair_gain,
    trans_gain,
    w_query,
    w_key,
    w_value,
    w_out,
    w_pair,
    chain_weight,
    w_hidden_gate,
    w_hidden_up,
    w_down,
    cotangent,
):
    copies = lax.axis_size("copy")
    toks = lax.axis_size("tok")
    _, rows, width = noisy.shape
    cols = pair.shape[1]
    channels = pair.shape[2]
    heads = w_pair.shape[1]
    head_width = width // heads
    own_heads = heads // toks
    own_width = own_heads * head_width
    tokens = rows * toks
    hidden = w_down.shape[0]
    cut = width // copies
    devices = copies * toks
    ids = jnp.stack([lax.axis_index("tok"), lax.axis_index("copy")]).astype(jnp.int32)
    where_am_i = (ids, SMEM)
    noisy2 = noisy.reshape(rows, width)
    pair2 = pair.reshape(rows * cols, channels)
    pair_gain2 = pair_gain.reshape(1, channels)
    norm_gain2 = norm_gain.reshape(1, width)

    entered = call(
        functools.partial(enter_kernel, toks, cols),
        "enter",
        [where_am_i]
        + [(array, "fetch") for array in (noisy2, single, restype.reshape(1, rows))]
        + [(array, "fetch") for array in (restype_table, norm_gain, pair2, pair_gain2, w_pair.T)],
        [((rows, width), bf16)] + [((own_heads * cols, rows), bf16)] * toks,
        [VMEM((rows * cols, channels), f32), VMEM((heads * cols, rows), f32)],
        flops=2 * heads * cols * rows * channels * cols,
        limit=60,
    )
    x_own, bias_parts = entered[0], entered[1:]
    bias_own = jnp.stack(
        [bias_parts[0]] + [swap_tok(bias_parts[r], r) for r in range(1, toks)]
    )
    x_parts = [x_own] + [swap_tok(x_own, r) for r in range(1, toks)]
    mask = copies // 2
    while mask > 1:
        bias_own = jnp.concatenate([bias_own, swap_copy(bias_own, mask)])
        mask //= 2
    bias_other = swap_copy(bias_own, 1)

    weights3 = [w_query, w_key, w_value]
    if own_width % 128:
        weights3 = [
            lax.dynamic_slice_in_dim(w, ids[0] * own_width, own_width, axis=1) for w in weights3
        ]
    slices, facts, chain_row = call(
        functools.partial(stage_kernel, own_heads),
        "stage",
        [where_am_i, chain.reshape(1, tokens), keymask.reshape(1, tokens), (chain_weight, SMEM)]
        + [(w, ANY) for w in weights3],
        [((3, width, own_width), bf16), ((tokens, 128), f32), ((1, tokens), f32)],
        [pltpu.SemaphoreType.DMA((3,))],
    )
    x, query, key, value = call(
        functools.partial(project_kernel, toks),
        "project",
        [where_am_i, slices] + x_parts,
        [((tokens, width), bf16)] + [((own_width, tokens), bf16)] * 3,
        flops=6 * tokens * width * own_width,
    )
    done = call(
        functools.partial(attention_kernel, copies, toks, cols, head_width),
        "attention",
        [where_am_i, query, key, value, bias_own, bias_other, facts, chain_row],
        [((own_heads, tokens, tokens), bf16), ((tokens, own_width), bf16)]
        + [((rows, own_width), bf16)] * toks,
        [VMEM((2, copies // 2, toks, own_heads * cols, rows), bf16)],
        flops=4 * tokens * tokens * own_width,
        limit=32,
    )
    weights, att, pieces = done[0], done[1], done[2:]
    att_parts = [pieces[0]] + [swap_tok(pieces[r], r) for r in range(1, toks)]

    d_hidden, upstream, noisy3, trans_gain2 = call(
        down_kernel,
        "down",
        [cotangent.reshape(rows, width), w_down, noisy2, trans_gain.reshape(1, width)],
        [((rows, hidden), f32), ((rows, width), bf16), ((rows, width), bf16), ((1, width), f32)],
        flops=2 * rows * hidden * width,
    )
    chunk = hidden // 3
    results = call(
        functools.partial(hidden_kernel, toks, chunk),
        "hidden",
        [where_am_i, noisy3, upstream, d_hidden, trans_gain2]
        + att_parts
        + [w_out, w_hidden_gate, w_hidden_up],
        [((rows, width), f32), ((rows, width), bf16)] + [((own_width, rows), bf16)] * toks,
        flops=2 * rows * width * (2 * width + 4 * hidden),
    )
    d_res, d_res_b, d_att = results[0], results[1], results[2:]
    d_att_parts = [d_att[0]] + [swap_tok(d_att[r], r) for r in range(1, toks)]
    d_res_b = after(d_res_b, *d_att_parts[1:])
    d_res_parts = [d_res_b] + [swap_tok(d_res_b, r) for r in range(1, toks)]

    bias_shape = (copies // 2, own_heads * cols, tokens)
    d_query, d_key, d_value, bias_kept, bias_sent = call(
        functools.partial(backward_kernel, copies, toks, cols, head_width),
        "backward",
        [where_am_i, query, key, value, weights] + d_att_parts,
        [((own_width, tokens), bf16)] * 3 + [(bias_shape, bf16)] * 2,
        [VMEM((toks, own_width, rows), bf16), VMEM((tokens, tokens), bf16)],
        flops=8 * tokens * tokens * own_width,
        limit=32,
    )
    bias_got = swap_copy(bias_sent, 1)

    wide_tiles = tile_count(cut, own_width)
    single_tiles = tile_count(cut, tokens)
    found = call(
        functools.partial(first_kernel, copies, toks),
        "first",
        [where_am_i, slices, x, d_query, d_key, d_value],
        [((copies // 2, 2 * wide_tiles + single_tiles, 16, 128), bf16)] * 2
        + [((width, rows), f32)]
        + [((width, rows), bf16)] * (toks - 1),
        [
            VMEM((own_width, width), f32),
            VMEM((toks, width, rows), f32),
            VMEM((width, tokens), f32),
        ],
        flops=10 * tokens * width * own_width,
    )
    kept, sent, d_own = found[:3]
    got = swap_copy(sent, 1)
    d_others = [swap_tok(found[2 + r], r) for r in range(1, toks)]
    kept_b, sent_b = call(
        functools.partial(second_kernel, copies, toks),
        "second",
        [where_am_i, x, att, d_value] + d_res_parts,
        [((copies // 2, 2 * wide_tiles, 16, 128), bf16)] * 2,
        [
            VMEM((tokens, width), bf16),
            VMEM((own_width, width), f32),
            VMEM((width, own_width), f32),
        ],
        flops=4 * tokens * width * own_width,
    )
    got_b = swap_copy(sent_b, 1)

    def halve(name, mask, left, kept, got):
        inner = 1 << sum(1 for other in left if other < mask)
        left.remove(mask)
        shape = (kept.shape[0] // 2,) + kept.shape[1:]
        kept, sent = call(
            functools.partial(halve_kernel, mask, inner),
            "%s_%d" % (name, mask),
            [where_am_i, kept, got],
            [(shape, bf16)] * 2,
        )
        return kept, swap_copy(sent, mask)

    masks = [1 << b for b in range(1, copies.bit_length() - 1)]
    bias_left, first_left, second_left = list(masks), list(masks), list(masks)
    first, second, bias_chain = (kept, got), (kept_b, got_b), (bias_kept, bias_got)
    for mask, mask_b in zip(masks, masks[1:] + masks[:1]):
        bias_chain = halve("bias", mask, bias_left, *bias_chain)
        first = halve("first", mask, first_left, *first)
        second = halve("second", mask_b, second_left, *second)

    group = copies // toks
    swaps = []
    for c in range(copies):
        for t in range(toks):
            swaps.append((c * toks + t, (t * group + c % group) * toks + c // group))

    bias_parts = call(
        functools.partial(last_bias_kernel, toks),
        "last_bias",
        [where_am_i, *bias_chain],
        [((own_heads * cols, rows), bf16)] * toks,
        [VMEM((toks, own_heads * cols, rows), bf16)],
    )
    bias_parts = [bias_parts[0]] + [swap_tok(bias_parts[r], r) for r in range(1, toks)]
    (grad_noisy,) = call(
        functools.partial(exit_kernel, toks),
        "exit",
        [noisy3, norm_gain2, d_res, d_own] + d_others,
        [((rows, width), bf16)],
    )
    grad_pair, weight_grad = call(
        functools.partial(pair_kernel, toks, cols),
        "pair",
        [where_am_i, pair2, pair_gain2, w_pair.T] + bias_parts,
        [((rows * cols, channels), bf16), ((devices, heads, channels), f32)],
        [VMEM((rows * cols, channels), f32)] * 2 + [VMEM((heads * cols, rows), f32)],
        flops=4 * heads * cols * rows * channels * cols,
    )
    weight_grad = jnp.sum(exchange(weight_grad), axis=0)

    moved_second, grad_out = call(
        last_second_kernel,
        "last_second",
        [*second],
        [((cut, own_width), bf16), ((cut, own_width), f32)],
    )
    moved_second = lax.ppermute(moved_second, ("copy", "tok"), swaps)
    done = call(
        functools.partial(last_first_kernel, toks),
        "last_first",
        [where_am_i, *first],
        [((2, cut, own_width), bf16)] + [((cut, rows), bf16)] * toks,
        [VMEM((toks, cut, rows), f32)],
    )
    moved_first, singles = done[0], done[1:]
    moved_first = lax.ppermute(moved_first, ("copy", "tok"), swaps)
    singles = [singles[0]] + [swap_tok(singles[r], r) for r in range(1, toks)]
    grad_query, grad_key, grad_value, grad_single = call(
        finish_kernel,
        "finish",
        [moved_first, moved_second] + singles,
        [((cut, own_width), f32)] * 3 + [((cut, rows), f32)],
    )
    return (
        grad_noisy[None],
        grad_single.T,
        grad_pair.reshape(rows, cols, channels),
        grad_query.T,
        grad_key.T,
        grad_value.T,
        grad_out.T,
        weight_grad.T,
    )


def solution(mesh):
    placed = (
        P("copy", "tok", None),
        P("tok", None),
        P("tok", "copy", None),
        P("tok"),
    ) + (P(),) * 15 + (P("copy", "tok", None),)
    return jax.shard_map(
        per_device,
        mesh=mesh,
        in_specs=placed,
        out_specs=(
            P("copy", "tok", None),
            P("tok", "copy"),
            P("tok", "copy", None),
            P("tok", "copy"),
            P("tok", "copy"),
            P("tok", "copy"),
            P("tok", "copy"),
            P(),
        ),
        check_vma=False,
    )
```

```python
import functools

import jax
import jax.numpy as jnp
from jax import lax
from jax.experimental import pallas as pl
from jax.experimental.pallas import tpu as pltpu
from jax.sharding import PartitionSpec as P

epsilon = 1e-05
f32 = jnp.float32
bf16 = jnp.bfloat16
VMEM, SMEM, ANY = pltpu.VMEM, pltpu.SMEM, pl.ANY
MIB = 1 << 20


def layer_forward(values, scales):
    average = jnp.mean(values, axis=-1, keepdims=True)
    centred = values - average
    inverse = lax.rsqrt(jnp.mean(centred * centred, axis=-1, keepdims=True) + epsilon)
    normed = centred * inverse
    return (normed * scales, normed, inverse)


def layer_backward(upstream, scales, normed, inverse):
    scaled = upstream * scales
    first_moment = jnp.mean(scaled, axis=-1, keepdims=True)
    second_moment = jnp.mean(scaled * normed, axis=-1, keepdims=True)
    return inverse * (scaled - first_moment - normed * second_moment)


NN = ((1,), (0,))
NT = ((1,), (1,))
TN = ((0,), (0,))


def mm(left, right, dims=NN):
    return lax.dot_general(left, right, (dims, ((), ())), preferred_element_type=f32)


def call(body, name, inputs, outs, scratch=(), flops=0, limit=16, deps=()):
    arrays, specs, moved, fetched = [], [], 0, []
    for item in inputs:
        array, space = item if isinstance(item, tuple) else (item, VMEM)
        if space == "fetch":
            fetched.append(len(arrays))
            space = pltpu.HBM
        arrays.append(array)
        specs.append(pl.BlockSpec(memory_space=space))
        moved += array.size * array.dtype.itemsize
    for shape, kind in outs:
        size = jnp.dtype(kind).itemsize
        for extent in shape:
            size *= extent
        moved += size
    read = len(arrays)
    for array in deps:
        arrays.append(array)
        specs.append(pl.BlockSpec(memory_space=ANY))
    extra = [VMEM(arrays[k].shape, arrays[k].dtype) for k in fetched]
    if fetched:
        extra.append(pltpu.SemaphoreType.DMA((len(fetched),)))

    def whole(*refs):
        refs = list(refs[:read]) + list(refs[read + len(deps) :])
        if fetched:
            held, sem = refs[-1 - len(fetched) : -1], refs[-1]
            refs = refs[: -1 - len(fetched)]
            transfers = []
            for n, k in enumerate(fetched):
                transfer = pltpu.make_async_copy(refs[k], held[n], sem.at[n])
                transfer.start()
                transfers.append(transfer)
                refs[k] = held[n]
            for transfer in transfers:
                transfer.wait()
        body(*refs)

    return pl.pallas_call(
        whole,
        name=name,
        out_shape=[jax.ShapeDtypeStruct(shape, kind) for shape, kind in outs],
        in_specs=specs,
        out_specs=[pl.BlockSpec(memory_space=VMEM)] * len(outs),
        scratch_shapes=list(scratch) + extra,
        compiler_params=pltpu.CompilerParams(vmem_limit_bytes=limit * MIB),
        cost_estimate=pl.CostEstimate(flops=flops, bytes_accessed=moved, transcendentals=0),
    )(*arrays)


def low_bits(index, size):
    return jnp.bitwise_and(index, size - 1)


def pair_weight_rows(w_pair, head_count, cols):
    rows = head_count * cols
    shift = cols.bit_length() - 1
    head = lax.shift_right_logical(
        lax.broadcasted_iota(jnp.int32, (rows, head_count), 0), jnp.int32(shift)
    )
    pick = (head == lax.broadcasted_iota(jnp.int32, (rows, head_count), 1)).astype(f32)
    spread = mm(pick.astype(bf16), w_pair)
    row_col = low_bits(lax.broadcasted_iota(jnp.int32, spread.shape, 0), cols)
    return spread, row_col


def enter_kernel(toks, cols, ids, noisy, single, restype, table, gain, pair, pair_gain, *rest):
    w_pair, x_out, bias_outs = rest[0], rest[1], rest[2 : 2 + toks]
    rounded, bias = rest[2 + toks :]
    rows = noisy.shape[0]
    pair_scaled, _, _ = layer_forward(pair[...].astype(f32), pair_gain[...])
    rounded[...] = pair_scaled.astype(bf16).astype(f32)
    head_count = w_pair.shape[0]
    spread, row_col = pair_weight_rows(w_pair[...], head_count, cols)
    total = jnp.zeros((head_count * cols, rows), f32)
    for j in range(cols):
        column = rounded[pl.ds(j, rows, stride=cols), :].astype(bf16)
        total = total + mm(jnp.where(row_col == j, spread, 0.0).astype(bf16), column, NT)
    bias[...] = total
    part = bias_outs[0].shape[0]
    for r in range(toks):
        start = pl.multiple_of(jnp.bitwise_xor(ids[0], r) * part, part)
        bias_outs[r][...] = bias[pl.ds(start, part), :].astype(bf16)
    normed_scaled, _, _ = layer_forward(noisy[...].astype(f32), gain[...])
    types = table.shape[0]
    onehot = (lax.broadcasted_iota(jnp.int32, (types, rows), 0) == restype[...]).astype(f32)
    condition = single[...].astype(f32) + mm(onehot.astype(bf16), table[...], TN)
    x_out[...] = (normed_scaled + condition).astype(bf16)


def own_slice(weight, t, own_width):
    if weight.shape[1] == own_width:
        return weight
    return weight.at[:, pl.ds(pl.multiple_of(t * own_width, own_width), own_width)]


def stage_kernel(own_heads, ids, chain, keymask, chain_weight, *rest):
    weights, (slices, facts_out, chain_out, sem) = rest[:3], rest[3:]
    t = ids[0]
    own_width = slices.shape[2]
    transfers = []
    for k in range(3):
        transfer = pltpu.make_async_copy(
            own_slice(weights[k], t, own_width), slices.at[k], sem.at[k]
        )
        transfer.start()
        transfers.append(transfer)
    chain_row = chain[...]
    tokens = chain_row.shape[1]
    keep_row = keymask[...].astype(f32)
    line = lax.broadcasted_iota(jnp.int32, (128, tokens), 0)
    facts = jnp.where(line == 0, chain_row.astype(f32), 0.0) + jnp.where(line == 1, keep_row, 0.0)
    for h in range(own_heads):
        weight_row = jnp.zeros((1, tokens), f32)
        for m in range(chain_weight.shape[0]):
            weight_row = jnp.where(chain_row == m, chain_weight[m, t * own_heads + h], weight_row)
        facts = jnp.where(line == 2 + h, weight_row, facts)
    facts_out[...] = jnp.transpose(facts)
    chain_out[...] = chain_row.astype(f32)
    for transfer in transfers:
        transfer.wait()


def project_kernel(toks, ids, slices, *rest):
    parts = rest[:toks]
    x_out, outs = rest[toks], rest[toks + 1 :]
    t = ids[0]
    rows = parts[0].shape[0]
    for r in range(toks):
        start = pl.multiple_of(jnp.bitwise_xor(t, r) * rows, rows)
        x_out[pl.ds(start, rows), :] = parts[r][...]
    x = x_out[...]
    for k in range(3):
        outs[k][...] = jnp.transpose(mm(x, slices[k])).astype(bf16)


def join_kernel(*refs):
    for n, ref in enumerate(refs[:-1]):
        refs[-1][n] = ref[...]


def attention_kernel(copies, toks, near, cols, head_width, ids, query, key, value, *rest):
    biases, (facts, chain, weights_out, att_out) = rest[:near], rest[near : near + 4]
    pieces, bias = rest[near + 4 : near + 4 + toks], rest[near + 4 + toks]
    t, low, high = ids[0], low_bits(ids[1], near), ids[1] // near
    for m in range(near):
        for rz in range(copies // near):
            c = jnp.bitwise_xor(high, rz) * near + jnp.bitwise_xor(low, m)
            for r in range(toks):
                bias[c, jnp.bitwise_xor(t, r)] = biases[m][rz * toks + r]
    own_heads = weights_out.shape[0]
    tokens = query.shape[1]
    rows = tokens // toks
    same = facts[:, 0:1] == chain[...]
    keep = facts[:, 1:2] > 0.0
    scale = head_width ** (-0.5)
    attended = []
    for h in range(own_heads):
        span = slice(h * head_width, (h + 1) * head_width)
        logits = mm(key[span, :], query[span, :], TN) * scale
        line = slice(h * cols, (h + 1) * cols)
        extra = jnp.concatenate(
            [
                jnp.concatenate(
                    [bias[c, a, line, :] for c in range(copies)], axis=0
                )
                for a in range(toks)
            ],
            axis=1,
        ).astype(f32)
        logits = logits + (extra + jnp.where(same, facts[:, 2 + h : 3 + h], 0.0))
        logits = jnp.where(keep, logits, -1e30)
        exponent = jnp.exp(logits - jnp.max(logits, axis=0, keepdims=True))
        weights = exponent / jnp.sum(exponent, axis=0, keepdims=True)
        weights_b = weights.astype(bf16)
        weights_out[h] = weights_b
        attended.append(mm(value[span, :], weights_b))
    att_out[...] = jnp.transpose(jnp.concatenate(attended, axis=0)).astype(bf16)
    for r in range(toks):
        start = pl.multiple_of(jnp.bitwise_xor(t, r) * rows, rows)
        pieces[r][...] = att_out[pl.ds(start, rows), :]


def down_kernel(upstream, w_down, noisy, gain, d_hidden, upstream_out, noisy_out, gain_out):
    d_hidden[...] = mm(upstream[...], w_down[...], NT)
    upstream_out[...] = upstream[...]
    noisy_out[...] = noisy[...]
    gain_out[...] = gain[...]


def hidden_kernel(toks, chunk, ids, noisy, upstream, d_hidden, gain, *rest):
    parts = rest[:toks]
    held_out, held_gate, held_up = rest[toks : toks + 3]
    d_res_out, d_res_b_out = rest[toks + 3 : toks + 5]
    d_att_outs = rest[toks + 5 :]
    t = ids[0]
    hidden = held_gate.shape[1]
    residual = noisy[...].astype(f32)
    own_width = parts[0].shape[1]
    for r in range(toks):
        start = pl.multiple_of(jnp.bitwise_xor(t, r) * own_width, own_width)
        residual = residual + mm(parts[r][...], held_out[pl.ds(start, own_width), :])
    trans_scaled, trans_hat, trans_inverse = layer_forward(residual, gain[...])
    trans_in = trans_scaled.astype(bf16)
    d_trans = jnp.zeros(residual.shape, f32)
    for k in range(hidden // chunk):
        span = slice(k * chunk, (k + 1) * chunk)
        gate = mm(trans_in, held_gate[:, span])
        up = mm(trans_in, held_up[:, span])
        incoming = d_hidden[:, span]
        sigmoid = jax.nn.sigmoid(gate)
        d_up = (incoming * gate * sigmoid).astype(bf16)
        d_gate = (incoming * up * sigmoid * (1.0 + gate * (1.0 - sigmoid))).astype(bf16)
        d_trans = d_trans + mm(d_gate, held_gate[:, span], NT) + mm(d_up, held_up[:, span], NT)
    d_res = upstream[...].astype(f32) + layer_backward(
        d_trans, gain[...], trans_hat, trans_inverse
    )
    d_res_out[...] = d_res
    d_res_b = d_res.astype(bf16)
    d_res_b_out[...] = d_res_b
    for r in range(toks):
        start = pl.multiple_of(jnp.bitwise_xor(t, r) * own_width, own_width)
        d_att_outs[r][...] = mm(held_out[pl.ds(start, own_width), :], d_res_b, NT).astype(bf16)


def backward_kernel(copies, toks, cols, head_width, ids, query, key, value, weights, *rest):
    parts, d_res_b = rest[:toks], rest[toks]
    d_query, d_key, d_value, bias_kept, bias_sent, d_res_out = rest[toks + 1 : toks + 7]
    blocks, d_logits = rest[toks + 7 :]
    d_res_out[...] = d_res_b[...]
    t = ids[0]
    core = low_bits(ids[1], 2)
    for r in range(toks):
        blocks[jnp.bitwise_xor(t, r)] = parts[r][...]
    d_att = jnp.concatenate([blocks[a] for a in range(toks)], axis=1)
    count = tile_count(cols, query.shape[1])
    scale = head_width ** (-0.5)
    for h in range(weights.shape[0]):
        span = slice(h * head_width, (h + 1) * head_width)
        d_att_h = d_att[span, :]
        weights_b = weights[h]
        d_weights = mm(value[span, :], d_att_h, TN)
        weights_f = weights_b.astype(f32)
        delta = jnp.sum(weights_f * d_weights, axis=0, keepdims=True)
        d_logits_b = (weights_f * (d_weights - delta)).astype(bf16)
        d_logits[...] = d_logits_b
        for q in range(copies // 2):
            for side, out in ((core, bias_kept), (1 - core, bias_sent)):
                start = pl.multiple_of((2 * q + side) * cols, cols)
                put(out, q, h * count, d_logits[pl.ds(start, cols), :])
        d_query[span, :] = (mm(key[span, :], d_logits_b) * scale).astype(bf16)
        d_key[span, :] = (mm(query[span, :], d_logits_b, NT) * scale).astype(bf16)
        d_value[span, :] = mm(d_att_h, weights_b, NT).astype(bf16)


def tile_count(rows, lanes):
    return -(-rows // 16) * -(-lanes // 128)


def put(out, q, base, value):
    rows, lanes = value.shape
    for i in range(0, rows, 16):
        for j in range(0, lanes, 128):
            part = value[i : i + 16, j : j + 128]
            if part.shape != (16, 128):
                out[q, base] = jnp.zeros((16, 128), out.dtype)
            out[q, base, : part.shape[0], : part.shape[1]] = part
            base += 1


def take(tiles, base, rows, lanes):
    across = -(-lanes // 128)
    lines = []
    for i in range(-(-rows // 16)):
        line = [tiles[base + i * across + j] for j in range(across)]
        lines.append(jnp.concatenate(line, axis=1) if across > 1 else line[0])
    whole = jnp.concatenate(lines, axis=0) if len(lines) > 1 else lines[0]
    return whole[:rows, :lanes]


def cut_wide(copies, toks, core, base, grad, kept, sent):
    group = copies // toks
    cut, depth = grad.shape[1] // copies, grad.shape[1] // toks
    for side, out in ((core, kept), (1 - core, sent)):
        for q in range(copies // 2):
            h = 2 * q // group
            first = pl.multiple_of((2 * q - h * group + side) * cut, 8)
            part = grad[pl.ds(first, cut), h * depth : (h + 1) * depth]
            put(out, q, base, part.astype(bf16))


def first_kernel(copies, toks, ids, slices, x, d_query, d_key, d_value, *rest):
    kept, sent, d_own = rest[:3]
    d_others, (wide, d_inputs, total_ref) = rest[3 : 2 + toks], rest[2 + toks :]
    t, core = ids[0], low_bits(ids[1], 2)
    rows = d_own.shape[1]
    cut = x.shape[1] // copies
    count = tile_count(cut, d_query.shape[0])
    for k, part in enumerate((d_query, d_key)):
        wide[...] = mm(part[...], x[...])
        cut_wide(copies, toks, core, k * count, wide, kept, sent)
    total = mm(slices[0], d_query[...]) + mm(slices[1], d_key[...])
    total = total + mm(slices[2], d_value[...])
    total_ref[...] = total
    for side, out in ((core, kept), (1 - core, sent)):
        for q in range(copies // 2):
            start = pl.multiple_of((2 * q + side) * cut, 8)
            put(out, q, 2 * count, total_ref[pl.ds(start, cut), :].astype(bf16))
    for a in range(toks):
        d_inputs[a] = total[:, a * rows : (a + 1) * rows]
    d_own[...] = d_inputs[t]
    for r in range(1, toks):
        d_others[r - 1][...] = d_inputs[jnp.bitwise_xor(t, r)].astype(bf16)


def second_kernel(copies, toks, ids, x, att, d_value, *rest):
    d_res_parts, (kept, sent, d_res, wide, narrow) = rest[:toks], rest[toks:]
    t, core = ids[0], low_bits(ids[1], 2)
    rows = d_res_parts[0].shape[0]
    wide[...] = mm(d_value[...], x[...])
    cut_wide(copies, toks, core, 0, wide, kept, sent)
    for r in range(toks):
        start = pl.multiple_of(jnp.bitwise_xor(t, r) * rows, rows)
        d_res[pl.ds(start, rows), :] = d_res_parts[r][...]
    narrow[...] = mm(d_res[...], att[...], TN)
    cut = narrow.shape[0] // copies
    count = tile_count(cut, narrow.shape[1])
    for side, out in ((core, kept), (1 - core, sent)):
        for q in range(copies // 2):
            first = pl.multiple_of((2 * q + side) * cut, 8)
            put(out, q, count, narrow[pl.ds(first, cut), :].astype(bf16))


def step_kernel(segments, ids, *refs):
    count = 1 + max(segment[0] for segment in segments)
    ins, outs = refs[: 2 * count], refs[2 * count :]
    for source, base, parts, tiles, mask, inner, target, start in segments:
        kept, got = ins[2 * source : 2 * source + 2]
        bit = low_bits(ids[1] // mask, 2)
        for q in range(parts // 2):
            for side, out in ((bit, outs[2 * target]), (1 - bit, outs[2 * target + 1])):
                k = q // inner * 2 * inner + side * inner + q % inner
                span = pl.ds(base + k * tiles, tiles)
                out[start + q * tiles : start + (q + 1) * tiles] = (
                    kept[span].astype(f32) + got[span].astype(f32)
                ).astype(bf16)


def last_bias_kernel(toks, base, count, cols, ids, kept, got, *rest):
    pieces, blocks = rest[:toks], rest[toks]
    span = slice(base, base + count)
    tiles = kept[span].astype(f32) + got[span].astype(f32)
    part_rows, rows = pieces[0].shape
    heads = part_rows // cols
    total = jnp.concatenate(
        [take(tiles, h * (count // heads), cols, rows * toks) for h in range(heads)], axis=0
    )
    for a in range(toks):
        blocks[a] = total[:, a * rows : (a + 1) * rows].astype(bf16)
    for r in range(toks):
        pieces[r][...] = blocks[jnp.bitwise_xor(ids[0], r)]


def last_kernel(toks, ids, kept, got, kept_b, got_b, moved, final, *rest):
    pieces, blocks = rest[:toks], rest[toks]
    first = kept[...].astype(f32) + got[...].astype(f32)
    second = kept_b[...].astype(f32) + got_b[...].astype(f32)
    _, cut, own_width = moved.shape
    count = tile_count(cut, own_width)
    for k in range(2):
        moved[k] = take(first, k * count, cut, own_width).astype(bf16)
    moved[2] = take(second, 0, cut, own_width).astype(bf16)
    final[...] = take(second, count, cut, own_width)
    rows = blocks.shape[2]
    single = take(first, 2 * count, cut, rows * toks)
    for a in range(toks):
        blocks[a] = single[:, a * rows : (a + 1) * rows]
    for r in range(toks):
        pieces[r][...] = blocks[jnp.bitwise_xor(ids[0], r)].astype(bf16)


def finish_kernel(moved, *rest):
    parts, outs = rest[:-4], rest[-4:]
    for k in range(3):
        outs[k][...] = moved[k].astype(f32)
    total = parts[0][...].astype(f32)
    for part in parts[1:]:
        total = total + part[...].astype(f32)
    outs[3][...] = total


def exit_kernel(toks, noisy, gain, d_res, d_own, *rest):
    others, (grad_noisy,) = rest[: toks - 1], rest[toks - 1 :]
    total = d_own[...]
    for part in others:
        total = total + part[...].astype(f32)
    _, noisy_hat, noisy_inverse = layer_forward(noisy[...].astype(f32), gain[...])
    grad_noisy[...] = (
        d_res[...] + layer_backward(jnp.transpose(total), gain[...], noisy_hat, noisy_inverse)
    ).astype(bf16)


def pair_kernel(toks, cols, ids, pair, gain, w_pair, *rest):
    parts, (grad_pair, weight_grad, rounded, spread_out, grads) = rest[:toks], rest[toks:]
    head_count = w_pair.shape[0]
    part_rows, rows = parts[0].shape
    for r in range(toks):
        start = pl.multiple_of(jnp.bitwise_xor(ids[0], r) * part_rows, part_rows)
        grads[pl.ds(start, part_rows), :] = parts[r][...].astype(f32)
    grad = grads[...]
    pair_scaled, pair_hat, pair_inverse = layer_forward(pair[...].astype(f32), gain[...])
    rounded[...] = pair_scaled.astype(bf16).astype(f32)
    spread, row_col = pair_weight_rows(w_pair[...], head_count, cols)
    grad_b = grad.astype(bf16)
    turned = jnp.transpose(grad).astype(bf16)
    sums = jnp.zeros(spread.shape, f32)
    for j in range(cols):
        here = row_col == j
        column = rounded[pl.ds(j, rows, stride=cols), :].astype(bf16)
        sums = sums + jnp.where(here, mm(grad_b, column), 0.0)
        spread_out[pl.ds(j, rows, stride=cols), :] = mm(
            turned, jnp.where(here, spread, 0.0).astype(bf16)
        )
    grad_pair[...] = layer_backward(
        spread_out[...], gain[...], pair_hat, pair_inverse
    ).astype(bf16)
    for h in range(head_count):
        line = jnp.sum(sums[h * cols : (h + 1) * cols, :], axis=0, keepdims=True)
        for n in range(weight_grad.shape[0]):
            weight_grad[n, h : h + 1, :] = line


def swap_copy(value, mask):
    size = lax.axis_size("copy")
    return lax.ppermute(value, "copy", [(i, i ^ mask) for i in range(size)])


def swap_tok(value, mask):
    size = lax.axis_size("tok")
    return lax.ppermute(value, "tok", [(i, i ^ mask) for i in range(size)])


def exchange(value):
    return lax.all_to_all(value, ("copy", "tok"), 0, 0)


def per_device(
    noisy,
    single,
    pair,
    restype,
    chain,
    keymask,
    restype_table,
    norm_gain,
    pair_gain,
    trans_gain,
    w_query,
    w_key,
    w_value,
    w_out,
    w_pair,
    chain_weight,
    w_hidden_gate,
    w_hidden_up,
    w_down,
    cotangent,
):
    copies = lax.axis_size("copy")
    toks = lax.axis_size("tok")
    _, rows, width = noisy.shape
    cols = pair.shape[1]
    channels = pair.shape[2]
    heads = w_pair.shape[1]
    head_width = width // heads
    own_heads = heads // toks
    own_width = own_heads * head_width
    tokens = rows * toks
    hidden = w_down.shape[0]
    cut = width // copies
    devices = copies * toks
    ids = jnp.stack([lax.axis_index("tok"), lax.axis_index("copy")]).astype(jnp.int32)
    where_am_i = (ids, SMEM)
    noisy2 = noisy.reshape(rows, width)
    pair2 = pair.reshape(rows * cols, channels)
    pair_gain2 = pair_gain.reshape(1, channels)
    norm_gain2 = norm_gain.reshape(1, width)

    entered = call(
        functools.partial(enter_kernel, toks, cols),
        "enter",
        [where_am_i]
        + [(array, "fetch") for array in (noisy2, single, restype.reshape(1, rows))]
        + [(array, "fetch") for array in (restype_table, norm_gain, pair2, pair_gain2, w_pair.T)],
        [((rows, width), bf16)] + [((own_heads * cols, rows), bf16)] * toks,
        [VMEM((rows * cols, channels), f32), VMEM((heads * cols, rows), f32)],
        flops=2 * heads * cols * rows * channels * cols,
        limit=60,
    )
    x_own, bias_parts = entered[0], entered[1:]
    x_parts = [x_own] + [swap_tok(x_own, r) for r in range(1, toks)]
    near = 4
    far = copies // near
    weights3 = [w_query, w_key, w_value]
    if own_width % 128:
        weights3 = [
            lax.dynamic_slice_in_dim(w, ids[0] * own_width, own_width, axis=1) for w in weights3
        ]
    slices, facts, chain_row = call(
        functools.partial(stage_kernel, own_heads),
        "stage",
        [where_am_i, chain.reshape(1, tokens), keymask.reshape(1, tokens), (chain_weight, SMEM)]
        + [(w, ANY) for w in weights3],
        [((3, width, own_width), bf16), ((tokens, 128), f32), ((1, tokens), f32)],
        [pltpu.SemaphoreType.DMA((3,))],
    )
    def join(name, parts, deps=()):
        shape = (len(parts),) + parts[0].shape
        return call(join_kernel, name, parts, [(shape, bf16)], deps=deps)[0]

    mine = join(
        "join_tok", [bias_parts[0]] + [swap_tok(bias_parts[r], r) for r in range(1, toks)]
    )
    lines = join(
        "join_far",
        [mine] + [swap_copy(mine, m * near) for m in range(1, far)],
        deps=x_parts[1:] + [chain_row],
    )
    lines = lines.reshape((far * toks,) + lines.shape[2:])
    biases = [lines] + [swap_copy(lines, m) for m in range(1, near)]
    x, query, key, value = call(
        functools.partial(project_kernel, toks),
        "project",
        [where_am_i, slices] + x_parts,
        [((tokens, width), bf16)] + [((own_width, tokens), bf16)] * 3,
        flops=6 * tokens * width * own_width,
    )
    done = call(
        functools.partial(attention_kernel, copies, toks, near, cols, head_width),
        "attention",
        [where_am_i, query, key, value] + biases + [facts, chain_row],
        [((own_heads, tokens, tokens), bf16), ((tokens, own_width), bf16)]
        + [((rows, own_width), bf16)] * toks,
        [VMEM((copies, toks, own_heads * cols, rows), bf16)],
        flops=4 * tokens * tokens * own_width,
        limit=32,
    )
    weights, att, pieces = done[0], done[1], done[2:]
    att_parts = [pieces[0]] + [swap_tok(pieces[r], r) for r in range(1, toks)]

    d_hidden, upstream, noisy3, trans_gain2 = call(
        down_kernel,
        "down",
        [cotangent.reshape(rows, width), w_down, noisy2, trans_gain.reshape(1, width)],
        [((rows, hidden), f32), ((rows, width), bf16), ((rows, width), bf16), ((1, width), f32)],
        flops=2 * rows * hidden * width,
    )
    chunk = hidden // 3
    results = call(
        functools.partial(hidden_kernel, toks, chunk),
        "hidden",
        [where_am_i, noisy3, upstream, d_hidden, trans_gain2]
        + att_parts
        + [w_out, w_hidden_gate, w_hidden_up],
        [((rows, width), f32), ((rows, width), bf16)] + [((own_width, rows), bf16)] * toks,
        flops=2 * rows * width * (2 * width + 4 * hidden),
    )
    d_res, d_res_b, d_att = results[0], results[1], results[2:]
    d_att_parts = [d_att[0]] + [swap_tok(d_att[r], r) for r in range(1, toks)]
    bias_tiles = own_heads * tile_count(cols, tokens)
    bias_shape = (copies // 2, bias_tiles, 16, 128)
    d_query, d_key, d_value, bias_kept, bias_sent, d_res_b = call(
        functools.partial(backward_kernel, copies, toks, cols, head_width),
        "backward",
        [where_am_i, query, key, value, weights] + d_att_parts + [d_res_b],
        [((own_width, tokens), bf16)] * 3 + [(bias_shape, bf16)] * 2 + [((rows, width), bf16)],
        [VMEM((toks, own_width, rows), bf16), VMEM((tokens, tokens), bf16)],
        flops=8 * tokens * tokens * own_width,
        limit=32,
    )
    d_res_parts = [d_res_b] + [swap_tok(d_res_b, r) for r in range(1, toks)]
    bias_kept, bias_got = [
        array.reshape((-1, 16, 128)) for array in (bias_kept, swap_copy(bias_sent, 1))
    ]

    wide_tiles = tile_count(cut, own_width)
    single_tiles = tile_count(cut, tokens)
    found = call(
        functools.partial(first_kernel, copies, toks),
        "first",
        [where_am_i, slices, x, d_query, d_key, d_value],
        [((copies // 2, 2 * wide_tiles + single_tiles, 16, 128), bf16)] * 2
        + [((width, rows), f32)]
        + [((width, rows), bf16)] * (toks - 1),
        [
            VMEM((own_width, width), f32),
            VMEM((toks, width, rows), f32),
            VMEM((width, tokens), f32),
        ],
        flops=10 * tokens * width * own_width,
    )
    kept, sent, d_own = found[:3]
    got = swap_copy(sent, 1)
    d_others = [swap_tok(found[2 + r], r) for r in range(1, toks)]

    def step(name, pairs, segments, deps=()):
        filled, full, masks_of = {}, [], {}
        for source, base, parts, tiles, mask, left, target in segments:
            inner = 1 << sum(1 for other in left if other < mask)
            start = filled.get(target, 0)
            full.append((source, base, parts, tiles, mask, inner, target, start))
            filled[target] = start + parts // 2 * tiles
            masks_of[target] = mask
        outs = []
        for target in range(len(filled)):
            outs += [((filled[target], 16, 128), bf16)] * 2
        results = call(
            functools.partial(step_kernel, full),
            name,
            [where_am_i] + [array for one in pairs for array in one],
            outs,
            deps=deps,
        )
        return [
            (results[2 * n], swap_copy(results[2 * n + 1], masks_of[n]))
            for n in range(len(filled))
        ]

    masks = [1 << b for b in range(1, copies.bit_length() - 1)]
    masks_b = masks[1:] + masks[:1]
    bias_left, bias_parts = list(masks), copies // 2
    (bias_pair,) = step(
        "bias_first",
        [(bias_kept, bias_got)],
        [(0, 0, bias_parts, bias_tiles, masks[0], bias_left, 0)],
    )
    kept_b, sent_b = call(
        functools.partial(second_kernel, copies, toks),
        "second",
        [where_am_i, x, att, d_value] + d_res_parts,
        [((copies // 2, 2 * wide_tiles, 16, 128), bf16)] * 2,
        [
            VMEM((tokens, width), bf16),
            VMEM((own_width, width), f32),
            VMEM((width, own_width), f32),
        ],
        flops=4 * tokens * width * own_width,
        deps=[bias_pair[0]],
    )
    got_b = swap_copy(sent_b, 1)

    (grad_noisy,) = call(
        functools.partial(exit_kernel, toks),
        "exit",
        [noisy3, norm_gain2, d_res, d_own] + d_others,
        [((rows, width), bf16)],
    )
    for mask in masks[:1:-1]:
        bias_left = [other for other in bias_left if other != masks[0]]
        bias_parts //= 2
        (bias_pair,) = step(
            "bias_%d" % mask,
            [bias_pair],
            [(0, 0, bias_parts, bias_tiles, mask, bias_left, 0)],
            deps=[sent_b],
        )
        bias_left = [other for other in bias_left if other != mask]
    first_tiles, second_tiles = 2 * wide_tiles + single_tiles, 2 * wide_tiles
    pairs = [
        tuple(array.reshape((-1, 16, 128)) for array in one)
        for one in ((kept, got), (kept_b, got_b))
    ]
    pairs.append(bias_pair)
    parts = copies // 2
    for n, (mask, mask_b) in enumerate(zip(masks, masks_b)):
        segments = [
            (0, 0, parts, first_tiles, mask, masks[n:], 0),
            (1, 0, parts, second_tiles, mask_b, masks_b[n:], 1),
        ]
        deps = []
        if n == 0:
            segments.append((2, 0, 2, bias_tiles, mask_b, [mask_b], 1))
        if n == 1:
            bias_ready = pairs[1]
            bias_base = parts * second_tiles
            deps = [grad_noisy]
        if n == 2:
            deps = [weight_grad]
        pairs = step("step_%d" % n, pairs, segments, deps=deps)
        parts //= 2
        if n == 1:
            bias_pieces = call(
                functools.partial(last_bias_kernel, toks, bias_base, bias_tiles, cols),
                "last_bias",
                [where_am_i, *bias_ready],
                [((own_heads * cols, rows), bf16)] * toks,
                [VMEM((toks, own_heads * cols, rows), bf16)],
                deps=[pairs[0][0]],
            )
            bias_pieces = [bias_pieces[0]] + [
                swap_tok(bias_pieces[r], r) for r in range(1, toks)
            ]
            grad_pair, weight_grad = call(
                functools.partial(pair_kernel, toks, cols),
                "pair",
                [where_am_i, pair2, pair_gain2, w_pair.T] + bias_pieces,
                [((rows * cols, channels), bf16), ((devices, heads, channels), f32)],
                [VMEM((rows * cols, channels), f32)] * 2 + [VMEM((heads * cols, rows), f32)],
                flops=4 * heads * cols * rows * channels * cols,
            )

    group = copies // toks
    swaps = []
    for c in range(copies):
        for t in range(toks):
            swaps.append((c * toks + t, (t * group + c % group) * toks + c // group))

    weight_grad = jnp.sum(exchange(weight_grad), axis=0)
    last = call(
        functools.partial(last_kernel, toks),
        "last",
        [where_am_i, *pairs[0], *pairs[1]],
        [((3, cut, own_width), bf16), ((cut, own_width), f32)] + [((cut, rows), bf16)] * toks,
        [VMEM((toks, cut, rows), f32)],
        deps=[weight_grad],
    )
    grad_out, singles = last[1], last[2:]
    singles = [singles[0]] + [swap_tok(singles[r], r) for r in range(1, toks)]
    moved = lax.ppermute(last[0], ("copy", "tok"), swaps)
    grad_query, grad_key, grad_value, grad_single = call(
        finish_kernel,
        "finish",
        [moved] + singles,
        [((cut, own_width), f32)] * 3 + [((cut, rows), f32)],
    )
    return (
        grad_noisy[None],
        grad_single.T,
        grad_pair.reshape(rows, cols, channels),
        grad_query.T,
        grad_key.T,
        grad_value.T,
        grad_out.T,
        weight_grad.T,
    )


def solution(mesh):
    placed = (
        P("copy", "tok", None),
        P("tok", None),
        P("tok", "copy", None),
        P("tok"),
    ) + (P(),) * 15 + (P("copy", "tok", None),)
    return jax.shard_map(
        per_device,
        mesh=mesh,
        in_specs=placed,
        out_specs=(
            P("copy", "tok", None),
            P("tok", "copy"),
            P("tok", "copy", None),
            P("tok", "copy"),
            P("tok", "copy"),
            P("tok", "copy"),
            P("tok", "copy"),
            P(),
        ),
        check_vma=False,
    )
```

```python
import functools

import jax
import jax.numpy as jnp
from jax import lax
from jax.experimental import pallas as pl
from jax.experimental.pallas import tpu as pltpu
from jax.sharding import PartitionSpec as P

epsilon = 1e-05
f32 = jnp.float32
bf16 = jnp.bfloat16
VMEM, SMEM, ANY = pltpu.VMEM, pltpu.SMEM, pl.ANY
MIB = 1 << 20


def layer_forward(values, scales):
    average = jnp.mean(values, axis=-1, keepdims=True)
    centred = values - average
    inverse = lax.rsqrt(jnp.mean(centred * centred, axis=-1, keepdims=True) + epsilon)
    normed = centred * inverse
    return (normed * scales, normed, inverse)


def layer_backward(upstream, scales, normed, inverse):
    scaled = upstream * scales
    first_moment = jnp.mean(scaled, axis=-1, keepdims=True)
    second_moment = jnp.mean(scaled * normed, axis=-1, keepdims=True)
    return inverse * (scaled - first_moment - normed * second_moment)


NN = ((1,), (0,))
NT = ((1,), (1,))
TN = ((0,), (0,))


def mm(left, right, dims=NN):
    return lax.dot_general(left, right, (dims, ((), ())), preferred_element_type=f32)


def call(body, name, inputs, outs, scratch=(), flops=0, limit=16, deps=()):
    arrays, specs, moved, fetched = [], [], 0, []
    for item in inputs:
        array, space = item if isinstance(item, tuple) else (item, VMEM)
        if space == "fetch":
            fetched.append(len(arrays))
            space = pltpu.HBM
        arrays.append(array)
        specs.append(pl.BlockSpec(memory_space=space))
        moved += array.size * array.dtype.itemsize
    for shape, kind, *_ in outs:
        size = jnp.dtype(kind).itemsize
        for extent in shape:
            size *= extent
        moved += size
    read = len(arrays)
    for array in deps:
        arrays.append(array)
        specs.append(pl.BlockSpec(memory_space=ANY))
    extra = [VMEM(arrays[k].shape, arrays[k].dtype) for k in fetched]
    if fetched:
        extra.append(pltpu.SemaphoreType.DMA((len(fetched),)))

    def whole(*refs):
        refs = list(refs[:read]) + list(refs[read + len(deps) :])
        if fetched:
            held, sem = refs[-1 - len(fetched) : -1], refs[-1]
            refs = refs[: -1 - len(fetched)]
            transfers = []
            for n, k in enumerate(fetched):
                transfer = pltpu.make_async_copy(refs[k], held[n], sem.at[n])
                transfer.start()
                transfers.append(transfer)
                refs[k] = held[n]
            for transfer in transfers:
                transfer.wait()
        body(*refs)

    return pl.pallas_call(
        whole,
        name=name,
        out_shape=[jax.ShapeDtypeStruct(one[0], one[1]) for one in outs],
        in_specs=specs,
        out_specs=[pl.BlockSpec(memory_space=(*one, VMEM)[2]) for one in outs],
        scratch_shapes=list(scratch) + extra,
        compiler_params=pltpu.CompilerParams(vmem_limit_bytes=limit * MIB),
        cost_estimate=pl.CostEstimate(flops=flops, bytes_accessed=moved, transcendentals=0),
    )(*arrays)


def low_bits(index, size):
    return jnp.bitwise_and(index, size - 1)


def pair_weight_rows(w_pair, head_count, cols):
    rows = head_count * cols
    shift = cols.bit_length() - 1
    head = lax.shift_right_logical(
        lax.broadcasted_iota(jnp.int32, (rows, head_count), 0), jnp.int32(shift)
    )
    pick = (head == lax.broadcasted_iota(jnp.int32, (rows, head_count), 1)).astype(f32)
    spread = mm(pick.astype(bf16), w_pair)
    row_col = low_bits(lax.broadcasted_iota(jnp.int32, spread.shape, 0), cols)
    return spread, row_col


def own_slice(weight, t, own_width):
    if weight.shape[1] == own_width:
        return weight
    return weight.at[:, pl.ds(pl.multiple_of(t * own_width, own_width), own_width)]


def enter_kernel(toks, cols, ids, *rest):
    noisy, single, restype, table, gain, pair, pair_gain, w_pair, chain, keymask = rest[:10]
    chain_weight, weights = rest[10], rest[11:14]
    x_out, columns, slices, facts_out, chain_out = rest[14:19]
    bias_outs, (rounded, bias, sem) = rest[19 : 19 + toks], rest[19 + toks :]
    t = ids[0]
    transfers = []
    for k in range(3):
        transfer = pltpu.make_async_copy(
            own_slice(weights[k], t, slices.shape[2]), slices.at[k], sem.at[k]
        )
        transfer.start()
        transfers.append(transfer)
    rows = noisy.shape[0]
    pair_scaled, _, _ = layer_forward(pair[...].astype(f32), pair_gain[...])
    rounded[...] = pair_scaled.astype(bf16).astype(f32)
    head_count = w_pair.shape[0]
    spread, row_col = pair_weight_rows(w_pair[...], head_count, cols)
    total = jnp.zeros((head_count * cols, rows), f32)
    for j in range(cols):
        column = rounded[pl.ds(j, rows, stride=cols), :].astype(bf16)
        columns[j] = column
        total = total + mm(jnp.where(row_col == j, spread, 0.0).astype(bf16), column, NT)
    bias[...] = total
    part = bias_outs[0].shape[0]
    for r in range(toks):
        start = pl.multiple_of(jnp.bitwise_xor(t, r) * part, part)
        bias_outs[r][...] = bias[pl.ds(start, part), :].astype(bf16)
    normed_scaled, _, _ = layer_forward(noisy[...].astype(f32), gain[...])
    types = table.shape[0]
    onehot = (lax.broadcasted_iota(jnp.int32, (types, rows), 0) == restype[...]).astype(f32)
    condition = single[...].astype(f32) + mm(onehot.astype(bf16), table[...], TN)
    x_out[...] = (normed_scaled + condition).astype(bf16)
    chain_row = chain[...]
    tokens = chain_row.shape[1]
    own_heads = head_count // toks
    keep_row = keymask[...].astype(f32)
    line = lax.broadcasted_iota(jnp.int32, (128, tokens), 0)
    facts = jnp.where(line == 0, chain_row.astype(f32), 0.0) + jnp.where(line == 1, keep_row, 0.0)
    for h in range(own_heads):
        weight_row = jnp.zeros((1, tokens), f32)
        for m in range(chain_weight.shape[0]):
            weight_row = jnp.where(chain_row == m, chain_weight[m, t * own_heads + h], weight_row)
        facts = jnp.where(line == 2 + h, weight_row, facts)
    facts_out[...] = jnp.transpose(facts)
    chain_out[...] = chain_row.astype(f32)
    for transfer in transfers:
        transfer.wait()


def project_kernel(toks, ids, slices, *rest):
    parts = rest[:toks]
    x_out, outs = rest[toks], rest[toks + 1 :]
    t = ids[0]
    rows = parts[0].shape[0]
    for r in range(toks):
        start = pl.multiple_of(jnp.bitwise_xor(t, r) * rows, rows)
        x_out[pl.ds(start, rows), :] = parts[r][...]
    x = x_out[...]
    for k in range(3):
        outs[k][...] = jnp.transpose(mm(x, slices[k])).astype(bf16)


def join_kernel(*refs):
    for n, ref in enumerate(refs[:-1]):
        refs[-1][n] = ref[...]


def join_tok_kernel(x, *refs):
    refs[-1][...] = x[...]
    join_kernel(*refs[:-1])


def attention_kernel(copies, toks, near, cols, head_width, ids, query, key, value, *rest):
    biases, (facts, chain, weights_out, att_out) = rest[:near], rest[near : near + 4]
    pieces, bias = rest[near + 4 : near + 4 + toks], rest[near + 4 + toks]
    t, low, high = ids[0], low_bits(ids[1], near), ids[1] // near
    for m in range(near):
        for rz in range(copies // near):
            c = jnp.bitwise_xor(high, rz) * near + jnp.bitwise_xor(low, m)
            for r in range(toks):
                bias[c, jnp.bitwise_xor(t, r)] = biases[m][rz * toks + r]
    own_heads = weights_out.shape[0]
    tokens = query.shape[1]
    rows = tokens // toks
    same = facts[:, 0:1] == chain[...]
    keep = facts[:, 1:2] > 0.0
    scale = head_width ** (-0.5)
    attended = []
    for h in range(own_heads):
        span = slice(h * head_width, (h + 1) * head_width)
        logits = mm(key[span, :], query[span, :], TN) * scale
        line = slice(h * cols, (h + 1) * cols)
        extra = jnp.concatenate(
            [
                jnp.concatenate(
                    [bias[c, a, line, :] for c in range(copies)], axis=0
                )
                for a in range(toks)
            ],
            axis=1,
        ).astype(f32)
        logits = logits + (extra + jnp.where(same, facts[:, 2 + h : 3 + h], 0.0))
        logits = jnp.where(keep, logits, -1e30)
        exponent = jnp.exp(logits - jnp.max(logits, axis=0, keepdims=True))
        weights = exponent / jnp.sum(exponent, axis=0, keepdims=True)
        weights_b = weights.astype(bf16)
        weights_out[h] = weights_b
        attended.append(mm(value[span, :], weights_b))
    att_out[...] = jnp.transpose(jnp.concatenate(attended, axis=0)).astype(bf16)
    for r in range(toks):
        start = pl.multiple_of(jnp.bitwise_xor(t, r) * rows, rows)
        pieces[r][...] = att_out[pl.ds(start, rows), :]


def down_kernel(upstream, w_down, noisy, gain, d_hidden, upstream_out, noisy_out, gain_out):
    d_hidden[...] = mm(upstream[...], w_down[...], NT)
    upstream_out[...] = upstream[...]
    noisy_out[...] = noisy[...]
    gain_out[...] = gain[...]


def hidden_kernel(toks, chunk, ids, noisy, upstream, d_hidden, gain, *rest):
    parts = rest[:toks]
    held_out, held_gate, held_up = rest[toks : toks + 3]
    d_res_out, d_res_b_out = rest[toks + 3 : toks + 5]
    d_att_outs = rest[toks + 5 :]
    t = ids[0]
    hidden = held_gate.shape[1]
    residual = noisy[...].astype(f32)
    own_width = parts[0].shape[1]
    for r in range(toks):
        start = pl.multiple_of(jnp.bitwise_xor(t, r) * own_width, own_width)
        residual = residual + mm(parts[r][...], held_out[pl.ds(start, own_width), :])
    trans_scaled, trans_hat, trans_inverse = layer_forward(residual, gain[...])
    trans_in = trans_scaled.astype(bf16)
    d_trans = jnp.zeros(residual.shape, f32)
    for k in range(hidden // chunk):
        span = slice(k * chunk, (k + 1) * chunk)
        gate = mm(trans_in, held_gate[:, span])
        up = mm(trans_in, held_up[:, span])
        incoming = d_hidden[:, span]
        sigmoid = jax.nn.sigmoid(gate)
        d_up = (incoming * gate * sigmoid).astype(bf16)
        d_gate = (incoming * up * sigmoid * (1.0 + gate * (1.0 - sigmoid))).astype(bf16)
        d_trans = d_trans + mm(d_gate, held_gate[:, span], NT) + mm(d_up, held_up[:, span], NT)
    d_res = upstream[...].astype(f32) + layer_backward(
        d_trans, gain[...], trans_hat, trans_inverse
    )
    d_res_out[...] = d_res
    d_res_b = d_res.astype(bf16)
    d_res_b_out[...] = d_res_b
    for r in range(toks):
        start = pl.multiple_of(jnp.bitwise_xor(t, r) * own_width, own_width)
        d_att_outs[r][...] = mm(held_out[pl.ds(start, own_width), :], d_res_b, NT).astype(bf16)


def backward_kernel(copies, toks, cols, head_width, ids, query, key, value, weights, *rest):
    parts, d_res_b = rest[:toks], rest[toks]
    d_query, d_key, d_value, bias_kept, bias_sent, d_res_out = rest[toks + 1 : toks + 7]
    blocks, d_logits = rest[toks + 7 :]
    d_res_out[...] = d_res_b[...]
    t = ids[0]
    bit = low_bits(ids[1] // 2, 2)
    heads = weights.shape[0]
    for r in range(toks):
        blocks[jnp.bitwise_xor(t, r)] = parts[r][...]
    d_att = jnp.concatenate([blocks[a] for a in range(toks)], axis=1)
    count = tile_count(cols, query.shape[1])
    scale = head_width ** (-0.5)
    for h in range(weights.shape[0]):
        span = slice(h * head_width, (h + 1) * head_width)
        d_att_h = d_att[span, :]
        weights_b = weights[h]
        d_weights = mm(value[span, :], d_att_h, TN)
        weights_f = weights_b.astype(f32)
        delta = jnp.sum(weights_f * d_weights, axis=0, keepdims=True)
        d_logits_b = (weights_f * (d_weights - delta)).astype(bf16)
        d_logits[...] = d_logits_b
        for k in range(copies // 2):
            for side, out in ((bit, bias_kept), (1 - bit, bias_sent)):
                start = pl.multiple_of((k // 2 * 4 + side * 2 + k % 2) * cols, cols)
                put(out, (k * heads + h) * count, d_logits[pl.ds(start, cols), :])
        d_query[span, :] = (mm(key[span, :], d_logits_b) * scale).astype(bf16)
        d_key[span, :] = (mm(query[span, :], d_logits_b, NT) * scale).astype(bf16)
        d_value[span, :] = mm(d_att_h, weights_b, NT).astype(bf16)


def tile_count(rows, lanes):
    return -(-rows // 16) * -(-lanes // 128)


def put(out, base, value):
    rows, lanes = value.shape
    for i in range(0, rows, 16):
        for j in range(0, lanes, 128):
            part = value[i : i + 16, j : j + 128]
            if part.shape != (16, 128):
                out[base] = jnp.zeros((16, 128), out.dtype)
            out[base, : part.shape[0], : part.shape[1]] = part
            base += 1


def take(tiles, base, rows, lanes):
    across = -(-lanes // 128)
    lines = []
    for i in range(-(-rows // 16)):
        line = [tiles[base + i * across + j] for j in range(across)]
        lines.append(jnp.concatenate(line, axis=1) if across > 1 else line[0])
    whole = jnp.concatenate(lines, axis=0) if len(lines) > 1 else lines[0]
    return whole[:rows, :lanes]


def cut_wide(copies, toks, core, base, stride, grad, kept, sent):
    group = copies // toks
    cut, depth = grad.shape[1] // copies, grad.shape[1] // toks
    for side, out in ((core, kept), (1 - core, sent)):
        for q in range(copies // 2):
            h = 2 * q // group
            first = pl.multiple_of((2 * q - h * group + side) * cut, 8)
            part = grad[pl.ds(first, cut), h * depth : (h + 1) * depth]
            put(out, q * stride + base, part.astype(bf16))


def first_kernel(copies, toks, ids, slices, x, d_query, d_key, d_value, *rest):
    kept, sent, d_own = rest[:3]
    d_others, (wide, d_inputs, total_ref) = rest[3 : 2 + toks], rest[2 + toks :]
    t, core = ids[0], low_bits(ids[1], 2)
    rows = d_own.shape[1]
    cut = x.shape[1] // copies
    count = tile_count(cut, d_query.shape[0])
    stride = 2 * count + tile_count(cut, rows * toks)
    for k, part in enumerate((d_query, d_key)):
        wide[...] = mm(part[...], x[...])
        cut_wide(copies, toks, core, k * count, stride, wide, kept, sent)
    total = mm(slices[0], d_query[...]) + mm(slices[1], d_key[...])
    total = total + mm(slices[2], d_value[...])
    total_ref[...] = total
    for side, out in ((core, kept), (1 - core, sent)):
        for q in range(copies // 2):
            start = pl.multiple_of((2 * q + side) * cut, 8)
            put(out, q * stride + 2 * count, total_ref[pl.ds(start, cut), :].astype(bf16))
    for a in range(toks):
        d_inputs[a] = total[:, a * rows : (a + 1) * rows]
    d_own[...] = d_inputs[t]
    for r in range(1, toks):
        d_others[r - 1][...] = d_inputs[jnp.bitwise_xor(t, r)].astype(bf16)


def second_kernel(copies, toks, ids, x, att, d_value, bias_kept, bias_got, *rest):
    d_res_parts, (kept, sent, d_res, wide, narrow) = rest[:toks], rest[toks:]
    t, core = ids[0], low_bits(ids[1], 2)
    rows = d_res_parts[0].shape[0]
    cut = narrow.shape[0] // copies
    count = tile_count(cut, narrow.shape[1])
    wide[...] = mm(d_value[...], x[...])
    cut_wide(copies, toks, core, 0, 2 * count, wide, kept, sent)
    for r in range(toks):
        start = pl.multiple_of(jnp.bitwise_xor(t, r) * rows, rows)
        d_res[pl.ds(start, rows), :] = d_res_parts[r][...]
    narrow[...] = mm(d_res[...], att[...], TN)
    base = copies * count
    bias_count = bias_kept.shape[0] // (copies // 2)
    for side, out in ((core, kept), (1 - core, sent)):
        for q in range(copies // 2):
            first = pl.multiple_of((2 * q + side) * cut, 8)
            put(out, (2 * q + 1) * count, narrow[pl.ds(first, cut), :].astype(bf16))
        for z in range(copies // 4):
            span = pl.ds((2 * z + side) * bias_count, bias_count)
            out[base + z * bias_count : base + (z + 1) * bias_count] = (
                bias_kept[span].astype(f32) + bias_got[span].astype(f32)
            ).astype(bf16)


def step_kernel(segments, ids, *refs):
    count = 1 + max(segment[0] for segment in segments)
    ins, outs = refs[: 2 * count], refs[2 * count :]
    for source, base, parts, tiles, mask, inner, target, start in segments:
        kept, got = ins[2 * source : 2 * source + 2]
        bit = low_bits(ids[1] // mask, 2)
        for q in range(parts // 2):
            for side, out in ((bit, outs[2 * target]), (1 - bit, outs[2 * target + 1])):
                k = q // inner * 2 * inner + side * inner + q % inner
                span = pl.ds(base + k * tiles, tiles)
                out[start + q * tiles : start + (q + 1) * tiles] = (
                    kept[span].astype(f32) + got[span].astype(f32)
                ).astype(bf16)


def last_bias_kernel(toks, base, count, cols, ids, kept, got, *rest):
    pieces, blocks = rest[:toks], rest[toks]
    span = slice(base, base + count)
    tiles = kept[span].astype(f32) + got[span].astype(f32)
    part_rows, rows = pieces[0].shape
    heads = part_rows // cols
    total = jnp.concatenate(
        [take(tiles, h * (count // heads), cols, rows * toks) for h in range(heads)], axis=0
    )
    for a in range(toks):
        blocks[a] = total[:, a * rows : (a + 1) * rows].astype(bf16)
    for r in range(toks):
        pieces[r][...] = blocks[jnp.bitwise_xor(ids[0], r)]


def last_kernel(toks, ids, kept, got, kept_b, got_b, moved, final, *rest):
    pieces, blocks = rest[:toks], rest[toks]
    first = kept[...].astype(f32) + got[...].astype(f32)
    second = kept_b[...].astype(f32) + got_b[...].astype(f32)
    _, cut, own_width = moved.shape
    count = tile_count(cut, own_width)
    for k in range(2):
        moved[k] = take(first, k * count, cut, own_width).astype(bf16)
    moved[2] = take(second, 0, cut, own_width).astype(bf16)
    final[...] = take(second, count, cut, own_width)
    rows = blocks.shape[2]
    single = take(first, 2 * count, cut, rows * toks)
    for a in range(toks):
        blocks[a] = single[:, a * rows : (a + 1) * rows]
    for r in range(toks):
        pieces[r][...] = blocks[jnp.bitwise_xor(ids[0], r)].astype(bf16)


def finish_kernel(moved, *rest):
    parts, outs = rest[:-4], rest[-4:]
    for k in range(3):
        outs[k][...] = moved[k].astype(f32)
    total = parts[0][...].astype(f32)
    for part in parts[1:]:
        total = total + part[...].astype(f32)
    outs[3][...] = total


def exit_kernel(toks, noisy, gain, d_res, d_own, *rest):
    others, (grad_noisy,) = rest[: toks - 1], rest[toks - 1 :]
    total = d_own[...]
    for part in others:
        total = total + part[...].astype(f32)
    _, noisy_hat, noisy_inverse = layer_forward(noisy[...].astype(f32), gain[...])
    grad_noisy[...] = (
        d_res[...] + layer_backward(jnp.transpose(total), gain[...], noisy_hat, noisy_inverse)
    ).astype(bf16)


def set_heads(toks, ids, parts, grads):
    part_rows = parts[0].shape[0]
    for r in range(toks):
        start = pl.multiple_of(jnp.bitwise_xor(ids[0], r) * part_rows, part_rows)
        grads[pl.ds(start, part_rows), :] = parts[r][...].astype(f32)


def pair_weight_kernel(toks, ids, columns, *rest):
    parts, (weight_grad, grads) = rest[:toks], rest[toks:]
    set_heads(toks, ids, parts, grads)
    grad_b = grads[...].astype(bf16)
    cols, _, channels = columns.shape
    row_col = low_bits(lax.broadcasted_iota(jnp.int32, (grad_b.shape[0], channels), 0), cols)
    sums = jnp.zeros((grad_b.shape[0], channels), f32)
    for j in range(cols):
        sums = sums + jnp.where(row_col == j, mm(grad_b, columns[j]), 0.0)
    for h in range(weight_grad.shape[1]):
        line = jnp.sum(sums[h * cols : (h + 1) * cols, :], axis=0, keepdims=True)
        for n in range(weight_grad.shape[0]):
            weight_grad[n, h : h + 1, :] = line


def pair_kernel(toks, cols, ids, pair, gain, w_pair, *rest):
    parts, (grad_pair, spread_out, grads) = rest[:toks], rest[toks:]
    set_heads(toks, ids, parts, grads)
    rows = parts[0].shape[1]
    _, pair_hat, pair_inverse = layer_forward(pair[...].astype(f32), gain[...])
    spread, row_col = pair_weight_rows(w_pair[...], w_pair.shape[0], cols)
    turned = jnp.transpose(grads[...]).astype(bf16)
    for j in range(cols):
        spread_out[pl.ds(j, rows, stride=cols), :] = mm(
            turned, jnp.where(row_col == j, spread, 0.0).astype(bf16)
        )
    grad_pair[...] = layer_backward(
        spread_out[...], gain[...], pair_hat, pair_inverse
    ).astype(bf16)


def swap_copy(value, mask):
    size = lax.axis_size("copy")
    return lax.ppermute(value, "copy", [(i, i ^ mask) for i in range(size)])


def swap_tok(value, mask):
    size = lax.axis_size("tok")
    return lax.ppermute(value, "tok", [(i, i ^ mask) for i in range(size)])


def exchange(value):
    return lax.all_to_all(value, ("copy", "tok"), 0, 0)


def per_device(
    noisy,
    single,
    pair,
    restype,
    chain,
    keymask,
    restype_table,
    norm_gain,
    pair_gain,
    trans_gain,
    w_query,
    w_key,
    w_value,
    w_out,
    w_pair,
    chain_weight,
    w_hidden_gate,
    w_hidden_up,
    w_down,
    cotangent,
):
    copies = lax.axis_size("copy")
    toks = lax.axis_size("tok")
    _, rows, width = noisy.shape
    cols = pair.shape[1]
    channels = pair.shape[2]
    heads = w_pair.shape[1]
    head_width = width // heads
    own_heads = heads // toks
    own_width = own_heads * head_width
    tokens = rows * toks
    hidden = w_down.shape[0]
    cut = width // copies
    devices = copies * toks
    ids = jnp.stack([lax.axis_index("tok"), lax.axis_index("copy")]).astype(jnp.int32)
    where_am_i = (ids, SMEM)
    noisy2 = noisy.reshape(rows, width)
    pair2 = pair.reshape(rows * cols, channels)
    pair_gain2 = pair_gain.reshape(1, channels)
    norm_gain2 = norm_gain.reshape(1, width)

    weights3 = [w_query, w_key, w_value]
    if own_width % 128:
        weights3 = [
            lax.dynamic_slice_in_dim(w, ids[0] * own_width, own_width, axis=1) for w in weights3
        ]
    small = [noisy2, single, restype.reshape(1, rows), restype_table, norm_gain, pair2, pair_gain2]
    small += [w_pair.T, chain.reshape(1, tokens), keymask.reshape(1, tokens)]
    entered = call(
        functools.partial(enter_kernel, toks, cols),
        "enter",
        [where_am_i]
        + [(array, "fetch") for array in small]
        + [(chain_weight, SMEM)]
        + [(w, ANY) for w in weights3],
        [((rows, width), bf16), ((cols, rows, channels), bf16)]
        + [((3, width, own_width), bf16, ANY), ((tokens, 128), f32), ((1, tokens), f32)]
        + [((own_heads * cols, rows), bf16)] * toks,
        [VMEM((rows * cols, channels), f32), VMEM((heads * cols, rows), f32)]
        + [pltpu.SemaphoreType.DMA((3,))],
        flops=2 * heads * cols * rows * channels * cols,
        limit=60,
    )
    x_own, columns, slices, facts, chain_row = entered[:5]
    bias_parts = entered[5:]
    near = 4
    far = copies // near
    part_shape = bias_parts[0].shape
    bias_tok = [bias_parts[0]] + [swap_tok(bias_parts[r], r) for r in range(1, toks)]
    mine, x_own = call(
        join_tok_kernel,
        "join_tok",
        [(array, "fetch") for array in [x_own] + bias_tok],
        [((toks,) + part_shape, bf16), ((rows, width), bf16)],
        limit=60,
    )
    x_parts = [x_own] + [swap_tok(x_own, r) for r in range(1, toks)]
    (lines,) = call(
        join_kernel,
        "join_far",
        [mine] + [swap_copy(mine, m * near) for m in range(1, far)],
        [((far, toks) + part_shape, bf16)],
        deps=x_parts[1:],
    )
    lines = lines.reshape((far * toks,) + lines.shape[2:])
    biases = [lines] + [swap_copy(lines, m) for m in range(1, near)]
    x, query, key, value = call(
        functools.partial(project_kernel, toks),
        "project",
        [where_am_i, slices] + x_parts,
        [((tokens, width), bf16)] + [((own_width, tokens), bf16)] * 3,
        flops=6 * tokens * width * own_width,
    )
    done = call(
        functools.partial(attention_kernel, copies, toks, near, cols, head_width),
        "attention",
        [where_am_i, query, key, value] + biases + [facts, chain_row],
        [((own_heads, tokens, tokens), bf16), ((tokens, own_width), bf16)]
        + [((rows, own_width), bf16)] * toks,
        [VMEM((copies, toks, own_heads * cols, rows), bf16)],
        flops=4 * tokens * tokens * own_width,
        limit=32,
    )
    weights, att, pieces = done[0], done[1], done[2:]
    att_parts = [pieces[0]] + [swap_tok(pieces[r], r) for r in range(1, toks)]

    d_hidden, upstream, noisy3, trans_gain2 = call(
        down_kernel,
        "down",
        [cotangent.reshape(rows, width), w_down, noisy2, trans_gain.reshape(1, width)],
        [((rows, hidden), f32), ((rows, width), bf16), ((rows, width), bf16), ((1, width), f32)],
        flops=2 * rows * hidden * width,
    )
    chunk = hidden // 3
    results = call(
        functools.partial(hidden_kernel, toks, chunk),
        "hidden",
        [where_am_i, noisy3, upstream, d_hidden, trans_gain2]
        + att_parts
        + [w_out, w_hidden_gate, w_hidden_up],
        [((rows, width), f32), ((rows, width), bf16)] + [((own_width, rows), bf16)] * toks,
        flops=2 * rows * width * (2 * width + 4 * hidden),
    )
    d_res, d_res_b, d_att = results[0], results[1], results[2:]
    d_att_parts = [d_att[0]] + [swap_tok(d_att[r], r) for r in range(1, toks)]
    bias_tiles = own_heads * tile_count(cols, tokens)
    bias_shape = (copies // 2 * bias_tiles, 16, 128)
    d_query, d_key, d_value, bias_kept, bias_sent, d_res_b = call(
        functools.partial(backward_kernel, copies, toks, cols, head_width),
        "backward",
        [where_am_i, query, key, value, weights] + d_att_parts + [d_res_b],
        [((own_width, tokens), bf16)] * 3 + [(bias_shape, bf16)] * 2 + [((rows, width), bf16)],
        [VMEM((toks, own_width, rows), bf16), VMEM((tokens, tokens), bf16)],
        flops=8 * tokens * tokens * own_width,
        limit=32,
    )
    d_res_parts = [d_res_b] + [swap_tok(d_res_b, r) for r in range(1, toks)]
    bias_got = swap_copy(bias_sent, 2)

    wide_tiles = tile_count(cut, own_width)
    single_tiles = tile_count(cut, tokens)
    first_tiles, second_tiles = 2 * wide_tiles + single_tiles, 2 * wide_tiles
    found = call(
        functools.partial(first_kernel, copies, toks),
        "first",
        [where_am_i, slices, x, d_query, d_key, d_value],
        [((copies // 2 * first_tiles, 16, 128), bf16)] * 2
        + [((width, rows), f32)]
        + [((width, rows), bf16)] * (toks - 1),
        [
            VMEM((own_width, width), f32),
            VMEM((toks, width, rows), f32),
            VMEM((width, tokens), f32),
        ],
        flops=10 * tokens * width * own_width,
    )
    kept, sent, d_own = found[:3]
    got = swap_copy(sent, 1)
    d_others = [swap_tok(found[2 + r], r) for r in range(1, toks)]

    def step(name, pairs, segments, deps=()):
        filled, full, masks_of = {}, [], {}
        for source, base, parts, tiles, mask, left, target in segments:
            inner = 1 << sum(1 for other in left if other < mask)
            start = filled.get(target, 0)
            full.append((source, base, parts, tiles, mask, inner, target, start))
            filled[target] = start + parts // 2 * tiles
            masks_of[target] = mask
        outs = []
        for target in range(len(filled)):
            outs += [((filled[target], 16, 128), bf16)] * 2
        results = call(
            functools.partial(step_kernel, full),
            name,
            [where_am_i] + [array for one in pairs for array in one],
            outs,
            deps=deps,
        )
        return [
            (results[2 * n], swap_copy(results[2 * n + 1], masks_of[n]))
            for n in range(len(filled))
        ]

    masks = [1 << b for b in range(1, copies.bit_length() - 1)]
    masks_b = masks[1:] + masks[:1]
    kept_b, sent_b = call(
        functools.partial(second_kernel, copies, toks),
        "second",
        [where_am_i, x, att, d_value, bias_kept, bias_got] + d_res_parts,
        [((copies // 2 * second_tiles + copies // 4 * bias_tiles, 16, 128), bf16)] * 2,
        [
            VMEM((tokens, width), bf16),
            VMEM((own_width, width), f32),
            VMEM((width, own_width), f32),
        ],
        flops=4 * tokens * width * own_width,
    )
    got_b = swap_copy(sent_b, 1)

    (grad_noisy,) = call(
        functools.partial(exit_kernel, toks),
        "exit",
        [noisy3, norm_gain2, d_res, d_own] + d_others,
        [((rows, width), bf16)],
    )
    pairs = [(kept, got), (kept_b, got_b)]
    parts = copies // 2
    for n, (mask, mask_b) in enumerate(zip(masks, masks_b)):
        segments = [
            (0, 0, parts, first_tiles, mask, masks[n:], 0),
            (1, 0, parts, second_tiles, mask_b, masks_b[n:], 1),
        ]
        bias_base = parts * second_tiles
        if n + 1 < len(masks):
            segments.append((1, bias_base, parts // 2, bias_tiles, mask_b, masks_b[n:-1], 1))
        else:
            bias_ready = pairs[1]
        pairs = step("step_%d" % n, pairs, segments, deps=[grad_noisy] if n == 1 else ())
        parts //= 2
    bias_pieces = call(
        functools.partial(last_bias_kernel, toks, bias_base, bias_tiles, cols),
        "last_bias",
        [where_am_i, *bias_ready],
        [((own_heads * cols, rows), bf16)] * toks,
        [VMEM((toks, own_heads * cols, rows), bf16)],
        deps=[pairs[0][0]],
    )
    bias_pieces = [bias_pieces[0]] + [swap_tok(bias_pieces[r], r) for r in range(1, toks)]

    group = copies // toks
    swaps = []
    for c in range(copies):
        for t in range(toks):
            swaps.append((c * toks + t, (t * group + c % group) * toks + c // group))

    last = call(
        functools.partial(last_kernel, toks),
        "last",
        [where_am_i, *pairs[0], *pairs[1]],
        [((3, cut, own_width), bf16), ((cut, own_width), f32)] + [((cut, rows), bf16)] * toks,
        [VMEM((toks, cut, rows), f32)],
        deps=bias_pieces[1:],
    )
    (weight_grad,) = call(
        functools.partial(pair_weight_kernel, toks),
        "pair_weight",
        [where_am_i, columns] + bias_pieces,
        [((devices, heads, channels), f32)],
        [VMEM((heads * cols, rows), f32)],
        flops=2 * heads * cols * rows * channels * cols,
        deps=[last[0]],
    )
    (grad_pair,) = call(
        functools.partial(pair_kernel, toks, cols),
        "pair",
        [where_am_i, pair2, pair_gain2, w_pair.T] + bias_pieces,
        [((rows * cols, channels), bf16)],
        [VMEM((rows * cols, channels), f32), VMEM((heads * cols, rows), f32)],
        flops=2 * heads * cols * rows * channels * cols,
        deps=[weight_grad],
    )
    weight_grad = jnp.sum(exchange(weight_grad), axis=0)
    grad_out, singles = last[1], last[2:]
    singles = [singles[0]] + [swap_tok(singles[r], r) for r in range(1, toks)]
    moved = lax.ppermute(last[0], ("copy", "tok"), swaps)
    grad_query, grad_key, grad_value, grad_single = call(
        finish_kernel,
        "finish",
        [moved] + singles,
        [((cut, own_width), f32)] * 3 + [((cut, rows), f32)],
    )
    return (
        grad_noisy[None],
        grad_single.T,
        grad_pair.reshape(rows, cols, channels),
        grad_query.T,
        grad_key.T,
        grad_value.T,
        grad_out.T,
        weight_grad.T,
    )


def solution(mesh):
    placed = (
        P("copy", "tok", None),
        P("tok", None),
        P("tok", "copy", None),
        P("tok"),
    ) + (P(),) * 15 + (P("copy", "tok", None),)
    return jax.shard_map(
        per_device,
        mesh=mesh,
        in_specs=placed,
        out_specs=(
            P("copy", "tok", None),
            P("tok", "copy"),
            P("tok", "copy", None),
            P("tok", "copy"),
            P("tok", "copy"),
            P("tok", "copy"),
            P("tok", "copy"),
            P(),
        ),
        check_vma=False,
    )
```

```python
import functools

import jax
import jax.numpy as jnp
from jax import lax
from jax.experimental import pallas as pl
from jax.experimental.pallas import tpu as pltpu
from jax.sharding import PartitionSpec as P

epsilon = 1e-05
f32 = jnp.float32
bf16 = jnp.bfloat16
VMEM, SMEM, ANY = pltpu.VMEM, pltpu.SMEM, pl.ANY
MIB = 1 << 20


def layer_forward(values, scales):
    average = jnp.mean(values, axis=-1, keepdims=True)
    centred = values - average
    inverse = lax.rsqrt(jnp.mean(centred * centred, axis=-1, keepdims=True) + epsilon)
    normed = centred * inverse
    return (normed * scales, normed, inverse)


def layer_backward(upstream, scales, normed, inverse):
    scaled = upstream * scales
    first_moment = jnp.mean(scaled, axis=-1, keepdims=True)
    second_moment = jnp.mean(scaled * normed, axis=-1, keepdims=True)
    return inverse * (scaled - first_moment - normed * second_moment)


NN = ((1,), (0,))
NT = ((1,), (1,))
TN = ((0,), (0,))


def mm(left, right, dims=NN):
    return lax.dot_general(left, right, (dims, ((), ())), preferred_element_type=f32)


def call(body, name, inputs, outs, scratch=(), flops=0, limit=16, deps=()):
    arrays, specs, moved, fetched = [], [], 0, []
    for item in inputs:
        array, space = item if isinstance(item, tuple) else (item, VMEM)
        if space == "fetch":
            fetched.append(len(arrays))
            space = pltpu.HBM
        arrays.append(array)
        specs.append(pl.BlockSpec(memory_space=space))
        moved += array.size * array.dtype.itemsize
    for shape, kind, *_ in outs:
        size = jnp.dtype(kind).itemsize
        for extent in shape:
            size *= extent
        moved += size
    read = len(arrays)
    for array in deps:
        arrays.append(array)
        specs.append(pl.BlockSpec(memory_space=ANY))
    extra = [VMEM(arrays[k].shape, arrays[k].dtype) for k in fetched]
    if fetched:
        extra.append(pltpu.SemaphoreType.DMA((len(fetched),)))

    def whole(*refs):
        refs = list(refs[:read]) + list(refs[read + len(deps) :])
        if fetched:
            held, sem = refs[-1 - len(fetched) : -1], refs[-1]
            refs = refs[: -1 - len(fetched)]
            transfers = []
            for n, k in enumerate(fetched):
                transfer = pltpu.make_async_copy(refs[k], held[n], sem.at[n])
                transfer.start()
                transfers.append(transfer)
                refs[k] = held[n]
            for transfer in transfers:
                transfer.wait()
        body(*refs)

    return pl.pallas_call(
        whole,
        name=name,
        out_shape=[jax.ShapeDtypeStruct(one[0], one[1]) for one in outs],
        in_specs=specs,
        out_specs=[pl.BlockSpec(memory_space=(*one, VMEM)[2]) for one in outs],
        scratch_shapes=list(scratch) + extra,
        compiler_params=pltpu.CompilerParams(vmem_limit_bytes=limit * MIB),
        cost_estimate=pl.CostEstimate(flops=flops, bytes_accessed=moved, transcendentals=0),
    )(*arrays)


def low_bits(index, size):
    return jnp.bitwise_and(index, size - 1)


def pair_weight_rows(w_pair, head_count, cols):
    rows = head_count * cols
    shift = cols.bit_length() - 1
    head = lax.shift_right_logical(
        lax.broadcasted_iota(jnp.int32, (rows, head_count), 0), jnp.int32(shift)
    )
    pick = (head == lax.broadcasted_iota(jnp.int32, (rows, head_count), 1)).astype(f32)
    spread = mm(pick.astype(bf16), w_pair)
    row_col = low_bits(lax.broadcasted_iota(jnp.int32, spread.shape, 0), cols)
    return spread, row_col


def own_slice(weight, t, own_width):
    if weight.shape[1] == own_width:
        return weight
    return weight.at[:, pl.ds(pl.multiple_of(t * own_width, own_width), own_width)]


def enter_kernel(toks, cols, ids, *rest):
    noisy, single, restype, table, gain, pair, pair_gain, w_pair, chain, keymask = rest[:10]
    chain_weight, x_out, columns, facts_out, chain_out, bias_out, rounded, bias = rest[10:]
    t = ids[0]
    rows = noisy.shape[0]
    pair_scaled, _, _ = layer_forward(pair[...].astype(f32), pair_gain[...])
    rounded[...] = pair_scaled.astype(bf16).astype(f32)
    head_count = w_pair.shape[0]
    spread, row_col = pair_weight_rows(w_pair[...], head_count, cols)
    total = jnp.zeros((head_count * cols, rows), f32)
    for j in range(cols):
        column = rounded[pl.ds(j, rows, stride=cols), :].astype(bf16)
        columns[j] = column
        total = total + mm(jnp.where(row_col == j, spread, 0.0).astype(bf16), column, NT)
    bias[...] = total
    part = bias_out.shape[1]
    for r in range(toks):
        start = pl.multiple_of(jnp.bitwise_xor(t, r) * part, part)
        bias_out[r] = bias[pl.ds(start, part), :].astype(bf16)
    normed_scaled, _, _ = layer_forward(noisy[...].astype(f32), gain[...])
    types = table.shape[0]
    onehot = (lax.broadcasted_iota(jnp.int32, (types, rows), 0) == restype[...]).astype(f32)
    condition = single[...].astype(f32) + mm(onehot.astype(bf16), table[...], TN)
    x_out[...] = (normed_scaled + condition).astype(bf16)
    chain_row = chain[...]
    tokens = chain_row.shape[1]
    own_heads = head_count // toks
    keep_row = keymask[...].astype(f32)
    line = lax.broadcasted_iota(jnp.int32, (128, tokens), 0)
    facts = jnp.where(line == 0, chain_row.astype(f32), 0.0) + jnp.where(line == 1, keep_row, 0.0)
    for h in range(own_heads):
        weight_row = jnp.zeros((1, tokens), f32)
        for m in range(chain_weight.shape[0]):
            weight_row = jnp.where(chain_row == m, chain_weight[m, t * own_heads + h], weight_row)
        facts = jnp.where(line == 2 + h, weight_row, facts)
    facts_out[...] = jnp.transpose(facts)
    chain_out[...] = chain_row.astype(f32)


def stage_kernel(ids, *rest):
    weights, (slices, sem) = rest[:3], rest[3:]
    transfers = []
    for k in range(3):
        transfer = pltpu.make_async_copy(
            own_slice(weights[k], ids[0], slices.shape[2]), slices.at[k], sem.at[k]
        )
        transfer.start()
        transfers.append(transfer)
    for transfer in transfers:
        transfer.wait()


def project_kernel(toks, ids, slices, *rest):
    parts = rest[:toks]
    x_out, outs = rest[toks], rest[toks + 1 :]
    t = ids[0]
    rows = parts[0].shape[0]
    for r in range(toks):
        start = pl.multiple_of(jnp.bitwise_xor(t, r) * rows, rows)
        x_out[pl.ds(start, rows), :] = parts[r][...]
    x = x_out[...]
    for k in range(3):
        outs[k][...] = jnp.transpose(mm(x, slices[k])).astype(bf16)


def split_kernel(count, *refs):
    for n in range(count):
        for r, out in enumerate(refs[count:]):
            out[n] = refs[n][r]


def join_kernel(*refs):
    for n, ref in enumerate(refs[:-1]):
        refs[-1][n] = ref[...]


def attention_kernel(copies, toks, near, cols, head_width, ids, query, key, value, *rest):
    biases, (facts, chain, weights_out, att_out) = rest[:near], rest[near : near + 4]
    pieces, bias = rest[near + 4 : near + 4 + toks], rest[near + 4 + toks]
    t, low, high = ids[0], low_bits(ids[1], near), ids[1] // near
    for m in range(near):
        for rz in range(copies // near):
            c = jnp.bitwise_xor(high, rz) * near + jnp.bitwise_xor(low, m)
            for r in range(toks):
                bias[c, jnp.bitwise_xor(t, r)] = biases[m][r, rz]
    own_heads = weights_out.shape[0]
    tokens = query.shape[1]
    rows = tokens // toks
    same = facts[:, 0:1] == chain[...]
    keep = facts[:, 1:2] > 0.0
    scale = head_width ** (-0.5)
    attended = []
    for h in range(own_heads):
        span = slice(h * head_width, (h + 1) * head_width)
        logits = mm(key[span, :], query[span, :], TN) * scale
        line = slice(h * cols, (h + 1) * cols)
        extra = jnp.concatenate(
            [
                jnp.concatenate(
                    [bias[c, a, line, :] for c in range(copies)], axis=0
                )
                for a in range(toks)
            ],
            axis=1,
        ).astype(f32)
        logits = logits + (extra + jnp.where(same, facts[:, 2 + h : 3 + h], 0.0))
        logits = jnp.where(keep, logits, -1e30)
        exponent = jnp.exp(logits - jnp.max(logits, axis=0, keepdims=True))
        weights = exponent / jnp.sum(exponent, axis=0, keepdims=True)
        weights_b = weights.astype(bf16)
        weights_out[h] = weights_b
        attended.append(mm(value[span, :], weights_b))
    att_out[...] = jnp.transpose(jnp.concatenate(attended, axis=0)).astype(bf16)
    for r in range(toks):
        start = pl.multiple_of(jnp.bitwise_xor(t, r) * rows, rows)
        pieces[r][...] = att_out[pl.ds(start, rows), :]


def down_kernel(upstream, w_down, noisy, gain, d_hidden, upstream_out, noisy_out, gain_out):
    d_hidden[...] = mm(upstream[...], w_down[...], NT)
    upstream_out[...] = upstream[...]
    noisy_out[...] = noisy[...]
    gain_out[...] = gain[...]


def hidden_kernel(toks, chunk, ids, noisy, upstream, d_hidden, gain, *rest):
    parts = rest[:toks]
    held_out, held_gate, held_up = rest[toks : toks + 3]
    d_res_out, d_res_b_out = rest[toks + 3 : toks + 5]
    d_att_outs = rest[toks + 5 :]
    t = ids[0]
    hidden = held_gate.shape[1]
    residual = noisy[...].astype(f32)
    own_width = parts[0].shape[1]
    for r in range(toks):
        start = pl.multiple_of(jnp.bitwise_xor(t, r) * own_width, own_width)
        residual = residual + mm(parts[r][...], held_out[pl.ds(start, own_width), :])
    trans_scaled, trans_hat, trans_inverse = layer_forward(residual, gain[...])
    trans_in = trans_scaled.astype(bf16)
    d_trans = jnp.zeros(residual.shape, f32)
    for k in range(hidden // chunk):
        span = slice(k * chunk, (k + 1) * chunk)
        gate = mm(trans_in, held_gate[:, span])
        up = mm(trans_in, held_up[:, span])
        incoming = d_hidden[:, span]
        sigmoid = jax.nn.sigmoid(gate)
        d_up = (incoming * gate * sigmoid).astype(bf16)
        d_gate = (incoming * up * sigmoid * (1.0 + gate * (1.0 - sigmoid))).astype(bf16)
        d_trans = d_trans + mm(d_gate, held_gate[:, span], NT) + mm(d_up, held_up[:, span], NT)
    d_res = upstream[...].astype(f32) + layer_backward(
        d_trans, gain[...], trans_hat, trans_inverse
    )
    d_res_out[...] = d_res
    d_res_b = d_res.astype(bf16)
    d_res_b_out[...] = d_res_b
    for r in range(toks):
        start = pl.multiple_of(jnp.bitwise_xor(t, r) * own_width, own_width)
        d_att_outs[r][...] = mm(held_out[pl.ds(start, own_width), :], d_res_b, NT).astype(bf16)


def backward_kernel(copies, toks, cols, head_width, ids, query, key, value, weights, *rest):
    parts, d_res_b = rest[:toks], rest[toks]
    d_query, d_key, d_value, bias_kept, bias_sent, d_res_out = rest[toks + 1 : toks + 7]
    blocks, d_logits = rest[toks + 7 :]
    d_res_out[...] = d_res_b[...]
    t = ids[0]
    bit = low_bits(ids[1] // 2, 2)
    heads = weights.shape[0]
    for r in range(toks):
        blocks[jnp.bitwise_xor(t, r)] = parts[r][...]
    d_att = jnp.concatenate([blocks[a] for a in range(toks)], axis=1)
    count = tile_count(cols, query.shape[1])
    scale = head_width ** (-0.5)
    for h in range(weights.shape[0]):
        span = slice(h * head_width, (h + 1) * head_width)
        d_att_h = d_att[span, :]
        weights_b = weights[h]
        d_weights = mm(value[span, :], d_att_h, TN)
        weights_f = weights_b.astype(f32)
        delta = jnp.sum(weights_f * d_weights, axis=0, keepdims=True)
        d_logits_b = (weights_f * (d_weights - delta)).astype(bf16)
        d_logits[...] = d_logits_b
        for k in range(copies // 2):
            for side, out in ((bit, bias_kept), (1 - bit, bias_sent)):
                start = pl.multiple_of((k // 2 * 4 + side * 2 + k % 2) * cols, cols)
                put(out, (k * heads + h) * count, d_logits[pl.ds(start, cols), :])
        d_query[span, :] = (mm(key[span, :], d_logits_b) * scale).astype(bf16)
        d_key[span, :] = (mm(query[span, :], d_logits_b, NT) * scale).astype(bf16)
        d_value[span, :] = mm(d_att_h, weights_b, NT).astype(bf16)


def tile_count(rows, lanes):
    return -(-rows // 16) * -(-lanes // 128)


def put(out, base, value):
    rows, lanes = value.shape
    for i in range(0, rows, 16):
        for j in range(0, lanes, 128):
            part = value[i : i + 16, j : j + 128]
            if part.shape != (16, 128):
                out[base] = jnp.zeros((16, 128), out.dtype)
            out[base, : part.shape[0], : part.shape[1]] = part
            base += 1


def take(tiles, base, rows, lanes):
    across = -(-lanes // 128)
    lines = []
    for i in range(-(-rows // 16)):
        line = [tiles[base + i * across + j] for j in range(across)]
        lines.append(jnp.concatenate(line, axis=1) if across > 1 else line[0])
    whole = jnp.concatenate(lines, axis=0) if len(lines) > 1 else lines[0]
    return whole[:rows, :lanes]


def cut_wide(copies, toks, core, base, stride, grad, kept, sent):
    group = copies // toks
    cut, depth = grad.shape[1] // copies, grad.shape[1] // toks
    for side, out in ((core, kept), (1 - core, sent)):
        for q in range(copies // 2):
            h = 2 * q // group
            first = pl.multiple_of((2 * q - h * group + side) * cut, 8)
            part = grad[pl.ds(first, cut), h * depth : (h + 1) * depth]
            put(out, q * stride + base, part.astype(bf16))


def first_kernel(copies, toks, ids, slices, x, d_query, d_key, d_value, *rest):
    kept, sent, d_own = rest[:3]
    d_others, (wide, d_inputs, total_ref) = rest[3 : 2 + toks], rest[2 + toks :]
    t, core = ids[0], low_bits(ids[1], 2)
    rows = d_own.shape[1]
    cut = x.shape[1] // copies
    count = tile_count(cut, d_query.shape[0])
    stride = 2 * count + tile_count(cut, rows * toks)
    for k, part in enumerate((d_query, d_key)):
        wide[...] = mm(part[...], x[...])
        cut_wide(copies, toks, core, k * count, stride, wide, kept, sent)
    total = mm(slices[0], d_query[...]) + mm(slices[1], d_key[...])
    total = total + mm(slices[2], d_value[...])
    total_ref[...] = total
    for side, out in ((core, kept), (1 - core, sent)):
        for q in range(copies // 2):
            start = pl.multiple_of((2 * q + side) * cut, 8)
            put(out, q * stride + 2 * count, total_ref[pl.ds(start, cut), :].astype(bf16))
    for a in range(toks):
        d_inputs[a] = total[:, a * rows : (a + 1) * rows]
    d_own[...] = d_inputs[t]
    for r in range(1, toks):
        d_others[r - 1][...] = d_inputs[jnp.bitwise_xor(t, r)].astype(bf16)


def second_kernel(copies, toks, ids, x, att, d_value, bias_kept, bias_got, *rest):
    d_res_parts, (kept, sent, d_res, wide, narrow) = rest[:toks], rest[toks:]
    t, core = ids[0], low_bits(ids[1], 2)
    rows = d_res_parts[0].shape[0]
    cut = narrow.shape[0] // copies
    count = tile_count(cut, narrow.shape[1])
    wide[...] = mm(d_value[...], x[...])
    cut_wide(copies, toks, core, 0, 2 * count, wide, kept, sent)
    for r in range(toks):
        start = pl.multiple_of(jnp.bitwise_xor(t, r) * rows, rows)
        d_res[pl.ds(start, rows), :] = d_res_parts[r][...]
    narrow[...] = mm(d_res[...], att[...], TN)
    base = copies * count
    bias_count = bias_kept.shape[0] // (copies // 2)
    for side, out in ((core, kept), (1 - core, sent)):
        for q in range(copies // 2):
            first = pl.multiple_of((2 * q + side) * cut, 8)
            put(out, (2 * q + 1) * count, narrow[pl.ds(first, cut), :].astype(bf16))
        for z in range(copies // 4):
            span = pl.ds((2 * z + side) * bias_count, bias_count)
            out[base + z * bias_count : base + (z + 1) * bias_count] = (
                bias_kept[span].astype(f32) + bias_got[span].astype(f32)
            ).astype(bf16)


def step_kernel(segments, ids, *refs):
    count = 1 + max(segment[0] for segment in segments)
    ins, outs = refs[: 2 * count], refs[2 * count :]
    for source, base, parts, tiles, mask, inner, target, start in segments:
        kept, got = ins[2 * source : 2 * source + 2]
        bit = low_bits(ids[1] // mask, 2)
        for q in range(parts // 2):
            for side, out in ((bit, outs[2 * target]), (1 - bit, outs[2 * target + 1])):
                k = q // inner * 2 * inner + side * inner + q % inner
                span = pl.ds(base + k * tiles, tiles)
                out[start + q * tiles : start + (q + 1) * tiles] = (
                    kept[span].astype(f32) + got[span].astype(f32)
                ).astype(bf16)


def last_bias_kernel(toks, base, count, cols, ids, kept, got, *rest):
    pieces, blocks = rest[:toks], rest[toks]
    span = slice(base, base + count)
    tiles = kept[span].astype(f32) + got[span].astype(f32)
    part_rows, rows = pieces[0].shape
    heads = part_rows // cols
    total = jnp.concatenate(
        [take(tiles, h * (count // heads), cols, rows * toks) for h in range(heads)], axis=0
    )
    for a in range(toks):
        blocks[a] = total[:, a * rows : (a + 1) * rows].astype(bf16)
    for r in range(toks):
        pieces[r][...] = blocks[jnp.bitwise_xor(ids[0], r)]


def last_kernel(toks, ids, kept, got, kept_b, got_b, moved, final, *rest):
    pieces, blocks = rest[:toks], rest[toks]
    first = kept[...].astype(f32) + got[...].astype(f32)
    second = kept_b[...].astype(f32) + got_b[...].astype(f32)
    _, cut, own_width = moved.shape
    count = tile_count(cut, own_width)
    for k in range(2):
        moved[k] = take(first, k * count, cut, own_width).astype(bf16)
    moved[2] = take(second, 0, cut, own_width).astype(bf16)
    final[...] = take(second, count, cut, own_width)
    rows = blocks.shape[2]
    single = take(first, 2 * count, cut, rows * toks)
    for a in range(toks):
        blocks[a] = single[:, a * rows : (a + 1) * rows]
    for r in range(toks):
        pieces[r][...] = blocks[jnp.bitwise_xor(ids[0], r)].astype(bf16)


def finish_kernel(moved, *rest):
    parts, outs = rest[:-4], rest[-4:]
    for k in range(3):
        outs[k][...] = moved[k].astype(f32)
    total = parts[0][...].astype(f32)
    for part in parts[1:]:
        total = total + part[...].astype(f32)
    outs[3][...] = total


def exit_kernel(toks, noisy, gain, d_res, d_own, *rest):
    others, (grad_noisy, token) = rest[: toks - 1], rest[toks - 1 :]
    token[...] = jnp.zeros(token.shape, f32)
    total = d_own[...]
    for part in others:
        total = total + part[...].astype(f32)
    _, noisy_hat, noisy_inverse = layer_forward(noisy[...].astype(f32), gain[...])
    grad_noisy[...] = (
        d_res[...] + layer_backward(jnp.transpose(total), gain[...], noisy_hat, noisy_inverse)
    ).astype(bf16)


def set_heads(toks, ids, parts, grads):
    part_rows = parts[0].shape[0]
    for r in range(toks):
        start = pl.multiple_of(jnp.bitwise_xor(ids[0], r) * part_rows, part_rows)
        grads[pl.ds(start, part_rows), :] = parts[r][...].astype(f32)


def pair_weight_kernel(toks, ids, columns, *rest):
    parts, (weight_grad, grads) = rest[:toks], rest[toks:]
    set_heads(toks, ids, parts, grads)
    grad_b = grads[...].astype(bf16)
    cols, _, channels = columns.shape
    row_col = low_bits(lax.broadcasted_iota(jnp.int32, (grad_b.shape[0], channels), 0), cols)
    sums = jnp.zeros((grad_b.shape[0], channels), f32)
    for j in range(cols):
        sums = sums + jnp.where(row_col == j, mm(grad_b, columns[j]), 0.0)
    for h in range(weight_grad.shape[1]):
        line = jnp.sum(sums[h * cols : (h + 1) * cols, :], axis=0, keepdims=True)
        for n in range(weight_grad.shape[0]):
            weight_grad[n, h : h + 1, :] = line


def pair_kernel(toks, cols, ids, pair, gain, w_pair, *rest):
    parts, (grad_pair, spread_out, grads) = rest[:toks], rest[toks:]
    set_heads(toks, ids, parts, grads)
    rows = parts[0].shape[1]
    _, pair_hat, pair_inverse = layer_forward(pair[...].astype(f32), gain[...])
    spread, row_col = pair_weight_rows(w_pair[...], w_pair.shape[0], cols)
    turned = jnp.transpose(grads[...]).astype(bf16)
    for j in range(cols):
        spread_out[pl.ds(j, rows, stride=cols), :] = mm(
            turned, jnp.where(row_col == j, spread, 0.0).astype(bf16)
        )
    grad_pair[...] = layer_backward(
        spread_out[...], gain[...], pair_hat, pair_inverse
    ).astype(bf16)


def swap_copy(value, mask):
    size = lax.axis_size("copy")
    return lax.ppermute(value, "copy", [(i, i ^ mask) for i in range(size)])


def swap_tok(value, mask):
    size = lax.axis_size("tok")
    return lax.ppermute(value, "tok", [(i, i ^ mask) for i in range(size)])


def exchange(value):
    return lax.all_to_all(value, ("copy", "tok"), 0, 0)


def per_device(
    noisy,
    single,
    pair,
    restype,
    chain,
    keymask,
    restype_table,
    norm_gain,
    pair_gain,
    trans_gain,
    w_query,
    w_key,
    w_value,
    w_out,
    w_pair,
    chain_weight,
    w_hidden_gate,
    w_hidden_up,
    w_down,
    cotangent,
):
    copies = lax.axis_size("copy")
    toks = lax.axis_size("tok")
    _, rows, width = noisy.shape
    cols = pair.shape[1]
    channels = pair.shape[2]
    heads = w_pair.shape[1]
    head_width = width // heads
    own_heads = heads // toks
    own_width = own_heads * head_width
    tokens = rows * toks
    hidden = w_down.shape[0]
    cut = width // copies
    devices = copies * toks
    ids = jnp.stack([lax.axis_index("tok"), lax.axis_index("copy")]).astype(jnp.int32)
    where_am_i = (ids, SMEM)
    noisy2 = noisy.reshape(rows, width)
    pair2 = pair.reshape(rows * cols, channels)
    pair_gain2 = pair_gain.reshape(1, channels)
    norm_gain2 = norm_gain.reshape(1, width)

    weights3 = [w_query, w_key, w_value]
    if own_width % 128:
        weights3 = [
            lax.dynamic_slice_in_dim(w, ids[0] * own_width, own_width, axis=1) for w in weights3
        ]
    small = [noisy2, single, restype.reshape(1, rows), restype_table, norm_gain, pair2, pair_gain2]
    small += [w_pair.T, chain.reshape(1, tokens), keymask.reshape(1, tokens)]
    entered = call(
        functools.partial(enter_kernel, toks, cols),
        "enter",
        [where_am_i]
        + [(array, "fetch") for array in small]
        + [(chain_weight, SMEM)],
        [((rows, width), bf16), ((cols, rows, channels), bf16)]
        + [((tokens, 128), f32), ((1, tokens), f32), ((toks, own_heads * cols, rows), bf16)],
        [VMEM((rows * cols, channels), f32), VMEM((heads * cols, rows), f32)],
        flops=2 * heads * cols * rows * channels * cols,
        limit=60,
    )
    x_own, columns, facts, chain_row, bias_mine = entered
    near = 4
    far = copies // near
    x_parts = [x_own] + [swap_tok(x_own, r) for r in range(1, toks)]
    (slices,) = call(
        stage_kernel,
        "stage",
        [where_am_i] + [(w, ANY) for w in weights3],
        [((3, width, own_width), bf16)],
        [pltpu.SemaphoreType.DMA((3,))],
        deps=[chain_row],
    )
    by_tok = call(
        functools.partial(split_kernel, far),
        "split_far",
        [bias_mine] + [swap_copy(bias_mine, m * near) for m in range(1, far)],
        [((far, own_heads * cols, rows), bf16)] * toks,
        deps=[slices] + x_parts[1:],
    )
    (lines,) = call(
        join_kernel,
        "join_tok",
        [by_tok[0]] + [swap_tok(by_tok[r], r) for r in range(1, toks)],
        [((toks, far, own_heads * cols, rows), bf16)],
    )
    biases = [lines] + [swap_copy(lines, m) for m in range(1, near)]
    x, query, key, value = call(
        functools.partial(project_kernel, toks),
        "project",
        [where_am_i, slices] + x_parts,
        [((tokens, width), bf16)] + [((own_width, tokens), bf16)] * 3,
        flops=6 * tokens * width * own_width,
    )
    done = call(
        functools.partial(attention_kernel, copies, toks, near, cols, head_width),
        "attention",
        [where_am_i, query, key, value] + biases + [facts, chain_row],
        [((own_heads, tokens, tokens), bf16), ((tokens, own_width), bf16)]
        + [((rows, own_width), bf16)] * toks,
        [VMEM((copies, toks, own_heads * cols, rows), bf16)],
        flops=4 * tokens * tokens * own_width,
        limit=32,
    )
    weights, att, pieces = done[0], done[1], done[2:]
    att_parts = [pieces[0]] + [swap_tok(pieces[r], r) for r in range(1, toks)]

    d_hidden, upstream, noisy3, trans_gain2 = call(
        down_kernel,
        "down",
        [cotangent.reshape(rows, width), w_down, noisy2, trans_gain.reshape(1, width)],
        [((rows, hidden), f32), ((rows, width), bf16), ((rows, width), bf16), ((1, width), f32)],
        flops=2 * rows * hidden * width,
    )
    chunk = hidden // 3
    results = call(
        functools.partial(hidden_kernel, toks, chunk),
        "hidden",
        [where_am_i, noisy3, upstream, d_hidden, trans_gain2]
        + att_parts
        + [w_out, w_hidden_gate, w_hidden_up],
        [((rows, width), f32), ((rows, width), bf16)] + [((own_width, rows), bf16)] * toks,
        flops=2 * rows * width * (2 * width + 4 * hidden),
    )
    d_res, d_res_b, d_att = results[0], results[1], results[2:]
    d_att_parts = [d_att[0]] + [swap_tok(d_att[r], r) for r in range(1, toks)]
    bias_tiles = own_heads * tile_count(cols, tokens)
    bias_shape = (copies // 2 * bias_tiles, 16, 128)
    d_query, d_key, d_value, bias_kept, bias_sent, d_res_b = call(
        functools.partial(backward_kernel, copies, toks, cols, head_width),
        "backward",
        [where_am_i, query, key, value, weights] + d_att_parts + [d_res_b],
        [((own_width, tokens), bf16)] * 3 + [(bias_shape, bf16)] * 2 + [((rows, width), bf16)],
        [VMEM((toks, own_width, rows), bf16), VMEM((tokens, tokens), bf16)],
        flops=8 * tokens * tokens * own_width,
        limit=32,
    )
    d_res_parts = [d_res_b] + [swap_tok(d_res_b, r) for r in range(1, toks)]
    bias_got = swap_copy(bias_sent, 2)

    wide_tiles = tile_count(cut, own_width)
    single_tiles = tile_count(cut, tokens)
    first_tiles, second_tiles = 2 * wide_tiles + single_tiles, 2 * wide_tiles
    found = call(
        functools.partial(first_kernel, copies, toks),
        "first",
        [where_am_i, slices, x, d_query, d_key, d_value],
        [((copies // 2 * first_tiles, 16, 128), bf16)] * 2
        + [((width, rows), f32)]
        + [((width, rows), bf16)] * (toks - 1),
        [
            VMEM((own_width, width), f32),
            VMEM((toks, width, rows), f32),
            VMEM((width, tokens), f32),
        ],
        flops=10 * tokens * width * own_width,
    )
    kept, sent, d_own = found[:3]
    got = swap_copy(sent, 1)
    d_others = [swap_tok(found[2 + r], r) for r in range(1, toks)]

    def step(name, pairs, segments, deps=()):
        filled, full, masks_of = {}, [], {}
        for source, base, parts, tiles, mask, left, target in segments:
            inner = 1 << sum(1 for other in left if other < mask)
            start = filled.get(target, 0)
            full.append((source, base, parts, tiles, mask, inner, target, start))
            filled[target] = start + parts // 2 * tiles
            masks_of[target] = mask
        outs = []
        for target in range(len(filled)):
            outs += [((filled[target], 16, 128), bf16)] * 2
        results = call(
            functools.partial(step_kernel, full),
            name,
            [where_am_i] + [array for one in pairs for array in one],
            outs,
            deps=deps,
        )
        return [
            (results[2 * n], swap_copy(results[2 * n + 1], masks_of[n]))
            for n in range(len(filled))
        ]

    masks = [1 << b for b in range(1, copies.bit_length() - 1)]
    masks_b = masks[1:] + masks[:1]
    kept_b, sent_b = call(
        functools.partial(second_kernel, copies, toks),
        "second",
        [where_am_i, x, att, d_value, bias_kept, bias_got] + d_res_parts,
        [((copies // 2 * second_tiles + copies // 4 * bias_tiles, 16, 128), bf16)] * 2,
        [
            VMEM((tokens, width), bf16),
            VMEM((own_width, width), f32),
            VMEM((width, own_width), f32),
        ],
        flops=4 * tokens * width * own_width,
    )
    got_b = swap_copy(sent_b, 1)

    grad_noisy, exited = call(
        functools.partial(exit_kernel, toks),
        "exit",
        [noisy3, norm_gain2, d_res, d_own] + d_others,
        [((rows, width), bf16), ((8, 128), f32)],
    )
    pairs = [(kept, got), (kept_b, got_b)]
    parts = copies // 2
    for n, (mask, mask_b) in enumerate(zip(masks, masks_b)):
        segments = [
            (0, 0, parts, first_tiles, mask, masks[n:], 0),
            (1, 0, parts, second_tiles, mask_b, masks_b[n:], 1),
        ]
        bias_base = parts * second_tiles
        if n + 1 < len(masks):
            segments.append((1, bias_base, parts // 2, bias_tiles, mask_b, masks_b[n:-1], 1))
        else:
            bias_ready = pairs[1]
        pairs = step("step_%d" % n, pairs, segments, deps=[exited] if n == 1 else ())
        parts //= 2
    bias_pieces = call(
        functools.partial(last_bias_kernel, toks, bias_base, bias_tiles, cols),
        "last_bias",
        [where_am_i, *bias_ready],
        [((own_heads * cols, rows), bf16)] * toks,
        [VMEM((toks, own_heads * cols, rows), bf16)],
        deps=[pairs[0][0]],
    )
    bias_pieces = [bias_pieces[0]] + [swap_tok(bias_pieces[r], r) for r in range(1, toks)]

    group = copies // toks
    swaps = []
    for c in range(copies):
        for t in range(toks):
            swaps.append((c * toks + t, (t * group + c % group) * toks + c // group))

    (weight_grad,) = call(
        functools.partial(pair_weight_kernel, toks),
        "pair_weight",
        [where_am_i, columns] + bias_pieces,
        [((devices, heads, channels), f32)],
        [VMEM((heads * cols, rows), f32)],
        flops=2 * heads * cols * rows * channels * cols,
    )
    last = call(
        functools.partial(last_kernel, toks),
        "last",
        [where_am_i, *pairs[0], *pairs[1]],
        [((3, cut, own_width), bf16), ((cut, own_width), f32)] + [((cut, rows), bf16)] * toks,
        [VMEM((toks, cut, rows), f32)],
        deps=[weight_grad],
    )
    (grad_pair,) = call(
        functools.partial(pair_kernel, toks, cols),
        "pair",
        [where_am_i, pair2, pair_gain2, w_pair.T] + bias_pieces,
        [((rows * cols, channels), bf16)],
        [VMEM((rows * cols, channels), f32), VMEM((heads * cols, rows), f32)],
        flops=2 * heads * cols * rows * channels * cols,
        deps=[last[0]],
    )
    weight_grad = jnp.sum(exchange(weight_grad), axis=0)
    grad_out, singles = last[1], last[2:]
    singles = [singles[0]] + [swap_tok(singles[r], r) for r in range(1, toks)]
    moved = lax.ppermute(last[0], ("copy", "tok"), swaps)
    grad_query, grad_key, grad_value, grad_single = call(
        finish_kernel,
        "finish",
        [moved] + singles,
        [((cut, own_width), f32)] * 3 + [((cut, rows), f32)],
    )
    return (
        grad_noisy[None],
        grad_single.T,
        grad_pair.reshape(rows, cols, channels),
        grad_query.T,
        grad_key.T,
        grad_value.T,
        grad_out.T,
        weight_grad.T,
    )


def solution(mesh):
    placed = (
        P("copy", "tok", None),
        P("tok", None),
        P("tok", "copy", None),
        P("tok"),
    ) + (P(),) * 15 + (P("copy", "tok", None),)
    return jax.shard_map(
        per_device,
        mesh=mesh,
        in_specs=placed,
        out_specs=(
            P("copy", "tok", None),
            P("tok", "copy"),
            P("tok", "copy", None),
            P("tok", "copy"),
            P("tok", "copy"),
            P("tok", "copy"),
            P("tok", "copy"),
            P(),
        ),
        check_vma=False,
    )
```

```python
import functools

import jax
import jax.numpy as jnp
from jax import lax
from jax.experimental import pallas as pl
from jax.experimental.pallas import tpu as pltpu
from jax.sharding import PartitionSpec as P

epsilon = 1e-05
f32 = jnp.float32
bf16 = jnp.bfloat16
VMEM, SMEM, ANY = pltpu.VMEM, pltpu.SMEM, pl.ANY
MIB = 1 << 20


def layer_forward(values, scales):
    average = jnp.mean(values, axis=-1, keepdims=True)
    centred = values - average
    inverse = lax.rsqrt(jnp.mean(centred * centred, axis=-1, keepdims=True) + epsilon)
    normed = centred * inverse
    return (normed * scales, normed, inverse)


def layer_backward(upstream, scales, normed, inverse):
    scaled = upstream * scales
    first_moment = jnp.mean(scaled, axis=-1, keepdims=True)
    second_moment = jnp.mean(scaled * normed, axis=-1, keepdims=True)
    return inverse * (scaled - first_moment - normed * second_moment)


NN = ((1,), (0,))
NT = ((1,), (1,))
TN = ((0,), (0,))


def mm(left, right, dims=NN):
    return lax.dot_general(left, right, (dims, ((), ())), preferred_element_type=f32)


def call(body, name, inputs, outs, scratch=(), flops=0, limit=16, deps=()):
    arrays, specs, moved, fetched = [], [], 0, []
    for item in inputs:
        array, space = item if isinstance(item, tuple) else (item, VMEM)
        if space == "fetch":
            fetched.append(len(arrays))
            space = pltpu.HBM
        arrays.append(array)
        specs.append(pl.BlockSpec(memory_space=space))
        moved += array.size * array.dtype.itemsize
    for shape, kind, *_ in outs:
        size = jnp.dtype(kind).itemsize
        for extent in shape:
            size *= extent
        moved += size
    read = len(arrays)
    for array in deps:
        arrays.append(array)
        specs.append(pl.BlockSpec(memory_space=ANY))
    extra = [VMEM(arrays[k].shape, arrays[k].dtype) for k in fetched]
    if fetched:
        extra.append(pltpu.SemaphoreType.DMA((len(fetched),)))

    def whole(*refs):
        refs = list(refs[:read]) + list(refs[read + len(deps) :])
        if fetched:
            held, sem = refs[-1 - len(fetched) : -1], refs[-1]
            refs = refs[: -1 - len(fetched)]
            transfers = []
            for n, k in enumerate(fetched):
                transfer = pltpu.make_async_copy(refs[k], held[n], sem.at[n])
                transfer.start()
                transfers.append(transfer)
                refs[k] = held[n]
            for transfer in transfers:
                transfer.wait()
        body(*refs)

    return pl.pallas_call(
        whole,
        name=name,
        out_shape=[jax.ShapeDtypeStruct(one[0], one[1]) for one in outs],
        in_specs=specs,
        out_specs=[pl.BlockSpec(memory_space=(*one, VMEM)[2]) for one in outs],
        scratch_shapes=list(scratch) + extra,
        compiler_params=pltpu.CompilerParams(vmem_limit_bytes=limit * MIB),
        cost_estimate=pl.CostEstimate(flops=flops, bytes_accessed=moved, transcendentals=0),
    )(*arrays)


def low_bits(index, size):
    return jnp.bitwise_and(index, size - 1)


def pair_weight_rows(w_pair, head_count, cols):
    rows = head_count * cols
    shift = cols.bit_length() - 1
    head = lax.shift_right_logical(
        lax.broadcasted_iota(jnp.int32, (rows, head_count), 0), jnp.int32(shift)
    )
    pick = (head == lax.broadcasted_iota(jnp.int32, (rows, head_count), 1)).astype(f32)
    spread = mm(pick.astype(bf16), w_pair)
    row_col = low_bits(lax.broadcasted_iota(jnp.int32, spread.shape, 0), cols)
    return spread, row_col


def own_slice(weight, t, own_width):
    if weight.shape[1] == own_width:
        return weight
    return weight.at[:, pl.ds(pl.multiple_of(t * own_width, own_width), own_width)]


def enter_kernel(toks, cols, ids, *rest):
    noisy, single, restype, table, gain, pair, pair_gain, w_pair, chain, keymask = rest[:10]
    chain_weight, x_out, columns, facts_out, chain_out, bias_out, rounded, bias = rest[10:]
    t = ids[0]
    rows = noisy.shape[0]
    pair_scaled, _, _ = layer_forward(pair[...].astype(f32), pair_gain[...])
    rounded[...] = pair_scaled.astype(bf16).astype(f32)
    head_count = w_pair.shape[0]
    spread, row_col = pair_weight_rows(w_pair[...], head_count, cols)
    total = jnp.zeros((head_count * cols, rows), f32)
    for j in range(cols):
        column = rounded[pl.ds(j, rows, stride=cols), :].astype(bf16)
        columns[j] = column
        total = total + mm(jnp.where(row_col == j, spread, 0.0).astype(bf16), column, NT)
    bias[...] = total
    part = bias_out.shape[1]
    for r in range(toks):
        start = pl.multiple_of(jnp.bitwise_xor(t, r) * part, part)
        bias_out[r] = bias[pl.ds(start, part), :].astype(bf16)
    normed_scaled, _, _ = layer_forward(noisy[...].astype(f32), gain[...])
    types = table.shape[0]
    onehot = (lax.broadcasted_iota(jnp.int32, (types, rows), 0) == restype[...]).astype(f32)
    condition = single[...].astype(f32) + mm(onehot.astype(bf16), table[...], TN)
    x_out[...] = (normed_scaled + condition).astype(bf16)
    chain_row = chain[...]
    tokens = chain_row.shape[1]
    own_heads = head_count // toks
    keep_row = keymask[...].astype(f32)
    line = lax.broadcasted_iota(jnp.int32, (128, tokens), 0)
    facts = jnp.where(line == 0, chain_row.astype(f32), 0.0) + jnp.where(line == 1, keep_row, 0.0)
    for h in range(own_heads):
        weight_row = jnp.zeros((1, tokens), f32)
        for m in range(chain_weight.shape[0]):
            weight_row = jnp.where(chain_row == m, chain_weight[m, t * own_heads + h], weight_row)
        facts = jnp.where(line == 2 + h, weight_row, facts)
    facts_out[...] = jnp.transpose(facts)
    chain_out[...] = chain_row.astype(f32)


def stage_kernel(ids, *rest):
    weights, (slices, sem) = rest[:3], rest[3:]
    transfers = []
    for k in range(3):
        transfer = pltpu.make_async_copy(
            own_slice(weights[k], ids[0], slices.shape[2]), slices.at[k], sem.at[k]
        )
        transfer.start()
        transfers.append(transfer)
    for transfer in transfers:
        transfer.wait()


def project_kernel(toks, ids, slices, *rest):
    parts = rest[:toks]
    x_out, outs = rest[toks], rest[toks + 1 :]
    t = ids[0]
    rows = parts[0].shape[0]
    for r in range(toks):
        start = pl.multiple_of(jnp.bitwise_xor(t, r) * rows, rows)
        x_out[pl.ds(start, rows), :] = parts[r][...]
    x = x_out[...]
    for k in range(3):
        outs[k][...] = jnp.transpose(mm(x, slices[k])).astype(bf16)


def split_kernel(count, *refs):
    for n in range(count):
        for r, out in enumerate(refs[count:]):
            out[n] = refs[n][r]


def join_kernel(*refs):
    for n, ref in enumerate(refs[:-1]):
        refs[-1][n] = ref[...]


def attention_kernel(copies, toks, near, cols, head_width, ids, query, key, value, *rest):
    biases, (facts, chain, weights_out, att_out) = rest[:2], rest[2:6]
    pieces, bias = rest[6 : 6 + toks], rest[6 + toks]
    t, low, high = ids[0], low_bits(ids[1], near), ids[1] // near
    for m in range(near):
        for rz in range(copies // near):
            c = jnp.bitwise_xor(high, rz) * near + jnp.bitwise_xor(low, m)
            for r in range(toks):
                bias[c, jnp.bitwise_xor(t, r)] = biases[m % 2][m // 2, r, rz]
    own_heads = weights_out.shape[0]
    tokens = query.shape[1]
    rows = tokens // toks
    same = facts[:, 0:1] == chain[...]
    keep = facts[:, 1:2] > 0.0
    scale = head_width ** (-0.5)
    attended = []
    for h in range(own_heads):
        span = slice(h * head_width, (h + 1) * head_width)
        logits = mm(key[span, :], query[span, :], TN) * scale
        line = slice(h * cols, (h + 1) * cols)
        extra = jnp.concatenate(
            [
                jnp.concatenate(
                    [bias[c, a, line, :] for c in range(copies)], axis=0
                )
                for a in range(toks)
            ],
            axis=1,
        ).astype(f32)
        logits = logits + (extra + jnp.where(same, facts[:, 2 + h : 3 + h], 0.0))
        logits = jnp.where(keep, logits, -1e30)
        exponent = jnp.exp(logits - jnp.max(logits, axis=0, keepdims=True))
        weights = exponent / jnp.sum(exponent, axis=0, keepdims=True)
        weights_b = weights.astype(bf16)
        weights_out[h] = weights_b
        attended.append(mm(value[span, :], weights_b))
    att_out[...] = jnp.transpose(jnp.concatenate(attended, axis=0)).astype(bf16)
    for r in range(toks):
        start = pl.multiple_of(jnp.bitwise_xor(t, r) * rows, rows)
        pieces[r][...] = att_out[pl.ds(start, rows), :]


def down_kernel(upstream, w_down, noisy, gain, d_hidden, upstream_out, noisy_out, gain_out):
    d_hidden[...] = mm(upstream[...], w_down[...], NT)
    upstream_out[...] = upstream[...]
    noisy_out[...] = noisy[...]
    gain_out[...] = gain[...]


def hidden_kernel(toks, chunk, ids, noisy, upstream, d_hidden, gain, *rest):
    parts = rest[:toks]
    held_out, held_gate, held_up = rest[toks : toks + 3]
    d_res_out, d_res_b_out = rest[toks + 3 : toks + 5]
    d_att_outs = rest[toks + 5 :]
    t = ids[0]
    hidden = held_gate.shape[1]
    residual = noisy[...].astype(f32)
    own_width = parts[0].shape[1]
    for r in range(toks):
        start = pl.multiple_of(jnp.bitwise_xor(t, r) * own_width, own_width)
        residual = residual + mm(parts[r][...], held_out[pl.ds(start, own_width), :])
    trans_scaled, trans_hat, trans_inverse = layer_forward(residual, gain[...])
    trans_in = trans_scaled.astype(bf16)
    d_trans = jnp.zeros(residual.shape, f32)
    for k in range(hidden // chunk):
        span = slice(k * chunk, (k + 1) * chunk)
        gate = mm(trans_in, held_gate[:, span])
        up = mm(trans_in, held_up[:, span])
        incoming = d_hidden[:, span]
        sigmoid = jax.nn.sigmoid(gate)
        d_up = (incoming * gate * sigmoid).astype(bf16)
        d_gate = (incoming * up * sigmoid * (1.0 + gate * (1.0 - sigmoid))).astype(bf16)
        d_trans = d_trans + mm(d_gate, held_gate[:, span], NT) + mm(d_up, held_up[:, span], NT)
    d_res = upstream[...].astype(f32) + layer_backward(
        d_trans, gain[...], trans_hat, trans_inverse
    )
    d_res_out[...] = d_res
    d_res_b = d_res.astype(bf16)
    d_res_b_out[...] = d_res_b
    for r in range(toks):
        start = pl.multiple_of(jnp.bitwise_xor(t, r) * own_width, own_width)
        d_att_outs[r][...] = mm(held_out[pl.ds(start, own_width), :], d_res_b, NT).astype(bf16)


def backward_kernel(copies, toks, cols, head_width, ids, query, key, value, weights, *rest):
    parts, d_res_b = rest[:toks], rest[toks]
    d_query, d_key, d_value, bias_kept, bias_sent, d_res_out = rest[toks + 1 : toks + 7]
    blocks, d_logits = rest[toks + 7 :]
    d_res_out[...] = d_res_b[...]
    t = ids[0]
    bit = low_bits(ids[1] // 2, 2)
    heads = weights.shape[0]
    for r in range(toks):
        blocks[jnp.bitwise_xor(t, r)] = parts[r][...]
    d_att = jnp.concatenate([blocks[a] for a in range(toks)], axis=1)
    count = tile_count(cols, query.shape[1])
    scale = head_width ** (-0.5)
    for h in range(weights.shape[0]):
        span = slice(h * head_width, (h + 1) * head_width)
        d_att_h = d_att[span, :]
        weights_b = weights[h]
        d_weights = mm(value[span, :], d_att_h, TN)
        weights_f = weights_b.astype(f32)
        delta = jnp.sum(weights_f * d_weights, axis=0, keepdims=True)
        d_logits_b = (weights_f * (d_weights - delta)).astype(bf16)
        d_logits[...] = d_logits_b
        for k in range(copies // 2):
            for side, out in ((bit, bias_kept), (1 - bit, bias_sent)):
                start = pl.multiple_of((k // 2 * 4 + side * 2 + k % 2) * cols, cols)
                put(out, (k * heads + h) * count, d_logits[pl.ds(start, cols), :])
        d_query[span, :] = (mm(key[span, :], d_logits_b) * scale).astype(bf16)
        d_key[span, :] = (mm(query[span, :], d_logits_b, NT) * scale).astype(bf16)
        d_value[span, :] = mm(d_att_h, weights_b, NT).astype(bf16)


def tile_count(rows, lanes):
    return -(-rows // 16) * -(-lanes // 128)


def put(out, base, value):
    rows, lanes = value.shape
    for i in range(0, rows, 16):
        for j in range(0, lanes, 128):
            part = value[i : i + 16, j : j + 128]
            if part.shape != (16, 128):
                out[base] = jnp.zeros((16, 128), out.dtype)
            out[base, : part.shape[0], : part.shape[1]] = part
            base += 1


def take(tiles, base, rows, lanes):
    across = -(-lanes // 128)
    lines = []
    for i in range(-(-rows // 16)):
        line = [tiles[base + i * across + j] for j in range(across)]
        lines.append(jnp.concatenate(line, axis=1) if across > 1 else line[0])
    whole = jnp.concatenate(lines, axis=0) if len(lines) > 1 else lines[0]
    return whole[:rows, :lanes]


def cut_wide(copies, toks, core, base, stride, grad, kept, sent):
    group = copies // toks
    cut, depth = grad.shape[1] // copies, grad.shape[1] // toks
    for side, out in ((core, kept), (1 - core, sent)):
        for q in range(copies // 2):
            h = 2 * q // group
            first = pl.multiple_of((2 * q - h * group + side) * cut, 8)
            part = grad[pl.ds(first, cut), h * depth : (h + 1) * depth]
            put(out, q * stride + base, part.astype(bf16))


def first_kernel(copies, toks, ids, slices, x, d_query, d_key, d_value, *rest):
    kept, sent, d_own = rest[:3]
    d_others, (wide, d_inputs, total_ref) = rest[3 : 2 + toks], rest[2 + toks :]
    t, core = ids[0], low_bits(ids[1], 2)
    rows = d_own.shape[1]
    cut = x.shape[1] // copies
    count = tile_count(cut, d_query.shape[0])
    stride = 2 * count + tile_count(cut, rows * toks)
    for k, part in enumerate((d_query, d_key)):
        wide[...] = mm(part[...], x[...])
        cut_wide(copies, toks, core, k * count, stride, wide, kept, sent)
    total = mm(slices[0], d_query[...]) + mm(slices[1], d_key[...])
    total = total + mm(slices[2], d_value[...])
    total_ref[...] = total
    for side, out in ((core, kept), (1 - core, sent)):
        for q in range(copies // 2):
            start = pl.multiple_of((2 * q + side) * cut, 8)
            put(out, q * stride + 2 * count, total_ref[pl.ds(start, cut), :].astype(bf16))
    for a in range(toks):
        d_inputs[a] = total[:, a * rows : (a + 1) * rows]
    d_own[...] = d_inputs[t]
    for r in range(1, toks):
        d_others[r - 1][...] = d_inputs[jnp.bitwise_xor(t, r)].astype(bf16)


def second_kernel(copies, toks, ids, x, att, d_value, bias_kept, bias_got, *rest):
    d_res_parts, (kept, sent, d_res, wide, narrow) = rest[:toks], rest[toks:]
    t, core = ids[0], low_bits(ids[1], 2)
    rows = d_res_parts[0].shape[0]
    cut = narrow.shape[0] // copies
    count = tile_count(cut, narrow.shape[1])
    wide[...] = mm(d_value[...], x[...])
    cut_wide(copies, toks, core, 0, 2 * count, wide, kept, sent)
    for r in range(toks):
        start = pl.multiple_of(jnp.bitwise_xor(t, r) * rows, rows)
        d_res[pl.ds(start, rows), :] = d_res_parts[r][...]
    narrow[...] = mm(d_res[...], att[...], TN)
    base = copies * count
    bias_count = bias_kept.shape[0] // (copies // 2)
    for side, out in ((core, kept), (1 - core, sent)):
        for q in range(copies // 2):
            first = pl.multiple_of((2 * q + side) * cut, 8)
            put(out, (2 * q + 1) * count, narrow[pl.ds(first, cut), :].astype(bf16))
        for z in range(copies // 4):
            span = pl.ds((2 * z + side) * bias_count, bias_count)
            out[base + z * bias_count : base + (z + 1) * bias_count] = (
                bias_kept[span].astype(f32) + bias_got[span].astype(f32)
            ).astype(bf16)


def step_kernel(segments, ids, *refs):
    count = 1 + max(segment[0] for segment in segments)
    ins, outs = refs[: 2 * count], refs[2 * count :]
    for source, base, parts, tiles, mask, inner, target, start in segments:
        kept, got = ins[2 * source : 2 * source + 2]
        bit = low_bits(ids[1] // mask, 2)
        for q in range(parts // 2):
            for side, out in ((bit, outs[2 * target]), (1 - bit, outs[2 * target + 1])):
                k = q // inner * 2 * inner + side * inner + q % inner
                span = pl.ds(base + k * tiles, tiles)
                out[start + q * tiles : start + (q + 1) * tiles] = (
                    kept[span].astype(f32) + got[span].astype(f32)
                ).astype(bf16)


def last_bias_kernel(toks, base, count, cols, ids, kept, got, *rest):
    pieces, blocks = rest[:toks], rest[toks]
    span = slice(base, base + count)
    tiles = kept[span].astype(f32) + got[span].astype(f32)
    part_rows, rows = pieces[0].shape
    heads = part_rows // cols
    total = jnp.concatenate(
        [take(tiles, h * (count // heads), cols, rows * toks) for h in range(heads)], axis=0
    )
    for a in range(toks):
        blocks[a] = total[:, a * rows : (a + 1) * rows].astype(bf16)
    for r in range(toks):
        pieces[r][...] = blocks[jnp.bitwise_xor(ids[0], r)]


def last_kernel(toks, ids, kept, got, kept_b, got_b, moved, final, *rest):
    pieces, blocks = rest[:toks], rest[toks]
    first = kept[...].astype(f32) + got[...].astype(f32)
    second = kept_b[...].astype(f32) + got_b[...].astype(f32)
    _, cut, own_width = moved.shape
    count = tile_count(cut, own_width)
    for k in range(2):
        moved[k] = take(first, k * count, cut, own_width).astype(bf16)
    moved[2] = take(second, 0, cut, own_width).astype(bf16)
    final[...] = take(second, count, cut, own_width)
    rows = blocks.shape[2]
    single = take(first, 2 * count, cut, rows * toks)
    for a in range(toks):
        blocks[a] = single[:, a * rows : (a + 1) * rows]
    for r in range(toks):
        pieces[r][...] = blocks[jnp.bitwise_xor(ids[0], r)].astype(bf16)


def finish_kernel(moved, *rest):
    parts, outs = rest[:-4], rest[-4:]
    for k in range(3):
        outs[k][...] = moved[k].astype(f32)
    total = parts[0][...].astype(f32)
    for part in parts[1:]:
        total = total + part[...].astype(f32)
    outs[3][...] = total


def exit_kernel(toks, noisy, gain, d_res, d_own, *rest):
    others, (grad_noisy, token) = rest[: toks - 1], rest[toks - 1 :]
    token[...] = jnp.zeros(token.shape, f32)
    total = d_own[...]
    for part in others:
        total = total + part[...].astype(f32)
    _, noisy_hat, noisy_inverse = layer_forward(noisy[...].astype(f32), gain[...])
    grad_noisy[...] = (
        d_res[...] + layer_backward(jnp.transpose(total), gain[...], noisy_hat, noisy_inverse)
    ).astype(bf16)


def set_heads(toks, ids, parts, grads):
    part_rows = parts[0].shape[0]
    for r in range(toks):
        start = pl.multiple_of(jnp.bitwise_xor(ids[0], r) * part_rows, part_rows)
        grads[pl.ds(start, part_rows), :] = parts[r][...].astype(f32)


def pair_weight_kernel(toks, ids, columns, *rest):
    parts, (weight_grad, grads) = rest[:toks], rest[toks:]
    set_heads(toks, ids, parts, grads)
    grad_b = grads[...].astype(bf16)
    cols, _, channels = columns.shape
    row_col = low_bits(lax.broadcasted_iota(jnp.int32, (grad_b.shape[0], channels), 0), cols)
    sums = jnp.zeros((grad_b.shape[0], channels), f32)
    for j in range(cols):
        sums = sums + jnp.where(row_col == j, mm(grad_b, columns[j]), 0.0)
    for h in range(weight_grad.shape[1]):
        line = jnp.sum(sums[h * cols : (h + 1) * cols, :], axis=0, keepdims=True)
        for n in range(weight_grad.shape[0]):
            weight_grad[n, h : h + 1, :] = line


def pair_kernel(toks, cols, ids, pair, gain, w_pair, *rest):
    parts, (grad_pair, spread_out, grads) = rest[:toks], rest[toks:]
    set_heads(toks, ids, parts, grads)
    rows = parts[0].shape[1]
    _, pair_hat, pair_inverse = layer_forward(pair[...].astype(f32), gain[...])
    spread, row_col = pair_weight_rows(w_pair[...], w_pair.shape[0], cols)
    turned = jnp.transpose(grads[...]).astype(bf16)
    for j in range(cols):
        spread_out[pl.ds(j, rows, stride=cols), :] = mm(
            turned, jnp.where(row_col == j, spread, 0.0).astype(bf16)
        )
    grad_pair[...] = layer_backward(
        spread_out[...], gain[...], pair_hat, pair_inverse
    ).astype(bf16)


def swap_copy(value, mask):
    size = lax.axis_size("copy")
    return lax.ppermute(value, "copy", [(i, i ^ mask) for i in range(size)])


def swap_tok(value, mask):
    size = lax.axis_size("tok")
    return lax.ppermute(value, "tok", [(i, i ^ mask) for i in range(size)])


def exchange(value):
    return lax.all_to_all(value, ("copy", "tok"), 0, 0)


def per_device(
    noisy,
    single,
    pair,
    restype,
    chain,
    keymask,
    restype_table,
    norm_gain,
    pair_gain,
    trans_gain,
    w_query,
    w_key,
    w_value,
    w_out,
    w_pair,
    chain_weight,
    w_hidden_gate,
    w_hidden_up,
    w_down,
    cotangent,
):
    copies = lax.axis_size("copy")
    toks = lax.axis_size("tok")
    _, rows, width = noisy.shape
    cols = pair.shape[1]
    channels = pair.shape[2]
    heads = w_pair.shape[1]
    head_width = width // heads
    own_heads = heads // toks
    own_width = own_heads * head_width
    tokens = rows * toks
    hidden = w_down.shape[0]
    cut = width // copies
    devices = copies * toks
    ids = jnp.stack([lax.axis_index("tok"), lax.axis_index("copy")]).astype(jnp.int32)
    where_am_i = (ids, SMEM)
    noisy2 = noisy.reshape(rows, width)
    pair2 = pair.reshape(rows * cols, channels)
    pair_gain2 = pair_gain.reshape(1, channels)
    norm_gain2 = norm_gain.reshape(1, width)

    weights3 = [w_query, w_key, w_value]
    if own_width % 128:
        weights3 = [
            lax.dynamic_slice_in_dim(w, ids[0] * own_width, own_width, axis=1) for w in weights3
        ]
    small = [noisy2, single, restype.reshape(1, rows), restype_table, norm_gain, pair2, pair_gain2]
    small += [w_pair.T, chain.reshape(1, tokens), keymask.reshape(1, tokens)]
    entered = call(
        functools.partial(enter_kernel, toks, cols),
        "enter",
        [where_am_i]
        + [(array, "fetch") for array in small]
        + [(chain_weight, SMEM)],
        [((rows, width), bf16), ((cols, rows, channels), bf16)]
        + [((tokens, 128), f32), ((1, tokens), f32), ((toks, own_heads * cols, rows), bf16)],
        [VMEM((rows * cols, channels), f32), VMEM((heads * cols, rows), f32)],
        flops=2 * heads * cols * rows * channels * cols,
        limit=60,
    )
    x_own, columns, facts, chain_row, bias_mine = entered
    near = 4
    far = copies // near
    x_parts = [x_own] + [swap_tok(x_own, r) for r in range(1, toks)]
    by_tok = call(
        functools.partial(split_kernel, far),
        "split_far",
        [bias_mine] + [swap_copy(bias_mine, m * near) for m in range(1, far)],
        [((far, own_heads * cols, rows), bf16)] * toks,
        deps=x_parts[1:],
    )
    (slices,) = call(
        stage_kernel,
        "stage",
        [where_am_i] + [(w, ANY) for w in weights3],
        [((3, width, own_width), bf16)],
        [pltpu.SemaphoreType.DMA((3,))],
        deps=[by_tok[0]],
    )
    (lines,) = call(
        join_kernel,
        "join_tok",
        [by_tok[0]] + [swap_tok(by_tok[r], r) for r in range(1, toks)],
        [((toks, far, own_heads * cols, rows), bf16)],
        deps=[slices],
    )
    x, query, key, value = call(
        functools.partial(project_kernel, toks),
        "project",
        [where_am_i, slices] + x_parts,
        [((tokens, width), bf16)] + [((own_width, tokens), bf16)] * 3,
        flops=6 * tokens * width * own_width,
    )
    (lines,) = call(
        join_kernel,
        "join_y",
        [lines, swap_copy(lines, 2)],
        [((2,) + lines.shape, bf16)],
        deps=[value],
    )
    biases = [lines, swap_copy(lines, 1)]
    done = call(
        functools.partial(attention_kernel, copies, toks, near, cols, head_width),
        "attention",
        [where_am_i, query, key, value] + biases + [facts, chain_row],
        [((own_heads, tokens, tokens), bf16), ((tokens, own_width), bf16)]
        + [((rows, own_width), bf16)] * toks,
        [VMEM((copies, toks, own_heads * cols, rows), bf16)],
        flops=4 * tokens * tokens * own_width,
        limit=32,
    )
    weights, att, pieces = done[0], done[1], done[2:]
    att_parts = [pieces[0]] + [swap_tok(pieces[r], r) for r in range(1, toks)]

    d_hidden, upstream, noisy3, trans_gain2 = call(
        down_kernel,
        "down",
        [cotangent.reshape(rows, width), w_down, noisy2, trans_gain.reshape(1, width)],
        [((rows, hidden), f32), ((rows, width), bf16), ((rows, width), bf16), ((1, width), f32)],
        flops=2 * rows * hidden * width,
    )
    chunk = hidden // 3
    results = call(
        functools.partial(hidden_kernel, toks, chunk),
        "hidden",
        [where_am_i, noisy3, upstream, d_hidden, trans_gain2]
        + att_parts
        + [w_out, w_hidden_gate, w_hidden_up],
        [((rows, width), f32), ((rows, width), bf16)] + [((own_width, rows), bf16)] * toks,
        flops=2 * rows * width * (2 * width + 4 * hidden),
    )
    d_res, d_res_b, d_att = results[0], results[1], results[2:]
    d_att_parts = [d_att[0]] + [swap_tok(d_att[r], r) for r in range(1, toks)]
    bias_tiles = own_heads * tile_count(cols, tokens)
    bias_shape = (copies // 2 * bias_tiles, 16, 128)
    d_query, d_key, d_value, bias_kept, bias_sent, d_res_b = call(
        functools.partial(backward_kernel, copies, toks, cols, head_width),
        "backward",
        [where_am_i, query, key, value, weights] + d_att_parts + [d_res_b],
        [((own_width, tokens), bf16)] * 3 + [(bias_shape, bf16)] * 2 + [((rows, width), bf16)],
        [VMEM((toks, own_width, rows), bf16), VMEM((tokens, tokens), bf16)],
        flops=8 * tokens * tokens * own_width,
        limit=32,
    )
    d_res_parts = [d_res_b] + [swap_tok(d_res_b, r) for r in range(1, toks)]
    bias_got = swap_copy(bias_sent, 2)

    wide_tiles = tile_count(cut, own_width)
    single_tiles = tile_count(cut, tokens)
    first_tiles, second_tiles = 2 * wide_tiles + single_tiles, 2 * wide_tiles
    found = call(
        functools.partial(first_kernel, copies, toks),
        "first",
        [where_am_i, slices, x, d_query, d_key, d_value],
        [((copies // 2 * first_tiles, 16, 128), bf16)] * 2
        + [((width, rows), f32)]
        + [((width, rows), bf16)] * (toks - 1),
        [
            VMEM((own_width, width), f32),
            VMEM((toks, width, rows), f32),
            VMEM((width, tokens), f32),
        ],
        flops=10 * tokens * width * own_width,
    )
    kept, sent, d_own = found[:3]
    got = swap_copy(sent, 1)
    d_others = [swap_tok(found[2 + r], r) for r in range(1, toks)]

    def step(name, pairs, segments, deps=()):
        filled, full, masks_of = {}, [], {}
        for source, base, parts, tiles, mask, left, target in segments:
            inner = 1 << sum(1 for other in left if other < mask)
            start = filled.get(target, 0)
            full.append((source, base, parts, tiles, mask, inner, target, start))
            filled[target] = start + parts // 2 * tiles
            masks_of[target] = mask
        outs = []
        for target in range(len(filled)):
            outs += [((filled[target], 16, 128), bf16)] * 2
        results = call(
            functools.partial(step_kernel, full),
            name,
            [where_am_i] + [array for one in pairs for array in one],
            outs,
            deps=deps,
        )
        return [
            (results[2 * n], swap_copy(results[2 * n + 1], masks_of[n]))
            for n in range(len(filled))
        ]

    masks = [1 << b for b in range(1, copies.bit_length() - 1)]
    masks_b = masks[1:] + masks[:1]
    kept_b, sent_b = call(
        functools.partial(second_kernel, copies, toks),
        "second",
        [where_am_i, x, att, d_value, bias_kept, bias_got] + d_res_parts,
        [((copies // 2 * second_tiles + copies // 4 * bias_tiles, 16, 128), bf16)] * 2,
        [
            VMEM((tokens, width), bf16),
            VMEM((own_width, width), f32),
            VMEM((width, own_width), f32),
        ],
        flops=4 * tokens * width * own_width,
    )
    got_b = swap_copy(sent_b, 1)

    grad_noisy, exited = call(
        functools.partial(exit_kernel, toks),
        "exit",
        [noisy3, norm_gain2, d_res, d_own] + d_others,
        [((rows, width), bf16), ((8, 128), f32)],
    )
    pairs = [(kept, got), (kept_b, got_b)]
    parts = copies // 2
    for n, (mask, mask_b) in enumerate(zip(masks, masks_b)):
        segments = [
            (0, 0, parts, first_tiles, mask, masks[n:], 0),
            (1, 0, parts, second_tiles, mask_b, masks_b[n:], 1),
        ]
        bias_base = parts * second_tiles
        if n + 1 < len(masks):
            segments.append((1, bias_base, parts // 2, bias_tiles, mask_b, masks_b[n:-1], 1))
        else:
            bias_ready = pairs[1]
        pairs = step("step_%d" % n, pairs, segments, deps=[exited] if n == 1 else ())
        parts //= 2
    bias_pieces = call(
        functools.partial(last_bias_kernel, toks, bias_base, bias_tiles, cols),
        "last_bias",
        [where_am_i, *bias_ready],
        [((own_heads * cols, rows), bf16)] * toks,
        [VMEM((toks, own_heads * cols, rows), bf16)],
        deps=[pairs[0][0]],
    )
    bias_pieces = [bias_pieces[0]] + [swap_tok(bias_pieces[r], r) for r in range(1, toks)]

    group = copies // toks
    swaps = []
    for c in range(copies):
        for t in range(toks):
            swaps.append((c * toks + t, (t * group + c % group) * toks + c // group))

    (weight_grad,) = call(
        functools.partial(pair_weight_kernel, toks),
        "pair_weight",
        [where_am_i, columns] + bias_pieces,
        [((devices, heads, channels), f32)],
        [VMEM((heads * cols, rows), f32)],
        flops=2 * heads * cols * rows * channels * cols,
        deps=[pairs[0][1], pairs[1][1]],
    )
    last = call(
        functools.partial(last_kernel, toks),
        "last",
        [where_am_i, *pairs[0], *pairs[1]],
        [((3, cut, own_width), bf16), ((cut, own_width), f32)] + [((cut, rows), bf16)] * toks,
        [VMEM((toks, cut, rows), f32)],
        deps=[weight_grad],
    )
    (grad_pair,) = call(
        functools.partial(pair_kernel, toks, cols),
        "pair",
        [where_am_i, pair2, pair_gain2, w_pair.T] + bias_pieces,
        [((rows * cols, channels), bf16)],
        [VMEM((rows * cols, channels), f32), VMEM((heads * cols, rows), f32)],
        flops=2 * heads * cols * rows * channels * cols,
        deps=[last[0]],
    )
    weight_grad = jnp.sum(exchange(weight_grad), axis=0)
    grad_out, singles = last[1], last[2:]
    singles = [singles[0]] + [swap_tok(singles[r], r) for r in range(1, toks)]
    moved = lax.ppermute(last[0], ("copy", "tok"), swaps)
    grad_query, grad_key, grad_value, grad_single = call(
        finish_kernel,
        "finish",
        [moved] + singles,
        [((cut, own_width), f32)] * 3 + [((cut, rows), f32)],
    )
    return (
        grad_noisy[None],
        grad_single.T,
        grad_pair.reshape(rows, cols, channels),
        grad_query.T,
        grad_key.T,
        grad_value.T,
        grad_out.T,
        weight_grad.T,
    )


def solution(mesh):
    placed = (
        P("copy", "tok", None),
        P("tok", None),
        P("tok", "copy", None),
        P("tok"),
    ) + (P(),) * 15 + (P("copy", "tok", None),)
    return jax.shard_map(
        per_device,
        mesh=mesh,
        in_specs=placed,
        out_specs=(
            P("copy", "tok", None),
            P("tok", "copy"),
            P("tok", "copy", None),
            P("tok", "copy"),
            P("tok", "copy"),
            P("tok", "copy"),
            P("tok", "copy"),
            P(),
        ),
        check_vma=False,
    )
```

```python
import functools

import jax
import jax.numpy as jnp
from jax import lax
from jax.experimental import pallas as pl
from jax.experimental.pallas import tpu as pltpu
from jax.sharding import PartitionSpec as P

epsilon = 1e-05
f32 = jnp.float32
bf16 = jnp.bfloat16
VMEM, SMEM, ANY = pltpu.VMEM, pltpu.SMEM, pl.ANY
MIB = 1 << 20


def layer_forward(values, scales):
    average = jnp.mean(values, axis=-1, keepdims=True)
    centred = values - average
    inverse = lax.rsqrt(jnp.mean(centred * centred, axis=-1, keepdims=True) + epsilon)
    normed = centred * inverse
    return (normed * scales, normed, inverse)


def layer_backward(upstream, scales, normed, inverse):
    scaled = upstream * scales
    first_moment = jnp.mean(scaled, axis=-1, keepdims=True)
    second_moment = jnp.mean(scaled * normed, axis=-1, keepdims=True)
    return inverse * (scaled - first_moment - normed * second_moment)


NN = ((1,), (0,))
NT = ((1,), (1,))
TN = ((0,), (0,))


def mm(left, right, dims=NN):
    return lax.dot_general(left, right, (dims, ((), ())), preferred_element_type=f32)


def call(body, name, inputs, outs, scratch=(), flops=0, limit=16, deps=()):
    arrays, specs, moved, fetched = [], [], 0, []
    for item in inputs:
        array, space = item if isinstance(item, tuple) else (item, VMEM)
        if space == "fetch":
            fetched.append(len(arrays))
            space = pltpu.HBM
        arrays.append(array)
        specs.append(pl.BlockSpec(memory_space=space))
        moved += array.size * array.dtype.itemsize
    for shape, kind, *_ in outs:
        size = jnp.dtype(kind).itemsize
        for extent in shape:
            size *= extent
        moved += size
    read = len(arrays)
    for array in deps:
        arrays.append(array)
        specs.append(pl.BlockSpec(memory_space=ANY))
    extra = [VMEM(arrays[k].shape, arrays[k].dtype) for k in fetched]
    if fetched:
        extra.append(pltpu.SemaphoreType.DMA((len(fetched),)))

    def whole(*refs):
        refs = list(refs[:read]) + list(refs[read + len(deps) :])
        if fetched:
            held, sem = refs[-1 - len(fetched) : -1], refs[-1]
            refs = refs[: -1 - len(fetched)]
            transfers = []
            for n, k in enumerate(fetched):
                transfer = pltpu.make_async_copy(refs[k], held[n], sem.at[n])
                transfer.start()
                transfers.append(transfer)
                refs[k] = held[n]
            for transfer in transfers:
                transfer.wait()
        body(*refs)

    return pl.pallas_call(
        whole,
        name=name,
        out_shape=[jax.ShapeDtypeStruct(one[0], one[1]) for one in outs],
        in_specs=specs,
        out_specs=[pl.BlockSpec(memory_space=(*one, VMEM)[2]) for one in outs],
        scratch_shapes=list(scratch) + extra,
        compiler_params=pltpu.CompilerParams(vmem_limit_bytes=limit * MIB),
        cost_estimate=pl.CostEstimate(flops=flops, bytes_accessed=moved, transcendentals=0),
    )(*arrays)


def low_bits(index, size):
    return jnp.bitwise_and(index, size - 1)


def pair_weight_rows(w_pair, head_count, cols):
    rows = head_count * cols
    shift = cols.bit_length() - 1
    head = lax.shift_right_logical(
        lax.broadcasted_iota(jnp.int32, (rows, head_count), 0), jnp.int32(shift)
    )
    pick = (head == lax.broadcasted_iota(jnp.int32, (rows, head_count), 1)).astype(f32)
    spread = mm(pick.astype(bf16), w_pair)
    row_col = low_bits(lax.broadcasted_iota(jnp.int32, spread.shape, 0), cols)
    return spread, row_col


def own_slice(weight, t, own_width):
    if weight.shape[1] == own_width:
        return weight
    return weight.at[:, pl.ds(pl.multiple_of(t * own_width, own_width), own_width)]


def enter_kernel(toks, cols, ids, *rest):
    noisy, single, restype, table, gain, pair, pair_gain, w_pair, chain, keymask = rest[:10]
    chain_weight, x_out, columns, facts_out, chain_out, bias_out, rounded, bias = rest[10:]
    t = ids[0]
    rows = noisy.shape[0]
    pair_scaled, _, _ = layer_forward(pair[...].astype(f32), pair_gain[...])
    rounded[...] = pair_scaled.astype(bf16).astype(f32)
    head_count = w_pair.shape[0]
    spread, row_col = pair_weight_rows(w_pair[...], head_count, cols)
    total = jnp.zeros((head_count * cols, rows), f32)
    for j in range(cols):
        column = rounded[pl.ds(j, rows, stride=cols), :].astype(bf16)
        columns[j] = column
        total = total + mm(jnp.where(row_col == j, spread, 0.0).astype(bf16), column, NT)
    bias[...] = total
    part = bias_out.shape[1]
    for r in range(toks):
        start = pl.multiple_of(jnp.bitwise_xor(t, r) * part, part)
        bias_out[r] = bias[pl.ds(start, part), :].astype(bf16)
    normed_scaled, _, _ = layer_forward(noisy[...].astype(f32), gain[...])
    types = table.shape[0]
    onehot = (lax.broadcasted_iota(jnp.int32, (types, rows), 0) == restype[...]).astype(f32)
    condition = single[...].astype(f32) + mm(onehot.astype(bf16), table[...], TN)
    x_out[...] = (normed_scaled + condition).astype(bf16)
    chain_row = chain[...]
    tokens = chain_row.shape[1]
    own_heads = head_count // toks
    keep_row = keymask[...].astype(f32)
    line = lax.broadcasted_iota(jnp.int32, (128, tokens), 0)
    facts = jnp.where(line == 0, chain_row.astype(f32), 0.0) + jnp.where(line == 1, keep_row, 0.0)
    for h in range(own_heads):
        weight_row = jnp.zeros((1, tokens), f32)
        for m in range(chain_weight.shape[0]):
            weight_row = jnp.where(chain_row == m, chain_weight[m, t * own_heads + h], weight_row)
        facts = jnp.where(line == 2 + h, weight_row, facts)
    facts_out[...] = jnp.transpose(facts)
    chain_out[...] = chain_row.astype(f32)


def stage_kernel(ids, *rest):
    weights, (slices, sem) = rest[:3], rest[3:]
    transfers = []
    for k in range(3):
        transfer = pltpu.make_async_copy(
            own_slice(weights[k], ids[0], slices.shape[2]), slices.at[k], sem.at[k]
        )
        transfer.start()
        transfers.append(transfer)
    for transfer in transfers:
        transfer.wait()


def project_kernel(toks, ids, slices, *rest):
    parts = rest[:toks]
    x_out, outs = rest[toks], rest[toks + 1 :]
    t = ids[0]
    rows = parts[0].shape[0]
    for r in range(toks):
        start = pl.multiple_of(jnp.bitwise_xor(t, r) * rows, rows)
        x_out[pl.ds(start, rows), :] = parts[r][...]
    x = x_out[...]
    for k in range(3):
        outs[k][...] = jnp.transpose(mm(x, slices[k])).astype(bf16)


def split_kernel(count, *refs):
    for n in range(count):
        for r, out in enumerate(refs[count:]):
            out[n] = refs[n][r]


def join_kernel(*refs):
    for n, ref in enumerate(refs[:-1]):
        refs[-1][n] = ref[...]


def attention_kernel(copies, toks, near, cols, head_width, ids, query, key, value, *rest):
    biases, (facts, chain, weights_out, att_out) = rest[:2], rest[2:6]
    pieces, bias = rest[6 : 6 + toks], rest[6 + toks]
    t, low, high = ids[0], low_bits(ids[1], near), ids[1] // near
    for m in range(near):
        for rz in range(copies // near):
            c = jnp.bitwise_xor(high, rz) * near + jnp.bitwise_xor(low, m)
            for r in range(toks):
                bias[c, jnp.bitwise_xor(t, r)] = biases[m % 2][m // 2, r, rz]
    own_heads = weights_out.shape[0]
    tokens = query.shape[1]
    rows = tokens // toks
    same = facts[:, 0:1] == chain[...]
    keep = facts[:, 1:2] > 0.0
    scale = head_width ** (-0.5)
    attended = []
    for h in range(own_heads):
        span = slice(h * head_width, (h + 1) * head_width)
        logits = mm(key[span, :], query[span, :], TN) * scale
        line = slice(h * cols, (h + 1) * cols)
        extra = jnp.concatenate(
            [
                jnp.concatenate(
                    [bias[c, a, line, :] for c in range(copies)], axis=0
                )
                for a in range(toks)
            ],
            axis=1,
        ).astype(f32)
        logits = logits + (extra + jnp.where(same, facts[:, 2 + h : 3 + h], 0.0))
        logits = jnp.where(keep, logits, -1e30)
        exponent = jnp.exp(logits - jnp.max(logits, axis=0, keepdims=True))
        weights = exponent / jnp.sum(exponent, axis=0, keepdims=True)
        weights_b = weights.astype(bf16)
        weights_out[h] = weights_b
        attended.append(mm(value[span, :], weights_b))
    att_out[...] = jnp.transpose(jnp.concatenate(attended, axis=0)).astype(bf16)
    for r in range(toks):
        start = pl.multiple_of(jnp.bitwise_xor(t, r) * rows, rows)
        pieces[r][...] = att_out[pl.ds(start, rows), :]


def down_kernel(upstream, w_down, noisy, gain, d_hidden, upstream_out, noisy_out, gain_out):
    d_hidden[...] = mm(upstream[...], w_down[...], NT)
    upstream_out[...] = upstream[...]
    noisy_out[...] = noisy[...]
    gain_out[...] = gain[...]


def hidden_kernel(toks, chunk, ids, noisy, upstream, d_hidden, gain, *rest):
    parts = rest[:toks]
    held_out, held_gate, held_up = rest[toks : toks + 3]
    d_res_out, d_res_b_out = rest[toks + 3 : toks + 5]
    d_att_outs = rest[toks + 5 :]
    t = ids[0]
    hidden = held_gate.shape[1]
    residual = noisy[...].astype(f32)
    own_width = parts[0].shape[1]
    for r in range(toks):
        start = pl.multiple_of(jnp.bitwise_xor(t, r) * own_width, own_width)
        residual = residual + mm(parts[r][...], held_out[pl.ds(start, own_width), :])
    trans_scaled, trans_hat, trans_inverse = layer_forward(residual, gain[...])
    trans_in = trans_scaled.astype(bf16)
    d_trans = jnp.zeros(residual.shape, f32)
    for k in range(hidden // chunk):
        span = slice(k * chunk, (k + 1) * chunk)
        gate = mm(trans_in, held_gate[:, span])
        up = mm(trans_in, held_up[:, span])
        incoming = d_hidden[:, span]
        sigmoid = jax.nn.sigmoid(gate)
        d_up = (incoming * gate * sigmoid).astype(bf16)
        d_gate = (incoming * up * sigmoid * (1.0 + gate * (1.0 - sigmoid))).astype(bf16)
        d_trans = d_trans + mm(d_gate, held_gate[:, span], NT) + mm(d_up, held_up[:, span], NT)
    d_res = upstream[...].astype(f32) + layer_backward(
        d_trans, gain[...], trans_hat, trans_inverse
    )
    d_res_out[...] = d_res
    d_res_b = d_res.astype(bf16)
    d_res_b_out[...] = d_res_b
    for r in range(toks):
        start = pl.multiple_of(jnp.bitwise_xor(t, r) * own_width, own_width)
        d_att_outs[r][...] = mm(held_out[pl.ds(start, own_width), :], d_res_b, NT).astype(bf16)


def backward_kernel(copies, toks, cols, head_width, ids, query, key, value, weights, *rest):
    parts, d_res_b = rest[:toks], rest[toks]
    d_query, d_key, d_value, bias_kept, bias_sent, d_res_out = rest[toks + 1 : toks + 7]
    blocks, d_logits = rest[toks + 7 :]
    d_res_out[...] = d_res_b[...]
    t = ids[0]
    bit = low_bits(ids[1] // 2, 2)
    heads = weights.shape[0]
    for r in range(toks):
        blocks[jnp.bitwise_xor(t, r)] = parts[r][...]
    d_att = jnp.concatenate([blocks[a] for a in range(toks)], axis=1)
    count = tile_count(cols, query.shape[1])
    scale = head_width ** (-0.5)
    for h in range(weights.shape[0]):
        span = slice(h * head_width, (h + 1) * head_width)
        d_att_h = d_att[span, :]
        weights_b = weights[h]
        d_weights = mm(value[span, :], d_att_h, TN)
        weights_f = weights_b.astype(f32)
        delta = jnp.sum(weights_f * d_weights, axis=0, keepdims=True)
        d_logits_b = (weights_f * (d_weights - delta)).astype(bf16)
        d_logits[...] = d_logits_b
        for k in range(copies // 2):
            for side, out in ((bit, bias_kept), (1 - bit, bias_sent)):
                start = pl.multiple_of((k // 2 * 4 + side * 2 + k % 2) * cols, cols)
                put(out, (k * heads + h) * count, d_logits[pl.ds(start, cols), :])
        d_query[span, :] = (mm(key[span, :], d_logits_b) * scale).astype(bf16)
        d_key[span, :] = (mm(query[span, :], d_logits_b, NT) * scale).astype(bf16)
        d_value[span, :] = mm(d_att_h, weights_b, NT).astype(bf16)


def tile_count(rows, lanes):
    return -(-rows // 16) * -(-lanes // 128)


def put(out, base, value):
    rows, lanes = value.shape
    for i in range(0, rows, 16):
        for j in range(0, lanes, 128):
            part = value[i : i + 16, j : j + 128]
            if part.shape != (16, 128):
                out[base] = jnp.zeros((16, 128), out.dtype)
            out[base, : part.shape[0], : part.shape[1]] = part
            base += 1


def take(tiles, base, rows, lanes):
    across = -(-lanes // 128)
    lines = []
    for i in range(-(-rows // 16)):
        line = [tiles[base + i * across + j] for j in range(across)]
        lines.append(jnp.concatenate(line, axis=1) if across > 1 else line[0])
    whole = jnp.concatenate(lines, axis=0) if len(lines) > 1 else lines[0]
    return whole[:rows, :lanes]


def cut_wide(copies, toks, core, base, stride, grad, kept, sent):
    group = copies // toks
    cut, depth = grad.shape[1] // copies, grad.shape[1] // toks
    for side, out in ((core, kept), (1 - core, sent)):
        for q in range(copies // 2):
            h = 2 * q // group
            first = pl.multiple_of((2 * q - h * group + side) * cut, 8)
            part = grad[pl.ds(first, cut), h * depth : (h + 1) * depth]
            put(out, q * stride + base, part.astype(bf16))


def first_kernel(copies, toks, ids, slices, x, d_query, d_key, d_value, *rest):
    kept, sent, d_own = rest[:3]
    d_others, (wide, d_inputs, total_ref) = rest[3 : 2 + toks], rest[2 + toks :]
    t, core = ids[0], low_bits(ids[1], 2)
    rows = d_own.shape[1]
    cut = x.shape[1] // copies
    count = tile_count(cut, d_query.shape[0])
    stride = 2 * count + tile_count(cut, rows * toks)
    for k, part in enumerate((d_query, d_key)):
        wide[...] = mm(part[...], x[...])
        cut_wide(copies, toks, core, k * count, stride, wide, kept, sent)
    total = mm(slices[0], d_query[...]) + mm(slices[1], d_key[...])
    total = total + mm(slices[2], d_value[...])
    total_ref[...] = total
    for side, out in ((core, kept), (1 - core, sent)):
        for q in range(copies // 2):
            start = pl.multiple_of((2 * q + side) * cut, 8)
            put(out, q * stride + 2 * count, total_ref[pl.ds(start, cut), :].astype(bf16))
    for a in range(toks):
        d_inputs[a] = total[:, a * rows : (a + 1) * rows]
    d_own[...] = d_inputs[t]
    for r in range(1, toks):
        d_others[r - 1][...] = d_inputs[jnp.bitwise_xor(t, r)].astype(bf16)


def second_kernel(copies, toks, ids, x, att, d_value, bias_kept, bias_got, *rest):
    d_res_parts, (kept, sent, d_res, wide, narrow) = rest[:toks], rest[toks:]
    t, core = ids[0], low_bits(ids[1], 2)
    rows = d_res_parts[0].shape[0]
    cut = narrow.shape[0] // copies
    count = tile_count(cut, narrow.shape[1])
    wide[...] = mm(d_value[...], x[...])
    cut_wide(copies, toks, core, 0, 2 * count, wide, kept, sent)
    for r in range(toks):
        start = pl.multiple_of(jnp.bitwise_xor(t, r) * rows, rows)
        d_res[pl.ds(start, rows), :] = d_res_parts[r][...]
    narrow[...] = mm(d_res[...], att[...], TN)
    base = copies * count
    bias_count = bias_kept.shape[0] // (copies // 2)
    for side, out in ((core, kept), (1 - core, sent)):
        for q in range(copies // 2):
            first = pl.multiple_of((2 * q + side) * cut, 8)
            put(out, (2 * q + 1) * count, narrow[pl.ds(first, cut), :].astype(bf16))
        for z in range(copies // 4):
            span = pl.ds((2 * z + side) * bias_count, bias_count)
            out[base + z * bias_count : base + (z + 1) * bias_count] = (
                bias_kept[span].astype(f32) + bias_got[span].astype(f32)
            ).astype(bf16)


def step_kernel(segments, ids, *refs):
    count = 1 + max(segment[0] for segment in segments)
    ins, outs = refs[: 2 * count], refs[2 * count :]
    for source, base, parts, tiles, mask, inner, target, start in segments:
        kept, got = ins[2 * source : 2 * source + 2]
        bit = low_bits(ids[1] // mask, 2)
        for q in range(parts // 2):
            for side, out in ((bit, outs[2 * target]), (1 - bit, outs[2 * target + 1])):
                k = q // inner * 2 * inner + side * inner + q % inner
                span = pl.ds(base + k * tiles, tiles)
                out[start + q * tiles : start + (q + 1) * tiles] = (
                    kept[span].astype(f32) + got[span].astype(f32)
                ).astype(bf16)


def last_bias_kernel(toks, base, count, cols, ids, kept, got, *rest):
    pieces, blocks = rest[:toks], rest[toks]
    span = slice(base, base + count)
    tiles = kept[span].astype(f32) + got[span].astype(f32)
    part_rows, rows = pieces[0].shape
    heads = part_rows // cols
    total = jnp.concatenate(
        [take(tiles, h * (count // heads), cols, rows * toks) for h in range(heads)], axis=0
    )
    for a in range(toks):
        blocks[a] = total[:, a * rows : (a + 1) * rows].astype(bf16)
    for r in range(toks):
        pieces[r][...] = blocks[jnp.bitwise_xor(ids[0], r)]


def last_kernel(toks, ids, kept, got, kept_b, got_b, moved, final, *rest):
    pieces, blocks = rest[:toks], rest[toks]
    first = kept[...].astype(f32) + got[...].astype(f32)
    second = kept_b[...].astype(f32) + got_b[...].astype(f32)
    _, cut, own_width = moved.shape
    count = tile_count(cut, own_width)
    for k in range(2):
        moved[k] = take(first, k * count, cut, own_width).astype(bf16)
    moved[2] = take(second, 0, cut, own_width).astype(bf16)
    final[...] = take(second, count, cut, own_width)
    rows = blocks.shape[2]
    single = take(first, 2 * count, cut, rows * toks)
    for a in range(toks):
        blocks[a] = single[:, a * rows : (a + 1) * rows]
    for r in range(toks):
        pieces[r][...] = blocks[jnp.bitwise_xor(ids[0], r)].astype(bf16)


def finish_kernel(group, ids, own, moved, terms, *rest):
    parts, outs = rest[:-5], rest[-5:]
    stays = jnp.where(ids[1] // group == ids[0], 1.0, 0.0).astype(f32)
    for k in range(3):
        outs[k][...] = own[k].astype(f32) * stays + moved[k].astype(f32) * (1.0 - stays)
    total = parts[0][...].astype(f32)
    for part in parts[1:]:
        total = total + part[...].astype(f32)
    outs[3][...] = total
    outs[4][...] = jnp.sum(terms[...], axis=0)


def exit_kernel(toks, noisy, gain, d_res, d_own, *rest):
    others, (grad_noisy, token) = rest[: toks - 1], rest[toks - 1 :]
    token[...] = jnp.zeros(token.shape, f32)
    total = d_own[...]
    for part in others:
        total = total + part[...].astype(f32)
    _, noisy_hat, noisy_inverse = layer_forward(noisy[...].astype(f32), gain[...])
    grad_noisy[...] = (
        d_res[...] + layer_backward(jnp.transpose(total), gain[...], noisy_hat, noisy_inverse)
    ).astype(bf16)


def set_heads(toks, ids, parts, grads):
    part_rows = parts[0].shape[0]
    for r in range(toks):
        start = pl.multiple_of(jnp.bitwise_xor(ids[0], r) * part_rows, part_rows)
        grads[pl.ds(start, part_rows), :] = parts[r][...].astype(f32)


def pair_weight_kernel(toks, ids, columns, *rest):
    parts, (weight_grad, grads) = rest[:toks], rest[toks:]
    set_heads(toks, ids, parts, grads)
    grad_b = grads[...].astype(bf16)
    cols, _, channels = columns.shape
    row_col = low_bits(lax.broadcasted_iota(jnp.int32, (grad_b.shape[0], channels), 0), cols)
    sums = jnp.zeros((grad_b.shape[0], channels), f32)
    for j in range(cols):
        sums = sums + jnp.where(row_col == j, mm(grad_b, columns[j]), 0.0)
    for h in range(weight_grad.shape[1]):
        line = jnp.sum(sums[h * cols : (h + 1) * cols, :], axis=0, keepdims=True)
        for n in range(weight_grad.shape[0]):
            weight_grad[n, h : h + 1, :] = line


def pair_kernel(toks, cols, ids, pair, gain, w_pair, *rest):
    parts, (grad_pair, spread_out, grads) = rest[:toks], rest[toks:]
    set_heads(toks, ids, parts, grads)
    rows = parts[0].shape[1]
    _, pair_hat, pair_inverse = layer_forward(pair[...].astype(f32), gain[...])
    spread, row_col = pair_weight_rows(w_pair[...], w_pair.shape[0], cols)
    turned = jnp.transpose(grads[...]).astype(bf16)
    for j in range(cols):
        spread_out[pl.ds(j, rows, stride=cols), :] = mm(
            turned, jnp.where(row_col == j, spread, 0.0).astype(bf16)
        )
    grad_pair[...] = layer_backward(
        spread_out[...], gain[...], pair_hat, pair_inverse
    ).astype(bf16)


def swap_copy(value, mask):
    size = lax.axis_size("copy")
    return lax.ppermute(value, "copy", [(i, i ^ mask) for i in range(size)])


def swap_tok(value, mask):
    size = lax.axis_size("tok")
    return lax.ppermute(value, "tok", [(i, i ^ mask) for i in range(size)])


def exchange(value):
    return lax.all_to_all(value, ("copy", "tok"), 0, 0)


def per_device(
    noisy,
    single,
    pair,
    restype,
    chain,
    keymask,
    restype_table,
    norm_gain,
    pair_gain,
    trans_gain,
    w_query,
    w_key,
    w_value,
    w_out,
    w_pair,
    chain_weight,
    w_hidden_gate,
    w_hidden_up,
    w_down,
    cotangent,
):
    copies = lax.axis_size("copy")
    toks = lax.axis_size("tok")
    _, rows, width = noisy.shape
    cols = pair.shape[1]
    channels = pair.shape[2]
    heads = w_pair.shape[1]
    head_width = width // heads
    own_heads = heads // toks
    own_width = own_heads * head_width
    tokens = rows * toks
    hidden = w_down.shape[0]
    cut = width // copies
    devices = copies * toks
    ids = jnp.stack([lax.axis_index("tok"), lax.axis_index("copy")]).astype(jnp.int32)
    where_am_i = (ids, SMEM)
    noisy2 = noisy.reshape(rows, width)
    pair2 = pair.reshape(rows * cols, channels)
    pair_gain2 = pair_gain.reshape(1, channels)
    norm_gain2 = norm_gain.reshape(1, width)

    weights3 = [w_query, w_key, w_value]
    if own_width % 128:
        weights3 = [
            lax.dynamic_slice_in_dim(w, ids[0] * own_width, own_width, axis=1) for w in weights3
        ]
    small = [noisy2, single, restype.reshape(1, rows), restype_table, norm_gain, pair2, pair_gain2]
    small += [w_pair.T, chain.reshape(1, tokens), keymask.reshape(1, tokens)]
    entered = call(
        functools.partial(enter_kernel, toks, cols),
        "enter",
        [where_am_i]
        + [(array, "fetch") for array in small]
        + [(chain_weight, SMEM)],
        [((rows, width), bf16), ((cols, rows, channels), bf16)]
        + [((tokens, 128), f32), ((1, tokens), f32), ((toks, own_heads * cols, rows), bf16)],
        [VMEM((rows * cols, channels), f32), VMEM((heads * cols, rows), f32)],
        flops=2 * heads * cols * rows * channels * cols,
        limit=60,
    )
    x_own, columns, facts, chain_row, bias_mine = entered
    near = 4
    far = copies // near
    x_parts = [x_own] + [swap_tok(x_own, r) for r in range(1, toks)]
    by_tok = call(
        functools.partial(split_kernel, far),
        "split_far",
        [bias_mine] + [swap_copy(bias_mine, m * near) for m in range(1, far)],
        [((far, own_heads * cols, rows), bf16)] * toks,
        deps=x_parts[1:],
    )
    (slices,) = call(
        stage_kernel,
        "stage",
        [where_am_i] + [(w, ANY) for w in weights3],
        [((3, width, own_width), bf16)],
        [pltpu.SemaphoreType.DMA((3,))],
        deps=[by_tok[0]],
    )
    (lines,) = call(
        join_kernel,
        "join_tok",
        [by_tok[0]] + [swap_tok(by_tok[r], r) for r in range(1, toks)],
        [((toks, far, own_heads * cols, rows), bf16)],
        deps=[slices],
    )
    x, query, key, value = call(
        functools.partial(project_kernel, toks),
        "project",
        [where_am_i, slices] + x_parts,
        [((tokens, width), bf16)] + [((own_width, tokens), bf16)] * 3,
        flops=6 * tokens * width * own_width,
    )
    (lines,) = call(
        join_kernel,
        "join_y",
        [lines, swap_copy(lines, 2)],
        [((2,) + lines.shape, bf16)],
        deps=[value],
    )
    biases = [lines, swap_copy(lines, 1)]
    done = call(
        functools.partial(attention_kernel, copies, toks, near, cols, head_width),
        "attention",
        [where_am_i, query, key, value] + biases + [facts, chain_row],
        [((own_heads, tokens, tokens), bf16), ((tokens, own_width), bf16)]
        + [((rows, own_width), bf16)] * toks,
        [VMEM((copies, toks, own_heads * cols, rows), bf16)],
        flops=4 * tokens * tokens * own_width,
        limit=32,
    )
    weights, att, pieces = done[0], done[1], done[2:]
    att_parts = [pieces[0]] + [swap_tok(pieces[r], r) for r in range(1, toks)]

    d_hidden, upstream, noisy3, trans_gain2 = call(
        down_kernel,
        "down",
        [cotangent.reshape(rows, width), w_down, noisy2, trans_gain.reshape(1, width)],
        [((rows, hidden), f32), ((rows, width), bf16), ((rows, width), bf16), ((1, width), f32)],
        flops=2 * rows * hidden * width,
    )
    chunk = hidden // 3
    results = call(
        functools.partial(hidden_kernel, toks, chunk),
        "hidden",
        [where_am_i, noisy3, upstream, d_hidden, trans_gain2]
        + att_parts
        + [w_out, w_hidden_gate, w_hidden_up],
        [((rows, width), f32), ((rows, width), bf16)] + [((own_width, rows), bf16)] * toks,
        flops=2 * rows * width * (2 * width + 4 * hidden),
    )
    d_res, d_res_b, d_att = results[0], results[1], results[2:]
    d_att_parts = [d_att[0]] + [swap_tok(d_att[r], r) for r in range(1, toks)]
    bias_tiles = own_heads * tile_count(cols, tokens)
    bias_shape = (copies // 2 * bias_tiles, 16, 128)
    d_query, d_key, d_value, bias_kept, bias_sent, d_res_b = call(
        functools.partial(backward_kernel, copies, toks, cols, head_width),
        "backward",
        [where_am_i, query, key, value, weights] + d_att_parts + [d_res_b],
        [((own_width, tokens), bf16)] * 3 + [(bias_shape, bf16)] * 2 + [((rows, width), bf16)],
        [VMEM((toks, own_width, rows), bf16), VMEM((tokens, tokens), bf16)],
        flops=8 * tokens * tokens * own_width,
        limit=32,
    )
    d_res_parts = [d_res_b] + [swap_tok(d_res_b, r) for r in range(1, toks)]
    bias_got = swap_copy(bias_sent, 2)

    wide_tiles = tile_count(cut, own_width)
    single_tiles = tile_count(cut, tokens)
    first_tiles, second_tiles = 2 * wide_tiles + single_tiles, 2 * wide_tiles
    found = call(
        functools.partial(first_kernel, copies, toks),
        "first",
        [where_am_i, slices, x, d_query, d_key, d_value],
        [((copies // 2 * first_tiles, 16, 128), bf16)] * 2
        + [((width, rows), f32)]
        + [((width, rows), bf16)] * (toks - 1),
        [
            VMEM((own_width, width), f32),
            VMEM((toks, width, rows), f32),
            VMEM((width, tokens), f32),
        ],
        flops=10 * tokens * width * own_width,
    )
    kept, sent, d_own = found[:3]
    got = swap_copy(sent, 1)
    d_others = [swap_tok(found[2 + r], r) for r in range(1, toks)]

    def step(name, pairs, segments, deps=()):
        filled, full, masks_of = {}, [], {}
        for source, base, parts, tiles, mask, left, target in segments:
            inner = 1 << sum(1 for other in left if other < mask)
            start = filled.get(target, 0)
            full.append((source, base, parts, tiles, mask, inner, target, start))
            filled[target] = start + parts // 2 * tiles
            masks_of[target] = mask
        outs = []
        for target in range(len(filled)):
            outs += [((filled[target], 16, 128), bf16)] * 2
        results = call(
            functools.partial(step_kernel, full),
            name,
            [where_am_i] + [array for one in pairs for array in one],
            outs,
            deps=deps,
        )
        return [
            (results[2 * n], swap_copy(results[2 * n + 1], masks_of[n]))
            for n in range(len(filled))
        ]

    masks = [1 << b for b in range(1, copies.bit_length() - 1)]
    masks_b = masks[1:] + masks[:1]
    (ahead,) = step(
        "step_ahead",
        [(kept, got)],
        [(0, 0, copies // 2, first_tiles, masks[0], masks, 0)],
    )
    kept_b, sent_b = call(
        functools.partial(second_kernel, copies, toks),
        "second",
        [where_am_i, x, att, d_value, bias_kept, bias_got] + d_res_parts,
        [((copies // 2 * second_tiles + copies // 4 * bias_tiles, 16, 128), bf16)] * 2,
        [
            VMEM((tokens, width), bf16),
            VMEM((own_width, width), f32),
            VMEM((width, own_width), f32),
        ],
        flops=4 * tokens * width * own_width,
        deps=[ahead[0]],
    )
    got_b = swap_copy(sent_b, 1)

    grad_noisy, exited = call(
        functools.partial(exit_kernel, toks),
        "exit",
        [noisy3, norm_gain2, d_res, d_own] + d_others,
        [((rows, width), bf16), ((8, 128), f32)],
    )
    pairs = [ahead, (kept_b, got_b)]
    parts = copies // 2
    for n, (mask, mask_b) in enumerate(zip(masks, masks_b)):
        segments = []
        if n > 0:
            segments.append((0, 0, parts, first_tiles, mask, masks[n:], 0))
        target = len(segments)
        segments.append((target, 0, parts, second_tiles, mask_b, masks_b[n:], target))
        bias_base = parts * second_tiles
        if n + 1 < len(masks):
            segments.append(
                (target, bias_base, parts // 2, bias_tiles, mask_b, masks_b[n:-1], target)
            )
        else:
            bias_ready = pairs[1]
        if n == 0:
            pairs = [ahead] + step("step_0", pairs[1:], segments)
        else:
            pairs = step("step_%d" % n, pairs, segments, deps=[exited] if n == 1 else ())
        parts //= 2
    bias_pieces = call(
        functools.partial(last_bias_kernel, toks, bias_base, bias_tiles, cols),
        "last_bias",
        [where_am_i, *bias_ready],
        [((own_heads * cols, rows), bf16)] * toks,
        [VMEM((toks, own_heads * cols, rows), bf16)],
        deps=[pairs[0][0]],
    )
    bias_pieces = [bias_pieces[0]] + [swap_tok(bias_pieces[r], r) for r in range(1, toks)]

    group = copies // toks
    swaps = []
    for c in range(copies):
        for t in range(toks):
            if c // group != t:
                swaps.append((c * toks + t, (t * group + c % group) * toks + c // group))

    (weight_grad,) = call(
        functools.partial(pair_weight_kernel, toks),
        "pair_weight",
        [where_am_i, columns] + bias_pieces,
        [((devices, heads, channels), f32)],
        [VMEM((heads * cols, rows), f32)],
        flops=2 * heads * cols * rows * channels * cols,
        deps=[pairs[0][1], pairs[1][1]],
    )
    last = call(
        functools.partial(last_kernel, toks),
        "last",
        [where_am_i, *pairs[0], *pairs[1]],
        [((3, cut, own_width), bf16), ((cut, own_width), f32)] + [((cut, rows), bf16)] * toks,
        [VMEM((toks, cut, rows), f32)],
        deps=[weight_grad],
    )
    (grad_pair,) = call(
        functools.partial(pair_kernel, toks, cols),
        "pair",
        [where_am_i, pair2, pair_gain2, w_pair.T] + bias_pieces,
        [((rows * cols, channels), bf16)],
        [VMEM((rows * cols, channels), f32), VMEM((heads * cols, rows), f32)],
        flops=2 * heads * cols * rows * channels * cols,
        deps=[last[0]],
    )
    weight_terms = exchange(weight_grad)
    grad_out, singles = last[1], last[2:]
    singles = [singles[0]] + [swap_tok(singles[r], r) for r in range(1, toks)]
    moved = lax.ppermute(last[0], ("copy", "tok"), swaps)
    grad_query, grad_key, grad_value, grad_single, weight_grad = call(
        functools.partial(finish_kernel, group),
        "finish",
        [where_am_i, last[0], moved, weight_terms] + singles,
        [((cut, own_width), f32)] * 3 + [((cut, rows), f32), ((heads, channels), f32)],
    )
    return (
        grad_noisy[None],
        grad_single.T,
        grad_pair.reshape(rows, cols, channels),
        grad_query.T,
        grad_key.T,
        grad_value.T,
        grad_out.T,
        weight_grad.T,
    )


def solution(mesh):
    placed = (
        P("copy", "tok", None),
        P("tok", None),
        P("tok", "copy", None),
        P("tok"),
    ) + (P(),) * 15 + (P("copy", "tok", None),)
    return jax.shard_map(
        per_device,
        mesh=mesh,
        in_specs=placed,
        out_specs=(
            P("copy", "tok", None),
            P("tok", "copy"),
            P("tok", "copy", None),
            P("tok", "copy"),
            P("tok", "copy"),
            P("tok", "copy"),
            P("tok", "copy"),
            P(),
        ),
        check_vma=False,
    )
```

```python
import functools

import jax
import jax.numpy as jnp
from jax import lax
from jax.experimental import pallas as pl
from jax.experimental.pallas import tpu as pltpu
from jax.sharding import PartitionSpec as P

epsilon = 1e-05
f32 = jnp.float32
bf16 = jnp.bfloat16
VMEM, SMEM, ANY = pltpu.VMEM, pltpu.SMEM, pl.ANY
MIB = 1 << 20


def layer_forward(values, scales):
    average = jnp.mean(values, axis=-1, keepdims=True)
    centred = values - average
    inverse = lax.rsqrt(jnp.mean(centred * centred, axis=-1, keepdims=True) + epsilon)
    normed = centred * inverse
    return (normed * scales, normed, inverse)


def layer_backward(upstream, scales, normed, inverse):
    scaled = upstream * scales
    first_moment = jnp.mean(scaled, axis=-1, keepdims=True)
    second_moment = jnp.mean(scaled * normed, axis=-1, keepdims=True)
    return inverse * (scaled - first_moment - normed * second_moment)


NN = ((1,), (0,))
NT = ((1,), (1,))
TN = ((0,), (0,))


def mm(left, right, dims=NN):
    return lax.dot_general(left, right, (dims, ((), ())), preferred_element_type=f32)


def call(body, name, inputs, outs, scratch=(), flops=0, limit=16, deps=()):
    arrays, specs, moved, fetched = [], [], 0, []
    for item in inputs:
        array, space = item if isinstance(item, tuple) else (item, VMEM)
        if space == "fetch":
            fetched.append(len(arrays))
            space = pltpu.HBM
        arrays.append(array)
        specs.append(pl.BlockSpec(memory_space=space))
        moved += array.size * array.dtype.itemsize
    for shape, kind, *_ in outs:
        size = jnp.dtype(kind).itemsize
        for extent in shape:
            size *= extent
        moved += size
    read = len(arrays)
    for array in deps:
        arrays.append(array)
        specs.append(pl.BlockSpec(memory_space=ANY))
    extra = [VMEM(arrays[k].shape, arrays[k].dtype) for k in fetched]
    if fetched:
        extra.append(pltpu.SemaphoreType.DMA((len(fetched),)))

    def whole(*refs):
        refs = list(refs[:read]) + list(refs[read + len(deps) :])
        if fetched:
            held, sem = refs[-1 - len(fetched) : -1], refs[-1]
            refs = refs[: -1 - len(fetched)]
            transfers = []
            for n, k in enumerate(fetched):
                transfer = pltpu.make_async_copy(refs[k], held[n], sem.at[n])
                transfer.start()
                transfers.append(transfer)
                refs[k] = held[n]
            for transfer in transfers:
                transfer.wait()
        body(*refs)

    return pl.pallas_call(
        whole,
        name=name,
        out_shape=[jax.ShapeDtypeStruct(one[0], one[1]) for one in outs],
        in_specs=specs,
        out_specs=[pl.BlockSpec(memory_space=(*one, VMEM)[2]) for one in outs],
        scratch_shapes=list(scratch) + extra,
        compiler_params=pltpu.CompilerParams(vmem_limit_bytes=limit * MIB),
        cost_estimate=pl.CostEstimate(flops=flops, bytes_accessed=moved, transcendentals=0),
    )(*arrays)


def low_bits(index, size):
    return jnp.bitwise_and(index, size - 1)


def pair_weight_rows(w_pair, head_count, cols):
    rows = head_count * cols
    shift = cols.bit_length() - 1
    head = lax.shift_right_logical(
        lax.broadcasted_iota(jnp.int32, (rows, head_count), 0), jnp.int32(shift)
    )
    pick = (head == lax.broadcasted_iota(jnp.int32, (rows, head_count), 1)).astype(f32)
    spread = mm(pick.astype(bf16), w_pair)
    row_col = low_bits(lax.broadcasted_iota(jnp.int32, spread.shape, 0), cols)
    return spread, row_col


def own_slice(weight, t, own_width):
    if weight.shape[1] == own_width:
        return weight
    return weight.at[:, pl.ds(pl.multiple_of(t * own_width, own_width), own_width)]


def enter_kernel(toks, cols, ids, *rest):
    noisy, single, restype, table, gain, pair, pair_gain, w_pair, chain, keymask = rest[:10]
    chain_weight, x_out, columns, facts_out, chain_out, bias_out, rounded, bias = rest[10:]
    t = ids[0]
    rows = noisy.shape[0]
    pair_scaled, _, _ = layer_forward(pair[...].astype(f32), pair_gain[...])
    rounded[...] = pair_scaled.astype(bf16).astype(f32)
    head_count = w_pair.shape[0]
    spread, row_col = pair_weight_rows(w_pair[...], head_count, cols)
    total = jnp.zeros((head_count * cols, rows), f32)
    for j in range(cols):
        column = rounded[pl.ds(j, rows, stride=cols), :].astype(bf16)
        columns[j] = column
        total = total + mm(jnp.where(row_col == j, spread, 0.0).astype(bf16), column, NT)
    bias[...] = total
    part = bias_out.shape[1]
    for r in range(toks):
        start = pl.multiple_of(jnp.bitwise_xor(t, r) * part, part)
        bias_out[r] = bias[pl.ds(start, part), :].astype(bf16)
    normed_scaled, _, _ = layer_forward(noisy[...].astype(f32), gain[...])
    types = table.shape[0]
    onehot = (lax.broadcasted_iota(jnp.int32, (types, rows), 0) == restype[...]).astype(f32)
    condition = single[...].astype(f32) + mm(onehot.astype(bf16), table[...], TN)
    x_out[...] = (normed_scaled + condition).astype(bf16)
    chain_row = chain[...]
    tokens = chain_row.shape[1]
    own_heads = head_count // toks
    keep_row = keymask[...].astype(f32)
    line = lax.broadcasted_iota(jnp.int32, (128, tokens), 0)
    facts = jnp.where(line == 0, chain_row.astype(f32), 0.0) + jnp.where(line == 1, keep_row, 0.0)
    for h in range(own_heads):
        weight_row = jnp.zeros((1, tokens), f32)
        for m in range(chain_weight.shape[0]):
            weight_row = jnp.where(chain_row == m, chain_weight[m, t * own_heads + h], weight_row)
        facts = jnp.where(line == 2 + h, weight_row, facts)
    facts_out[...] = jnp.transpose(facts)
    chain_out[...] = chain_row.astype(f32)


def stage_kernel(ids, *rest):
    weights, (slices, sem) = rest[:3], rest[3:]
    transfers = []
    for k in range(3):
        transfer = pltpu.make_async_copy(
            own_slice(weights[k], ids[0], slices.shape[2]), slices.at[k], sem.at[k]
        )
        transfer.start()
        transfers.append(transfer)
    for transfer in transfers:
        transfer.wait()


def project_kernel(toks, ids, slices, *rest):
    parts = rest[:toks]
    x_out, outs = rest[toks], rest[toks + 1 :]
    t = ids[0]
    rows = parts[0].shape[0]
    for r in range(toks):
        start = pl.multiple_of(jnp.bitwise_xor(t, r) * rows, rows)
        x_out[pl.ds(start, rows), :] = parts[r][...]
    x = x_out[...]
    for k in range(3):
        outs[k][...] = jnp.transpose(mm(x, slices[k])).astype(bf16)


def split_kernel(count, *refs):
    for n in range(count):
        for r, out in enumerate(refs[count:]):
            out[n] = refs[n][r]


def join_kernel(*refs):
    for n, ref in enumerate(refs[:-1]):
        refs[-1][n] = ref[...]


def attention_kernel(copies, toks, near, cols, head_width, ids, query, key, value, *rest):
    biases, (facts, chain, weights_out, att_out) = rest[:2], rest[2:6]
    pieces, bias = rest[6 : 6 + toks], rest[6 + toks]
    t, low, high = ids[0], low_bits(ids[1], near), ids[1] // near
    for m in range(near):
        for rz in range(copies // near):
            c = jnp.bitwise_xor(high, rz) * near + jnp.bitwise_xor(low, m)
            for r in range(toks):
                bias[c, jnp.bitwise_xor(t, r)] = biases[m % 2][m // 2, r, rz]
    own_heads = weights_out.shape[0]
    tokens = query.shape[1]
    rows = tokens // toks
    same = facts[:, 0:1] == chain[...]
    keep = facts[:, 1:2] > 0.0
    scale = head_width ** (-0.5)
    attended = []
    for h in range(own_heads):
        span = slice(h * head_width, (h + 1) * head_width)
        logits = mm(key[span, :], query[span, :], TN) * scale
        line = slice(h * cols, (h + 1) * cols)
        extra = jnp.concatenate(
            [
                jnp.concatenate(
                    [bias[c, a, line, :] for c in range(copies)], axis=0
                )
                for a in range(toks)
            ],
            axis=1,
        ).astype(f32)
        logits = logits + (extra + jnp.where(same, facts[:, 2 + h : 3 + h], 0.0))
        logits = jnp.where(keep, logits, -1e30)
        exponent = jnp.exp(logits - jnp.max(logits, axis=0, keepdims=True))
        weights = exponent / jnp.sum(exponent, axis=0, keepdims=True)
        weights_b = weights.astype(bf16)
        weights_out[h] = weights_b
        attended.append(mm(value[span, :], weights_b))
    att_out[...] = jnp.transpose(jnp.concatenate(attended, axis=0)).astype(bf16)
    for r in range(toks):
        start = pl.multiple_of(jnp.bitwise_xor(t, r) * rows, rows)
        pieces[r][...] = att_out[pl.ds(start, rows), :]


def down_kernel(upstream, w_down, noisy, gain, d_hidden, upstream_out, noisy_out, gain_out):
    d_hidden[...] = mm(upstream[...], w_down[...], NT)
    upstream_out[...] = upstream[...]
    noisy_out[...] = noisy[...]
    gain_out[...] = gain[...]


def hidden_kernel(toks, chunk, ids, noisy, upstream, d_hidden, gain, *rest):
    parts = rest[:toks]
    held_out, held_gate, held_up = rest[toks : toks + 3]
    d_res_out, d_res_b_out = rest[toks + 3 : toks + 5]
    d_att_outs = rest[toks + 5 :]
    t = ids[0]
    hidden = held_gate.shape[1]
    residual = noisy[...].astype(f32)
    own_width = parts[0].shape[1]
    for r in range(toks):
        start = pl.multiple_of(jnp.bitwise_xor(t, r) * own_width, own_width)
        residual = residual + mm(parts[r][...], held_out[pl.ds(start, own_width), :])
    trans_scaled, trans_hat, trans_inverse = layer_forward(residual, gain[...])
    trans_in = trans_scaled.astype(bf16)
    d_trans = jnp.zeros(residual.shape, f32)
    for k in range(hidden // chunk):
        span = slice(k * chunk, (k + 1) * chunk)
        gate = mm(trans_in, held_gate[:, span])
        up = mm(trans_in, held_up[:, span])
        incoming = d_hidden[:, span]
        sigmoid = jax.nn.sigmoid(gate)
        d_up = (incoming * gate * sigmoid).astype(bf16)
        d_gate = (incoming * up * sigmoid * (1.0 + gate * (1.0 - sigmoid))).astype(bf16)
        d_trans = d_trans + mm(d_gate, held_gate[:, span], NT) + mm(d_up, held_up[:, span], NT)
    d_res = upstream[...].astype(f32) + layer_backward(
        d_trans, gain[...], trans_hat, trans_inverse
    )
    d_res_out[...] = d_res
    d_res_b = d_res.astype(bf16)
    d_res_b_out[...] = d_res_b
    for r in range(toks):
        start = pl.multiple_of(jnp.bitwise_xor(t, r) * own_width, own_width)
        d_att_outs[r][...] = mm(held_out[pl.ds(start, own_width), :], d_res_b, NT).astype(bf16)


def backward_kernel(copies, toks, cols, head_width, ids, query, key, value, weights, *rest):
    parts, d_res_b = rest[:toks], rest[toks]
    d_query, d_key, d_value, bias_kept, bias_sent, d_res_out = rest[toks + 1 : toks + 7]
    blocks, d_logits = rest[toks + 7 :]
    d_res_out[...] = d_res_b[...]
    t = ids[0]
    bit = low_bits(ids[1] // 2, 2)
    heads = weights.shape[0]
    for r in range(toks):
        blocks[jnp.bitwise_xor(t, r)] = parts[r][...]
    d_att = jnp.concatenate([blocks[a] for a in range(toks)], axis=1)
    count = tile_count(cols, query.shape[1])
    scale = head_width ** (-0.5)
    for h in range(weights.shape[0]):
        span = slice(h * head_width, (h + 1) * head_width)
        d_att_h = d_att[span, :]
        weights_b = weights[h]
        d_weights = mm(value[span, :], d_att_h, TN)
        weights_f = weights_b.astype(f32)
        delta = jnp.sum(weights_f * d_weights, axis=0, keepdims=True)
        d_logits_b = (weights_f * (d_weights - delta)).astype(bf16)
        d_logits[...] = d_logits_b
        for k in range(copies // 2):
            for side, out in ((bit, bias_kept), (1 - bit, bias_sent)):
                start = pl.multiple_of((k // 2 * 4 + side * 2 + k % 2) * cols, cols)
                put(out, (k * heads + h) * count, d_logits[pl.ds(start, cols), :])
        d_query[span, :] = (mm(key[span, :], d_logits_b) * scale).astype(bf16)
        d_key[span, :] = (mm(query[span, :], d_logits_b, NT) * scale).astype(bf16)
        d_value[span, :] = mm(d_att_h, weights_b, NT).astype(bf16)


def tile_count(rows, lanes):
    return -(-rows // 16) * -(-lanes // 128)


def put(out, base, value):
    rows, lanes = value.shape
    for i in range(0, rows, 16):
        for j in range(0, lanes, 128):
            part = value[i : i + 16, j : j + 128]
            if part.shape != (16, 128):
                out[base] = jnp.zeros((16, 128), out.dtype)
            out[base, : part.shape[0], : part.shape[1]] = part
            base += 1


def take(tiles, base, rows, lanes):
    across = -(-lanes // 128)
    lines = []
    for i in range(-(-rows // 16)):
        line = [tiles[base + i * across + j] for j in range(across)]
        lines.append(jnp.concatenate(line, axis=1) if across > 1 else line[0])
    whole = jnp.concatenate(lines, axis=0) if len(lines) > 1 else lines[0]
    return whole[:rows, :lanes]


def cut_wide(copies, toks, core, base, stride, grad, kept, sent):
    group = copies // toks
    cut, depth = grad.shape[1] // copies, grad.shape[1] // toks
    for side, out in ((core, kept), (1 - core, sent)):
        for q in range(copies // 2):
            h = 2 * q // group
            first = pl.multiple_of((2 * q - h * group + side) * cut, 8)
            part = grad[pl.ds(first, cut), h * depth : (h + 1) * depth]
            put(out, q * stride + base, part.astype(bf16))


def first_kernel(copies, toks, ids, slices, x, d_query, d_key, d_value, *rest):
    kept, sent, d_own = rest[:3]
    d_others, (wide, d_inputs, total_ref) = rest[3 : 2 + toks], rest[2 + toks :]
    t, core = ids[0], low_bits(ids[1], 2)
    rows = d_own.shape[1]
    cut = x.shape[1] // copies
    count = tile_count(cut, d_query.shape[0])
    stride = 2 * count + tile_count(cut, rows * toks)
    for k, part in enumerate((d_query, d_key)):
        wide[...] = mm(part[...], x[...])
        cut_wide(copies, toks, core, k * count, stride, wide, kept, sent)
    total = mm(slices[0], d_query[...]) + mm(slices[1], d_key[...])
    total = total + mm(slices[2], d_value[...])
    total_ref[...] = total
    for side, out in ((core, kept), (1 - core, sent)):
        for q in range(copies // 2):
            start = pl.multiple_of((2 * q + side) * cut, 8)
            put(out, q * stride + 2 * count, total_ref[pl.ds(start, cut), :].astype(bf16))
    for a in range(toks):
        d_inputs[a] = total[:, a * rows : (a + 1) * rows]
    d_own[...] = d_inputs[t]
    for r in range(1, toks):
        d_others[r - 1][...] = d_inputs[jnp.bitwise_xor(t, r)].astype(bf16)


def second_kernel(copies, toks, ids, x, att, d_value, bias_kept, bias_got, *rest):
    d_res_parts, (kept, sent, d_res, wide, narrow) = rest[:toks], rest[toks:]
    t, core = ids[0], low_bits(ids[1], 2)
    rows = d_res_parts[0].shape[0]
    cut = narrow.shape[0] // copies
    count = tile_count(cut, narrow.shape[1])
    wide[...] = mm(d_value[...], x[...])
    cut_wide(copies, toks, core, 0, 2 * count, wide, kept, sent)
    for r in range(toks):
        start = pl.multiple_of(jnp.bitwise_xor(t, r) * rows, rows)
        d_res[pl.ds(start, rows), :] = d_res_parts[r][...]
    narrow[...] = mm(d_res[...], att[...], TN)
    base = copies * count
    bias_count = bias_kept.shape[0] // (copies // 2)
    for side, out in ((core, kept), (1 - core, sent)):
        for q in range(copies // 2):
            first = pl.multiple_of((2 * q + side) * cut, 8)
            put(out, (2 * q + 1) * count, narrow[pl.ds(first, cut), :].astype(bf16))
        for z in range(copies // 4):
            span = pl.ds((2 * z + side) * bias_count, bias_count)
            out[base + z * bias_count : base + (z + 1) * bias_count] = (
                bias_kept[span].astype(f32) + bias_got[span].astype(f32)
            ).astype(bf16)


def step_kernel(segments, ids, *refs):
    count = 1 + max(segment[0] for segment in segments)
    ins, outs = refs[: 2 * count], refs[2 * count :]
    for source, base, parts, tiles, mask, inner, target, start in segments:
        kept, got = ins[2 * source : 2 * source + 2]
        bit = low_bits(ids[1] // mask, 2)
        for q in range(parts // 2):
            for side, out in ((bit, outs[2 * target]), (1 - bit, outs[2 * target + 1])):
                k = q // inner * 2 * inner + side * inner + q % inner
                span = pl.ds(base + k * tiles, tiles)
                out[start + q * tiles : start + (q + 1) * tiles] = (
                    kept[span].astype(f32) + got[span].astype(f32)
                ).astype(bf16)


def last_bias_kernel(toks, base, count, cols, ids, kept, got, *rest):
    pieces, blocks = rest[:toks], rest[toks]
    span = slice(base, base + count)
    tiles = kept[span].astype(f32) + got[span].astype(f32)
    part_rows, rows = pieces[0].shape
    heads = part_rows // cols
    total = jnp.concatenate(
        [take(tiles, h * (count // heads), cols, rows * toks) for h in range(heads)], axis=0
    )
    for a in range(toks):
        blocks[a] = total[:, a * rows : (a + 1) * rows].astype(bf16)
    for r in range(toks):
        pieces[r][...] = blocks[jnp.bitwise_xor(ids[0], r)]


def last_kernel(toks, ids, kept, got, kept_b, got_b, moved, final, *rest):
    pieces, blocks = rest[:toks], rest[toks]
    first = kept[...].astype(f32) + got[...].astype(f32)
    second = kept_b[...].astype(f32) + got_b[...].astype(f32)
    _, cut, own_width = moved.shape
    count = tile_count(cut, own_width)
    for k in range(2):
        moved[k] = take(first, k * count, cut, own_width).astype(bf16)
    moved[2] = take(second, 0, cut, own_width).astype(bf16)
    final[...] = take(second, count, cut, own_width)
    rows = blocks.shape[2]
    single = take(first, 2 * count, cut, rows * toks)
    for a in range(toks):
        blocks[a] = single[:, a * rows : (a + 1) * rows]
    for r in range(toks):
        pieces[r][...] = blocks[jnp.bitwise_xor(ids[0], r)].astype(bf16)


def finish_kernel(group, ids, own, moved, terms, *rest):
    parts, outs = rest[:-5], rest[-5:]
    stays = jnp.where(ids[1] // group == ids[0], 1.0, 0.0).astype(f32)
    for k in range(3):
        outs[k][...] = own[k].astype(f32) * stays + moved[k].astype(f32) * (1.0 - stays)
    total = parts[0][...].astype(f32)
    for part in parts[1:]:
        total = total + part[...].astype(f32)
    outs[3][...] = total
    outs[4][...] = jnp.sum(terms[...], axis=0)


def exit_kernel(toks, noisy, gain, d_res, d_own, *rest):
    others, (grad_noisy, token) = rest[: toks - 1], rest[toks - 1 :]
    token[...] = jnp.zeros(token.shape, f32)
    total = d_own[...]
    for part in others:
        total = total + part[...].astype(f32)
    _, noisy_hat, noisy_inverse = layer_forward(noisy[...].astype(f32), gain[...])
    grad_noisy[...] = (
        d_res[...] + layer_backward(jnp.transpose(total), gain[...], noisy_hat, noisy_inverse)
    ).astype(bf16)


def set_heads(toks, ids, parts, grads):
    part_rows = parts[0].shape[0]
    for r in range(toks):
        start = pl.multiple_of(jnp.bitwise_xor(ids[0], r) * part_rows, part_rows)
        grads[pl.ds(start, part_rows), :] = parts[r][...].astype(f32)


def pair_weight_kernel(toks, ids, columns, *rest):
    parts, (weight_grad, grads) = rest[:toks], rest[toks:]
    set_heads(toks, ids, parts, grads)
    grad_b = grads[...].astype(bf16)
    cols, _, channels = columns.shape
    row_col = low_bits(lax.broadcasted_iota(jnp.int32, (grad_b.shape[0], channels), 0), cols)
    sums = jnp.zeros((grad_b.shape[0], channels), f32)
    for j in range(cols):
        sums = sums + jnp.where(row_col == j, mm(grad_b, columns[j]), 0.0)
    for h in range(weight_grad.shape[0]):
        line = jnp.sum(sums[h * cols : (h + 1) * cols, :], axis=0, keepdims=True)
        weight_grad[h : h + 1, :] = line


def pair_kernel(toks, cols, ids, pair, gain, w_pair, *rest):
    parts, (grad_pair, spread_out, grads) = rest[:toks], rest[toks:]
    set_heads(toks, ids, parts, grads)
    rows = parts[0].shape[1]
    _, pair_hat, pair_inverse = layer_forward(pair[...].astype(f32), gain[...])
    spread, row_col = pair_weight_rows(w_pair[...], w_pair.shape[0], cols)
    turned = jnp.transpose(grads[...]).astype(bf16)
    for j in range(cols):
        spread_out[pl.ds(j, rows, stride=cols), :] = mm(
            turned, jnp.where(row_col == j, spread, 0.0).astype(bf16)
        )
    grad_pair[...] = layer_backward(
        spread_out[...], gain[...], pair_hat, pair_inverse
    ).astype(bf16)


def swap_copy(value, mask):
    size = lax.axis_size("copy")
    return lax.ppermute(value, "copy", [(i, i ^ mask) for i in range(size)])


def swap_tok(value, mask):
    size = lax.axis_size("tok")
    return lax.ppermute(value, "tok", [(i, i ^ mask) for i in range(size)])


def per_device(
    noisy,
    single,
    pair,
    restype,
    chain,
    keymask,
    restype_table,
    norm_gain,
    pair_gain,
    trans_gain,
    w_query,
    w_key,
    w_value,
    w_out,
    w_pair,
    chain_weight,
    w_hidden_gate,
    w_hidden_up,
    w_down,
    cotangent,
):
    copies = lax.axis_size("copy")
    toks = lax.axis_size("tok")
    _, rows, width = noisy.shape
    cols = pair.shape[1]
    channels = pair.shape[2]
    heads = w_pair.shape[1]
    head_width = width // heads
    own_heads = heads // toks
    own_width = own_heads * head_width
    tokens = rows * toks
    hidden = w_down.shape[0]
    cut = width // copies
    ids = jnp.stack([lax.axis_index("tok"), lax.axis_index("copy")]).astype(jnp.int32)
    where_am_i = (ids, SMEM)
    noisy2 = noisy.reshape(rows, width)
    pair2 = pair.reshape(rows * cols, channels)
    pair_gain2 = pair_gain.reshape(1, channels)
    norm_gain2 = norm_gain.reshape(1, width)

    weights3 = [w_query, w_key, w_value]
    if own_width % 128:
        weights3 = [
            lax.dynamic_slice_in_dim(w, ids[0] * own_width, own_width, axis=1) for w in weights3
        ]
    small = [noisy2, single, restype.reshape(1, rows), restype_table, norm_gain, pair2, pair_gain2]
    small += [w_pair.T, chain.reshape(1, tokens), keymask.reshape(1, tokens)]
    entered = call(
        functools.partial(enter_kernel, toks, cols),
        "enter",
        [where_am_i]
        + [(array, "fetch") for array in small]
        + [(chain_weight, SMEM)],
        [((rows, width), bf16), ((cols, rows, channels), bf16)]
        + [((tokens, 128), f32), ((1, tokens), f32), ((toks, own_heads * cols, rows), bf16)],
        [VMEM((rows * cols, channels), f32), VMEM((heads * cols, rows), f32)],
        flops=2 * heads * cols * rows * channels * cols,
        limit=60,
    )
    x_own, columns, facts, chain_row, bias_mine = entered
    near = 4
    far = copies // near
    x_parts = [x_own] + [swap_tok(x_own, r) for r in range(1, toks)]
    by_tok = call(
        functools.partial(split_kernel, far),
        "split_far",
        [bias_mine] + [swap_copy(bias_mine, m * near) for m in range(1, far)],
        [((far, own_heads * cols, rows), bf16)] * toks,
        deps=x_parts[1:],
    )
    (lines,) = call(
        join_kernel,
        "join_tok",
        [by_tok[0]] + [swap_tok(by_tok[r], r) for r in range(1, toks)],
        [((toks, far, own_heads * cols, rows), bf16)],
    )
    (slices,) = call(
        stage_kernel,
        "stage",
        [where_am_i] + [(w, ANY) for w in weights3],
        [((3, width, own_width), bf16)],
        [pltpu.SemaphoreType.DMA((3,))],
        deps=[lines],
    )
    (lines,) = call(
        join_kernel,
        "join_y",
        [lines, swap_copy(lines, 2)],
        [((2,) + lines.shape, bf16)],
        deps=[slices],
    )
    biases = [lines, swap_copy(lines, 1)]
    x, query, key, value = call(
        functools.partial(project_kernel, toks),
        "project",
        [where_am_i, slices] + x_parts,
        [((tokens, width), bf16)] + [((own_width, tokens), bf16)] * 3,
        flops=6 * tokens * width * own_width,
    )
    done = call(
        functools.partial(attention_kernel, copies, toks, near, cols, head_width),
        "attention",
        [where_am_i, query, key, value] + biases + [facts, chain_row],
        [((own_heads, tokens, tokens), bf16), ((tokens, own_width), bf16)]
        + [((rows, own_width), bf16)] * toks,
        [VMEM((copies, toks, own_heads * cols, rows), bf16)],
        flops=4 * tokens * tokens * own_width,
        limit=32,
    )
    weights, att, pieces = done[0], done[1], done[2:]
    att_parts = [pieces[0]] + [swap_tok(pieces[r], r) for r in range(1, toks)]

    d_hidden, upstream, noisy3, trans_gain2 = call(
        down_kernel,
        "down",
        [cotangent.reshape(rows, width), w_down, noisy2, trans_gain.reshape(1, width)],
        [((rows, hidden), f32), ((rows, width), bf16), ((rows, width), bf16), ((1, width), f32)],
        flops=2 * rows * hidden * width,
    )
    chunk = hidden // 3
    results = call(
        functools.partial(hidden_kernel, toks, chunk),
        "hidden",
        [where_am_i, noisy3, upstream, d_hidden, trans_gain2]
        + att_parts
        + [w_out, w_hidden_gate, w_hidden_up],
        [((rows, width), f32), ((rows, width), bf16)] + [((own_width, rows), bf16)] * toks,
        flops=2 * rows * width * (2 * width + 4 * hidden),
    )
    d_res, d_res_b, d_att = results[0], results[1], results[2:]
    d_att_parts = [d_att[0]] + [swap_tok(d_att[r], r) for r in range(1, toks)]
    bias_tiles = own_heads * tile_count(cols, tokens)
    bias_shape = (copies // 2 * bias_tiles, 16, 128)
    d_query, d_key, d_value, bias_kept, bias_sent, d_res_b = call(
        functools.partial(backward_kernel, copies, toks, cols, head_width),
        "backward",
        [where_am_i, query, key, value, weights] + d_att_parts + [d_res_b],
        [((own_width, tokens), bf16)] * 3 + [(bias_shape, bf16)] * 2 + [((rows, width), bf16)],
        [VMEM((toks, own_width, rows), bf16), VMEM((tokens, tokens), bf16)],
        flops=8 * tokens * tokens * own_width,
        limit=32,
    )
    d_res_parts = [d_res_b] + [swap_tok(d_res_b, r) for r in range(1, toks)]
    bias_got = swap_copy(bias_sent, 2)

    wide_tiles = tile_count(cut, own_width)
    single_tiles = tile_count(cut, tokens)
    first_tiles, second_tiles = 2 * wide_tiles + single_tiles, 2 * wide_tiles
    found = call(
        functools.partial(first_kernel, copies, toks),
        "first",
        [where_am_i, slices, x, d_query, d_key, d_value],
        [((copies // 2 * first_tiles, 16, 128), bf16)] * 2
        + [((width, rows), f32)]
        + [((width, rows), bf16)] * (toks - 1),
        [
            VMEM((own_width, width), f32),
            VMEM((toks, width, rows), f32),
            VMEM((width, tokens), f32),
        ],
        flops=10 * tokens * width * own_width,
    )
    kept, sent, d_own = found[:3]
    got = swap_copy(sent, 1)
    d_others = [swap_tok(found[2 + r], r) for r in range(1, toks)]

    def step(name, pairs, segments, deps=()):
        filled, full, masks_of = {}, [], {}
        for source, base, parts, tiles, mask, left, target in segments:
            inner = 1 << sum(1 for other in left if other < mask)
            start = filled.get(target, 0)
            full.append((source, base, parts, tiles, mask, inner, target, start))
            filled[target] = start + parts // 2 * tiles
            masks_of[target] = mask
        outs = []
        for target in range(len(filled)):
            outs += [((filled[target], 16, 128), bf16)] * 2
        results = call(
            functools.partial(step_kernel, full),
            name,
            [where_am_i] + [array for one in pairs for array in one],
            outs,
            deps=deps,
        )
        return [
            (results[2 * n], swap_copy(results[2 * n + 1], masks_of[n]))
            for n in range(len(filled))
        ]

    masks = [1 << b for b in range(1, copies.bit_length() - 1)]
    masks_b = masks[1:] + masks[:1]
    kept_b, sent_b = call(
        functools.partial(second_kernel, copies, toks),
        "second",
        [where_am_i, x, att, d_value, bias_kept, bias_got] + d_res_parts,
        [((copies // 2 * second_tiles + copies // 4 * bias_tiles, 16, 128), bf16)] * 2,
        [
            VMEM((tokens, width), bf16),
            VMEM((own_width, width), f32),
            VMEM((width, own_width), f32),
        ],
        flops=4 * tokens * width * own_width,
    )
    got_b = swap_copy(sent_b, 1)

    grad_noisy, exited = call(
        functools.partial(exit_kernel, toks),
        "exit",
        [noisy3, norm_gain2, d_res, d_own] + d_others,
        [((rows, width), bf16), ((8, 128), f32)],
    )
    pairs = [(kept, got), (kept_b, got_b)]
    parts = copies // 2
    for n, (mask, mask_b) in enumerate(zip(masks, masks_b)):
        segments = [
            (0, 0, parts, first_tiles, mask, masks[n:], 0),
            (1, 0, parts, second_tiles, mask_b, masks_b[n:], 1),
        ]
        bias_base = parts * second_tiles
        if n + 1 < len(masks):
            segments.append((1, bias_base, parts // 2, bias_tiles, mask_b, masks_b[n:-1], 1))
        else:
            bias_ready = pairs[1]
        pairs = step("step_%d" % n, pairs, segments, deps=[exited] if n == 1 else ())
        parts //= 2
    bias_pieces = call(
        functools.partial(last_bias_kernel, toks, bias_base, bias_tiles, cols),
        "last_bias",
        [where_am_i, *bias_ready],
        [((own_heads * cols, rows), bf16)] * toks,
        [VMEM((toks, own_heads * cols, rows), bf16)],
        deps=[pairs[0][0]],
    )
    bias_pieces = [bias_pieces[0]] + [swap_tok(bias_pieces[r], r) for r in range(1, toks)]

    group = copies // toks
    swaps = []
    for c in range(copies):
        for t in range(toks):
            if c // group != t:
                swaps.append((c * toks + t, (t * group + c % group) * toks + c // group))

    (weight_grad,) = call(
        functools.partial(pair_weight_kernel, toks),
        "pair_weight",
        [where_am_i, columns] + bias_pieces,
        [((heads, channels), f32)],
        [VMEM((heads * cols, rows), f32)],
        flops=2 * heads * cols * rows * channels * cols,
        deps=[pairs[0][1], pairs[1][1]],
    )
    last = call(
        functools.partial(last_kernel, toks),
        "last",
        [where_am_i, *pairs[0], *pairs[1]],
        [((3, cut, own_width), bf16), ((cut, own_width), f32)] + [((cut, rows), bf16)] * toks,
        [VMEM((toks, cut, rows), f32)],
        deps=[weight_grad],
    )
    (grad_pair,) = call(
        functools.partial(pair_kernel, toks, cols),
        "pair",
        [where_am_i, pair2, pair_gain2, w_pair.T] + bias_pieces,
        [((rows * cols, channels), bf16)],
        [VMEM((rows * cols, channels), f32), VMEM((heads * cols, rows), f32)],
        flops=2 * heads * cols * rows * channels * cols,
        deps=[last[0]],
    )
    weight_terms = lax.all_gather(weight_grad, ("copy", "tok"))
    grad_out, singles = last[1], last[2:]
    singles = [singles[0]] + [swap_tok(singles[r], r) for r in range(1, toks)]
    moved = lax.ppermute(last[0], ("copy", "tok"), swaps)
    grad_query, grad_key, grad_value, grad_single, weight_grad = call(
        functools.partial(finish_kernel, group),
        "finish",
        [where_am_i, last[0], moved, weight_terms] + singles,
        [((cut, own_width), f32)] * 3 + [((cut, rows), f32), ((heads, channels), f32)],
    )
    return (
        grad_noisy[None],
        grad_single.T,
        grad_pair.reshape(rows, cols, channels),
        grad_query.T,
        grad_key.T,
        grad_value.T,
        grad_out.T,
        weight_grad.T,
    )


def solution(mesh):
    placed = (
        P("copy", "tok", None),
        P("tok", None),
        P("tok", "copy", None),
        P("tok"),
    ) + (P(),) * 15 + (P("copy", "tok", None),)
    return jax.shard_map(
        per_device,
        mesh=mesh,
        in_specs=placed,
        out_specs=(
            P("copy", "tok", None),
            P("tok", "copy"),
            P("tok", "copy", None),
            P("tok", "copy"),
            P("tok", "copy"),
            P("tok", "copy"),
            P("tok", "copy"),
            P(),
        ),
        check_vma=False,
    )
```

```python
import functools

import jax
import jax.numpy as jnp
from jax import lax
from jax.experimental import pallas as pl
from jax.experimental.pallas import tpu as pltpu
from jax.sharding import PartitionSpec as P

epsilon = 1e-05
f32 = jnp.float32
bf16 = jnp.bfloat16
VMEM, SMEM, ANY = pltpu.VMEM, pltpu.SMEM, pl.ANY
MIB = 1 << 20


def layer_forward(values, scales):
    average = jnp.mean(values, axis=-1, keepdims=True)
    centred = values - average
    inverse = lax.rsqrt(jnp.mean(centred * centred, axis=-1, keepdims=True) + epsilon)
    normed = centred * inverse
    return (normed * scales, normed, inverse)


def layer_backward(upstream, scales, normed, inverse):
    scaled = upstream * scales
    first_moment = jnp.mean(scaled, axis=-1, keepdims=True)
    second_moment = jnp.mean(scaled * normed, axis=-1, keepdims=True)
    return inverse * (scaled - first_moment - normed * second_moment)


NN = ((1,), (0,))
NT = ((1,), (1,))
TN = ((0,), (0,))


def mm(left, right, dims=NN):
    return lax.dot_general(left, right, (dims, ((), ())), preferred_element_type=f32)


def call(body, name, inputs, outs, scratch=(), flops=0, limit=16, deps=()):
    arrays, specs, moved, fetched = [], [], 0, []
    for item in inputs:
        array, space = item if isinstance(item, tuple) else (item, VMEM)
        if space == "fetch":
            fetched.append(len(arrays))
            space = pltpu.HBM
        arrays.append(array)
        specs.append(pl.BlockSpec(memory_space=space))
        moved += array.size * array.dtype.itemsize
    for shape, kind, *_ in outs:
        size = jnp.dtype(kind).itemsize
        for extent in shape:
            size *= extent
        moved += size
    read = len(arrays)
    for array in deps:
        arrays.append(array)
        specs.append(pl.BlockSpec(memory_space=ANY))
    extra = [VMEM(arrays[k].shape, arrays[k].dtype) for k in fetched]
    if fetched:
        extra.append(pltpu.SemaphoreType.DMA((len(fetched),)))

    def whole(*refs):
        refs = list(refs[:read]) + list(refs[read + len(deps) :])
        if fetched:
            held, sem = refs[-1 - len(fetched) : -1], refs[-1]
            refs = refs[: -1 - len(fetched)]
            transfers = []
            for n, k in enumerate(fetched):
                transfer = pltpu.make_async_copy(refs[k], held[n], sem.at[n])
                transfer.start()
                transfers.append(transfer)
                refs[k] = held[n]
            for transfer in transfers:
                transfer.wait()
        body(*refs)

    return pl.pallas_call(
        whole,
        name=name,
        out_shape=[jax.ShapeDtypeStruct(one[0], one[1]) for one in outs],
        in_specs=specs,
        out_specs=[pl.BlockSpec(memory_space=(*one, VMEM)[2]) for one in outs],
        scratch_shapes=list(scratch) + extra,
        compiler_params=pltpu.CompilerParams(vmem_limit_bytes=limit * MIB),
        cost_estimate=pl.CostEstimate(flops=flops, bytes_accessed=moved, transcendentals=0),
    )(*arrays)


def low_bits(index, size):
    return jnp.bitwise_and(index, size - 1)


def pair_weight_rows(w_pair, head_count, cols):
    rows = head_count * cols
    shift = cols.bit_length() - 1
    head = lax.shift_right_logical(
        lax.broadcasted_iota(jnp.int32, (rows, head_count), 0), jnp.int32(shift)
    )
    pick = (head == lax.broadcasted_iota(jnp.int32, (rows, head_count), 1)).astype(f32)
    spread = mm(pick.astype(bf16), w_pair)
    row_col = low_bits(lax.broadcasted_iota(jnp.int32, spread.shape, 0), cols)
    return spread, row_col


def own_slice(weight, t, own_width):
    if weight.shape[1] == own_width:
        return weight
    return weight.at[:, pl.ds(pl.multiple_of(t * own_width, own_width), own_width)]


def enter_kernel(toks, cols, ids, *rest):
    noisy, single, restype, table, gain, pair, pair_gain, w_pair, chain, keymask = rest[:10]
    chain_weight, x_out, columns, facts_out, chain_out, bias_out, rounded, bias = rest[10:]
    t = ids[0]
    rows = noisy.shape[0]
    pair_scaled, _, _ = layer_forward(pair[...].astype(f32), pair_gain[...])
    rounded[...] = pair_scaled.astype(bf16).astype(f32)
    head_count = w_pair.shape[0]
    spread, row_col = pair_weight_rows(w_pair[...], head_count, cols)
    total = jnp.zeros((head_count * cols, rows), f32)
    for j in range(cols):
        column = rounded[pl.ds(j, rows, stride=cols), :].astype(bf16)
        columns[j] = column
        total = total + mm(jnp.where(row_col == j, spread, 0.0).astype(bf16), column, NT)
    bias[...] = total
    part = bias_out.shape[1]
    for r in range(toks):
        start = pl.multiple_of(jnp.bitwise_xor(t, r) * part, part)
        bias_out[r] = bias[pl.ds(start, part), :].astype(bf16)
    normed_scaled, _, _ = layer_forward(noisy[...].astype(f32), gain[...])
    types = table.shape[0]
    onehot = (lax.broadcasted_iota(jnp.int32, (types, rows), 0) == restype[...]).astype(f32)
    condition = single[...].astype(f32) + mm(onehot.astype(bf16), table[...], TN)
    x_out[...] = (normed_scaled + condition).astype(bf16)
    chain_row = chain[...]
    tokens = chain_row.shape[1]
    own_heads = head_count // toks
    keep_row = keymask[...].astype(f32)
    line = lax.broadcasted_iota(jnp.int32, (128, tokens), 0)
    facts = jnp.where(line == 0, chain_row.astype(f32), 0.0) + jnp.where(line == 1, keep_row, 0.0)
    for h in range(own_heads):
        weight_row = jnp.zeros((1, tokens), f32)
        for m in range(chain_weight.shape[0]):
            weight_row = jnp.where(chain_row == m, chain_weight[m, t * own_heads + h], weight_row)
        facts = jnp.where(line == 2 + h, weight_row, facts)
    facts_out[...] = jnp.transpose(facts)
    chain_out[...] = chain_row.astype(f32)


def stage_kernel(ids, *rest):
    weights, (slices, sem) = rest[:3], rest[3:]
    transfers = []
    for k in range(3):
        transfer = pltpu.make_async_copy(
            own_slice(weights[k], ids[0], slices.shape[2]), slices.at[k], sem.at[k]
        )
        transfer.start()
        transfers.append(transfer)
    for transfer in transfers:
        transfer.wait()


def project_kernel(toks, ids, slices, *rest):
    parts = rest[:toks]
    x_out, outs = rest[toks], rest[toks + 1 :]
    t = ids[0]
    rows = parts[0].shape[0]
    for r in range(toks):
        start = pl.multiple_of(jnp.bitwise_xor(t, r) * rows, rows)
        x_out[pl.ds(start, rows), :] = parts[r][...]
    x = x_out[...]
    for k in range(3):
        outs[k][...] = jnp.transpose(mm(x, slices[k])).astype(bf16)


def split_kernel(count, *refs):
    for n in range(count):
        for r, out in enumerate(refs[count:]):
            out[n] = refs[n][r]


def join_kernel(*refs):
    for n, ref in enumerate(refs[:-1]):
        refs[-1][n] = ref[...]


def attention_kernel(copies, toks, near, cols, head_width, ids, query, key, value, *rest):
    biases, (facts, chain, weights_out, att_out) = rest[:2], rest[2:6]
    pieces, bias = rest[6 : 6 + toks], rest[6 + toks]
    t, low, high = ids[0], low_bits(ids[1], near), ids[1] // near
    for m in range(near):
        for rz in range(copies // near):
            c = jnp.bitwise_xor(high, rz) * near + jnp.bitwise_xor(low, m)
            for r in range(toks):
                bias[c, jnp.bitwise_xor(t, r)] = biases[m % 2][m // 2, r, rz]
    own_heads = weights_out.shape[0]
    tokens = query.shape[1]
    rows = tokens // toks
    same = facts[:, 0:1] == chain[...]
    keep = facts[:, 1:2] > 0.0
    scale = head_width ** (-0.5)
    attended = []
    for h in range(own_heads):
        span = slice(h * head_width, (h + 1) * head_width)
        logits = mm(key[span, :], query[span, :], TN) * scale
        line = slice(h * cols, (h + 1) * cols)
        extra = jnp.concatenate(
            [
                jnp.concatenate(
                    [bias[c, a, line, :] for c in range(copies)], axis=0
                )
                for a in range(toks)
            ],
            axis=1,
        ).astype(f32)
        logits = logits + (extra + jnp.where(same, facts[:, 2 + h : 3 + h], 0.0))
        logits = jnp.where(keep, logits, -1e30)
        exponent = jnp.exp(logits - jnp.max(logits, axis=0, keepdims=True))
        weights = exponent / jnp.sum(exponent, axis=0, keepdims=True)
        weights_b = weights.astype(bf16)
        weights_out[h] = weights_b
        attended.append(mm(value[span, :], weights_b))
    att_out[...] = jnp.transpose(jnp.concatenate(attended, axis=0)).astype(bf16)
    for r in range(toks):
        start = pl.multiple_of(jnp.bitwise_xor(t, r) * rows, rows)
        pieces[r][...] = att_out[pl.ds(start, rows), :]


def down_kernel(upstream, w_down, noisy, gain, d_hidden, upstream_out, noisy_out, gain_out):
    d_hidden[...] = mm(upstream[...], w_down[...], NT)
    upstream_out[...] = upstream[...]
    noisy_out[...] = noisy[...]
    gain_out[...] = gain[...]


def hidden_kernel(toks, chunk, ids, noisy, upstream, d_hidden, gain, *rest):
    parts = rest[:toks]
    held_out, held_gate, held_up = rest[toks : toks + 3]
    d_res_out, d_res_b_out = rest[toks + 3 : toks + 5]
    d_att_outs = rest[toks + 5 :]
    t = ids[0]
    hidden = held_gate.shape[1]
    residual = noisy[...].astype(f32)
    own_width = parts[0].shape[1]
    for r in range(toks):
        start = pl.multiple_of(jnp.bitwise_xor(t, r) * own_width, own_width)
        residual = residual + mm(parts[r][...], held_out[pl.ds(start, own_width), :])
    trans_scaled, trans_hat, trans_inverse = layer_forward(residual, gain[...])
    trans_in = trans_scaled.astype(bf16)
    d_trans = jnp.zeros(residual.shape, f32)
    for k in range(hidden // chunk):
        span = slice(k * chunk, (k + 1) * chunk)
        gate = mm(trans_in, held_gate[:, span])
        up = mm(trans_in, held_up[:, span])
        incoming = d_hidden[:, span]
        sigmoid = jax.nn.sigmoid(gate)
        d_up = (incoming * gate * sigmoid).astype(bf16)
        d_gate = (incoming * up * sigmoid * (1.0 + gate * (1.0 - sigmoid))).astype(bf16)
        d_trans = d_trans + mm(d_gate, held_gate[:, span], NT) + mm(d_up, held_up[:, span], NT)
    d_res = upstream[...].astype(f32) + layer_backward(
        d_trans, gain[...], trans_hat, trans_inverse
    )
    d_res_out[...] = d_res
    d_res_b = d_res.astype(bf16)
    d_res_b_out[...] = d_res_b
    for r in range(toks):
        start = pl.multiple_of(jnp.bitwise_xor(t, r) * own_width, own_width)
        d_att_outs[r][...] = mm(held_out[pl.ds(start, own_width), :], d_res_b, NT).astype(bf16)


def backward_kernel(copies, toks, cols, head_width, ids, query, key, value, weights, *rest):
    parts, d_res_b = rest[:toks], rest[toks]
    d_query, d_key, d_value, bias_kept, bias_sent, d_res_out = rest[toks + 1 : toks + 7]
    blocks, d_logits = rest[toks + 7 :]
    d_res_out[...] = d_res_b[...]
    t = ids[0]
    bit = low_bits(ids[1] // 2, 2)
    heads = weights.shape[0]
    for r in range(toks):
        blocks[jnp.bitwise_xor(t, r)] = parts[r][...]
    d_att = jnp.concatenate([blocks[a] for a in range(toks)], axis=1)
    count = tile_count(cols, query.shape[1])
    scale = head_width ** (-0.5)
    for h in range(weights.shape[0]):
        span = slice(h * head_width, (h + 1) * head_width)
        d_att_h = d_att[span, :]
        weights_b = weights[h]
        d_weights = mm(value[span, :], d_att_h, TN)
        weights_f = weights_b.astype(f32)
        delta = jnp.sum(weights_f * d_weights, axis=0, keepdims=True)
        d_logits_b = (weights_f * (d_weights - delta)).astype(bf16)
        d_logits[...] = d_logits_b
        for k in range(copies // 2):
            for side, out in ((bit, bias_kept), (1 - bit, bias_sent)):
                start = pl.multiple_of((k // 2 * 4 + side * 2 + k % 2) * cols, cols)
                put(out, (k * heads + h) * count, d_logits[pl.ds(start, cols), :])
        d_query[span, :] = (mm(key[span, :], d_logits_b) * scale).astype(bf16)
        d_key[span, :] = (mm(query[span, :], d_logits_b, NT) * scale).astype(bf16)
        d_value[span, :] = mm(d_att_h, weights_b, NT).astype(bf16)


def tile_count(rows, lanes):
    return -(-rows // 16) * -(-lanes // 128)


def put(out, base, value):
    rows, lanes = value.shape
    for i in range(0, rows, 16):
        for j in range(0, lanes, 128):
            part = value[i : i + 16, j : j + 128]
            if part.shape != (16, 128):
                out[base] = jnp.zeros((16, 128), out.dtype)
            out[base, : part.shape[0], : part.shape[1]] = part
            base += 1


def take(tiles, base, rows, lanes):
    across = -(-lanes // 128)
    lines = []
    for i in range(-(-rows // 16)):
        line = [tiles[base + i * across + j] for j in range(across)]
        lines.append(jnp.concatenate(line, axis=1) if across > 1 else line[0])
    whole = jnp.concatenate(lines, axis=0) if len(lines) > 1 else lines[0]
    return whole[:rows, :lanes]


def cut_wide(copies, toks, core, base, stride, grad, kept, sent):
    group = copies // toks
    cut, depth = grad.shape[1] // copies, grad.shape[1] // toks
    for side, out in ((core, kept), (1 - core, sent)):
        for q in range(copies // 2):
            h = 2 * q // group
            first = pl.multiple_of((2 * q - h * group + side) * cut, 8)
            part = grad[pl.ds(first, cut), h * depth : (h + 1) * depth]
            put(out, q * stride + base, part.astype(bf16))


def first_kernel(copies, toks, ids, slices, x, d_query, d_key, d_value, *rest):
    kept, sent, d_own = rest[:3]
    d_others, (wide, d_inputs, total_ref) = rest[3 : 2 + toks], rest[2 + toks :]
    t, core = ids[0], low_bits(ids[1], 2)
    rows = d_own.shape[1]
    cut = x.shape[1] // copies
    count = tile_count(cut, d_query.shape[0])
    stride = 3 * count + tile_count(cut, rows * toks)
    for k, part in enumerate((d_query, d_key, d_value)):
        wide[...] = mm(part[...], x[...])
        cut_wide(copies, toks, core, k * count, stride, wide, kept, sent)
    total = mm(slices[0], d_query[...]) + mm(slices[1], d_key[...])
    total = total + mm(slices[2], d_value[...])
    total_ref[...] = total
    for side, out in ((core, kept), (1 - core, sent)):
        for q in range(copies // 2):
            start = pl.multiple_of((2 * q + side) * cut, 8)
            put(out, q * stride + 3 * count, total_ref[pl.ds(start, cut), :].astype(bf16))
    for a in range(toks):
        d_inputs[a] = total[:, a * rows : (a + 1) * rows]
    d_own[...] = d_inputs[t]
    for r in range(1, toks):
        d_others[r - 1][...] = d_inputs[jnp.bitwise_xor(t, r)].astype(bf16)


def second_kernel(copies, toks, ids, att, bias_kept, bias_got, *rest):
    d_res_parts, (kept, sent, d_res, narrow) = rest[:toks], rest[toks:]
    t, core = ids[0], low_bits(ids[1], 2)
    rows = d_res_parts[0].shape[0]
    cut = narrow.shape[0] // copies
    count = tile_count(cut, narrow.shape[1])
    for r in range(toks):
        start = pl.multiple_of(jnp.bitwise_xor(t, r) * rows, rows)
        d_res[pl.ds(start, rows), :] = d_res_parts[r][...]
    narrow[...] = mm(d_res[...], att[...], TN)
    base = copies // 2 * count
    bias_count = bias_kept.shape[0] // (copies // 2)
    for side, out in ((core, kept), (1 - core, sent)):
        for q in range(copies // 2):
            first = pl.multiple_of((2 * q + side) * cut, 8)
            put(out, q * count, narrow[pl.ds(first, cut), :].astype(bf16))
        for z in range(copies // 4):
            span = pl.ds((2 * z + side) * bias_count, bias_count)
            out[base + z * bias_count : base + (z + 1) * bias_count] = (
                bias_kept[span].astype(f32) + bias_got[span].astype(f32)
            ).astype(bf16)


def step_kernel(segments, ids, *refs):
    count = 1 + max(segment[0] for segment in segments)
    ins, outs = refs[: 2 * count], refs[2 * count :]
    for source, base, parts, tiles, mask, inner, target, start in segments:
        kept, got = ins[2 * source : 2 * source + 2]
        bit = low_bits(ids[1] // mask, 2)
        for q in range(parts // 2):
            for side, out in ((bit, outs[2 * target]), (1 - bit, outs[2 * target + 1])):
                k = q // inner * 2 * inner + side * inner + q % inner
                span = pl.ds(base + k * tiles, tiles)
                out[start + q * tiles : start + (q + 1) * tiles] = (
                    kept[span].astype(f32) + got[span].astype(f32)
                ).astype(bf16)


def last_bias_kernel(toks, base, count, cols, ids, kept, got, *rest):
    pieces, blocks = rest[:toks], rest[toks]
    span = slice(base, base + count)
    tiles = kept[span].astype(f32) + got[span].astype(f32)
    part_rows, rows = pieces[0].shape
    heads = part_rows // cols
    total = jnp.concatenate(
        [take(tiles, h * (count // heads), cols, rows * toks) for h in range(heads)], axis=0
    )
    for a in range(toks):
        blocks[a] = total[:, a * rows : (a + 1) * rows].astype(bf16)
    for r in range(toks):
        pieces[r][...] = blocks[jnp.bitwise_xor(ids[0], r)]


def across_kernel(wide, lines, segment, ids, kept, got, kept_b, got_b, *outs):
    t = ids[0]
    stride = kept.shape[0] // 2
    step_kernel([(0, 0) + segment], ids, kept_b, got_b, *outs[2:])
    for side, out in ((t, outs[0]), (1 - t, outs[1])):
        span = pl.ds(side * stride, wide)
        out[:wide] = (kept[span].astype(f32) + got[span].astype(f32)).astype(bf16)
        for a in range(2):
            for i in range(lines):
                k = a * stride + wide + 2 * i + side
                out[wide + a * lines + i] = (
                    kept[k].astype(f32) + got[k].astype(f32)
                ).astype(bf16)


def far_kernel(wide, lines, half, ids, kept, got, kept_out, sent_out, groups):
    t, a = ids[0], ids[1] // half
    groups[t] = kept[:wide]
    groups[1 - t] = got[:wide]
    for side, out in ((a, kept_out), (1 - a, sent_out)):
        out[:wide] = groups[side]
        span = pl.ds(wide + side * lines, lines)
        out[wide:] = (kept[span].astype(f32) + got[span].astype(f32)).astype(bf16)


def close_kernel(kept, got, kept_b, got_b, terms, *outs):
    total = kept[...].astype(f32) + got[...].astype(f32)
    cut, own_width = outs[0].shape
    count = tile_count(cut, own_width)
    for k in range(3):
        outs[k][...] = take(total, k * count, cut, own_width)
    outs[3][...] = take(kept_b[...].astype(f32) + got_b[...].astype(f32), 0, cut, own_width)
    outs[4][...] = take(total, 3 * count, cut, outs[4].shape[1])
    outs[5][...] = jnp.sum(terms[...], axis=0)


def last_kernel(toks, ids, kept, got, kept_b, got_b, moved, final, *rest):
    pieces, blocks = rest[:toks], rest[toks]
    first = kept[...].astype(f32) + got[...].astype(f32)
    second = kept_b[...].astype(f32) + got_b[...].astype(f32)
    _, cut, own_width = moved.shape
    count = tile_count(cut, own_width)
    for k in range(3):
        moved[k] = take(first, k * count, cut, own_width).astype(bf16)
    final[...] = take(second, 0, cut, own_width)
    rows = blocks.shape[2]
    single = take(first, 3 * count, cut, rows * toks)
    for a in range(toks):
        blocks[a] = single[:, a * rows : (a + 1) * rows]
    for r in range(toks):
        pieces[r][...] = blocks[jnp.bitwise_xor(ids[0], r)].astype(bf16)


def finish_kernel(moved, *rest):
    parts, outs = rest[:-4], rest[-4:]
    for k in range(3):
        outs[k][...] = moved[k].astype(f32)
    total = parts[0][...].astype(f32)
    for part in parts[1:]:
        total = total + part[...].astype(f32)
    outs[3][...] = total


def exit_kernel(toks, noisy, gain, d_res, d_own, *rest):
    others, (grad_noisy, token) = rest[: toks - 1], rest[toks - 1 :]
    token[...] = jnp.zeros(token.shape, f32)
    total = d_own[...]
    for part in others:
        total = total + part[...].astype(f32)
    _, noisy_hat, noisy_inverse = layer_forward(noisy[...].astype(f32), gain[...])
    grad_noisy[...] = (
        d_res[...] + layer_backward(jnp.transpose(total), gain[...], noisy_hat, noisy_inverse)
    ).astype(bf16)


def set_heads(toks, ids, parts, grads):
    part_rows = parts[0].shape[0]
    for r in range(toks):
        start = pl.multiple_of(jnp.bitwise_xor(ids[0], r) * part_rows, part_rows)
        grads[pl.ds(start, part_rows), :] = parts[r][...].astype(f32)


def pair_weight_kernel(toks, ids, columns, *rest):
    parts, (weight_grad, grads) = rest[:toks], rest[toks:]
    set_heads(toks, ids, parts, grads)
    grad_b = grads[...].astype(bf16)
    cols, _, channels = columns.shape
    row_col = low_bits(lax.broadcasted_iota(jnp.int32, (grad_b.shape[0], channels), 0), cols)
    sums = jnp.zeros((grad_b.shape[0], channels), f32)
    for j in range(cols):
        sums = sums + jnp.where(row_col == j, mm(grad_b, columns[j]), 0.0)
    for h in range(weight_grad.shape[1]):
        line = jnp.sum(sums[h * cols : (h + 1) * cols, :], axis=0, keepdims=True)
        for n in range(weight_grad.shape[0]):
            weight_grad[n, h : h + 1, :] = line


def pair_kernel(toks, cols, ids, pair, gain, w_pair, *rest):
    parts, (grad_pair, spread_out, grads) = rest[:toks], rest[toks:]
    set_heads(toks, ids, parts, grads)
    rows = parts[0].shape[1]
    _, pair_hat, pair_inverse = layer_forward(pair[...].astype(f32), gain[...])
    spread, row_col = pair_weight_rows(w_pair[...], w_pair.shape[0], cols)
    turned = jnp.transpose(grads[...]).astype(bf16)
    for j in range(cols):
        spread_out[pl.ds(j, rows, stride=cols), :] = mm(
            turned, jnp.where(row_col == j, spread, 0.0).astype(bf16)
        )
    grad_pair[...] = layer_backward(
        spread_out[...], gain[...], pair_hat, pair_inverse
    ).astype(bf16)


def swap_copy(value, mask):
    size = lax.axis_size("copy")
    return lax.ppermute(value, "copy", [(i, i ^ mask) for i in range(size)])


def swap_tok(value, mask):
    size = lax.axis_size("tok")
    return lax.ppermute(value, "tok", [(i, i ^ mask) for i in range(size)])


def exchange(value):
    return lax.all_to_all(value, ("copy", "tok"), 0, 0)


def per_device(
    noisy,
    single,
    pair,
    restype,
    chain,
    keymask,
    restype_table,
    norm_gain,
    pair_gain,
    trans_gain,
    w_query,
    w_key,
    w_value,
    w_out,
    w_pair,
    chain_weight,
    w_hidden_gate,
    w_hidden_up,
    w_down,
    cotangent,
):
    copies = lax.axis_size("copy")
    toks = lax.axis_size("tok")
    _, rows, width = noisy.shape
    cols = pair.shape[1]
    channels = pair.shape[2]
    heads = w_pair.shape[1]
    head_width = width // heads
    own_heads = heads // toks
    own_width = own_heads * head_width
    tokens = rows * toks
    hidden = w_down.shape[0]
    cut = width // copies
    devices = copies * toks
    ids = jnp.stack([lax.axis_index("tok"), lax.axis_index("copy")]).astype(jnp.int32)
    where_am_i = (ids, SMEM)
    noisy2 = noisy.reshape(rows, width)
    pair2 = pair.reshape(rows * cols, channels)
    pair_gain2 = pair_gain.reshape(1, channels)
    norm_gain2 = norm_gain.reshape(1, width)

    weights3 = [w_query, w_key, w_value]
    if own_width % 128:
        weights3 = [
            lax.dynamic_slice_in_dim(w, ids[0] * own_width, own_width, axis=1) for w in weights3
        ]
    small = [noisy2, single, restype.reshape(1, rows), restype_table, norm_gain, pair2, pair_gain2]
    small += [w_pair.T, chain.reshape(1, tokens), keymask.reshape(1, tokens)]
    entered = call(
        functools.partial(enter_kernel, toks, cols),
        "enter",
        [where_am_i]
        + [(array, "fetch") for array in small]
        + [(chain_weight, SMEM)],
        [((rows, width), bf16), ((cols, rows, channels), bf16)]
        + [((tokens, 128), f32), ((1, tokens), f32), ((toks, own_heads * cols, rows), bf16)],
        [VMEM((rows * cols, channels), f32), VMEM((heads * cols, rows), f32)],
        flops=2 * heads * cols * rows * channels * cols,
        limit=60,
    )
    x_own, columns, facts, chain_row, bias_mine = entered
    near = 4
    far = copies // near
    x_parts = [x_own] + [swap_tok(x_own, r) for r in range(1, toks)]
    by_tok = call(
        functools.partial(split_kernel, far),
        "split_far",
        [bias_mine] + [swap_copy(bias_mine, m * near) for m in range(1, far)],
        [((far, own_heads * cols, rows), bf16)] * toks,
        deps=x_parts[1:],
    )
    (slices,) = call(
        stage_kernel,
        "stage",
        [where_am_i] + [(w, ANY) for w in weights3],
        [((3, width, own_width), bf16)],
        [pltpu.SemaphoreType.DMA((3,))],
        deps=[by_tok[0]],
    )
    (lines,) = call(
        join_kernel,
        "join_tok",
        [by_tok[0]] + [swap_tok(by_tok[r], r) for r in range(1, toks)],
        [((toks, far, own_heads * cols, rows), bf16)],
        deps=[slices],
    )
    x, query, key, value = call(
        functools.partial(project_kernel, toks),
        "project",
        [where_am_i, slices] + x_parts,
        [((tokens, width), bf16)] + [((own_width, tokens), bf16)] * 3,
        flops=6 * tokens * width * own_width,
    )
    (lines,) = call(
        join_kernel,
        "join_y",
        [lines, swap_copy(lines, 2)],
        [((2,) + lines.shape, bf16)],
        deps=[value],
    )
    biases = [lines, swap_copy(lines, 1)]
    done = call(
        functools.partial(attention_kernel, copies, toks, near, cols, head_width),
        "attention",
        [where_am_i, query, key, value] + biases + [facts, chain_row],
        [((own_heads, tokens, tokens), bf16), ((tokens, own_width), bf16)]
        + [((rows, own_width), bf16)] * toks,
        [VMEM((copies, toks, own_heads * cols, rows), bf16)],
        flops=4 * tokens * tokens * own_width,
        limit=32,
    )
    weights, att, pieces = done[0], done[1], done[2:]
    att_parts = [pieces[0]] + [swap_tok(pieces[r], r) for r in range(1, toks)]

    d_hidden, upstream, noisy3, trans_gain2 = call(
        down_kernel,
        "down",
        [cotangent.reshape(rows, width), w_down, noisy2, trans_gain.reshape(1, width)],
        [((rows, hidden), f32), ((rows, width), bf16), ((rows, width), bf16), ((1, width), f32)],
        flops=2 * rows * hidden * width,
    )
    chunk = hidden // 3
    results = call(
        functools.partial(hidden_kernel, toks, chunk),
        "hidden",
        [where_am_i, noisy3, upstream, d_hidden, trans_gain2]
        + att_parts
        + [w_out, w_hidden_gate, w_hidden_up],
        [((rows, width), f32), ((rows, width), bf16)] + [((own_width, rows), bf16)] * toks,
        flops=2 * rows * width * (2 * width + 4 * hidden),
    )
    d_res, d_res_b, d_att = results[0], results[1], results[2:]
    d_att_parts = [d_att[0]] + [swap_tok(d_att[r], r) for r in range(1, toks)]
    bias_tiles = own_heads * tile_count(cols, tokens)
    bias_shape = (copies // 2 * bias_tiles, 16, 128)
    d_query, d_key, d_value, bias_kept, bias_sent, d_res_b = call(
        functools.partial(backward_kernel, copies, toks, cols, head_width),
        "backward",
        [where_am_i, query, key, value, weights] + d_att_parts + [d_res_b],
        [((own_width, tokens), bf16)] * 3 + [(bias_shape, bf16)] * 2 + [((rows, width), bf16)],
        [VMEM((toks, own_width, rows), bf16), VMEM((tokens, tokens), bf16)],
        flops=8 * tokens * tokens * own_width,
        limit=32,
    )
    d_res_parts = [d_res_b] + [swap_tok(d_res_b, r) for r in range(1, toks)]
    bias_got = swap_copy(bias_sent, 2)

    wide_tiles = tile_count(cut, own_width)
    single_tiles = tile_count(cut, tokens)
    first_tiles, second_tiles = 3 * wide_tiles + single_tiles, wide_tiles
    found = call(
        functools.partial(first_kernel, copies, toks),
        "first",
        [where_am_i, slices, x, d_query, d_key, d_value],
        [((copies // 2 * first_tiles, 16, 128), bf16)] * 2
        + [((width, rows), f32)]
        + [((width, rows), bf16)] * (toks - 1),
        [
            VMEM((own_width, width), f32),
            VMEM((toks, width, rows), f32),
            VMEM((width, tokens), f32),
        ],
        flops=12 * tokens * width * own_width,
    )
    kept, sent, d_own = found[:3]
    got = swap_copy(sent, 1)
    d_others = [swap_tok(found[2 + r], r) for r in range(1, toks)]

    def step(name, pairs, segments, deps=()):
        filled, full, masks_of = {}, [], {}
        for source, base, parts, tiles, mask, left, target in segments:
            inner = 1 << sum(1 for other in left if other < mask)
            start = filled.get(target, 0)
            full.append((source, base, parts, tiles, mask, inner, target, start))
            filled[target] = start + parts // 2 * tiles
            masks_of[target] = mask
        outs = []
        for target in range(len(filled)):
            outs += [((filled[target], 16, 128), bf16)] * 2
        results = call(
            functools.partial(step_kernel, full),
            name,
            [where_am_i] + [array for one in pairs for array in one],
            outs,
            deps=deps,
        )
        return [
            (results[2 * n], swap_copy(results[2 * n + 1], masks_of[n]))
            for n in range(len(filled))
        ]

    masks = [1 << b for b in range(1, copies.bit_length() - 1)]
    masks_b = masks[1:] + masks[:1]
    kept_b, sent_b = call(
        functools.partial(second_kernel, copies, toks),
        "second",
        [where_am_i, att, bias_kept, bias_got] + d_res_parts,
        [((copies // 2 * second_tiles + copies // 4 * bias_tiles, 16, 128), bf16)] * 2,
        [VMEM((tokens, width), bf16), VMEM((width, own_width), f32)],
        flops=2 * tokens * width * own_width,
    )
    got_b = swap_copy(sent_b, 1)

    grad_noisy, exited = call(
        functools.partial(exit_kernel, toks),
        "exit",
        [noisy3, norm_gain2, d_res, d_own] + d_others,
        [((rows, width), bf16), ((8, 128), f32)],
    )
    pairs = [(kept, got), (kept_b, got_b)]
    parts = copies // 2
    for n, (mask, mask_b) in enumerate(zip(masks, masks_b)):
        segments = [
            (0, 0, parts, first_tiles, mask, masks[n:], 0),
            (1, 0, parts, second_tiles, mask_b, masks_b[n:], 1),
        ]
        bias_base = parts * second_tiles
        if n + 1 < len(masks):
            segments.append((1, bias_base, parts // 2, bias_tiles, mask_b, masks_b[n:-1], 1))
        else:
            bias_ready = pairs[1]
            if toks == 2:
                break
        pairs = step("step_%d" % n, pairs, segments, deps=[exited] if n == 1 else ())
        parts //= 2
    if toks == 2:
        wide, lines = 3 * wide_tiles, single_tiles // 2
        kept, sent, kept_b, sent_b = call(
            functools.partial(
                across_kernel, wide, lines, (2, second_tiles, masks_b[-1], 1, 0, 0)
            ),
            "across",
            [where_am_i] + [array for one in pairs for array in one],
            [((wide + 2 * lines, 16, 128), bf16)] * 2 + [((second_tiles, 16, 128), bf16)] * 2,
        )
        pairs = [(kept, swap_tok(sent, 1)), (kept_b, swap_copy(sent_b, masks_b[-1]))]
    bias_pieces = call(
        functools.partial(last_bias_kernel, toks, bias_base, bias_tiles, cols),
        "last_bias",
        [where_am_i, *bias_ready],
        [((own_heads * cols, rows), bf16)] * toks,
        [VMEM((toks, own_heads * cols, rows), bf16)],
        deps=[pairs[0][0]],
    )
    bias_pieces = [bias_pieces[0]] + [swap_tok(bias_pieces[r], r) for r in range(1, toks)]
    ready = [pairs[0][1], pairs[1][1]]
    if toks == 2:
        kept, sent = call(
            functools.partial(far_kernel, wide, lines, copies // 2),
            "far",
            [where_am_i, *pairs[0]],
            [((wide + lines, 16, 128), bf16)] * 2,
            [VMEM((2, wide, 16, 128), bf16)],
            deps=[pairs[1][1]] + bias_pieces[1:],
        )
        pairs[0] = (kept, swap_copy(sent, copies // 2))
        ready = [kept]

    group = copies // toks
    swaps = []
    for c in range(copies):
        for t in range(toks):
            swaps.append((c * toks + t, (t * group + c % group) * toks + c // group))

    (weight_grad,) = call(
        functools.partial(pair_weight_kernel, toks),
        "pair_weight",
        [where_am_i, columns] + bias_pieces,
        [((devices, heads, channels), f32)],
        [VMEM((heads * cols, rows), f32)],
        flops=2 * heads * cols * rows * channels * cols,
        deps=ready,
    )
    (grad_pair,) = call(
        functools.partial(pair_kernel, toks, cols),
        "pair",
        [where_am_i, pair2, pair_gain2, w_pair.T] + bias_pieces,
        [((rows * cols, channels), bf16)],
        [VMEM((rows * cols, channels), f32), VMEM((heads * cols, rows), f32)],
        flops=2 * heads * cols * rows * channels * cols,
    )
    weight_terms = exchange(weight_grad)
    if toks == 2:
        grad_query, grad_key, grad_value, grad_out, grad_single, weight_grad = call(
            close_kernel,
            "close",
            [*pairs[0], *pairs[1], weight_terms],
            [((cut, own_width), f32)] * 4 + [((cut, rows), f32), ((heads, channels), f32)],
        )
    else:
        last = call(
            functools.partial(last_kernel, toks),
            "last",
            [where_am_i, *pairs[0], *pairs[1]],
            [((3, cut, own_width), bf16), ((cut, own_width), f32)] + [((cut, rows), bf16)] * toks,
            [VMEM((toks, cut, rows), f32)],
        )
        weight_grad = jnp.sum(weight_terms, axis=0)
        grad_out, singles = last[1], last[2:]
        singles = [singles[0]] + [swap_tok(singles[r], r) for r in range(1, toks)]
        moved = lax.ppermute(last[0], ("copy", "tok"), swaps)
        grad_query, grad_key, grad_value, grad_single = call(
            finish_kernel,
            "finish",
            [moved] + singles,
            [((cut, own_width), f32)] * 3 + [((cut, rows), f32)],
        )
    return (
        grad_noisy[None],
        grad_single.T,
        grad_pair.reshape(rows, cols, channels),
        grad_query.T,
        grad_key.T,
        grad_value.T,
        grad_out.T,
        weight_grad.T,
    )


def solution(mesh):
    placed = (
        P("copy", "tok", None),
        P("tok", None),
        P("tok", "copy", None),
        P("tok"),
    ) + (P(),) * 15 + (P("copy", "tok", None),)
    return jax.shard_map(
        per_device,
        mesh=mesh,
        in_specs=placed,
        out_specs=(
            P("copy", "tok", None),
            P("tok", "copy"),
            P("tok", "copy", None),
            P("tok", "copy"),
            P("tok", "copy"),
            P("tok", "copy"),
            P("tok", "copy"),
            P(),
        ),
        check_vma=False,
    )
```

```python
import functools

import jax
import jax.numpy as jnp
from jax import lax
from jax.experimental import pallas as pl
from jax.experimental.pallas import tpu as pltpu
from jax.sharding import PartitionSpec as P

epsilon = 1e-05
f32 = jnp.float32
bf16 = jnp.bfloat16
VMEM, SMEM, ANY = pltpu.VMEM, pltpu.SMEM, pl.ANY
MIB = 1 << 20


def layer_forward(values, scales):
    average = jnp.mean(values, axis=-1, keepdims=True)
    centred = values - average
    inverse = lax.rsqrt(jnp.mean(centred * centred, axis=-1, keepdims=True) + epsilon)
    normed = centred * inverse
    return (normed * scales, normed, inverse)


def layer_backward(upstream, scales, normed, inverse):
    scaled = upstream * scales
    first_moment = jnp.mean(scaled, axis=-1, keepdims=True)
    second_moment = jnp.mean(scaled * normed, axis=-1, keepdims=True)
    return inverse * (scaled - first_moment - normed * second_moment)


NN = ((1,), (0,))
NT = ((1,), (1,))
TN = ((0,), (0,))


def mm(left, right, dims=NN):
    return lax.dot_general(left, right, (dims, ((), ())), preferred_element_type=f32)


def call(body, name, inputs, outs, scratch=(), flops=0, limit=16, deps=()):
    arrays, specs, moved, fetched = [], [], 0, []
    for item in inputs:
        array, space = item if isinstance(item, tuple) else (item, VMEM)
        if space == "fetch":
            fetched.append(len(arrays))
            space = pltpu.HBM
        arrays.append(array)
        specs.append(pl.BlockSpec(memory_space=space))
        moved += array.size * array.dtype.itemsize
    for shape, kind, *_ in outs:
        size = jnp.dtype(kind).itemsize
        for extent in shape:
            size *= extent
        moved += size
    read = len(arrays)
    for array in deps:
        arrays.append(array)
        specs.append(pl.BlockSpec(memory_space=ANY))
    extra = [VMEM(arrays[k].shape, arrays[k].dtype) for k in fetched]
    if fetched:
        extra.append(pltpu.SemaphoreType.DMA((len(fetched),)))

    def whole(*refs):
        refs = list(refs[:read]) + list(refs[read + len(deps) :])
        if fetched:
            held, sem = refs[-1 - len(fetched) : -1], refs[-1]
            refs = refs[: -1 - len(fetched)]
            transfers = []
            for n, k in enumerate(fetched):
                transfer = pltpu.make_async_copy(refs[k], held[n], sem.at[n])
                transfer.start()
                transfers.append(transfer)
                refs[k] = held[n]
            for transfer in transfers:
                transfer.wait()
        body(*refs)

    return pl.pallas_call(
        whole,
        name=name,
        out_shape=[jax.ShapeDtypeStruct(one[0], one[1]) for one in outs],
        in_specs=specs,
        out_specs=[pl.BlockSpec(memory_space=(*one, VMEM)[2]) for one in outs],
        scratch_shapes=list(scratch) + extra,
        compiler_params=pltpu.CompilerParams(vmem_limit_bytes=limit * MIB),
        cost_estimate=pl.CostEstimate(flops=flops, bytes_accessed=moved, transcendentals=0),
    )(*arrays)


def low_bits(index, size):
    return jnp.bitwise_and(index, size - 1)


def pair_weight_rows(w_pair, head_count, cols):
    rows = head_count * cols
    shift = cols.bit_length() - 1
    head = lax.shift_right_logical(
        lax.broadcasted_iota(jnp.int32, (rows, head_count), 0), jnp.int32(shift)
    )
    pick = (head == lax.broadcasted_iota(jnp.int32, (rows, head_count), 1)).astype(f32)
    spread = mm(pick.astype(bf16), w_pair)
    row_col = low_bits(lax.broadcasted_iota(jnp.int32, spread.shape, 0), cols)
    return spread, row_col


def own_slice(weight, t, own_width):
    if weight.shape[1] == own_width:
        return weight
    return weight.at[:, pl.ds(pl.multiple_of(t * own_width, own_width), own_width)]


def enter_kernel(toks, cols, ids, *rest):
    noisy, single, restype, table, gain, pair, pair_gain, w_pair, chain, keymask = rest[:10]
    chain_weight, x_out, columns, facts_out, chain_out, bias_out, rounded, bias = rest[10:]
    t = ids[0]
    rows = noisy.shape[0]
    pair_scaled, _, _ = layer_forward(pair[...].astype(f32), pair_gain[...])
    rounded[...] = pair_scaled.astype(bf16).astype(f32)
    head_count = w_pair.shape[0]
    spread, row_col = pair_weight_rows(w_pair[...], head_count, cols)
    total = jnp.zeros((head_count * cols, rows), f32)
    for j in range(cols):
        column = rounded[pl.ds(j, rows, stride=cols), :].astype(bf16)
        columns[j] = column
        total = total + mm(jnp.where(row_col == j, spread, 0.0).astype(bf16), column, NT)
    bias[...] = total
    part = bias_out.shape[1]
    for r in range(toks):
        start = pl.multiple_of(jnp.bitwise_xor(t, r) * part, part)
        bias_out[r] = bias[pl.ds(start, part), :].astype(bf16)
    normed_scaled, _, _ = layer_forward(noisy[...].astype(f32), gain[...])
    types = table.shape[0]
    onehot = (lax.broadcasted_iota(jnp.int32, (types, rows), 0) == restype[...]).astype(f32)
    condition = single[...].astype(f32) + mm(onehot.astype(bf16), table[...], TN)
    x_out[...] = (normed_scaled + condition).astype(bf16)
    chain_row = chain[...]
    tokens = chain_row.shape[1]
    own_heads = head_count // toks
    keep_row = keymask[...].astype(f32)
    line = lax.broadcasted_iota(jnp.int32, (128, tokens), 0)
    facts = jnp.where(line == 0, chain_row.astype(f32), 0.0) + jnp.where(line == 1, keep_row, 0.0)
    for h in range(own_heads):
        weight_row = jnp.zeros((1, tokens), f32)
        for m in range(chain_weight.shape[0]):
            weight_row = jnp.where(chain_row == m, chain_weight[m, t * own_heads + h], weight_row)
        facts = jnp.where(line == 2 + h, weight_row, facts)
    facts_out[...] = jnp.transpose(facts)
    chain_out[...] = chain_row.astype(f32)


def stage_kernel(ids, *rest):
    weights, (slices, sem) = rest[:3], rest[3:]
    transfers = []
    for k in range(3):
        transfer = pltpu.make_async_copy(
            own_slice(weights[k], ids[0], slices.shape[2]), slices.at[k], sem.at[k]
        )
        transfer.start()
        transfers.append(transfer)
    for transfer in transfers:
        transfer.wait()


def project_kernel(toks, ids, slices, *rest):
    parts = rest[:toks]
    x_out, outs = rest[toks], rest[toks + 1 :]
    t = ids[0]
    rows = parts[0].shape[0]
    for r in range(toks):
        start = pl.multiple_of(jnp.bitwise_xor(t, r) * rows, rows)
        x_out[pl.ds(start, rows), :] = parts[r][...]
    x = x_out[...]
    for k in range(3):
        outs[k][...] = jnp.transpose(mm(x, slices[k])).astype(bf16)


def split_kernel(count, *refs):
    for n in range(count):
        for r, out in enumerate(refs[count:]):
            out[n] = refs[n][r]


def join_kernel(*refs):
    for n, ref in enumerate(refs[:-1]):
        refs[-1][n] = ref[...]


def attention_kernel(copies, toks, near, cols, head_width, ids, query, key, value, *rest):
    biases, (facts, chain, weights_out, att_out) = rest[:2], rest[2:6]
    pieces, bias = rest[6 : 6 + toks], rest[6 + toks]
    t, low, high = ids[0], low_bits(ids[1], near), ids[1] // near
    for m in range(near):
        for rz in range(copies // near):
            c = jnp.bitwise_xor(high, rz) * near + jnp.bitwise_xor(low, m)
            for r in range(toks):
                bias[c, jnp.bitwise_xor(t, r)] = biases[m % 2][m // 2, r, rz]
    own_heads = weights_out.shape[0]
    tokens = query.shape[1]
    rows = tokens // toks
    same = facts[:, 0:1] == chain[...]
    keep = facts[:, 1:2] > 0.0
    scale = head_width ** (-0.5)
    attended = []
    for h in range(own_heads):
        span = slice(h * head_width, (h + 1) * head_width)
        logits = mm(key[span, :], query[span, :], TN) * scale
        line = slice(h * cols, (h + 1) * cols)
        extra = jnp.concatenate(
            [
                jnp.concatenate(
                    [bias[c, a, line, :] for c in range(copies)], axis=0
                )
                for a in range(toks)
            ],
            axis=1,
        ).astype(f32)
        logits = logits + (extra + jnp.where(same, facts[:, 2 + h : 3 + h], 0.0))
        logits = jnp.where(keep, logits, -1e30)
        exponent = jnp.exp(logits - jnp.max(logits, axis=0, keepdims=True))
        weights = exponent / jnp.sum(exponent, axis=0, keepdims=True)
        weights_b = weights.astype(bf16)
        weights_out[h] = weights_b
        attended.append(mm(value[span, :], weights_b))
    att_out[...] = jnp.transpose(jnp.concatenate(attended, axis=0)).astype(bf16)
    for r in range(toks):
        start = pl.multiple_of(jnp.bitwise_xor(t, r) * rows, rows)
        pieces[r][...] = att_out[pl.ds(start, rows), :]


def down_kernel(upstream, w_down, noisy, gain, d_hidden, upstream_out, noisy_out, gain_out):
    d_hidden[...] = mm(upstream[...], w_down[...], NT)
    upstream_out[...] = upstream[...]
    noisy_out[...] = noisy[...]
    gain_out[...] = gain[...]


def hidden_kernel(toks, chunk, ids, noisy, upstream, d_hidden, gain, *rest):
    parts = rest[:toks]
    held_out, held_gate, held_up = rest[toks : toks + 3]
    d_res_out, d_res_b_out = rest[toks + 3 : toks + 5]
    d_att_outs = rest[toks + 5 :]
    t = ids[0]
    hidden = held_gate.shape[1]
    residual = noisy[...].astype(f32)
    own_width = parts[0].shape[1]
    for r in range(toks):
        start = pl.multiple_of(jnp.bitwise_xor(t, r) * own_width, own_width)
        residual = residual + mm(parts[r][...], held_out[pl.ds(start, own_width), :])
    trans_scaled, trans_hat, trans_inverse = layer_forward(residual, gain[...])
    trans_in = trans_scaled.astype(bf16)
    d_trans = jnp.zeros(residual.shape, f32)
    for k in range(hidden // chunk):
        span = slice(k * chunk, (k + 1) * chunk)
        gate = mm(trans_in, held_gate[:, span])
        up = mm(trans_in, held_up[:, span])
        incoming = d_hidden[:, span]
        sigmoid = jax.nn.sigmoid(gate)
        d_up = (incoming * gate * sigmoid).astype(bf16)
        d_gate = (incoming * up * sigmoid * (1.0 + gate * (1.0 - sigmoid))).astype(bf16)
        d_trans = d_trans + mm(d_gate, held_gate[:, span], NT) + mm(d_up, held_up[:, span], NT)
    d_res = upstream[...].astype(f32) + layer_backward(
        d_trans, gain[...], trans_hat, trans_inverse
    )
    d_res_out[...] = d_res
    d_res_b = d_res.astype(bf16)
    d_res_b_out[...] = d_res_b
    for r in range(toks):
        start = pl.multiple_of(jnp.bitwise_xor(t, r) * own_width, own_width)
        d_att_outs[r][...] = mm(held_out[pl.ds(start, own_width), :], d_res_b, NT).astype(bf16)


def backward_kernel(copies, toks, cols, head_width, ids, query, key, value, weights, *rest):
    parts, d_res_b = rest[:toks], rest[toks]
    d_query, d_key, d_value, bias_kept, bias_sent, d_res_out = rest[toks + 1 : toks + 7]
    blocks, d_logits = rest[toks + 7 :]
    d_res_out[...] = d_res_b[...]
    t = ids[0]
    bit = low_bits(ids[1] // 2, 2)
    heads = weights.shape[0]
    for r in range(toks):
        blocks[jnp.bitwise_xor(t, r)] = parts[r][...]
    d_att = jnp.concatenate([blocks[a] for a in range(toks)], axis=1)
    count = tile_count(cols, query.shape[1])
    scale = head_width ** (-0.5)
    for h in range(weights.shape[0]):
        span = slice(h * head_width, (h + 1) * head_width)
        d_att_h = d_att[span, :]
        weights_b = weights[h]
        d_weights = mm(value[span, :], d_att_h, TN)
        weights_f = weights_b.astype(f32)
        delta = jnp.sum(weights_f * d_weights, axis=0, keepdims=True)
        d_logits_b = (weights_f * (d_weights - delta)).astype(bf16)
        d_logits[...] = d_logits_b
        for k in range(copies // 2):
            for side, out in ((bit, bias_kept), (1 - bit, bias_sent)):
                start = pl.multiple_of((k // 2 * 4 + side * 2 + k % 2) * cols, cols)
                put(out, (k * heads + h) * count, d_logits[pl.ds(start, cols), :])
        d_query[span, :] = (mm(key[span, :], d_logits_b) * scale).astype(bf16)
        d_key[span, :] = (mm(query[span, :], d_logits_b, NT) * scale).astype(bf16)
        d_value[span, :] = mm(d_att_h, weights_b, NT).astype(bf16)


def tile_count(rows, lanes):
    return -(-rows // 16) * -(-lanes // 128)


def put(out, base, value):
    rows, lanes = value.shape
    for i in range(0, rows, 16):
        for j in range(0, lanes, 128):
            part = value[i : i + 16, j : j + 128]
            if part.shape != (16, 128):
                out[base] = jnp.zeros((16, 128), out.dtype)
            out[base, : part.shape[0], : part.shape[1]] = part
            base += 1


def take(tiles, base, rows, lanes):
    across = -(-lanes // 128)
    lines = []
    for i in range(-(-rows // 16)):
        line = [tiles[base + i * across + j] for j in range(across)]
        lines.append(jnp.concatenate(line, axis=1) if across > 1 else line[0])
    whole = jnp.concatenate(lines, axis=0) if len(lines) > 1 else lines[0]
    return whole[:rows, :lanes]


def cut_wide(copies, toks, core, base, stride, grad, kept, sent):
    group = copies // toks
    cut, depth = grad.shape[1] // copies, grad.shape[1] // toks
    for side, out in ((core, kept), (1 - core, sent)):
        for q in range(copies // 2):
            h = 2 * q // group
            first = pl.multiple_of((2 * q - h * group + side) * cut, 8)
            part = grad[pl.ds(first, cut), h * depth : (h + 1) * depth]
            put(out, q * stride + base, part.astype(bf16))


def first_kernel(copies, toks, ids, slices, x, d_query, d_key, d_value, *rest):
    kept, sent, d_own, single_all = rest[:4]
    d_others, (wide, d_inputs) = rest[4 : 3 + toks], rest[3 + toks :]
    t, core = ids[0], low_bits(ids[1], 2)
    rows = d_own.shape[1]
    cut = x.shape[1] // copies
    count = tile_count(cut, d_query.shape[0])
    stride = 3 * count
    for k, part in enumerate((d_query, d_key, d_value)):
        wide[...] = mm(part[...], x[...])
        cut_wide(copies, toks, core, k * count, stride, wide, kept, sent)
    total = mm(slices[0], d_query[...]) + mm(slices[1], d_key[...])
    total = total + mm(slices[2], d_value[...])
    single_all[...] = total
    for a in range(toks):
        d_inputs[a] = total[:, a * rows : (a + 1) * rows]
    d_own[...] = d_inputs[t]
    for r in range(1, toks):
        d_others[r - 1][...] = d_inputs[jnp.bitwise_xor(t, r)].astype(bf16)


def second_kernel(copies, toks, ids, att, single_all, bias_kept, bias_got, *rest):
    d_res_parts, (kept, sent, d_res, narrow) = rest[:toks], rest[toks:]
    t, core = ids[0], low_bits(ids[1], 2)
    rows = d_res_parts[0].shape[0]
    cut = narrow.shape[0] // copies
    count = tile_count(cut, narrow.shape[1])
    for r in range(toks):
        start = pl.multiple_of(jnp.bitwise_xor(t, r) * rows, rows)
        d_res[pl.ds(start, rows), :] = d_res_parts[r][...]
    narrow[...] = mm(d_res[...], att[...], TN)
    stride = count + tile_count(cut, rows * toks)
    base = copies // 2 * stride
    bias_count = bias_kept.shape[0] // (copies // 2)
    for side, out in ((core, kept), (1 - core, sent)):
        for q in range(copies // 2):
            first = pl.multiple_of((2 * q + side) * cut, 8)
            put(out, q * stride, narrow[pl.ds(first, cut), :].astype(bf16))
            put(out, q * stride + count, single_all[pl.ds(first, cut), :].astype(bf16))
        for z in range(copies // 4):
            span = pl.ds((2 * z + side) * bias_count, bias_count)
            out[base + z * bias_count : base + (z + 1) * bias_count] = (
                bias_kept[span].astype(f32) + bias_got[span].astype(f32)
            ).astype(bf16)


def step_kernel(segments, ids, *refs):
    count = 1 + max(segment[0] for segment in segments)
    ins, outs = refs[: 2 * count], refs[2 * count :]
    for source, base, parts, tiles, mask, inner, target, start in segments:
        kept, got = ins[2 * source : 2 * source + 2]
        bit = low_bits(ids[1] // mask, 2)
        for q in range(parts // 2):
            for side, out in ((bit, outs[2 * target]), (1 - bit, outs[2 * target + 1])):
                k = q // inner * 2 * inner + side * inner + q % inner
                span = pl.ds(base + k * tiles, tiles)
                out[start + q * tiles : start + (q + 1) * tiles] = (
                    kept[span].astype(f32) + got[span].astype(f32)
                ).astype(bf16)


def last_bias_kernel(toks, base, count, cols, ids, kept, got, *rest):
    pieces, blocks = rest[:toks], rest[toks]
    span = slice(base, base + count)
    tiles = kept[span].astype(f32) + got[span].astype(f32)
    part_rows, rows = pieces[0].shape
    heads = part_rows // cols
    total = jnp.concatenate(
        [take(tiles, h * (count // heads), cols, rows * toks) for h in range(heads)], axis=0
    )
    for a in range(toks):
        blocks[a] = total[:, a * rows : (a + 1) * rows].astype(bf16)
    for r in range(toks):
        pieces[r][...] = blocks[jnp.bitwise_xor(ids[0], r)]


def across_kernel(segment, ids, kept, got, kept_b, got_b, *outs):
    t = ids[0]
    stride = kept.shape[0] // 2
    step_kernel([(0, 0) + segment], ids, kept_b, got_b, *outs[2:])
    for side, out in ((t, outs[0]), (1 - t, outs[1])):
        span = pl.ds(side * stride, stride)
        out[...] = (kept[span].astype(f32) + got[span].astype(f32)).astype(bf16)


def far_kernel(half, ids, kept, got, kept_b, got_b, kept_out, sent_out, single, other, *scratch):
    groups, blocks = scratch
    t, a = ids[0], ids[1] // half
    groups[t] = kept[...]
    groups[1 - t] = got[...]
    kept_out[...] = groups[a]
    sent_out[...] = groups[1 - a]
    lines = single.shape[0]
    base = kept_b.shape[0] - 2 * lines
    for i in range(lines):
        for j in range(2):
            k = base + 2 * i + j
            blocks[j, i] = (kept_b[k].astype(f32) + got_b[k].astype(f32)).astype(bf16)
    single[...] = blocks[t]
    other[...] = blocks[1 - t]


def close_kernel(kept, got, kept_b, got_b, single, got_single, terms, *outs):
    total = kept[...].astype(f32) + got[...].astype(f32)
    cut, own_width = outs[0].shape
    count = tile_count(cut, own_width)
    for k in range(3):
        outs[k][...] = take(total, k * count, cut, own_width)
    total = kept_b[:count].astype(f32) + got_b[:count].astype(f32)
    outs[3][...] = take(total, 0, cut, own_width)
    total = single[...].astype(f32) + got_single[...].astype(f32)
    outs[4][...] = take(total, 0, cut, outs[4].shape[1])
    outs[5][...] = jnp.sum(terms[...], axis=0)


def last_kernel(toks, ids, kept, got, kept_b, got_b, moved, final, *rest):
    pieces, blocks = rest[:toks], rest[toks]
    first = kept[...].astype(f32) + got[...].astype(f32)
    second = kept_b[...].astype(f32) + got_b[...].astype(f32)
    _, cut, own_width = moved.shape
    count = tile_count(cut, own_width)
    for k in range(3):
        moved[k] = take(first, k * count, cut, own_width).astype(bf16)
    final[...] = take(second, 0, cut, own_width)
    rows = blocks.shape[2]
    single = take(second, count, cut, rows * toks)
    for a in range(toks):
        blocks[a] = single[:, a * rows : (a + 1) * rows]
    for r in range(toks):
        pieces[r][...] = blocks[jnp.bitwise_xor(ids[0], r)].astype(bf16)


def finish_kernel(moved, *rest):
    parts, outs = rest[:-4], rest[-4:]
    for k in range(3):
        outs[k][...] = moved[k].astype(f32)
    total = parts[0][...].astype(f32)
    for part in parts[1:]:
        total = total + part[...].astype(f32)
    outs[3][...] = total


def exit_kernel(toks, noisy, gain, d_res, d_own, *rest):
    others, (grad_noisy, token) = rest[: toks - 1], rest[toks - 1 :]
    token[...] = jnp.zeros(token.shape, f32)
    total = d_own[...]
    for part in others:
        total = total + part[...].astype(f32)
    _, noisy_hat, noisy_inverse = layer_forward(noisy[...].astype(f32), gain[...])
    grad_noisy[...] = (
        d_res[...] + layer_backward(jnp.transpose(total), gain[...], noisy_hat, noisy_inverse)
    ).astype(bf16)


def set_heads(toks, ids, parts, grads):
    part_rows = parts[0].shape[0]
    for r in range(toks):
        start = pl.multiple_of(jnp.bitwise_xor(ids[0], r) * part_rows, part_rows)
        grads[pl.ds(start, part_rows), :] = parts[r][...].astype(f32)


def pair_weight_kernel(toks, ids, columns, *rest):
    parts, (weight_grad, grads) = rest[:toks], rest[toks:]
    set_heads(toks, ids, parts, grads)
    grad_b = grads[...].astype(bf16)
    cols, _, channels = columns.shape
    row_col = low_bits(lax.broadcasted_iota(jnp.int32, (grad_b.shape[0], channels), 0), cols)
    sums = jnp.zeros((grad_b.shape[0], channels), f32)
    for j in range(cols):
        sums = sums + jnp.where(row_col == j, mm(grad_b, columns[j]), 0.0)
    heads = weight_grad.shape[1]
    lines = [
        jnp.sum(sums[h * cols : (h + 1) * cols, :], axis=0, keepdims=True) for h in range(heads)
    ]
    whole = jnp.concatenate(lines, axis=0)
    for n in range(weight_grad.shape[0]):
        weight_grad[n] = whole


def pair_kernel(toks, cols, ids, pair, gain, w_pair, *rest):
    parts, (grad_pair, spread_out, grads) = rest[:toks], rest[toks:]
    set_heads(toks, ids, parts, grads)
    rows = parts[0].shape[1]
    _, pair_hat, pair_inverse = layer_forward(pair[...].astype(f32), gain[...])
    spread, row_col = pair_weight_rows(w_pair[...], w_pair.shape[0], cols)
    turned = jnp.transpose(grads[...]).astype(bf16)
    for j in range(cols):
        spread_out[pl.ds(j, rows, stride=cols), :] = mm(
            turned, jnp.where(row_col == j, spread, 0.0).astype(bf16)
        )
    grad_pair[...] = layer_backward(
        spread_out[...], gain[...], pair_hat, pair_inverse
    ).astype(bf16)


def swap_copy(value, mask):
    size = lax.axis_size("copy")
    return lax.ppermute(value, "copy", [(i, i ^ mask) for i in range(size)])


def swap_tok(value, mask):
    size = lax.axis_size("tok")
    return lax.ppermute(value, "tok", [(i, i ^ mask) for i in range(size)])


def exchange(value):
    return lax.all_to_all(value, ("copy", "tok"), 0, 0)


def per_device(
    noisy,
    single,
    pair,
    restype,
    chain,
    keymask,
    restype_table,
    norm_gain,
    pair_gain,
    trans_gain,
    w_query,
    w_key,
    w_value,
    w_out,
    w_pair,
    chain_weight,
    w_hidden_gate,
    w_hidden_up,
    w_down,
    cotangent,
):
    copies = lax.axis_size("copy")
    toks = lax.axis_size("tok")
    _, rows, width = noisy.shape
    cols = pair.shape[1]
    channels = pair.shape[2]
    heads = w_pair.shape[1]
    head_width = width // heads
    own_heads = heads // toks
    own_width = own_heads * head_width
    tokens = rows * toks
    hidden = w_down.shape[0]
    cut = width // copies
    devices = copies * toks
    ids = jnp.stack([lax.axis_index("tok"), lax.axis_index("copy")]).astype(jnp.int32)
    where_am_i = (ids, SMEM)
    noisy2 = noisy.reshape(rows, width)
    pair2 = pair.reshape(rows * cols, channels)
    pair_gain2 = pair_gain.reshape(1, channels)
    norm_gain2 = norm_gain.reshape(1, width)

    weights3 = [w_query, w_key, w_value]
    if own_width % 128:
        weights3 = [
            lax.dynamic_slice_in_dim(w, ids[0] * own_width, own_width, axis=1) for w in weights3
        ]
    small = [noisy2, single, restype.reshape(1, rows), restype_table, norm_gain, pair2, pair_gain2]
    small += [w_pair.T, chain.reshape(1, tokens), keymask.reshape(1, tokens)]
    entered = call(
        functools.partial(enter_kernel, toks, cols),
        "enter",
        [where_am_i]
        + [(array, "fetch") for array in small]
        + [(chain_weight, SMEM)],
        [((rows, width), bf16), ((cols, rows, channels), bf16)]
        + [((tokens, 128), f32), ((1, tokens), f32), ((toks, own_heads * cols, rows), bf16)],
        [VMEM((rows * cols, channels), f32), VMEM((heads * cols, rows), f32)],
        flops=2 * heads * cols * rows * channels * cols,
        limit=60,
    )
    x_own, columns, facts, chain_row, bias_mine = entered
    near = 4
    far = copies // near
    x_parts = [x_own] + [swap_tok(x_own, r) for r in range(1, toks)]
    by_tok = call(
        functools.partial(split_kernel, far),
        "split_far",
        [bias_mine] + [swap_copy(bias_mine, m * near) for m in range(1, far)],
        [((far, own_heads * cols, rows), bf16)] * toks,
        deps=x_parts[1:],
    )
    (slices,) = call(
        stage_kernel,
        "stage",
        [where_am_i] + [(w, ANY) for w in weights3],
        [((3, width, own_width), bf16)],
        [pltpu.SemaphoreType.DMA((3,))],
        deps=[by_tok[0]],
    )
    (lines,) = call(
        join_kernel,
        "join_tok",
        [by_tok[0]] + [swap_tok(by_tok[r], r) for r in range(1, toks)],
        [((toks, far, own_heads * cols, rows), bf16)],
        deps=[slices],
    )
    x, query, key, value = call(
        functools.partial(project_kernel, toks),
        "project",
        [where_am_i, slices] + x_parts,
        [((tokens, width), bf16)] + [((own_width, tokens), bf16)] * 3,
        flops=6 * tokens * width * own_width,
    )
    (lines,) = call(
        join_kernel,
        "join_y",
        [lines, swap_copy(lines, 2)],
        [((2,) + lines.shape, bf16)],
        deps=[value],
    )
    biases = [lines, swap_copy(lines, 1)]
    done = call(
        functools.partial(attention_kernel, copies, toks, near, cols, head_width),
        "attention",
        [where_am_i, query, key, value] + biases + [facts, chain_row],
        [((own_heads, tokens, tokens), bf16), ((tokens, own_width), bf16)]
        + [((rows, own_width), bf16)] * toks,
        [VMEM((copies, toks, own_heads * cols, rows), bf16)],
        flops=4 * tokens * tokens * own_width,
        limit=32,
    )
    weights, att, pieces = done[0], done[1], done[2:]
    att_parts = [pieces[0]] + [swap_tok(pieces[r], r) for r in range(1, toks)]

    d_hidden, upstream, noisy3, trans_gain2 = call(
        down_kernel,
        "down",
        [cotangent.reshape(rows, width), w_down, noisy2, trans_gain.reshape(1, width)],
        [((rows, hidden), f32), ((rows, width), bf16), ((rows, width), bf16), ((1, width), f32)],
        flops=2 * rows * hidden * width,
    )
    chunk = hidden // 3
    results = call(
        functools.partial(hidden_kernel, toks, chunk),
        "hidden",
        [where_am_i, noisy3, upstream, d_hidden, trans_gain2]
        + att_parts
        + [w_out, w_hidden_gate, w_hidden_up],
        [((rows, width), f32), ((rows, width), bf16)] + [((own_width, rows), bf16)] * toks,
        flops=2 * rows * width * (2 * width + 4 * hidden),
    )
    d_res, d_res_b, d_att = results[0], results[1], results[2:]
    d_att_parts = [d_att[0]] + [swap_tok(d_att[r], r) for r in range(1, toks)]
    bias_tiles = own_heads * tile_count(cols, tokens)
    bias_shape = (copies // 2 * bias_tiles, 16, 128)
    d_query, d_key, d_value, bias_kept, bias_sent, d_res_b = call(
        functools.partial(backward_kernel, copies, toks, cols, head_width),
        "backward",
        [where_am_i, query, key, value, weights] + d_att_parts + [d_res_b],
        [((own_width, tokens), bf16)] * 3 + [(bias_shape, bf16)] * 2 + [((rows, width), bf16)],
        [VMEM((toks, own_width, rows), bf16), VMEM((tokens, tokens), bf16)],
        flops=8 * tokens * tokens * own_width,
        limit=32,
    )
    d_res_parts = [d_res_b] + [swap_tok(d_res_b, r) for r in range(1, toks)]
    bias_got = swap_copy(bias_sent, 2)

    wide_tiles = tile_count(cut, own_width)
    single_tiles = tile_count(cut, tokens)
    first_tiles, second_tiles = 3 * wide_tiles, wide_tiles + single_tiles
    found = call(
        functools.partial(first_kernel, copies, toks),
        "first",
        [where_am_i, slices, x, d_query, d_key, d_value],
        [((copies // 2 * first_tiles, 16, 128), bf16)] * 2
        + [((width, rows), f32), ((width, tokens), f32)]
        + [((width, rows), bf16)] * (toks - 1),
        [VMEM((own_width, width), f32), VMEM((toks, width, rows), f32)],
        flops=12 * tokens * width * own_width,
    )
    kept, sent, d_own, single_all = found[:4]
    got = swap_copy(sent, 1)
    d_others = [swap_tok(found[3 + r], r) for r in range(1, toks)]

    def step(name, pairs, segments, deps=()):
        filled, full, masks_of = {}, [], {}
        for source, base, parts, tiles, mask, left, target in segments:
            inner = 1 << sum(1 for other in left if other < mask)
            start = filled.get(target, 0)
            full.append((source, base, parts, tiles, mask, inner, target, start))
            filled[target] = start + parts // 2 * tiles
            masks_of[target] = mask
        outs = []
        for target in range(len(filled)):
            outs += [((filled[target], 16, 128), bf16)] * 2
        results = call(
            functools.partial(step_kernel, full),
            name,
            [where_am_i] + [array for one in pairs for array in one],
            outs,
            deps=deps,
        )
        return [
            (results[2 * n], swap_copy(results[2 * n + 1], masks_of[n]))
            for n in range(len(filled))
        ]

    masks = [1 << b for b in range(1, copies.bit_length() - 1)]
    masks_b = masks[1:] + masks[:1]
    kept_b, sent_b = call(
        functools.partial(second_kernel, copies, toks),
        "second",
        [where_am_i, att, single_all, bias_kept, bias_got] + d_res_parts,
        [((copies // 2 * second_tiles + copies // 4 * bias_tiles, 16, 128), bf16)] * 2,
        [VMEM((tokens, width), bf16), VMEM((width, own_width), f32)],
        flops=20 * tokens * width * own_width,
    )
    got_b = swap_copy(sent_b, 1)

    grad_noisy, exited = call(
        functools.partial(exit_kernel, toks),
        "exit",
        [noisy3, norm_gain2, d_res, d_own] + d_others,
        [((rows, width), bf16), ((8, 128), f32)],
    )
    pairs = [(kept, got), (kept_b, got_b)]
    parts = copies // 2
    for n, (mask, mask_b) in enumerate(zip(masks, masks_b)):
        segments = [
            (0, 0, parts, first_tiles, mask, masks[n:], 0),
            (1, 0, parts, second_tiles, mask_b, masks_b[n:], 1),
        ]
        bias_base = parts * second_tiles
        if n + 1 < len(masks):
            segments.append((1, bias_base, parts // 2, bias_tiles, mask_b, masks_b[n:-1], 1))
        else:
            bias_ready = pairs[1]
            if toks == 2:
                break
        pairs = step("step_%d" % n, pairs, segments, deps=[exited] if n == 1 else ())
        parts //= 2
    if toks == 2:
        kept, sent, kept_b, sent_b = call(
            functools.partial(across_kernel, (2, second_tiles, masks_b[-1], 1, 0, 0)),
            "across",
            [where_am_i] + [array for one in pairs for array in one],
            [((first_tiles, 16, 128), bf16)] * 2 + [((second_tiles, 16, 128), bf16)] * 2,
        )
        pairs = [(kept, swap_tok(sent, 1)), (kept_b, swap_copy(sent_b, masks_b[-1]))]
    bias_pieces = call(
        functools.partial(last_bias_kernel, toks, bias_base, bias_tiles, cols),
        "last_bias",
        [where_am_i, *bias_ready],
        [((own_heads * cols, rows), bf16)] * toks,
        [VMEM((toks, own_heads * cols, rows), bf16)],
        deps=[pairs[0][0]],
    )
    bias_pieces = [bias_pieces[0]] + [swap_tok(bias_pieces[r], r) for r in range(1, toks)]
    ready = [pairs[0][1], pairs[1][1]]
    if toks == 2:
        lines = single_tiles // 2
        kept, sent, single_kept, single_sent = call(
            functools.partial(far_kernel, copies // 2),
            "far",
            [where_am_i, *pairs[0], *pairs[1]],
            [((first_tiles, 16, 128), bf16)] * 2 + [((lines, 16, 128), bf16)] * 2,
            [VMEM((2, first_tiles, 16, 128), bf16), VMEM((2, lines, 16, 128), bf16)],
            deps=bias_pieces[1:],
        )
        pairs[0] = (kept, swap_copy(sent, copies // 2))
        single_pair = (single_kept, swap_tok(single_sent, 1))
        ready = []

    group = copies // toks
    swaps = []
    for c in range(copies):
        for t in range(toks):
            swaps.append((c * toks + t, (t * group + c % group) * toks + c // group))

    (weight_grad,) = call(
        functools.partial(pair_weight_kernel, toks),
        "pair_weight",
        [where_am_i, columns] + bias_pieces,
        [((devices, heads, channels), f32)],
        [VMEM((heads * cols, rows), f32)],
        flops=2 * heads * cols * rows * channels * cols,
        deps=ready,
    )
    (grad_pair,) = call(
        functools.partial(pair_kernel, toks, cols),
        "pair",
        [where_am_i, pair2, pair_gain2, w_pair.T] + bias_pieces,
        [((rows * cols, channels), bf16)],
        [VMEM((rows * cols, channels), f32), VMEM((heads * cols, rows), f32)],
        flops=2 * heads * cols * rows * channels * cols,
    )
    weight_terms = exchange(weight_grad)
    if toks == 2:
        grad_query, grad_key, grad_value, grad_out, grad_single, weight_grad = call(
            close_kernel,
            "close",
            [*pairs[0], *pairs[1], *single_pair, weight_terms],
            [((cut, own_width), f32)] * 4 + [((cut, rows), f32), ((heads, channels), f32)],
        )
    else:
        last = call(
            functools.partial(last_kernel, toks),
            "last",
            [where_am_i, *pairs[0], *pairs[1]],
            [((3, cut, own_width), bf16), ((cut, own_width), f32)] + [((cut, rows), bf16)] * toks,
            [VMEM((toks, cut, rows), f32)],
        )
        weight_grad = jnp.sum(weight_terms, axis=0)
        grad_out, singles = last[1], last[2:]
        singles = [singles[0]] + [swap_tok(singles[r], r) for r in range(1, toks)]
        moved = lax.ppermute(last[0], ("copy", "tok"), swaps)
        grad_query, grad_key, grad_value, grad_single = call(
            finish_kernel,
            "finish",
            [moved] + singles,
            [((cut, own_width), f32)] * 3 + [((cut, rows), f32)],
        )
    return (
        grad_noisy[None],
        grad_single.T,
        grad_pair.reshape(rows, cols, channels),
        grad_query.T,
        grad_key.T,
        grad_value.T,
        grad_out.T,
        weight_grad.T,
    )


def solution(mesh):
    placed = (
        P("copy", "tok", None),
        P("tok", None),
        P("tok", "copy", None),
        P("tok"),
    ) + (P(),) * 15 + (P("copy", "tok", None),)
    return jax.shard_map(
        per_device,
        mesh=mesh,
        in_specs=placed,
        out_specs=(
            P("copy", "tok", None),
            P("tok", "copy"),
            P("tok", "copy", None),
            P("tok", "copy"),
            P("tok", "copy"),
            P("tok", "copy"),
            P("tok", "copy"),
            P(),
        ),
        check_vma=False,
    )
```

```python
import functools

import jax
import jax.numpy as jnp
from jax import lax
from jax.experimental import pallas as pl
from jax.experimental.pallas import tpu as pltpu
from jax.sharding import PartitionSpec as P

epsilon = 1e-05
f32 = jnp.float32
bf16 = jnp.bfloat16
VMEM, SMEM, ANY = pltpu.VMEM, pltpu.SMEM, pl.ANY
MIB = 1 << 20


def layer_forward(values, scales):
    average = jnp.mean(values, axis=-1, keepdims=True)
    centred = values - average
    inverse = lax.rsqrt(jnp.mean(centred * centred, axis=-1, keepdims=True) + epsilon)
    normed = centred * inverse
    return (normed * scales, normed, inverse)


def layer_backward(upstream, scales, normed, inverse):
    scaled = upstream * scales
    first_moment = jnp.mean(scaled, axis=-1, keepdims=True)
    second_moment = jnp.mean(scaled * normed, axis=-1, keepdims=True)
    return inverse * (scaled - first_moment - normed * second_moment)


NN = ((1,), (0,))
NT = ((1,), (1,))
TN = ((0,), (0,))


def mm(left, right, dims=NN):
    return lax.dot_general(left, right, (dims, ((), ())), preferred_element_type=f32)


def call(body, name, inputs, outs, scratch=(), flops=0, limit=16, deps=()):
    arrays, specs, moved, fetched = [], [], 0, []
    for item in inputs:
        array, space = item if isinstance(item, tuple) else (item, VMEM)
        if space == "fetch":
            fetched.append(len(arrays))
            space = pltpu.HBM
        arrays.append(array)
        specs.append(pl.BlockSpec(memory_space=space))
        moved += array.size * array.dtype.itemsize
    for shape, kind, *_ in outs:
        size = jnp.dtype(kind).itemsize
        for extent in shape:
            size *= extent
        moved += size
    read = len(arrays)
    for array in deps:
        arrays.append(array)
        specs.append(pl.BlockSpec(memory_space=ANY))
    extra = [VMEM(arrays[k].shape, arrays[k].dtype) for k in fetched]
    if fetched:
        extra.append(pltpu.SemaphoreType.DMA((len(fetched),)))

    def whole(*refs):
        refs = list(refs[:read]) + list(refs[read + len(deps) :])
        if fetched:
            held, sem = refs[-1 - len(fetched) : -1], refs[-1]
            refs = refs[: -1 - len(fetched)]
            transfers = []
            for n, k in enumerate(fetched):
                transfer = pltpu.make_async_copy(refs[k], held[n], sem.at[n])
                transfer.start()
                transfers.append(transfer)
                refs[k] = held[n]
            for transfer in transfers:
                transfer.wait()
        body(*refs)

    return pl.pallas_call(
        whole,
        name=name,
        out_shape=[jax.ShapeDtypeStruct(one[0], one[1]) for one in outs],
        in_specs=specs,
        out_specs=[pl.BlockSpec(memory_space=(*one, VMEM)[2]) for one in outs],
        scratch_shapes=list(scratch) + extra,
        compiler_params=pltpu.CompilerParams(vmem_limit_bytes=limit * MIB),
        cost_estimate=pl.CostEstimate(flops=flops, bytes_accessed=moved, transcendentals=0),
    )(*arrays)


def low_bits(index, size):
    return jnp.bitwise_and(index, size - 1)


def pair_weight_rows(w_pair, head_count, cols):
    rows = head_count * cols
    shift = cols.bit_length() - 1
    head = lax.shift_right_logical(
        lax.broadcasted_iota(jnp.int32, (rows, head_count), 0), jnp.int32(shift)
    )
    pick = (head == lax.broadcasted_iota(jnp.int32, (rows, head_count), 1)).astype(f32)
    spread = mm(pick.astype(bf16), w_pair)
    row_col = low_bits(lax.broadcasted_iota(jnp.int32, spread.shape, 0), cols)
    return spread, row_col


def own_slice(weight, t, own_width):
    if weight.shape[1] == own_width:
        return weight
    return weight.at[:, pl.ds(pl.multiple_of(t * own_width, own_width), own_width)]


def enter_kernel(toks, cols, ids, *rest):
    noisy, single, restype, table, gain, pair, pair_gain, w_pair, chain, keymask = rest[:10]
    chain_weight, x_out, columns, facts_out, chain_out, bias_out, rounded, bias = rest[10:]
    t = ids[0]
    rows = noisy.shape[0]
    pair_scaled, _, _ = layer_forward(pair[...].astype(f32), pair_gain[...])
    rounded[...] = pair_scaled.astype(bf16).astype(f32)
    head_count = w_pair.shape[0]
    spread, row_col = pair_weight_rows(w_pair[...], head_count, cols)
    total = jnp.zeros((head_count * cols, rows), f32)
    for j in range(cols):
        column = rounded[pl.ds(j, rows, stride=cols), :].astype(bf16)
        columns[j] = column
        total = total + mm(jnp.where(row_col == j, spread, 0.0).astype(bf16), column, NT)
    bias[...] = total
    part = bias_out.shape[1]
    for r in range(toks):
        start = pl.multiple_of(jnp.bitwise_xor(t, r) * part, part)
        bias_out[r] = bias[pl.ds(start, part), :].astype(bf16)
    normed_scaled, _, _ = layer_forward(noisy[...].astype(f32), gain[...])
    types = table.shape[0]
    onehot = (lax.broadcasted_iota(jnp.int32, (types, rows), 0) == restype[...]).astype(f32)
    condition = single[...].astype(f32) + mm(onehot.astype(bf16), table[...], TN)
    x_out[...] = (normed_scaled + condition).astype(bf16)
    chain_row = chain[...]
    tokens = chain_row.shape[1]
    own_heads = head_count // toks
    keep_row = keymask[...].astype(f32)
    line = lax.broadcasted_iota(jnp.int32, (128, tokens), 0)
    facts = jnp.where(line == 0, chain_row.astype(f32), 0.0) + jnp.where(line == 1, keep_row, 0.0)
    for h in range(own_heads):
        weight_row = jnp.zeros((1, tokens), f32)
        for m in range(chain_weight.shape[0]):
            weight_row = jnp.where(chain_row == m, chain_weight[m, t * own_heads + h], weight_row)
        facts = jnp.where(line == 2 + h, weight_row, facts)
    facts_out[...] = jnp.transpose(facts)
    chain_out[...] = chain_row.astype(f32)


def stage_kernel(ids, *rest):
    weights, (slices, sem) = rest[:3], rest[3:]
    transfers = []
    for k in range(3):
        transfer = pltpu.make_async_copy(
            own_slice(weights[k], ids[0], slices.shape[2]), slices.at[k], sem.at[k]
        )
        transfer.start()
        transfers.append(transfer)
    for transfer in transfers:
        transfer.wait()


def project_kernel(toks, ids, slices, *rest):
    parts = rest[:toks]
    x_out, outs = rest[toks], rest[toks + 1 :]
    t = ids[0]
    rows = parts[0].shape[0]
    for r in range(toks):
        start = pl.multiple_of(jnp.bitwise_xor(t, r) * rows, rows)
        x_out[pl.ds(start, rows), :] = parts[r][...]
    x = x_out[...]
    for k in range(3):
        outs[k][...] = jnp.transpose(mm(x, slices[k])).astype(bf16)


def split_kernel(count, *refs):
    for n in range(count):
        for r, out in enumerate(refs[count:]):
            out[n] = refs[n][r]


def join_kernel(*refs):
    for n, ref in enumerate(refs[:-1]):
        refs[-1][n] = ref[...]


def attention_kernel(copies, toks, near, cols, head_width, ids, query, key, value, *rest):
    biases, (facts, chain, weights_out, att_out) = rest[:2], rest[2:6]
    pieces, bias = rest[6 : 6 + toks], rest[6 + toks]
    t, low, high = ids[0], low_bits(ids[1], near), ids[1] // near
    for m in range(near):
        for rz in range(copies // near):
            c = jnp.bitwise_xor(high, rz) * near + jnp.bitwise_xor(low, m)
            for r in range(toks):
                bias[c, jnp.bitwise_xor(t, r)] = biases[m % 2][m // 2, r, rz]
    own_heads = weights_out.shape[0]
    tokens = query.shape[1]
    rows = tokens // toks
    same = facts[:, 0:1] == chain[...]
    keep = facts[:, 1:2] > 0.0
    scale = head_width ** (-0.5)
    attended = []
    for h in range(own_heads):
        span = slice(h * head_width, (h + 1) * head_width)
        logits = mm(key[span, :], query[span, :], TN) * scale
        line = slice(h * cols, (h + 1) * cols)
        extra = jnp.concatenate(
            [
                jnp.concatenate(
                    [bias[c, a, line, :] for c in range(copies)], axis=0
                )
                for a in range(toks)
            ],
            axis=1,
        ).astype(f32)
        logits = logits + (extra + jnp.where(same, facts[:, 2 + h : 3 + h], 0.0))
        logits = jnp.where(keep, logits, -1e30)
        exponent = jnp.exp(logits - jnp.max(logits, axis=0, keepdims=True))
        weights = exponent / jnp.sum(exponent, axis=0, keepdims=True)
        weights_b = weights.astype(bf16)
        weights_out[h] = weights_b
        attended.append(mm(value[span, :], weights_b))
    att_out[...] = jnp.transpose(jnp.concatenate(attended, axis=0)).astype(bf16)
    for r in range(toks):
        start = pl.multiple_of(jnp.bitwise_xor(t, r) * rows, rows)
        pieces[r][...] = att_out[pl.ds(start, rows), :]


def down_kernel(upstream, w_down, noisy, gain, d_hidden, upstream_out, noisy_out, gain_out):
    d_hidden[...] = mm(upstream[...], w_down[...], NT)
    upstream_out[...] = upstream[...]
    noisy_out[...] = noisy[...]
    gain_out[...] = gain[...]


def hidden_kernel(toks, chunk, ids, noisy, upstream, d_hidden, gain, *rest):
    parts = rest[:toks]
    held_out, held_gate, held_up = rest[toks : toks + 3]
    d_res_out, d_res_b_out = rest[toks + 3 : toks + 5]
    d_att_outs = rest[toks + 5 :]
    t = ids[0]
    hidden = held_gate.shape[1]
    residual = noisy[...].astype(f32)
    own_width = parts[0].shape[1]
    for r in range(toks):
        start = pl.multiple_of(jnp.bitwise_xor(t, r) * own_width, own_width)
        residual = residual + mm(parts[r][...], held_out[pl.ds(start, own_width), :])
    trans_scaled, trans_hat, trans_inverse = layer_forward(residual, gain[...])
    trans_in = trans_scaled.astype(bf16)
    d_trans = jnp.zeros(residual.shape, f32)
    for k in range(hidden // chunk):
        span = slice(k * chunk, (k + 1) * chunk)
        gate = mm(trans_in, held_gate[:, span])
        up = mm(trans_in, held_up[:, span])
        incoming = d_hidden[:, span]
        sigmoid = jax.nn.sigmoid(gate)
        d_up = (incoming * gate * sigmoid).astype(bf16)
        d_gate = (incoming * up * sigmoid * (1.0 + gate * (1.0 - sigmoid))).astype(bf16)
        d_trans = d_trans + mm(d_gate, held_gate[:, span], NT) + mm(d_up, held_up[:, span], NT)
    d_res = upstream[...].astype(f32) + layer_backward(
        d_trans, gain[...], trans_hat, trans_inverse
    )
    d_res_out[...] = d_res
    d_res_b = d_res.astype(bf16)
    d_res_b_out[...] = d_res_b
    for r in range(toks):
        start = pl.multiple_of(jnp.bitwise_xor(t, r) * own_width, own_width)
        d_att_outs[r][...] = mm(held_out[pl.ds(start, own_width), :], d_res_b, NT).astype(bf16)


def backward_kernel(copies, toks, cols, head_width, ids, query, key, value, weights, *rest):
    parts, d_res_b = rest[:toks], rest[toks]
    d_query, d_key, d_value, bias_kept, bias_sent, d_res_out = rest[toks + 1 : toks + 7]
    blocks, d_logits = rest[toks + 7 :]
    d_res_out[...] = d_res_b[...]
    t = ids[0]
    bit = low_bits(ids[1] // 2, 2)
    heads = weights.shape[0]
    for r in range(toks):
        blocks[jnp.bitwise_xor(t, r)] = parts[r][...]
    d_att = jnp.concatenate([blocks[a] for a in range(toks)], axis=1)
    count = tile_count(cols, query.shape[1])
    scale = head_width ** (-0.5)
    for h in range(weights.shape[0]):
        span = slice(h * head_width, (h + 1) * head_width)
        d_att_h = d_att[span, :]
        weights_b = weights[h]
        d_weights = mm(value[span, :], d_att_h, TN)
        weights_f = weights_b.astype(f32)
        delta = jnp.sum(weights_f * d_weights, axis=0, keepdims=True)
        d_logits_b = (weights_f * (d_weights - delta)).astype(bf16)
        d_logits[...] = d_logits_b
        for k in range(copies // 2):
            for side, out in ((bit, bias_kept), (1 - bit, bias_sent)):
                start = pl.multiple_of((k // 2 * 4 + side * 2 + k % 2) * cols, cols)
                put(out, (k * heads + h) * count, d_logits[pl.ds(start, cols), :])
        d_query[span, :] = (mm(key[span, :], d_logits_b) * scale).astype(bf16)
        d_key[span, :] = (mm(query[span, :], d_logits_b, NT) * scale).astype(bf16)
        d_value[span, :] = mm(d_att_h, weights_b, NT).astype(bf16)


def tile_count(rows, lanes):
    return -(-rows // 16) * -(-lanes // 128)


def put(out, base, value):
    rows, lanes = value.shape
    for i in range(0, rows, 16):
        for j in range(0, lanes, 128):
            part = value[i : i + 16, j : j + 128]
            if part.shape != (16, 128):
                out[base] = jnp.zeros((16, 128), out.dtype)
            out[base, : part.shape[0], : part.shape[1]] = part
            base += 1


def take(tiles, base, rows, lanes):
    across = -(-lanes // 128)
    lines = []
    for i in range(-(-rows // 16)):
        line = [tiles[base + i * across + j] for j in range(across)]
        lines.append(jnp.concatenate(line, axis=1) if across > 1 else line[0])
    whole = jnp.concatenate(lines, axis=0) if len(lines) > 1 else lines[0]
    return whole[:rows, :lanes]


def cut_wide(copies, toks, core, base, stride, grad, kept, sent):
    group = copies // toks
    cut, depth = grad.shape[1] // copies, grad.shape[1] // toks
    for side, out in ((core, kept), (1 - core, sent)):
        for q in range(copies // 2):
            h = 2 * q // group
            first = pl.multiple_of((2 * q - h * group + side) * cut, 8)
            part = grad[pl.ds(first, cut), h * depth : (h + 1) * depth]
            put(out, q * stride + base, part.astype(bf16))


def first_kernel(copies, toks, ids, slices, x, d_query, d_key, d_value, *rest):
    kept, sent, d_own, single_all = rest[:4]
    d_others, (wide, d_inputs) = rest[4 : 3 + toks], rest[3 + toks :]
    t, core = ids[0], low_bits(ids[1], 2)
    rows = d_own.shape[1]
    cut = x.shape[1] // copies
    count = tile_count(cut, d_query.shape[0])
    stride = 3 * count
    for k, part in enumerate((d_query, d_key, d_value)):
        wide[...] = mm(part[...], x[...])
        cut_wide(copies, toks, core, k * count, stride, wide, kept, sent)
    total = mm(slices[0], d_query[...]) + mm(slices[1], d_key[...])
    total = total + mm(slices[2], d_value[...])
    single_all[...] = total
    for a in range(toks):
        d_inputs[a] = total[:, a * rows : (a + 1) * rows]
    d_own[...] = d_inputs[t]
    for r in range(1, toks):
        d_others[r - 1][...] = d_inputs[jnp.bitwise_xor(t, r)].astype(bf16)


def second_kernel(copies, toks, ids, att, single_all, bias_kept, bias_got, *rest):
    d_res_parts, (kept, sent, d_res, narrow) = rest[:toks], rest[toks:]
    t, core = ids[0], low_bits(ids[1], 2)
    rows = d_res_parts[0].shape[0]
    cut = narrow.shape[0] // copies
    count = tile_count(cut, narrow.shape[1])
    for r in range(toks):
        start = pl.multiple_of(jnp.bitwise_xor(t, r) * rows, rows)
        d_res[pl.ds(start, rows), :] = d_res_parts[r][...]
    narrow[...] = mm(d_res[...], att[...], TN)
    stride = count + tile_count(cut, rows * toks)
    base = copies // 2 * stride
    bias_count = bias_kept.shape[0] // (copies // 2)
    for side, out in ((core, kept), (1 - core, sent)):
        for q in range(copies // 2):
            first = pl.multiple_of((2 * q + side) * cut, 8)
            put(out, q * stride, narrow[pl.ds(first, cut), :].astype(bf16))
            put(out, q * stride + count, single_all[pl.ds(first, cut), :].astype(bf16))
        for z in range(copies // 4):
            span = pl.ds((2 * z + side) * bias_count, bias_count)
            out[base + z * bias_count : base + (z + 1) * bias_count] = (
                bias_kept[span].astype(f32) + bias_got[span].astype(f32)
            ).astype(bf16)


def step_kernel(segments, ids, *refs):
    count = 1 + max(segment[0] for segment in segments)
    ins, outs = refs[: 2 * count], refs[2 * count :]
    for source, base, parts, tiles, mask, inner, target, start in segments:
        kept, got = ins[2 * source : 2 * source + 2]
        bit = low_bits(ids[1] // mask, 2)
        for q in range(parts // 2):
            for side, out in ((bit, outs[2 * target]), (1 - bit, outs[2 * target + 1])):
                k = q // inner * 2 * inner + side * inner + q % inner
                span = pl.ds(base + k * tiles, tiles)
                out[start + q * tiles : start + (q + 1) * tiles] = (
                    kept[span].astype(f32) + got[span].astype(f32)
                ).astype(bf16)


def last_bias_kernel(toks, base, count, cols, ids, kept, got, *rest):
    pieces, blocks = rest[:toks], rest[toks]
    span = slice(base, base + count)
    tiles = kept[span].astype(f32) + got[span].astype(f32)
    part_rows, rows = pieces[0].shape
    heads = part_rows // cols
    total = jnp.concatenate(
        [take(tiles, h * (count // heads), cols, rows * toks) for h in range(heads)], axis=0
    )
    for a in range(toks):
        blocks[a] = total[:, a * rows : (a + 1) * rows].astype(bf16)
    for r in range(toks):
        pieces[r][...] = blocks[jnp.bitwise_xor(ids[0], r)]


def across_kernel(segment, ids, kept, got, kept_b, got_b, *outs):
    t = ids[0]
    stride = kept.shape[0] // 2
    step_kernel([(0, 0) + segment], ids, kept_b, got_b, *outs[2:])
    for side, out in ((t, outs[0]), (1 - t, outs[1])):
        span = pl.ds(side * stride, stride)
        out[...] = (kept[span].astype(f32) + got[span].astype(f32)).astype(bf16)


def far_kernel(half, ids, kept, got, kept_b, got_b, kept_out, sent_out, single, other, *scratch):
    groups, blocks = scratch
    t, a = ids[0], ids[1] // half
    groups[t] = kept[...]
    groups[1 - t] = got[...]
    kept_out[...] = groups[a]
    sent_out[...] = groups[1 - a]
    lines = single.shape[0]
    base = kept_b.shape[0] - 2 * lines
    for i in range(lines):
        for j in range(2):
            k = base + 2 * i + j
            blocks[j, i] = (kept_b[k].astype(f32) + got_b[k].astype(f32)).astype(bf16)
    single[...] = blocks[t]
    other[...] = blocks[1 - t]


def close_kernel(kept, got, kept_b, got_b, single, got_single, terms, *outs):
    total = kept[...].astype(f32) + got[...].astype(f32)
    cut, own_width = outs[0].shape
    count = tile_count(cut, own_width)
    for k in range(3):
        outs[k][...] = take(total, k * count, cut, own_width)
    total = kept_b[:count].astype(f32) + got_b[:count].astype(f32)
    outs[3][...] = take(total, 0, cut, own_width)
    total = single[...].astype(f32) + got_single[...].astype(f32)
    outs[4][...] = take(total, 0, cut, outs[4].shape[1])
    outs[5][...] = jnp.sum(terms[...], axis=0)


def last_kernel(toks, ids, kept, got, kept_b, got_b, moved, final, *rest):
    pieces, blocks = rest[:toks], rest[toks]
    first = kept[...].astype(f32) + got[...].astype(f32)
    second = kept_b[...].astype(f32) + got_b[...].astype(f32)
    _, cut, own_width = moved.shape
    count = tile_count(cut, own_width)
    for k in range(3):
        moved[k] = take(first, k * count, cut, own_width).astype(bf16)
    final[...] = take(second, 0, cut, own_width)
    rows = blocks.shape[2]
    single = take(second, count, cut, rows * toks)
    for a in range(toks):
        blocks[a] = single[:, a * rows : (a + 1) * rows]
    for r in range(toks):
        pieces[r][...] = blocks[jnp.bitwise_xor(ids[0], r)].astype(bf16)


def finish_kernel(moved, *rest):
    parts, outs = rest[:-4], rest[-4:]
    for k in range(3):
        outs[k][...] = moved[k].astype(f32)
    total = parts[0][...].astype(f32)
    for part in parts[1:]:
        total = total + part[...].astype(f32)
    outs[3][...] = total


def exit_kernel(toks, noisy, gain, d_res, d_own, *rest):
    others, (grad_noisy, token) = rest[: toks - 1], rest[toks - 1 :]
    token[...] = jnp.zeros(token.shape, f32)
    total = d_own[...]
    for part in others:
        total = total + part[...].astype(f32)
    _, noisy_hat, noisy_inverse = layer_forward(noisy[...].astype(f32), gain[...])
    grad_noisy[...] = (
        d_res[...] + layer_backward(jnp.transpose(total), gain[...], noisy_hat, noisy_inverse)
    ).astype(bf16)


def set_heads(toks, ids, parts, grads):
    part_rows = parts[0].shape[0]
    for r in range(toks):
        start = pl.multiple_of(jnp.bitwise_xor(ids[0], r) * part_rows, part_rows)
        grads[pl.ds(start, part_rows), :] = parts[r][...].astype(f32)


def pair_weight_kernel(toks, ids, columns, *rest):
    parts, (weight_grad, grads) = rest[:toks], rest[toks:]
    set_heads(toks, ids, parts, grads)
    cols, _, channels = columns.shape
    heads = weight_grad.shape[1]
    sums = jnp.zeros((heads, channels), f32)
    for j in range(cols):
        lines = grads[pl.ds(j, heads, stride=cols), :].astype(bf16)
        sums = sums + mm(lines, columns[j])
    for n in range(weight_grad.shape[0]):
        weight_grad[n] = sums


def pair_kernel(toks, cols, ids, pair, gain, w_pair, *rest):
    parts, (grad_pair, spread_out, grads) = rest[:toks], rest[toks:]
    set_heads(toks, ids, parts, grads)
    rows = parts[0].shape[1]
    _, pair_hat, pair_inverse = layer_forward(pair[...].astype(f32), gain[...])
    spread, row_col = pair_weight_rows(w_pair[...], w_pair.shape[0], cols)
    turned = jnp.transpose(grads[...]).astype(bf16)
    for j in range(cols):
        spread_out[pl.ds(j, rows, stride=cols), :] = mm(
            turned, jnp.where(row_col == j, spread, 0.0).astype(bf16)
        )
    grad_pair[...] = layer_backward(
        spread_out[...], gain[...], pair_hat, pair_inverse
    ).astype(bf16)


def swap_copy(value, mask):
    size = lax.axis_size("copy")
    return lax.ppermute(value, "copy", [(i, i ^ mask) for i in range(size)])


def swap_tok(value, mask):
    size = lax.axis_size("tok")
    return lax.ppermute(value, "tok", [(i, i ^ mask) for i in range(size)])


def exchange(value):
    return lax.all_to_all(value, ("copy", "tok"), 0, 0)


def per_device(
    noisy,
    single,
    pair,
    restype,
    chain,
    keymask,
    restype_table,
    norm_gain,
    pair_gain,
    trans_gain,
    w_query,
    w_key,
    w_value,
    w_out,
    w_pair,
    chain_weight,
    w_hidden_gate,
    w_hidden_up,
    w_down,
    cotangent,
):
    copies = lax.axis_size("copy")
    toks = lax.axis_size("tok")
    _, rows, width = noisy.shape
    cols = pair.shape[1]
    channels = pair.shape[2]
    heads = w_pair.shape[1]
    head_width = width // heads
    own_heads = heads // toks
    own_width = own_heads * head_width
    tokens = rows * toks
    hidden = w_down.shape[0]
    cut = width // copies
    devices = copies * toks
    ids = jnp.stack([lax.axis_index("tok"), lax.axis_index("copy")]).astype(jnp.int32)
    where_am_i = (ids, SMEM)
    noisy2 = noisy.reshape(rows, width)
    pair2 = pair.reshape(rows * cols, channels)
    pair_gain2 = pair_gain.reshape(1, channels)
    norm_gain2 = norm_gain.reshape(1, width)

    weights3 = [w_query, w_key, w_value]
    if own_width % 128:
        weights3 = [
            lax.dynamic_slice_in_dim(w, ids[0] * own_width, own_width, axis=1) for w in weights3
        ]
    small = [noisy2, single, restype.reshape(1, rows), restype_table, norm_gain, pair2, pair_gain2]
    small += [w_pair.T, chain.reshape(1, tokens), keymask.reshape(1, tokens)]
    entered = call(
        functools.partial(enter_kernel, toks, cols),
        "enter",
        [where_am_i]
        + [(array, "fetch") for array in small]
        + [(chain_weight, SMEM)],
        [((rows, width), bf16), ((cols, rows, channels), bf16)]
        + [((tokens, 128), f32), ((1, tokens), f32), ((toks, own_heads * cols, rows), bf16)],
        [VMEM((rows * cols, channels), f32), VMEM((heads * cols, rows), f32)],
        flops=2 * heads * cols * rows * channels * cols,
        limit=60,
    )
    x_own, columns, facts, chain_row, bias_mine = entered
    near = 4
    far = copies // near
    x_parts = [x_own] + [swap_tok(x_own, r) for r in range(1, toks)]
    by_tok = call(
        functools.partial(split_kernel, far),
        "split_far",
        [bias_mine] + [swap_copy(bias_mine, m * near) for m in range(1, far)],
        [((far, own_heads * cols, rows), bf16)] * toks,
        deps=x_parts[1:],
    )
    (slices,) = call(
        stage_kernel,
        "stage",
        [where_am_i] + [(w, ANY) for w in weights3],
        [((3, width, own_width), bf16)],
        [pltpu.SemaphoreType.DMA((3,))],
        deps=[by_tok[0]],
    )
    (lines,) = call(
        join_kernel,
        "join_tok",
        [by_tok[0]] + [swap_tok(by_tok[r], r) for r in range(1, toks)],
        [((toks, far, own_heads * cols, rows), bf16)],
        deps=[slices],
    )
    x, query, key, value = call(
        functools.partial(project_kernel, toks),
        "project",
        [where_am_i, slices] + x_parts,
        [((tokens, width), bf16)] + [((own_width, tokens), bf16)] * 3,
        flops=6 * tokens * width * own_width,
    )
    (lines,) = call(
        join_kernel,
        "join_y",
        [lines, swap_copy(lines, 2)],
        [((2,) + lines.shape, bf16)],
        deps=[value],
    )
    biases = [lines, swap_copy(lines, 1)]
    done = call(
        functools.partial(attention_kernel, copies, toks, near, cols, head_width),
        "attention",
        [where_am_i, query, key, value] + biases + [facts, chain_row],
        [((own_heads, tokens, tokens), bf16), ((tokens, own_width), bf16)]
        + [((rows, own_width), bf16)] * toks,
        [VMEM((copies, toks, own_heads * cols, rows), bf16)],
        flops=4 * tokens * tokens * own_width,
        limit=32,
    )
    weights, att, pieces = done[0], done[1], done[2:]
    att_parts = [pieces[0]] + [swap_tok(pieces[r], r) for r in range(1, toks)]

    d_hidden, upstream, noisy3, trans_gain2 = call(
        down_kernel,
        "down",
        [cotangent.reshape(rows, width), w_down, noisy2, trans_gain.reshape(1, width)],
        [((rows, hidden), f32), ((rows, width), bf16), ((rows, width), bf16), ((1, width), f32)],
        flops=2 * rows * hidden * width,
    )
    chunk = hidden // 3
    results = call(
        functools.partial(hidden_kernel, toks, chunk),
        "hidden",
        [where_am_i, noisy3, upstream, d_hidden, trans_gain2]
        + att_parts
        + [w_out, w_hidden_gate, w_hidden_up],
        [((rows, width), f32), ((rows, width), bf16)] + [((own_width, rows), bf16)] * toks,
        flops=2 * rows * width * (2 * width + 4 * hidden),
    )
    d_res, d_res_b, d_att = results[0], results[1], results[2:]
    d_att_parts = [d_att[0]] + [swap_tok(d_att[r], r) for r in range(1, toks)]
    bias_tiles = own_heads * tile_count(cols, tokens)
    bias_shape = (copies // 2 * bias_tiles, 16, 128)
    d_query, d_key, d_value, bias_kept, bias_sent, d_res_b = call(
        functools.partial(backward_kernel, copies, toks, cols, head_width),
        "backward",
        [where_am_i, query, key, value, weights] + d_att_parts + [d_res_b],
        [((own_width, tokens), bf16)] * 3 + [(bias_shape, bf16)] * 2 + [((rows, width), bf16)],
        [VMEM((toks, own_width, rows), bf16), VMEM((tokens, tokens), bf16)],
        flops=8 * tokens * tokens * own_width,
        limit=32,
    )
    d_res_parts = [d_res_b] + [swap_tok(d_res_b, r) for r in range(1, toks)]
    bias_got = swap_copy(bias_sent, 2)

    wide_tiles = tile_count(cut, own_width)
    single_tiles = tile_count(cut, tokens)
    first_tiles, second_tiles = 3 * wide_tiles, wide_tiles + single_tiles
    found = call(
        functools.partial(first_kernel, copies, toks),
        "first",
        [where_am_i, slices, x, d_query, d_key, d_value],
        [((copies // 2 * first_tiles, 16, 128), bf16)] * 2
        + [((width, rows), f32), ((width, tokens), f32)]
        + [((width, rows), bf16)] * (toks - 1),
        [VMEM((own_width, width), f32), VMEM((toks, width, rows), f32)],
        flops=12 * tokens * width * own_width,
    )
    kept, sent, d_own, single_all = found[:4]
    got = swap_copy(sent, 1)
    d_others = [swap_tok(found[3 + r], r) for r in range(1, toks)]

    def step(name, pairs, segments, deps=()):
        filled, full, masks_of = {}, [], {}
        for source, base, parts, tiles, mask, left, target in segments:
            inner = 1 << sum(1 for other in left if other < mask)
            start = filled.get(target, 0)
            full.append((source, base, parts, tiles, mask, inner, target, start))
            filled[target] = start + parts // 2 * tiles
            masks_of[target] = mask
        outs = []
        for target in range(len(filled)):
            outs += [((filled[target], 16, 128), bf16)] * 2
        results = call(
            functools.partial(step_kernel, full),
            name,
            [where_am_i] + [array for one in pairs for array in one],
            outs,
            deps=deps,
        )
        return [
            (results[2 * n], swap_copy(results[2 * n + 1], masks_of[n]))
            for n in range(len(filled))
        ]

    masks = [1 << b for b in range(1, copies.bit_length() - 1)]
    masks_b = masks[1:] + masks[:1]
    kept_b, sent_b = call(
        functools.partial(second_kernel, copies, toks),
        "second",
        [where_am_i, att, single_all, bias_kept, bias_got] + d_res_parts,
        [((copies // 2 * second_tiles + copies // 4 * bias_tiles, 16, 128), bf16)] * 2,
        [VMEM((tokens, width), bf16), VMEM((width, own_width), f32)],
        flops=20 * tokens * width * own_width,
    )
    got_b = swap_copy(sent_b, 1)

    grad_noisy, exited = call(
        functools.partial(exit_kernel, toks),
        "exit",
        [noisy3, norm_gain2, d_res, d_own] + d_others,
        [((rows, width), bf16), ((8, 128), f32)],
    )
    pairs = [(kept, got), (kept_b, got_b)]
    parts = copies // 2
    for n, (mask, mask_b) in enumerate(zip(masks, masks_b)):
        segments = [
            (0, 0, parts, first_tiles, mask, masks[n:], 0),
            (1, 0, parts, second_tiles, mask_b, masks_b[n:], 1),
        ]
        bias_base = parts * second_tiles
        if n + 1 < len(masks):
            segments.append((1, bias_base, parts // 2, bias_tiles, mask_b, masks_b[n:-1], 1))
        else:
            bias_ready = pairs[1]
            if toks == 2:
                break
        pairs = step("step_%d" % n, pairs, segments, deps=[exited] if n == 2 else ())
        parts //= 2
    if toks == 2:
        kept, sent, kept_b, sent_b = call(
            functools.partial(across_kernel, (2, second_tiles, masks_b[-1], 1, 0, 0)),
            "across",
            [where_am_i] + [array for one in pairs for array in one],
            [((first_tiles, 16, 128), bf16)] * 2 + [((second_tiles, 16, 128), bf16)] * 2,
            deps=[exited],
        )
        pairs = [(kept, swap_tok(sent, 1)), (kept_b, swap_copy(sent_b, masks_b[-1]))]
    bias_pieces = call(
        functools.partial(last_bias_kernel, toks, bias_base, bias_tiles, cols),
        "last_bias",
        [where_am_i, *bias_ready],
        [((own_heads * cols, rows), bf16)] * toks,
        [VMEM((toks, own_heads * cols, rows), bf16)],
        deps=[pairs[0][0]],
    )
    bias_pieces = [bias_pieces[0]] + [swap_tok(bias_pieces[r], r) for r in range(1, toks)]
    ready = [pairs[0][1], pairs[1][1]]
    if toks == 2:
        lines = single_tiles // 2
        kept, sent, single_kept, single_sent = call(
            functools.partial(far_kernel, copies // 2),
            "far",
            [where_am_i, *pairs[0], *pairs[1]],
            [((first_tiles, 16, 128), bf16)] * 2 + [((lines, 16, 128), bf16)] * 2,
            [VMEM((2, first_tiles, 16, 128), bf16), VMEM((2, lines, 16, 128), bf16)],
            deps=bias_pieces[1:],
        )
        pairs[0] = (kept, swap_copy(sent, copies // 2))
        single_pair = (single_kept, swap_tok(single_sent, 1))

    group = copies // toks
    swaps = []
    for c in range(copies):
        for t in range(toks):
            swaps.append((c * toks + t, (t * group + c % group) * toks + c // group))

    (weight_grad,) = call(
        functools.partial(pair_weight_kernel, toks),
        "pair_weight",
        [where_am_i, columns] + bias_pieces,
        [((devices, heads, channels), f32)],
        [VMEM((heads * cols, rows), f32)],
        flops=2 * heads * cols * rows * channels * cols,
        deps=ready,
    )
    (grad_pair,) = call(
        functools.partial(pair_kernel, toks, cols),
        "pair",
        [where_am_i, pair2, pair_gain2, w_pair.T] + bias_pieces,
        [((rows * cols, channels), bf16)],
        [VMEM((rows * cols, channels), f32), VMEM((heads * cols, rows), f32)],
        flops=2 * heads * cols * rows * channels * cols,
    )
    weight_terms = exchange(weight_grad)
    if toks == 2:
        grad_query, grad_key, grad_value, grad_out, grad_single, weight_grad = call(
            close_kernel,
            "close",
            [*pairs[0], *pairs[1], *single_pair, weight_terms],
            [((cut, own_width), f32)] * 4 + [((cut, rows), f32), ((heads, channels), f32)],
        )
    else:
        last = call(
            functools.partial(last_kernel, toks),
            "last",
            [where_am_i, *pairs[0], *pairs[1]],
            [((3, cut, own_width), bf16), ((cut, own_width), f32)] + [((cut, rows), bf16)] * toks,
            [VMEM((toks, cut, rows), f32)],
        )
        weight_grad = jnp.sum(weight_terms, axis=0)
        grad_out, singles = last[1], last[2:]
        singles = [singles[0]] + [swap_tok(singles[r], r) for r in range(1, toks)]
        moved = lax.ppermute(last[0], ("copy", "tok"), swaps)
        grad_query, grad_key, grad_value, grad_single = call(
            finish_kernel,
            "finish",
            [moved] + singles,
            [((cut, own_width), f32)] * 3 + [((cut, rows), f32)],
        )
    return (
        grad_noisy[None],
        grad_single.T,
        grad_pair.reshape(rows, cols, channels),
        grad_query.T,
        grad_key.T,
        grad_value.T,
        grad_out.T,
        weight_grad.T,
    )


def solution(mesh):
    placed = (
        P("copy", "tok", None),
        P("tok", None),
        P("tok", "copy", None),
        P("tok"),
    ) + (P(),) * 15 + (P("copy", "tok", None),)
    return jax.shard_map(
        per_device,
        mesh=mesh,
        in_specs=placed,
        out_specs=(
            P("copy", "tok", None),
            P("tok", "copy"),
            P("tok", "copy", None),
            P("tok", "copy"),
            P("tok", "copy"),
            P("tok", "copy"),
            P("tok", "copy"),
            P(),
        ),
        check_vma=False,
    )
```

```python
import functools

import jax
import jax.numpy as jnp
from jax import lax
from jax.experimental import pallas as pl
from jax.experimental.pallas import tpu as pltpu
from jax.sharding import PartitionSpec as P

epsilon = 1e-05
f32 = jnp.float32
bf16 = jnp.bfloat16
VMEM, SMEM, ANY = pltpu.VMEM, pltpu.SMEM, pl.ANY
MIB = 1 << 20


def layer_forward(values, scales):
    average = jnp.mean(values, axis=-1, keepdims=True)
    centred = values - average
    inverse = lax.rsqrt(jnp.mean(centred * centred, axis=-1, keepdims=True) + epsilon)
    normed = centred * inverse
    return (normed * scales, normed, inverse)


def layer_backward(upstream, scales, normed, inverse):
    scaled = upstream * scales
    first_moment = jnp.mean(scaled, axis=-1, keepdims=True)
    second_moment = jnp.mean(scaled * normed, axis=-1, keepdims=True)
    return inverse * (scaled - first_moment - normed * second_moment)


NN = ((1,), (0,))
NT = ((1,), (1,))
TN = ((0,), (0,))


def mm(left, right, dims=NN):
    return lax.dot_general(left, right, (dims, ((), ())), preferred_element_type=f32)


def call(body, name, inputs, outs, scratch=(), flops=0, limit=16, deps=()):
    arrays, specs, moved, fetched = [], [], 0, []
    for item in inputs:
        array, space = item if isinstance(item, tuple) else (item, VMEM)
        if space == "fetch":
            fetched.append(len(arrays))
            space = pltpu.HBM
        arrays.append(array)
        specs.append(pl.BlockSpec(memory_space=space))
        moved += array.size * array.dtype.itemsize
    for shape, kind, *_ in outs:
        size = jnp.dtype(kind).itemsize
        for extent in shape:
            size *= extent
        moved += size
    read = len(arrays)
    for array in deps:
        arrays.append(array)
        specs.append(pl.BlockSpec(memory_space=ANY))
    extra = [VMEM(arrays[k].shape, arrays[k].dtype) for k in fetched]
    if fetched:
        extra.append(pltpu.SemaphoreType.DMA((len(fetched),)))

    def whole(*refs):
        refs = list(refs[:read]) + list(refs[read + len(deps) :])
        if fetched:
            held, sem = refs[-1 - len(fetched) : -1], refs[-1]
            refs = refs[: -1 - len(fetched)]
            transfers = []
            for n, k in enumerate(fetched):
                transfer = pltpu.make_async_copy(refs[k], held[n], sem.at[n])
                transfer.start()
                transfers.append(transfer)
                refs[k] = held[n]
            for transfer in transfers:
                transfer.wait()
        body(*refs)

    return pl.pallas_call(
        whole,
        name=name,
        out_shape=[jax.ShapeDtypeStruct(one[0], one[1]) for one in outs],
        in_specs=specs,
        out_specs=[pl.BlockSpec(memory_space=(*one, VMEM)[2]) for one in outs],
        scratch_shapes=list(scratch) + extra,
        compiler_params=pltpu.CompilerParams(vmem_limit_bytes=limit * MIB),
        cost_estimate=pl.CostEstimate(flops=flops, bytes_accessed=moved, transcendentals=0),
    )(*arrays)


def low_bits(index, size):
    return jnp.bitwise_and(index, size - 1)


def pair_weight_rows(w_pair, head_count, cols):
    rows = head_count * cols
    shift = cols.bit_length() - 1
    head = lax.shift_right_logical(
        lax.broadcasted_iota(jnp.int32, (rows, head_count), 0), jnp.int32(shift)
    )
    pick = (head == lax.broadcasted_iota(jnp.int32, (rows, head_count), 1)).astype(f32)
    spread = mm(pick.astype(bf16), w_pair)
    row_col = low_bits(lax.broadcasted_iota(jnp.int32, spread.shape, 0), cols)
    return spread, row_col


def own_slice(weight, t, own_width):
    if weight.shape[1] == own_width:
        return weight
    return weight.at[:, pl.ds(pl.multiple_of(t * own_width, own_width), own_width)]


def enter_kernel(toks, cols, ids, *rest):
    noisy, single, restype, table, gain, pair, pair_gain, w_pair, chain, keymask = rest[:10]
    chain_weight, x_out, columns, facts_out, chain_out, bias_out, rounded, bias = rest[10:]
    t = ids[0]
    rows = noisy.shape[0]
    pair_scaled, _, _ = layer_forward(pair[...].astype(f32), pair_gain[...])
    rounded[...] = pair_scaled.astype(bf16).astype(f32)
    head_count = w_pair.shape[0]
    spread, row_col = pair_weight_rows(w_pair[...], head_count, cols)
    total = jnp.zeros((head_count * cols, rows), f32)
    for j in range(cols):
        column = rounded[pl.ds(j, rows, stride=cols), :].astype(bf16)
        columns[j] = column
        total = total + mm(jnp.where(row_col == j, spread, 0.0).astype(bf16), column, NT)
    bias[...] = total
    part = bias_out.shape[1]
    for r in range(toks):
        start = pl.multiple_of(jnp.bitwise_xor(t, r) * part, part)
        bias_out[r] = bias[pl.ds(start, part), :].astype(bf16)
    normed_scaled, _, _ = layer_forward(noisy[...].astype(f32), gain[...])
    types = table.shape[0]
    onehot = (lax.broadcasted_iota(jnp.int32, (types, rows), 0) == restype[...]).astype(f32)
    condition = single[...].astype(f32) + mm(onehot.astype(bf16), table[...], TN)
    x_out[...] = (normed_scaled + condition).astype(bf16)
    chain_row = chain[...]
    tokens = chain_row.shape[1]
    own_heads = head_count // toks
    keep_row = keymask[...].astype(f32)
    line = lax.broadcasted_iota(jnp.int32, (128, tokens), 0)
    facts = jnp.where(line == 0, chain_row.astype(f32), 0.0) + jnp.where(line == 1, keep_row, 0.0)
    for h in range(own_heads):
        weight_row = jnp.zeros((1, tokens), f32)
        for m in range(chain_weight.shape[0]):
            weight_row = jnp.where(chain_row == m, chain_weight[m, t * own_heads + h], weight_row)
        facts = jnp.where(line == 2 + h, weight_row, facts)
    facts_out[...] = jnp.transpose(facts)
    chain_out[...] = chain_row.astype(f32)


def stage_kernel(ids, *rest):
    weights, (slices, sem) = rest[:3], rest[3:]
    transfers = []
    for k in range(3):
        transfer = pltpu.make_async_copy(
            own_slice(weights[k], ids[0], slices.shape[2]), slices.at[k], sem.at[k]
        )
        transfer.start()
        transfers.append(transfer)
    for transfer in transfers:
        transfer.wait()


def project_kernel(toks, ids, slices, *rest):
    parts = rest[:toks]
    x_out, outs = rest[toks], rest[toks + 1 :]
    t = ids[0]
    rows = parts[0].shape[0]
    for r in range(toks):
        start = pl.multiple_of(jnp.bitwise_xor(t, r) * rows, rows)
        x_out[pl.ds(start, rows), :] = parts[r][...]
    x = x_out[...]
    for k in range(3):
        outs[k][...] = jnp.transpose(mm(x, slices[k])).astype(bf16)


def split_kernel(count, *refs):
    for n in range(count):
        for r, out in enumerate(refs[count:]):
            out[n] = refs[n][r]


def join_kernel(*refs):
    for n, ref in enumerate(refs[:-1]):
        refs[-1][n] = ref[...]


def attention_kernel(copies, toks, near, cols, head_width, ids, query, key, value, *rest):
    biases, (facts, chain, weights_out, att_out) = rest[:2], rest[2:6]
    pieces, bias = rest[6 : 6 + toks], rest[6 + toks]
    t, low, high = ids[0], low_bits(ids[1], near), ids[1] // near
    for m in range(near):
        for rz in range(copies // near):
            c = jnp.bitwise_xor(high, rz) * near + jnp.bitwise_xor(low, m)
            for r in range(toks):
                bias[c, jnp.bitwise_xor(t, r)] = biases[m % 2][m // 2, r, rz]
    own_heads = weights_out.shape[0]
    tokens = query.shape[1]
    rows = tokens // toks
    same = facts[:, 0:1] == chain[...]
    keep = facts[:, 1:2] > 0.0
    scale = head_width ** (-0.5)
    attended = []
    for h in range(own_heads):
        span = slice(h * head_width, (h + 1) * head_width)
        logits = mm(key[span, :], query[span, :], TN) * scale
        line = slice(h * cols, (h + 1) * cols)
        extra = jnp.concatenate(
            [
                jnp.concatenate(
                    [bias[c, a, line, :] for c in range(copies)], axis=0
                )
                for a in range(toks)
            ],
            axis=1,
        ).astype(f32)
        logits = logits + (extra + jnp.where(same, facts[:, 2 + h : 3 + h], 0.0))
        logits = jnp.where(keep, logits, -1e30)
        exponent = jnp.exp(logits - jnp.max(logits, axis=0, keepdims=True))
        weights = exponent / jnp.sum(exponent, axis=0, keepdims=True)
        weights_b = weights.astype(bf16)
        weights_out[h] = weights_b
        attended.append(mm(value[span, :], weights_b))
    att_out[...] = jnp.transpose(jnp.concatenate(attended, axis=0)).astype(bf16)
    for r in range(toks):
        start = pl.multiple_of(jnp.bitwise_xor(t, r) * rows, rows)
        pieces[r][...] = att_out[pl.ds(start, rows), :]


def down_kernel(upstream, w_down, noisy, gain, d_hidden, upstream_out, noisy_out, gain_out):
    d_hidden[...] = mm(upstream[...], w_down[...], NT)
    upstream_out[...] = upstream[...]
    noisy_out[...] = noisy[...]
    gain_out[...] = gain[...]


def hidden_kernel(toks, chunk, ids, noisy, upstream, d_hidden, gain, *rest):
    parts = rest[:toks]
    held_out, held_gate, held_up = rest[toks : toks + 3]
    d_res_out, d_res_b_out = rest[toks + 3 : toks + 5]
    d_att_outs = rest[toks + 5 :]
    t = ids[0]
    hidden = held_gate.shape[1]
    residual = noisy[...].astype(f32)
    own_width = parts[0].shape[1]
    for r in range(toks):
        start = pl.multiple_of(jnp.bitwise_xor(t, r) * own_width, own_width)
        residual = residual + mm(parts[r][...], held_out[pl.ds(start, own_width), :])
    trans_scaled, trans_hat, trans_inverse = layer_forward(residual, gain[...])
    trans_in = trans_scaled.astype(bf16)
    d_trans = jnp.zeros(residual.shape, f32)
    for k in range(hidden // chunk):
        span = slice(k * chunk, (k + 1) * chunk)
        gate = mm(trans_in, held_gate[:, span])
        up = mm(trans_in, held_up[:, span])
        incoming = d_hidden[:, span]
        sigmoid = jax.nn.sigmoid(gate)
        d_up = (incoming * gate * sigmoid).astype(bf16)
        d_gate = (incoming * up * sigmoid * (1.0 + gate * (1.0 - sigmoid))).astype(bf16)
        d_trans = d_trans + mm(d_gate, held_gate[:, span], NT) + mm(d_up, held_up[:, span], NT)
    d_res = upstream[...].astype(f32) + layer_backward(
        d_trans, gain[...], trans_hat, trans_inverse
    )
    d_res_out[...] = d_res
    d_res_b = d_res.astype(bf16)
    d_res_b_out[...] = d_res_b
    for r in range(toks):
        start = pl.multiple_of(jnp.bitwise_xor(t, r) * own_width, own_width)
        d_att_outs[r][...] = mm(held_out[pl.ds(start, own_width), :], d_res_b, NT).astype(bf16)


def backward_kernel(copies, toks, cols, head_width, ids, query, key, value, weights, *rest):
    parts, d_res_b = rest[:toks], rest[toks]
    d_query, d_key, d_value, bias_kept, bias_sent, d_res_out = rest[toks + 1 : toks + 7]
    blocks, d_logits = rest[toks + 7 :]
    d_res_out[...] = d_res_b[...]
    t = ids[0]
    bit = low_bits(ids[1] // 2, 2)
    heads = weights.shape[0]
    for r in range(toks):
        blocks[jnp.bitwise_xor(t, r)] = parts[r][...]
    d_att = jnp.concatenate([blocks[a] for a in range(toks)], axis=1)
    count = tile_count(cols, query.shape[1])
    scale = head_width ** (-0.5)
    for h in range(weights.shape[0]):
        span = slice(h * head_width, (h + 1) * head_width)
        d_att_h = d_att[span, :]
        weights_b = weights[h]
        d_weights = mm(value[span, :], d_att_h, TN)
        weights_f = weights_b.astype(f32)
        delta = jnp.sum(weights_f * d_weights, axis=0, keepdims=True)
        d_logits_b = (weights_f * (d_weights - delta)).astype(bf16)
        d_logits[...] = d_logits_b
        for k in range(copies // 2):
            for side, out in ((bit, bias_kept), (1 - bit, bias_sent)):
                start = pl.multiple_of((k // 2 * 4 + side * 2 + k % 2) * cols, cols)
                put(out, (k * heads + h) * count, d_logits[pl.ds(start, cols), :])
        d_query[span, :] = (mm(key[span, :], d_logits_b) * scale).astype(bf16)
        d_key[span, :] = (mm(query[span, :], d_logits_b, NT) * scale).astype(bf16)
        d_value[span, :] = mm(d_att_h, weights_b, NT).astype(bf16)


def tile_count(rows, lanes):
    return -(-rows // 16) * -(-lanes // 128)


def put(out, base, value):
    rows, lanes = value.shape
    for i in range(0, rows, 16):
        for j in range(0, lanes, 128):
            part = value[i : i + 16, j : j + 128]
            if part.shape != (16, 128):
                out[base] = jnp.zeros((16, 128), out.dtype)
            out[base, : part.shape[0], : part.shape[1]] = part
            base += 1


def take(tiles, base, rows, lanes):
    across = -(-lanes // 128)
    lines = []
    for i in range(-(-rows // 16)):
        line = [tiles[base + i * across + j] for j in range(across)]
        lines.append(jnp.concatenate(line, axis=1) if across > 1 else line[0])
    whole = jnp.concatenate(lines, axis=0) if len(lines) > 1 else lines[0]
    return whole[:rows, :lanes]


def cut_wide(copies, toks, core, base, stride, grad, kept, sent):
    group = copies // toks
    cut, depth = grad.shape[1] // copies, grad.shape[1] // toks
    for side, out in ((core, kept), (1 - core, sent)):
        for q in range(copies // 2):
            h = 2 * q // group
            first = pl.multiple_of((2 * q - h * group + side) * cut, 8)
            part = grad[pl.ds(first, cut), h * depth : (h + 1) * depth]
            put(out, q * stride + base, part.astype(bf16))


def first_kernel(copies, toks, ids, slices, x, d_query, d_key, d_value, *rest):
    kept, sent, d_own, single_all = rest[:4]
    d_others, (wide, d_inputs) = rest[4 : 3 + toks], rest[3 + toks :]
    t, core = ids[0], low_bits(ids[1], 2)
    rows = d_own.shape[1]
    cut = x.shape[1] // copies
    count = tile_count(cut, d_query.shape[0])
    stride = 3 * count
    for k, part in enumerate((d_query, d_key, d_value)):
        wide[...] = mm(part[...], x[...])
        cut_wide(copies, toks, core, k * count, stride, wide, kept, sent)
    total = mm(slices[0], d_query[...]) + mm(slices[1], d_key[...])
    total = total + mm(slices[2], d_value[...])
    single_all[...] = total
    for a in range(toks):
        d_inputs[a] = total[:, a * rows : (a + 1) * rows]
    d_own[...] = d_inputs[t]
    for r in range(1, toks):
        d_others[r - 1][...] = d_inputs[jnp.bitwise_xor(t, r)].astype(bf16)


def second_kernel(copies, toks, ids, att, single_all, bias_kept, bias_got, *rest):
    d_res_parts, (kept, sent, d_res, narrow) = rest[:toks], rest[toks:]
    t, core = ids[0], low_bits(ids[1], 2)
    rows = d_res_parts[0].shape[0]
    cut = narrow.shape[0] // copies
    count = tile_count(cut, narrow.shape[1])
    for r in range(toks):
        start = pl.multiple_of(jnp.bitwise_xor(t, r) * rows, rows)
        d_res[pl.ds(start, rows), :] = d_res_parts[r][...]
    narrow[...] = mm(d_res[...], att[...], TN)
    stride = count + tile_count(cut, rows * toks)
    base = copies // 2 * stride
    bias_count = bias_kept.shape[0] // (copies // 2)
    for side, out in ((core, kept), (1 - core, sent)):
        for q in range(copies // 2):
            first = pl.multiple_of((2 * q + side) * cut, 8)
            put(out, q * stride, narrow[pl.ds(first, cut), :].astype(bf16))
            put(out, q * stride + count, single_all[pl.ds(first, cut), :].astype(bf16))
        for z in range(copies // 4):
            span = pl.ds((2 * z + side) * bias_count, bias_count)
            out[base + z * bias_count : base + (z + 1) * bias_count] = (
                bias_kept[span].astype(f32) + bias_got[span].astype(f32)
            ).astype(bf16)


def step_kernel(segments, ids, *refs):
    count = 1 + max(segment[0] for segment in segments)
    ins, outs = refs[: 2 * count], refs[2 * count :]
    for source, base, parts, tiles, mask, inner, target, start in segments:
        kept, got = ins[2 * source : 2 * source + 2]
        bit = low_bits(ids[1] // mask, 2)
        for q in range(parts // 2):
            for side, out in ((bit, outs[2 * target]), (1 - bit, outs[2 * target + 1])):
                k = q // inner * 2 * inner + side * inner + q % inner
                span = pl.ds(base + k * tiles, tiles)
                out[start + q * tiles : start + (q + 1) * tiles] = (
                    kept[span].astype(f32) + got[span].astype(f32)
                ).astype(bf16)


def last_bias_kernel(toks, base, count, cols, ids, kept, got, *rest):
    pieces, blocks = rest[:toks], rest[toks]
    span = slice(base, base + count)
    tiles = kept[span].astype(f32) + got[span].astype(f32)
    part_rows, rows = pieces[0].shape
    heads = part_rows // cols
    total = jnp.concatenate(
        [take(tiles, h * (count // heads), cols, rows * toks) for h in range(heads)], axis=0
    )
    for a in range(toks):
        blocks[a] = total[:, a * rows : (a + 1) * rows].astype(bf16)
    for r in range(toks):
        pieces[r][...] = blocks[jnp.bitwise_xor(ids[0], r)]


def across_kernel(segment, ids, kept, got, kept_b, got_b, *outs):
    t = ids[0]
    stride = kept.shape[0] // 2
    step_kernel([(0, 0) + segment], ids, kept_b, got_b, *outs[2:])
    for side, out in ((t, outs[0]), (1 - t, outs[1])):
        span = pl.ds(side * stride, stride)
        out[...] = (kept[span].astype(f32) + got[span].astype(f32)).astype(bf16)


def far_kernel(half, ids, kept, got, kept_b, got_b, kept_out, sent_out, single, other, *scratch):
    groups, blocks = scratch
    t, a = ids[0], ids[1] // half
    groups[t] = kept[...]
    groups[1 - t] = got[...]
    kept_out[...] = groups[a]
    sent_out[...] = groups[1 - a]
    lines = single.shape[0]
    base = kept_b.shape[0] - 2 * lines
    for i in range(lines):
        for j in range(2):
            k = base + 2 * i + j
            blocks[j, i] = (kept_b[k].astype(f32) + got_b[k].astype(f32)).astype(bf16)
    single[...] = blocks[t]
    other[...] = blocks[1 - t]


def close_kernel(kept, got, kept_b, got_b, single, got_single, terms, *outs):
    total = kept[...].astype(f32) + got[...].astype(f32)
    cut, own_width = outs[0].shape
    count = tile_count(cut, own_width)
    for k in range(3):
        outs[k][...] = take(total, k * count, cut, own_width)
    total = kept_b[:count].astype(f32) + got_b[:count].astype(f32)
    outs[3][...] = take(total, 0, cut, own_width)
    total = single[...].astype(f32) + got_single[...].astype(f32)
    outs[4][...] = take(total, 0, cut, outs[4].shape[1])
    outs[5][...] = jnp.sum(terms[...], axis=0)


def last_kernel(toks, ids, kept, got, kept_b, got_b, moved, final, *rest):
    pieces, blocks = rest[:toks], rest[toks]
    first = kept[...].astype(f32) + got[...].astype(f32)
    second = kept_b[...].astype(f32) + got_b[...].astype(f32)
    _, cut, own_width = moved.shape
    count = tile_count(cut, own_width)
    for k in range(3):
        moved[k] = take(first, k * count, cut, own_width).astype(bf16)
    final[...] = take(second, 0, cut, own_width)
    rows = blocks.shape[2]
    single = take(second, count, cut, rows * toks)
    for a in range(toks):
        blocks[a] = single[:, a * rows : (a + 1) * rows]
    for r in range(toks):
        pieces[r][...] = blocks[jnp.bitwise_xor(ids[0], r)].astype(bf16)


def finish_kernel(moved, *rest):
    parts, outs = rest[:-4], rest[-4:]
    for k in range(3):
        outs[k][...] = moved[k].astype(f32)
    total = parts[0][...].astype(f32)
    for part in parts[1:]:
        total = total + part[...].astype(f32)
    outs[3][...] = total


def exit_kernel(toks, noisy, gain, d_res, d_own, columns, *rest):
    others, (grad_noisy, token, columns_out) = rest[: toks - 1], rest[toks - 1 :]
    token[...] = jnp.zeros(token.shape, f32)
    columns_out[...] = columns[...]
    total = d_own[...]
    for part in others:
        total = total + part[...].astype(f32)
    _, noisy_hat, noisy_inverse = layer_forward(noisy[...].astype(f32), gain[...])
    grad_noisy[...] = (
        d_res[...] + layer_backward(jnp.transpose(total), gain[...], noisy_hat, noisy_inverse)
    ).astype(bf16)


def set_heads(toks, ids, parts, grads):
    part_rows = parts[0].shape[0]
    for r in range(toks):
        start = pl.multiple_of(jnp.bitwise_xor(ids[0], r) * part_rows, part_rows)
        grads[pl.ds(start, part_rows), :] = parts[r][...].astype(f32)


def pair_weight_kernel(toks, ids, columns, *rest):
    parts, (weight_grad, grads) = rest[:toks], rest[toks:]
    set_heads(toks, ids, parts, grads)
    cols, _, channels = columns.shape
    heads = weight_grad.shape[1]
    sums = jnp.zeros((heads, channels), f32)
    for j in range(cols):
        lines = grads[pl.ds(j, heads, stride=cols), :].astype(bf16)
        sums = sums + mm(lines, columns[j])
    for n in range(weight_grad.shape[0]):
        weight_grad[n] = sums


def pair_kernel(toks, cols, ids, pair, gain, w_pair, *rest):
    parts, (grad_pair, spread_out, grads) = rest[:toks], rest[toks:]
    set_heads(toks, ids, parts, grads)
    rows = parts[0].shape[1]
    _, pair_hat, pair_inverse = layer_forward(pair[...].astype(f32), gain[...])
    spread, row_col = pair_weight_rows(w_pair[...], w_pair.shape[0], cols)
    turned = jnp.transpose(grads[...]).astype(bf16)
    for j in range(cols):
        spread_out[pl.ds(j, rows, stride=cols), :] = mm(
            turned, jnp.where(row_col == j, spread, 0.0).astype(bf16)
        )
    grad_pair[...] = layer_backward(
        spread_out[...], gain[...], pair_hat, pair_inverse
    ).astype(bf16)


def swap_copy(value, mask):
    size = lax.axis_size("copy")
    return lax.ppermute(value, "copy", [(i, i ^ mask) for i in range(size)])


def swap_tok(value, mask):
    size = lax.axis_size("tok")
    return lax.ppermute(value, "tok", [(i, i ^ mask) for i in range(size)])


def exchange(value):
    return lax.all_to_all(value, ("copy", "tok"), 0, 0)


def per_device(
    noisy,
    single,
    pair,
    restype,
    chain,
    keymask,
    restype_table,
    norm_gain,
    pair_gain,
    trans_gain,
    w_query,
    w_key,
    w_value,
    w_out,
    w_pair,
    chain_weight,
    w_hidden_gate,
    w_hidden_up,
    w_down,
    cotangent,
):
    copies = lax.axis_size("copy")
    toks = lax.axis_size("tok")
    _, rows, width = noisy.shape
    cols = pair.shape[1]
    channels = pair.shape[2]
    heads = w_pair.shape[1]
    head_width = width // heads
    own_heads = heads // toks
    own_width = own_heads * head_width
    tokens = rows * toks
    hidden = w_down.shape[0]
    cut = width // copies
    devices = copies * toks
    ids = jnp.stack([lax.axis_index("tok"), lax.axis_index("copy")]).astype(jnp.int32)
    where_am_i = (ids, SMEM)
    noisy2 = noisy.reshape(rows, width)
    pair2 = pair.reshape(rows * cols, channels)
    pair_gain2 = pair_gain.reshape(1, channels)
    norm_gain2 = norm_gain.reshape(1, width)

    weights3 = [w_query, w_key, w_value]
    if own_width % 128:
        weights3 = [
            lax.dynamic_slice_in_dim(w, ids[0] * own_width, own_width, axis=1) for w in weights3
        ]
    small = [noisy2, single, restype.reshape(1, rows), restype_table, norm_gain, pair2, pair_gain2]
    small += [w_pair.T, chain.reshape(1, tokens), keymask.reshape(1, tokens)]
    entered = call(
        functools.partial(enter_kernel, toks, cols),
        "enter",
        [where_am_i]
        + [(array, "fetch") for array in small]
        + [(chain_weight, SMEM)],
        [((rows, width), bf16), ((cols, rows, channels), bf16)]
        + [((tokens, 128), f32), ((1, tokens), f32), ((toks, own_heads * cols, rows), bf16)],
        [VMEM((rows * cols, channels), f32), VMEM((heads * cols, rows), f32)],
        flops=2 * heads * cols * rows * channels * cols,
        limit=60,
    )
    x_own, columns, facts, chain_row, bias_mine = entered
    near = 4
    far = copies // near
    x_parts = [x_own] + [swap_tok(x_own, r) for r in range(1, toks)]
    by_tok = call(
        functools.partial(split_kernel, far),
        "split_far",
        [bias_mine] + [swap_copy(bias_mine, m * near) for m in range(1, far)],
        [((far, own_heads * cols, rows), bf16)] * toks,
        deps=x_parts[1:],
    )
    (slices,) = call(
        stage_kernel,
        "stage",
        [where_am_i] + [(w, ANY) for w in weights3],
        [((3, width, own_width), bf16)],
        [pltpu.SemaphoreType.DMA((3,))],
        deps=[by_tok[0]],
    )
    (lines,) = call(
        join_kernel,
        "join_tok",
        [by_tok[0]] + [swap_tok(by_tok[r], r) for r in range(1, toks)],
        [((toks, far, own_heads * cols, rows), bf16)],
        deps=[slices],
    )
    x, query, key, value = call(
        functools.partial(project_kernel, toks),
        "project",
        [where_am_i, slices] + x_parts,
        [((tokens, width), bf16)] + [((own_width, tokens), bf16)] * 3,
        flops=6 * tokens * width * own_width,
    )
    (lines,) = call(
        join_kernel,
        "join_y",
        [lines, swap_copy(lines, 2)],
        [((2,) + lines.shape, bf16)],
        deps=[value],
    )
    biases = [lines, swap_copy(lines, 1)]
    done = call(
        functools.partial(attention_kernel, copies, toks, near, cols, head_width),
        "attention",
        [where_am_i, query, key, value] + biases + [facts, chain_row],
        [((own_heads, tokens, tokens), bf16), ((tokens, own_width), bf16)]
        + [((rows, own_width), bf16)] * toks,
        [VMEM((copies, toks, own_heads * cols, rows), bf16)],
        flops=4 * tokens * tokens * own_width,
        limit=32,
    )
    weights, att, pieces = done[0], done[1], done[2:]
    att_parts = [pieces[0]] + [swap_tok(pieces[r], r) for r in range(1, toks)]

    d_hidden, upstream, noisy3, trans_gain2 = call(
        down_kernel,
        "down",
        [cotangent.reshape(rows, width), w_down, noisy2, trans_gain.reshape(1, width)],
        [((rows, hidden), f32), ((rows, width), bf16), ((rows, width), bf16), ((1, width), f32)],
        flops=2 * rows * hidden * width,
    )
    chunk = hidden // 3
    results = call(
        functools.partial(hidden_kernel, toks, chunk),
        "hidden",
        [where_am_i, noisy3, upstream, d_hidden, trans_gain2]
        + att_parts
        + [w_out, w_hidden_gate, w_hidden_up],
        [((rows, width), f32), ((rows, width), bf16)] + [((own_width, rows), bf16)] * toks,
        flops=2 * rows * width * (2 * width + 4 * hidden),
    )
    d_res, d_res_b, d_att = results[0], results[1], results[2:]
    d_att_parts = [d_att[0]] + [swap_tok(d_att[r], r) for r in range(1, toks)]
    bias_tiles = own_heads * tile_count(cols, tokens)
    bias_shape = (copies // 2 * bias_tiles, 16, 128)
    d_query, d_key, d_value, bias_kept, bias_sent, d_res_b = call(
        functools.partial(backward_kernel, copies, toks, cols, head_width),
        "backward",
        [where_am_i, query, key, value, weights] + d_att_parts + [d_res_b],
        [((own_width, tokens), bf16)] * 3 + [(bias_shape, bf16)] * 2 + [((rows, width), bf16)],
        [VMEM((toks, own_width, rows), bf16), VMEM((tokens, tokens), bf16)],
        flops=8 * tokens * tokens * own_width,
        limit=32,
    )
    d_res_parts = [d_res_b] + [swap_tok(d_res_b, r) for r in range(1, toks)]
    bias_got = swap_copy(bias_sent, 2)

    wide_tiles = tile_count(cut, own_width)
    single_tiles = tile_count(cut, tokens)
    first_tiles, second_tiles = 3 * wide_tiles, wide_tiles + single_tiles
    found = call(
        functools.partial(first_kernel, copies, toks),
        "first",
        [where_am_i, slices, x, d_query, d_key, d_value],
        [((copies // 2 * first_tiles, 16, 128), bf16)] * 2
        + [((width, rows), f32), ((width, tokens), f32)]
        + [((width, rows), bf16)] * (toks - 1),
        [VMEM((own_width, width), f32), VMEM((toks, width, rows), f32)],
        flops=12 * tokens * width * own_width,
    )
    kept, sent, d_own, single_all = found[:4]
    got = swap_copy(sent, 1)
    d_others = [swap_tok(found[3 + r], r) for r in range(1, toks)]

    def step(name, pairs, segments, deps=()):
        filled, full, masks_of = {}, [], {}
        for source, base, parts, tiles, mask, left, target in segments:
            inner = 1 << sum(1 for other in left if other < mask)
            start = filled.get(target, 0)
            full.append((source, base, parts, tiles, mask, inner, target, start))
            filled[target] = start + parts // 2 * tiles
            masks_of[target] = mask
        outs = []
        for target in range(len(filled)):
            outs += [((filled[target], 16, 128), bf16)] * 2
        results = call(
            functools.partial(step_kernel, full),
            name,
            [where_am_i] + [array for one in pairs for array in one],
            outs,
            deps=deps,
        )
        return [
            (results[2 * n], swap_copy(results[2 * n + 1], masks_of[n]))
            for n in range(len(filled))
        ]

    masks = [1 << b for b in range(1, copies.bit_length() - 1)]
    masks_b = masks[1:] + masks[:1]
    kept_b, sent_b = call(
        functools.partial(second_kernel, copies, toks),
        "second",
        [where_am_i, att, single_all, bias_kept, bias_got] + d_res_parts,
        [((copies // 2 * second_tiles + copies // 4 * bias_tiles, 16, 128), bf16)] * 2,
        [VMEM((tokens, width), bf16), VMEM((width, own_width), f32)],
        flops=20 * tokens * width * own_width,
    )
    got_b = swap_copy(sent_b, 1)

    grad_noisy, exited, columns = call(
        functools.partial(exit_kernel, toks),
        "exit",
        [noisy3, norm_gain2, d_res, d_own, columns] + d_others,
        [((rows, width), bf16), ((8, 128), f32), (columns.shape, bf16)],
    )
    pairs = [(kept, got), (kept_b, got_b)]
    parts = copies // 2
    for n, (mask, mask_b) in enumerate(zip(masks, masks_b)):
        segments = [
            (0, 0, parts, first_tiles, mask, masks[n:], 0),
            (1, 0, parts, second_tiles, mask_b, masks_b[n:], 1),
        ]
        bias_base = parts * second_tiles
        if n + 1 < len(masks):
            segments.append((1, bias_base, parts // 2, bias_tiles, mask_b, masks_b[n:-1], 1))
        else:
            bias_ready = pairs[1]
            if toks == 2:
                break
        pairs = step("step_%d" % n, pairs, segments, deps=[exited] if n == 1 else ())
        parts //= 2
    if toks == 2:
        kept, sent, kept_b, sent_b = call(
            functools.partial(across_kernel, (2, second_tiles, masks_b[-1], 1, 0, 0)),
            "across",
            [where_am_i] + [array for one in pairs for array in one],
            [((first_tiles, 16, 128), bf16)] * 2 + [((second_tiles, 16, 128), bf16)] * 2,
        )
        pairs = [(kept, swap_tok(sent, 1)), (kept_b, swap_copy(sent_b, masks_b[-1]))]
    bias_pieces = call(
        functools.partial(last_bias_kernel, toks, bias_base, bias_tiles, cols),
        "last_bias",
        [where_am_i, *bias_ready],
        [((own_heads * cols, rows), bf16)] * toks,
        [VMEM((toks, own_heads * cols, rows), bf16)],
        deps=[pairs[0][0]],
    )
    bias_pieces = [bias_pieces[0]] + [swap_tok(bias_pieces[r], r) for r in range(1, toks)]
    ready = [pairs[0][1], pairs[1][1]]
    if toks == 2:
        lines = single_tiles // 2
        kept, sent, single_kept, single_sent = call(
            functools.partial(far_kernel, copies // 2),
            "far",
            [where_am_i, *pairs[0], *pairs[1]],
            [((first_tiles, 16, 128), bf16)] * 2 + [((lines, 16, 128), bf16)] * 2,
            [VMEM((2, first_tiles, 16, 128), bf16), VMEM((2, lines, 16, 128), bf16)],
            deps=bias_pieces[1:],
        )
        pairs[0] = (kept, swap_copy(sent, copies // 2))
        single_pair = (single_kept, swap_tok(single_sent, 1))
        ready = [pairs[0][1], single_pair[1]]

    group = copies // toks
    swaps = []
    for c in range(copies):
        for t in range(toks):
            swaps.append((c * toks + t, (t * group + c % group) * toks + c // group))

    (weight_grad,) = call(
        functools.partial(pair_weight_kernel, toks),
        "pair_weight",
        [where_am_i, columns] + bias_pieces,
        [((devices, heads, channels), f32)],
        [VMEM((heads * cols, rows), f32)],
        flops=2 * heads * cols * rows * channels * cols,
        deps=ready,
    )
    (grad_pair,) = call(
        functools.partial(pair_kernel, toks, cols),
        "pair",
        [where_am_i, pair2, pair_gain2, w_pair.T] + bias_pieces,
        [((rows * cols, channels), bf16)],
        [VMEM((rows * cols, channels), f32), VMEM((heads * cols, rows), f32)],
        flops=2 * heads * cols * rows * channels * cols,
    )
    weight_terms = exchange(weight_grad)
    if toks == 2:
        grad_query, grad_key, grad_value, grad_out, grad_single, weight_grad = call(
            close_kernel,
            "close",
            [*pairs[0], *pairs[1], *single_pair, weight_terms],
            [((cut, own_width), f32)] * 4 + [((cut, rows), f32), ((heads, channels), f32)],
        )
    else:
        last = call(
            functools.partial(last_kernel, toks),
            "last",
            [where_am_i, *pairs[0], *pairs[1]],
            [((3, cut, own_width), bf16), ((cut, own_width), f32)] + [((cut, rows), bf16)] * toks,
            [VMEM((toks, cut, rows), f32)],
        )
        weight_grad = jnp.sum(weight_terms, axis=0)
        grad_out, singles = last[1], last[2:]
        singles = [singles[0]] + [swap_tok(singles[r], r) for r in range(1, toks)]
        moved = lax.ppermute(last[0], ("copy", "tok"), swaps)
        grad_query, grad_key, grad_value, grad_single = call(
            finish_kernel,
            "finish",
            [moved] + singles,
            [((cut, own_width), f32)] * 3 + [((cut, rows), f32)],
        )
    return (
        grad_noisy[None],
        grad_single.T,
        grad_pair.reshape(rows, cols, channels),
        grad_query.T,
        grad_key.T,
        grad_value.T,
        grad_out.T,
        weight_grad.T,
    )


def solution(mesh):
    placed = (
        P("copy", "tok", None),
        P("tok", None),
        P("tok", "copy", None),
        P("tok"),
    ) + (P(),) * 15 + (P("copy", "tok", None),)
    return jax.shard_map(
        per_device,
        mesh=mesh,
        in_specs=placed,
        out_specs=(
            P("copy", "tok", None),
            P("tok", "copy"),
            P("tok", "copy", None),
            P("tok", "copy"),
            P("tok", "copy"),
            P("tok", "copy"),
            P("tok", "copy"),
            P(),
        ),
        check_vma=False,
    )
```

```python
import functools

import jax
import jax.numpy as jnp
from jax import lax
from jax.experimental import pallas as pl
from jax.experimental.pallas import tpu as pltpu
from jax.sharding import PartitionSpec as P

epsilon = 1e-05
f32 = jnp.float32
bf16 = jnp.bfloat16
VMEM, SMEM, ANY = pltpu.VMEM, pltpu.SMEM, pl.ANY
MIB = 1 << 20


def layer_forward(values, scales):
    average = jnp.mean(values, axis=-1, keepdims=True)
    centred = values - average
    inverse = lax.rsqrt(jnp.mean(centred * centred, axis=-1, keepdims=True) + epsilon)
    normed = centred * inverse
    return (normed * scales, normed, inverse)


def layer_backward(upstream, scales, normed, inverse):
    scaled = upstream * scales
    first_moment = jnp.mean(scaled, axis=-1, keepdims=True)
    second_moment = jnp.mean(scaled * normed, axis=-1, keepdims=True)
    return inverse * (scaled - first_moment - normed * second_moment)


NN = ((1,), (0,))
NT = ((1,), (1,))
TN = ((0,), (0,))


def mm(left, right, dims=NN):
    return lax.dot_general(left, right, (dims, ((), ())), preferred_element_type=f32)


def call(body, name, inputs, outs, scratch=(), flops=0, limit=16, deps=()):
    arrays, specs, moved, fetched = [], [], 0, []
    for item in inputs:
        array, space = item if isinstance(item, tuple) else (item, VMEM)
        if space == "fetch":
            fetched.append(len(arrays))
            space = pltpu.HBM
        arrays.append(array)
        specs.append(pl.BlockSpec(memory_space=space))
        moved += array.size * array.dtype.itemsize
    for shape, kind, *_ in outs:
        size = jnp.dtype(kind).itemsize
        for extent in shape:
            size *= extent
        moved += size
    read = len(arrays)
    for array in deps:
        arrays.append(array)
        specs.append(pl.BlockSpec(memory_space=ANY))
    extra = [VMEM(arrays[k].shape, arrays[k].dtype) for k in fetched]
    if fetched:
        extra.append(pltpu.SemaphoreType.DMA((len(fetched),)))

    def whole(*refs):
        refs = list(refs[:read]) + list(refs[read + len(deps) :])
        if fetched:
            held, sem = refs[-1 - len(fetched) : -1], refs[-1]
            refs = refs[: -1 - len(fetched)]
            transfers = []
            for n, k in enumerate(fetched):
                transfer = pltpu.make_async_copy(refs[k], held[n], sem.at[n])
                transfer.start()
                transfers.append(transfer)
                refs[k] = held[n]
            for transfer in transfers:
                transfer.wait()
        body(*refs)

    return pl.pallas_call(
        whole,
        name=name,
        out_shape=[jax.ShapeDtypeStruct(one[0], one[1]) for one in outs],
        in_specs=specs,
        out_specs=[pl.BlockSpec(memory_space=(*one, VMEM)[2]) for one in outs],
        scratch_shapes=list(scratch) + extra,
        compiler_params=pltpu.CompilerParams(vmem_limit_bytes=limit * MIB),
        cost_estimate=pl.CostEstimate(flops=flops, bytes_accessed=moved, transcendentals=0),
    )(*arrays)


def low_bits(index, size):
    return jnp.bitwise_and(index, size - 1)


def pair_weight_rows(w_pair, head_count, cols):
    rows = head_count * cols
    shift = cols.bit_length() - 1
    head = lax.shift_right_logical(
        lax.broadcasted_iota(jnp.int32, (rows, head_count), 0), jnp.int32(shift)
    )
    pick = (head == lax.broadcasted_iota(jnp.int32, (rows, head_count), 1)).astype(f32)
    spread = mm(pick.astype(bf16), w_pair)
    row_col = low_bits(lax.broadcasted_iota(jnp.int32, spread.shape, 0), cols)
    return spread, row_col


def own_slice(weight, t, own_width):
    if weight.shape[1] == own_width:
        return weight
    return weight.at[:, pl.ds(pl.multiple_of(t * own_width, own_width), own_width)]


def enter_kernel(toks, cols, ids, *rest):
    noisy, single, restype, table, gain, pair, pair_gain, w_pair, chain, keymask = rest[:10]
    chain_weight, x_out, columns, facts_out, chain_out, bias_out, rounded, bias = rest[10:]
    t = ids[0]
    rows = noisy.shape[0]
    pair_scaled, _, _ = layer_forward(pair[...].astype(f32), pair_gain[...])
    rounded[...] = pair_scaled.astype(bf16).astype(f32)
    head_count = w_pair.shape[0]
    spread, row_col = pair_weight_rows(w_pair[...], head_count, cols)
    total = jnp.zeros((head_count * cols, rows), f32)
    for j in range(cols):
        column = rounded[pl.ds(j, rows, stride=cols), :].astype(bf16)
        columns[j] = column
        total = total + mm(jnp.where(row_col == j, spread, 0.0).astype(bf16), column, NT)
    bias[...] = total
    part = bias_out.shape[1]
    for r in range(toks):
        start = pl.multiple_of(jnp.bitwise_xor(t, r) * part, part)
        bias_out[r] = bias[pl.ds(start, part), :].astype(bf16)
    normed_scaled, _, _ = layer_forward(noisy[...].astype(f32), gain[...])
    types = table.shape[0]
    onehot = (lax.broadcasted_iota(jnp.int32, (types, rows), 0) == restype[...]).astype(f32)
    condition = single[...].astype(f32) + mm(onehot.astype(bf16), table[...], TN)
    x_out[...] = (normed_scaled + condition).astype(bf16)
    chain_row = chain[...]
    tokens = chain_row.shape[1]
    own_heads = head_count // toks
    keep_row = keymask[...].astype(f32)
    line = lax.broadcasted_iota(jnp.int32, (128, tokens), 0)
    facts = jnp.where(line == 0, chain_row.astype(f32), 0.0) + jnp.where(line == 1, keep_row, 0.0)
    for h in range(own_heads):
        weight_row = jnp.zeros((1, tokens), f32)
        for m in range(chain_weight.shape[0]):
            weight_row = jnp.where(chain_row == m, chain_weight[m, t * own_heads + h], weight_row)
        facts = jnp.where(line == 2 + h, weight_row, facts)
    facts_out[...] = jnp.transpose(facts)
    chain_out[...] = chain_row.astype(f32)


def stage_kernel(ids, *rest):
    weights, (slices, sem) = rest[:3], rest[3:]
    transfers = []
    for k in range(3):
        transfer = pltpu.make_async_copy(
            own_slice(weights[k], ids[0], slices.shape[2]), slices.at[k], sem.at[k]
        )
        transfer.start()
        transfers.append(transfer)
    for transfer in transfers:
        transfer.wait()


def project_kernel(toks, ids, slices, *rest):
    parts = rest[:toks]
    x_out, outs = rest[toks], rest[toks + 1 :]
    t = ids[0]
    rows = parts[0].shape[0]
    for r in range(toks):
        start = pl.multiple_of(jnp.bitwise_xor(t, r) * rows, rows)
        x_out[pl.ds(start, rows), :] = parts[r][...]
    x = x_out[...]
    for k in range(3):
        outs[k][...] = jnp.transpose(mm(x, slices[k])).astype(bf16)


def split_kernel(count, *refs):
    for n in range(count):
        for r, out in enumerate(refs[count:]):
            out[n] = refs[n][r]


def join_kernel(*refs):
    for n, ref in enumerate(refs[:-1]):
        refs[-1][n] = ref[...]


def attention_kernel(copies, toks, near, cols, head_width, ids, query, key, value, *rest):
    biases, (facts, chain, weights_out, att_out) = rest[:2], rest[2:6]
    pieces, bias = rest[6 : 6 + toks], rest[6 + toks]
    t, low, high = ids[0], low_bits(ids[1], near), ids[1] // near
    for m in range(near):
        for rz in range(copies // near):
            c = jnp.bitwise_xor(high, rz) * near + jnp.bitwise_xor(low, m)
            for r in range(toks):
                bias[c, jnp.bitwise_xor(t, r)] = biases[m % 2][m // 2, r, rz]
    own_heads = weights_out.shape[0]
    tokens = query.shape[1]
    rows = tokens // toks
    same = facts[:, 0:1] == chain[...]
    keep = facts[:, 1:2] > 0.0
    scale = head_width ** (-0.5)
    attended = []
    for h in range(own_heads):
        span = slice(h * head_width, (h + 1) * head_width)
        logits = mm(key[span, :], query[span, :], TN) * scale
        line = slice(h * cols, (h + 1) * cols)
        extra = jnp.concatenate(
            [
                jnp.concatenate(
                    [bias[c, a, line, :] for c in range(copies)], axis=0
                )
                for a in range(toks)
            ],
            axis=1,
        ).astype(f32)
        logits = logits + (extra + jnp.where(same, facts[:, 2 + h : 3 + h], 0.0))
        logits = jnp.where(keep, logits, -1e30)
        exponent = jnp.exp(logits - jnp.max(logits, axis=0, keepdims=True))
        weights = exponent / jnp.sum(exponent, axis=0, keepdims=True)
        weights_b = weights.astype(bf16)
        weights_out[h] = weights_b
        attended.append(mm(value[span, :], weights_b))
    att_out[...] = jnp.transpose(jnp.concatenate(attended, axis=0)).astype(bf16)
    for r in range(toks):
        start = pl.multiple_of(jnp.bitwise_xor(t, r) * rows, rows)
        pieces[r][...] = att_out[pl.ds(start, rows), :]


def down_kernel(upstream, w_down, noisy, gain, d_hidden, upstream_out, noisy_out, gain_out):
    d_hidden[...] = mm(upstream[...], w_down[...], NT)
    upstream_out[...] = upstream[...]
    noisy_out[...] = noisy[...]
    gain_out[...] = gain[...]


def hidden_kernel(toks, chunk, ids, noisy, upstream, d_hidden, gain, *rest):
    parts = rest[:toks]
    held_out, held_gate, held_up = rest[toks : toks + 3]
    d_res_out, d_res_b_out = rest[toks + 3 : toks + 5]
    d_att_outs = rest[toks + 5 :]
    t = ids[0]
    hidden = held_gate.shape[1]
    residual = noisy[...].astype(f32)
    own_width = parts[0].shape[1]
    for r in range(toks):
        start = pl.multiple_of(jnp.bitwise_xor(t, r) * own_width, own_width)
        residual = residual + mm(parts[r][...], held_out[pl.ds(start, own_width), :])
    trans_scaled, trans_hat, trans_inverse = layer_forward(residual, gain[...])
    trans_in = trans_scaled.astype(bf16)
    d_trans = jnp.zeros(residual.shape, f32)
    for k in range(hidden // chunk):
        span = slice(k * chunk, (k + 1) * chunk)
        gate = mm(trans_in, held_gate[:, span])
        up = mm(trans_in, held_up[:, span])
        incoming = d_hidden[:, span]
        sigmoid = jax.nn.sigmoid(gate)
        d_up = (incoming * gate * sigmoid).astype(bf16)
        d_gate = (incoming * up * sigmoid * (1.0 + gate * (1.0 - sigmoid))).astype(bf16)
        d_trans = d_trans + mm(d_gate, held_gate[:, span], NT) + mm(d_up, held_up[:, span], NT)
    d_res = upstream[...].astype(f32) + layer_backward(
        d_trans, gain[...], trans_hat, trans_inverse
    )
    d_res_out[...] = d_res
    d_res_b = d_res.astype(bf16)
    d_res_b_out[...] = d_res_b
    for r in range(toks):
        start = pl.multiple_of(jnp.bitwise_xor(t, r) * own_width, own_width)
        d_att_outs[r][...] = mm(held_out[pl.ds(start, own_width), :], d_res_b, NT).astype(bf16)


def backward_kernel(copies, toks, cols, head_width, ids, query, key, value, weights, *rest):
    parts, d_res_b = rest[:toks], rest[toks]
    d_query, d_key, d_value, bias_kept, bias_sent, d_res_out = rest[toks + 1 : toks + 7]
    blocks, d_logits = rest[toks + 7 :]
    d_res_out[...] = d_res_b[...]
    t = ids[0]
    bit = low_bits(ids[1] // 2, 2)
    heads = weights.shape[0]
    for r in range(toks):
        blocks[jnp.bitwise_xor(t, r)] = parts[r][...]
    d_att = jnp.concatenate([blocks[a] for a in range(toks)], axis=1)
    count = tile_count(cols, query.shape[1])
    scale = head_width ** (-0.5)
    for h in range(weights.shape[0]):
        span = slice(h * head_width, (h + 1) * head_width)
        d_att_h = d_att[span, :]
        weights_b = weights[h]
        d_weights = mm(value[span, :], d_att_h, TN)
        weights_f = weights_b.astype(f32)
        delta = jnp.sum(weights_f * d_weights, axis=0, keepdims=True)
        d_logits_b = (weights_f * (d_weights - delta)).astype(bf16)
        d_logits[...] = d_logits_b
        for k in range(copies // 2):
            for side, out in ((bit, bias_kept), (1 - bit, bias_sent)):
                start = pl.multiple_of((k // 2 * 4 + side * 2 + k % 2) * cols, cols)
                put(out, (k * heads + h) * count, d_logits[pl.ds(start, cols), :])
        d_query[span, :] = (mm(key[span, :], d_logits_b) * scale).astype(bf16)
        d_key[span, :] = (mm(query[span, :], d_logits_b, NT) * scale).astype(bf16)
        d_value[span, :] = mm(d_att_h, weights_b, NT).astype(bf16)


def tile_count(rows, lanes):
    return -(-rows // 16) * -(-lanes // 128)


def put(out, base, value):
    rows, lanes = value.shape
    for i in range(0, rows, 16):
        for j in range(0, lanes, 128):
            part = value[i : i + 16, j : j + 128]
            if part.shape != (16, 128):
                out[base] = jnp.zeros((16, 128), out.dtype)
            out[base, : part.shape[0], : part.shape[1]] = part
            base += 1


def take(tiles, base, rows, lanes):
    across = -(-lanes // 128)
    lines = []
    for i in range(-(-rows // 16)):
        line = [tiles[base + i * across + j] for j in range(across)]
        lines.append(jnp.concatenate(line, axis=1) if across > 1 else line[0])
    whole = jnp.concatenate(lines, axis=0) if len(lines) > 1 else lines[0]
    return whole[:rows, :lanes]


def cut_wide(copies, toks, core, base, stride, grad, kept, sent):
    group = copies // toks
    cut, depth = grad.shape[1] // copies, grad.shape[1] // toks
    for side, out in ((core, kept), (1 - core, sent)):
        for q in range(copies // 2):
            h = 2 * q // group
            first = pl.multiple_of((2 * q - h * group + side) * cut, 8)
            part = grad[pl.ds(first, cut), h * depth : (h + 1) * depth]
            put(out, q * stride + base, part.astype(bf16))


def first_kernel(copies, toks, ids, slices, x, d_query, d_key, d_value, *rest):
    kept, sent, d_own, single_all = rest[:4]
    d_others, (wide, d_inputs) = rest[4 : 3 + toks], rest[3 + toks :]
    t, core = ids[0], low_bits(ids[1], 2)
    rows = d_own.shape[1]
    cut = x.shape[1] // copies
    count = tile_count(cut, d_query.shape[0])
    stride = 3 * count
    for k, part in enumerate((d_query, d_key, d_value)):
        wide[...] = mm(part[...], x[...])
        cut_wide(copies, toks, core, k * count, stride, wide, kept, sent)
    total = mm(slices[0], d_query[...]) + mm(slices[1], d_key[...])
    total = total + mm(slices[2], d_value[...])
    single_all[...] = total
    for a in range(toks):
        d_inputs[a] = total[:, a * rows : (a + 1) * rows]
    d_own[...] = d_inputs[t]
    for r in range(1, toks):
        d_others[r - 1][...] = d_inputs[jnp.bitwise_xor(t, r)].astype(bf16)


def second_kernel(copies, toks, ids, att, single_all, bias_kept, bias_got, *rest):
    d_res_parts, (kept, sent, d_res, narrow) = rest[:toks], rest[toks:]
    t, core = ids[0], low_bits(ids[1], 2)
    rows = d_res_parts[0].shape[0]
    cut = narrow.shape[0] // copies
    count = tile_count(cut, narrow.shape[1])
    for r in range(toks):
        start = pl.multiple_of(jnp.bitwise_xor(t, r) * rows, rows)
        d_res[pl.ds(start, rows), :] = d_res_parts[r][...]
    narrow[...] = mm(d_res[...], att[...], TN)
    stride = count + tile_count(cut, rows * toks)
    base = copies // 2 * stride
    bias_count = bias_kept.shape[0] // (copies // 2)
    for side, out in ((core, kept), (1 - core, sent)):
        for q in range(copies // 2):
            first = pl.multiple_of((2 * q + side) * cut, 8)
            put(out, q * stride, narrow[pl.ds(first, cut), :].astype(bf16))
            put(out, q * stride + count, single_all[pl.ds(first, cut), :].astype(bf16))
        for z in range(copies // 4):
            span = pl.ds((2 * z + side) * bias_count, bias_count)
            out[base + z * bias_count : base + (z + 1) * bias_count] = (
                bias_kept[span].astype(f32) + bias_got[span].astype(f32)
            ).astype(bf16)


def step_kernel(segments, ids, *refs):
    count = 1 + max(segment[0] for segment in segments)
    ins, outs = refs[: 2 * count], refs[2 * count :]
    for source, base, parts, tiles, mask, inner, target, start in segments:
        kept, got = ins[2 * source : 2 * source + 2]
        bit = low_bits(ids[1] // mask, 2)
        for q in range(parts // 2):
            for side, out in ((bit, outs[2 * target]), (1 - bit, outs[2 * target + 1])):
                k = q // inner * 2 * inner + side * inner + q % inner
                span = pl.ds(base + k * tiles, tiles)
                out[start + q * tiles : start + (q + 1) * tiles] = (
                    kept[span].astype(f32) + got[span].astype(f32)
                ).astype(bf16)


def last_bias_kernel(toks, base, count, cols, ids, kept, got, *rest):
    pieces, blocks = rest[:toks], rest[toks]
    span = slice(base, base + count)
    tiles = kept[span].astype(f32) + got[span].astype(f32)
    part_rows, rows = pieces[0].shape
    heads = part_rows // cols
    total = jnp.concatenate(
        [take(tiles, h * (count // heads), cols, rows * toks) for h in range(heads)], axis=0
    )
    for a in range(toks):
        blocks[a] = total[:, a * rows : (a + 1) * rows].astype(bf16)
    for r in range(toks):
        pieces[r][...] = blocks[jnp.bitwise_xor(ids[0], r)]


def across_kernel(segment, ids, kept, got, kept_b, got_b, *outs):
    t = ids[0]
    stride = kept.shape[0] // 2
    step_kernel([(0, 0) + segment], ids, kept_b, got_b, *outs[2:])
    for side, out in ((t, outs[0]), (1 - t, outs[1])):
        span = pl.ds(side * stride, stride)
        out[...] = (kept[span].astype(f32) + got[span].astype(f32)).astype(bf16)


def far_kernel(half, ids, kept, got, kept_b, got_b, kept_out, sent_out, single, other, *scratch):
    groups, blocks = scratch
    t, a = ids[0], ids[1] // half
    groups[t] = kept[...]
    groups[1 - t] = got[...]
    kept_out[...] = groups[a]
    sent_out[...] = groups[1 - a]
    lines = single.shape[0]
    base = kept_b.shape[0] - 2 * lines
    for i in range(lines):
        for j in range(2):
            k = base + 2 * i + j
            blocks[j, i] = (kept_b[k].astype(f32) + got_b[k].astype(f32)).astype(bf16)
    single[...] = blocks[t]
    other[...] = blocks[1 - t]


def close_kernel(kept, got, kept_b, got_b, single, got_single, terms, *outs):
    total = kept[...].astype(f32) + got[...].astype(f32)
    cut, own_width = outs[0].shape
    count = tile_count(cut, own_width)
    for k in range(3):
        outs[k][...] = take(total, k * count, cut, own_width)
    total = kept_b[:count].astype(f32) + got_b[:count].astype(f32)
    outs[3][...] = take(total, 0, cut, own_width)
    total = single[...].astype(f32) + got_single[...].astype(f32)
    outs[4][...] = take(total, 0, cut, outs[4].shape[1])
    outs[5][...] = jnp.sum(terms[...], axis=0)


def last_kernel(toks, ids, kept, got, kept_b, got_b, moved, final, *rest):
    pieces, blocks = rest[:toks], rest[toks]
    first = kept[...].astype(f32) + got[...].astype(f32)
    second = kept_b[...].astype(f32) + got_b[...].astype(f32)
    _, cut, own_width = moved.shape
    count = tile_count(cut, own_width)
    for k in range(3):
        moved[k] = take(first, k * count, cut, own_width).astype(bf16)
    final[...] = take(second, 0, cut, own_width)
    rows = blocks.shape[2]
    single = take(second, count, cut, rows * toks)
    for a in range(toks):
        blocks[a] = single[:, a * rows : (a + 1) * rows]
    for r in range(toks):
        pieces[r][...] = blocks[jnp.bitwise_xor(ids[0], r)].astype(bf16)


def finish_kernel(moved, *rest):
    parts, outs = rest[:-4], rest[-4:]
    for k in range(3):
        outs[k][...] = moved[k].astype(f32)
    total = parts[0][...].astype(f32)
    for part in parts[1:]:
        total = total + part[...].astype(f32)
    outs[3][...] = total


def exit_kernel(toks, noisy, gain, d_res, d_own, columns, *rest):
    others, (grad_noisy, token, columns_out) = rest[: toks - 1], rest[toks - 1 :]
    token[...] = jnp.zeros(token.shape, f32)
    columns_out[...] = columns[...]
    total = d_own[...]
    for part in others:
        total = total + part[...].astype(f32)
    _, noisy_hat, noisy_inverse = layer_forward(noisy[...].astype(f32), gain[...])
    grad_noisy[...] = (
        d_res[...] + layer_backward(jnp.transpose(total), gain[...], noisy_hat, noisy_inverse)
    ).astype(bf16)


def set_heads(toks, ids, parts, grads):
    part_rows = parts[0].shape[0]
    for r in range(toks):
        start = pl.multiple_of(jnp.bitwise_xor(ids[0], r) * part_rows, part_rows)
        grads[pl.ds(start, part_rows), :] = parts[r][...].astype(f32)


def pair_weight_kernel(toks, ids, columns, *rest):
    parts, (weight_grad, grads) = rest[:toks], rest[toks:]
    set_heads(toks, ids, parts, grads)
    cols, rows, channels = columns.shape
    heads = weight_grad.shape[1]
    lines = [grads[pl.ds(j, heads, stride=cols), :].astype(bf16) for j in range(cols)]
    sums = mm(jnp.concatenate(lines, axis=1), columns[...].reshape(cols * rows, channels))
    for n in range(weight_grad.shape[0]):
        weight_grad[n] = sums


def pair_kernel(toks, cols, ids, pair, gain, w_pair, *rest):
    parts, (grad_pair, spread_out, grads) = rest[:toks], rest[toks:]
    set_heads(toks, ids, parts, grads)
    rows = parts[0].shape[1]
    _, pair_hat, pair_inverse = layer_forward(pair[...].astype(f32), gain[...])
    spread, row_col = pair_weight_rows(w_pair[...], w_pair.shape[0], cols)
    turned = jnp.transpose(grads[...]).astype(bf16)
    for j in range(cols):
        spread_out[pl.ds(j, rows, stride=cols), :] = mm(
            turned, jnp.where(row_col == j, spread, 0.0).astype(bf16)
        )
    grad_pair[...] = layer_backward(
        spread_out[...], gain[...], pair_hat, pair_inverse
    ).astype(bf16)


def swap_copy(value, mask):
    size = lax.axis_size("copy")
    return lax.ppermute(value, "copy", [(i, i ^ mask) for i in range(size)])


def swap_tok(value, mask):
    size = lax.axis_size("tok")
    return lax.ppermute(value, "tok", [(i, i ^ mask) for i in range(size)])


def exchange(value):
    return lax.all_to_all(value, ("copy", "tok"), 0, 0)


def per_device(
    noisy,
    single,
    pair,
    restype,
    chain,
    keymask,
    restype_table,
    norm_gain,
    pair_gain,
    trans_gain,
    w_query,
    w_key,
    w_value,
    w_out,
    w_pair,
    chain_weight,
    w_hidden_gate,
    w_hidden_up,
    w_down,
    cotangent,
):
    copies = lax.axis_size("copy")
    toks = lax.axis_size("tok")
    _, rows, width = noisy.shape
    cols = pair.shape[1]
    channels = pair.shape[2]
    heads = w_pair.shape[1]
    head_width = width // heads
    own_heads = heads // toks
    own_width = own_heads * head_width
    tokens = rows * toks
    hidden = w_down.shape[0]
    cut = width // copies
    devices = copies * toks
    ids = jnp.stack([lax.axis_index("tok"), lax.axis_index("copy")]).astype(jnp.int32)
    where_am_i = (ids, SMEM)
    noisy2 = noisy.reshape(rows, width)
    pair2 = pair.reshape(rows * cols, channels)
    pair_gain2 = pair_gain.reshape(1, channels)
    norm_gain2 = norm_gain.reshape(1, width)

    weights3 = [w_query, w_key, w_value]
    if own_width % 128:
        weights3 = [
            lax.dynamic_slice_in_dim(w, ids[0] * own_width, own_width, axis=1) for w in weights3
        ]
    small = [noisy2, single, restype.reshape(1, rows), restype_table, norm_gain, pair2, pair_gain2]
    small += [w_pair.T, chain.reshape(1, tokens), keymask.reshape(1, tokens)]
    entered = call(
        functools.partial(enter_kernel, toks, cols),
        "enter",
        [where_am_i]
        + [(array, "fetch") for array in small]
        + [(chain_weight, SMEM)],
        [((rows, width), bf16), ((cols, rows, channels), bf16)]
        + [((tokens, 128), f32), ((1, tokens), f32), ((toks, own_heads * cols, rows), bf16)],
        [VMEM((rows * cols, channels), f32), VMEM((heads * cols, rows), f32)],
        flops=2 * heads * cols * rows * channels * cols,
        limit=60,
    )
    x_own, columns, facts, chain_row, bias_mine = entered
    near = 4
    far = copies // near
    x_parts = [x_own] + [swap_tok(x_own, r) for r in range(1, toks)]
    by_tok = call(
        functools.partial(split_kernel, far),
        "split_far",
        [bias_mine] + [swap_copy(bias_mine, m * near) for m in range(1, far)],
        [((far, own_heads * cols, rows), bf16)] * toks,
        deps=x_parts[1:],
    )
    (slices,) = call(
        stage_kernel,
        "stage",
        [where_am_i] + [(w, ANY) for w in weights3],
        [((3, width, own_width), bf16)],
        [pltpu.SemaphoreType.DMA((3,))],
        deps=[by_tok[0]],
    )
    (lines,) = call(
        join_kernel,
        "join_tok",
        [by_tok[0]] + [swap_tok(by_tok[r], r) for r in range(1, toks)],
        [((toks, far, own_heads * cols, rows), bf16)],
        deps=[slices],
    )
    x, query, key, value = call(
        functools.partial(project_kernel, toks),
        "project",
        [where_am_i, slices] + x_parts,
        [((tokens, width), bf16)] + [((own_width, tokens), bf16)] * 3,
        flops=6 * tokens * width * own_width,
    )
    (lines,) = call(
        join_kernel,
        "join_y",
        [lines, swap_copy(lines, 2)],
        [((2,) + lines.shape, bf16)],
        deps=[value],
    )
    biases = [lines, swap_copy(lines, 1)]
    done = call(
        functools.partial(attention_kernel, copies, toks, near, cols, head_width),
        "attention",
        [where_am_i, query, key, value] + biases + [facts, chain_row],
        [((own_heads, tokens, tokens), bf16), ((tokens, own_width), bf16)]
        + [((rows, own_width), bf16)] * toks,
        [VMEM((copies, toks, own_heads * cols, rows), bf16)],
        flops=4 * tokens * tokens * own_width,
        limit=32,
    )
    weights, att, pieces = done[0], done[1], done[2:]
    att_parts = [pieces[0]] + [swap_tok(pieces[r], r) for r in range(1, toks)]

    d_hidden, upstream, noisy3, trans_gain2 = call(
        down_kernel,
        "down",
        [cotangent.reshape(rows, width), w_down, noisy2, trans_gain.reshape(1, width)],
        [((rows, hidden), f32), ((rows, width), bf16), ((rows, width), bf16), ((1, width), f32)],
        flops=2 * rows * hidden * width,
    )
    chunk = hidden // 3
    results = call(
        functools.partial(hidden_kernel, toks, chunk),
        "hidden",
        [where_am_i, noisy3, upstream, d_hidden, trans_gain2]
        + att_parts
        + [w_out, w_hidden_gate, w_hidden_up],
        [((rows, width), f32), ((rows, width), bf16)] + [((own_width, rows), bf16)] * toks,
        flops=2 * rows * width * (2 * width + 4 * hidden),
    )
    d_res, d_res_b, d_att = results[0], results[1], results[2:]
    d_att_parts = [d_att[0]] + [swap_tok(d_att[r], r) for r in range(1, toks)]
    bias_tiles = own_heads * tile_count(cols, tokens)
    bias_shape = (copies // 2 * bias_tiles, 16, 128)
    d_query, d_key, d_value, bias_kept, bias_sent, d_res_b = call(
        functools.partial(backward_kernel, copies, toks, cols, head_width),
        "backward",
        [where_am_i, query, key, value, weights] + d_att_parts + [d_res_b],
        [((own_width, tokens), bf16)] * 3 + [(bias_shape, bf16)] * 2 + [((rows, width), bf16)],
        [VMEM((toks, own_width, rows), bf16), VMEM((tokens, tokens), bf16)],
        flops=8 * tokens * tokens * own_width,
        limit=32,
    )
    d_res_parts = [d_res_b] + [swap_tok(d_res_b, r) for r in range(1, toks)]
    bias_got = swap_copy(bias_sent, 2)

    wide_tiles = tile_count(cut, own_width)
    single_tiles = tile_count(cut, tokens)
    first_tiles, second_tiles = 3 * wide_tiles, wide_tiles + single_tiles
    found = call(
        functools.partial(first_kernel, copies, toks),
        "first",
        [where_am_i, slices, x, d_query, d_key, d_value],
        [((copies // 2 * first_tiles, 16, 128), bf16)] * 2
        + [((width, rows), f32), ((width, tokens), f32)]
        + [((width, rows), bf16)] * (toks - 1),
        [VMEM((own_width, width), f32), VMEM((toks, width, rows), f32)],
        flops=12 * tokens * width * own_width,
    )
    kept, sent, d_own, single_all = found[:4]
    got = swap_copy(sent, 1)
    d_others = [swap_tok(found[3 + r], r) for r in range(1, toks)]

    def step(name, pairs, segments, deps=()):
        filled, full, masks_of = {}, [], {}
        for source, base, parts, tiles, mask, left, target in segments:
            inner = 1 << sum(1 for other in left if other < mask)
            start = filled.get(target, 0)
            full.append((source, base, parts, tiles, mask, inner, target, start))
            filled[target] = start + parts // 2 * tiles
            masks_of[target] = mask
        outs = []
        for target in range(len(filled)):
            outs += [((filled[target], 16, 128), bf16)] * 2
        results = call(
            functools.partial(step_kernel, full),
            name,
            [where_am_i] + [array for one in pairs for array in one],
            outs,
            deps=deps,
        )
        return [
            (results[2 * n], swap_copy(results[2 * n + 1], masks_of[n]))
            for n in range(len(filled))
        ]

    masks = [1 << b for b in range(1, copies.bit_length() - 1)]
    masks_b = masks[1:] + masks[:1]
    kept_b, sent_b = call(
        functools.partial(second_kernel, copies, toks),
        "second",
        [where_am_i, att, single_all, bias_kept, bias_got] + d_res_parts,
        [((copies // 2 * second_tiles + copies // 4 * bias_tiles, 16, 128), bf16)] * 2,
        [VMEM((tokens, width), bf16), VMEM((width, own_width), f32)],
        flops=20 * tokens * width * own_width,
    )
    got_b = swap_copy(sent_b, 1)

    grad_noisy, exited, columns = call(
        functools.partial(exit_kernel, toks),
        "exit",
        [noisy3, norm_gain2, d_res, d_own, columns] + d_others,
        [((rows, width), bf16), ((8, 128), f32), (columns.shape, bf16)],
    )
    pairs = [(kept, got), (kept_b, got_b)]
    parts = copies // 2
    for n, (mask, mask_b) in enumerate(zip(masks, masks_b)):
        segments = [
            (0, 0, parts, first_tiles, mask, masks[n:], 0),
            (1, 0, parts, second_tiles, mask_b, masks_b[n:], 1),
        ]
        bias_base = parts * second_tiles
        if n + 1 < len(masks):
            segments.append((1, bias_base, parts // 2, bias_tiles, mask_b, masks_b[n:-1], 1))
        else:
            bias_ready = pairs[1]
            if toks == 2:
                break
        pairs = step("step_%d" % n, pairs, segments, deps=[exited] if n == 1 else ())
        parts //= 2
    if toks == 2:
        kept, sent, kept_b, sent_b = call(
            functools.partial(across_kernel, (2, second_tiles, masks_b[-1], 1, 0, 0)),
            "across",
            [where_am_i] + [array for one in pairs for array in one],
            [((first_tiles, 16, 128), bf16)] * 2 + [((second_tiles, 16, 128), bf16)] * 2,
        )
        pairs = [(kept, swap_tok(sent, 1)), (kept_b, swap_copy(sent_b, masks_b[-1]))]
    bias_pieces = call(
        functools.partial(last_bias_kernel, toks, bias_base, bias_tiles, cols),
        "last_bias",
        [where_am_i, *bias_ready],
        [((own_heads * cols, rows), bf16)] * toks,
        [VMEM((toks, own_heads * cols, rows), bf16)],
        deps=[pairs[0][0]],
    )
    bias_pieces = [bias_pieces[0]] + [swap_tok(bias_pieces[r], r) for r in range(1, toks)]
    ready = [pairs[0][1], pairs[1][1]]
    if toks == 2:
        lines = single_tiles // 2
        kept, sent, single_kept, single_sent = call(
            functools.partial(far_kernel, copies // 2),
            "far",
            [where_am_i, *pairs[0], *pairs[1]],
            [((first_tiles, 16, 128), bf16)] * 2 + [((lines, 16, 128), bf16)] * 2,
            [VMEM((2, first_tiles, 16, 128), bf16), VMEM((2, lines, 16, 128), bf16)],
            deps=bias_pieces[1:],
        )
        pairs[0] = (kept, swap_copy(sent, copies // 2))
        single_pair = (single_kept, swap_tok(single_sent, 1))

    group = copies // toks
    swaps = []
    for c in range(copies):
        for t in range(toks):
            swaps.append((c * toks + t, (t * group + c % group) * toks + c // group))

    (weight_grad,) = call(
        functools.partial(pair_weight_kernel, toks),
        "pair_weight",
        [where_am_i, columns] + bias_pieces,
        [((devices, heads, channels), f32)],
        [VMEM((heads * cols, rows), f32)],
        flops=2 * heads * cols * rows * channels * cols,
        deps=ready,
    )
    (grad_pair,) = call(
        functools.partial(pair_kernel, toks, cols),
        "pair",
        [where_am_i, pair2, pair_gain2, w_pair.T] + bias_pieces,
        [((rows * cols, channels), bf16)],
        [VMEM((rows * cols, channels), f32), VMEM((heads * cols, rows), f32)],
        flops=2 * heads * cols * rows * channels * cols,
    )
    weight_terms = exchange(weight_grad)
    if toks == 2:
        grad_query, grad_key, grad_value, grad_out, grad_single, weight_grad = call(
            close_kernel,
            "close",
            [*pairs[0], *pairs[1], *single_pair, weight_terms],
            [((cut, own_width), f32)] * 4 + [((cut, rows), f32), ((heads, channels), f32)],
        )
    else:
        last = call(
            functools.partial(last_kernel, toks),
            "last",
            [where_am_i, *pairs[0], *pairs[1]],
            [((3, cut, own_width), bf16), ((cut, own_width), f32)] + [((cut, rows), bf16)] * toks,
            [VMEM((toks, cut, rows), f32)],
        )
        weight_grad = jnp.sum(weight_terms, axis=0)
        grad_out, singles = last[1], last[2:]
        singles = [singles[0]] + [swap_tok(singles[r], r) for r in range(1, toks)]
        moved = lax.ppermute(last[0], ("copy", "tok"), swaps)
        grad_query, grad_key, grad_value, grad_single = call(
            finish_kernel,
            "finish",
            [moved] + singles,
            [((cut, own_width), f32)] * 3 + [((cut, rows), f32)],
        )
    return (
        grad_noisy[None],
        grad_single.T,
        grad_pair.reshape(rows, cols, channels),
        grad_query.T,
        grad_key.T,
        grad_value.T,
        grad_out.T,
        weight_grad.T,
    )


def solution(mesh):
    placed = (
        P("copy", "tok", None),
        P("tok", None),
        P("tok", "copy", None),
        P("tok"),
    ) + (P(),) * 15 + (P("copy", "tok", None),)
    return jax.shard_map(
        per_device,
        mesh=mesh,
        in_specs=placed,
        out_specs=(
            P("copy", "tok", None),
            P("tok", "copy"),
            P("tok", "copy", None),
            P("tok", "copy"),
            P("tok", "copy"),
            P("tok", "copy"),
            P("tok", "copy"),
            P(),
        ),
        check_vma=False,
    )
```

```python
import functools

import jax
import jax.numpy as jnp
from jax import lax
from jax.experimental import pallas as pl
from jax.experimental.pallas import tpu as pltpu
from jax.sharding import PartitionSpec as P

epsilon = 1e-05
f32 = jnp.float32
bf16 = jnp.bfloat16
VMEM, SMEM, ANY = pltpu.VMEM, pltpu.SMEM, pl.ANY
MIB = 1 << 20


def layer_forward(values, scales):
    average = jnp.mean(values, axis=-1, keepdims=True)
    centred = values - average
    inverse = lax.rsqrt(jnp.mean(centred * centred, axis=-1, keepdims=True) + epsilon)
    normed = centred * inverse
    return (normed * scales, normed, inverse)


def layer_backward(upstream, scales, normed, inverse):
    scaled = upstream * scales
    first_moment = jnp.mean(scaled, axis=-1, keepdims=True)
    second_moment = jnp.mean(scaled * normed, axis=-1, keepdims=True)
    return inverse * (scaled - first_moment - normed * second_moment)


NN = ((1,), (0,))
NT = ((1,), (1,))
TN = ((0,), (0,))


def mm(left, right, dims=NN):
    return lax.dot_general(left, right, (dims, ((), ())), preferred_element_type=f32)


def call(body, name, inputs, outs, scratch=(), flops=0, limit=16, deps=()):
    arrays, specs, moved, fetched = [], [], 0, []
    for item in inputs:
        array, space = item if isinstance(item, tuple) else (item, VMEM)
        if space == "fetch":
            fetched.append(len(arrays))
            space = pltpu.HBM
        arrays.append(array)
        specs.append(pl.BlockSpec(memory_space=space))
        moved += array.size * array.dtype.itemsize
    for shape, kind, *_ in outs:
        size = jnp.dtype(kind).itemsize
        for extent in shape:
            size *= extent
        moved += size
    read = len(arrays)
    for array in deps:
        arrays.append(array)
        specs.append(pl.BlockSpec(memory_space=ANY))
    extra = [VMEM(arrays[k].shape, arrays[k].dtype) for k in fetched]
    if fetched:
        extra.append(pltpu.SemaphoreType.DMA((len(fetched),)))

    def whole(*refs):
        refs = list(refs[:read]) + list(refs[read + len(deps) :])
        if fetched:
            held, sem = refs[-1 - len(fetched) : -1], refs[-1]
            refs = refs[: -1 - len(fetched)]
            transfers = []
            for n, k in enumerate(fetched):
                transfer = pltpu.make_async_copy(refs[k], held[n], sem.at[n])
                transfer.start()
                transfers.append(transfer)
                refs[k] = held[n]
            for transfer in transfers:
                transfer.wait()
        body(*refs)

    return pl.pallas_call(
        whole,
        name=name,
        out_shape=[jax.ShapeDtypeStruct(one[0], one[1]) for one in outs],
        in_specs=specs,
        out_specs=[pl.BlockSpec(memory_space=(*one, VMEM)[2]) for one in outs],
        scratch_shapes=list(scratch) + extra,
        compiler_params=pltpu.CompilerParams(vmem_limit_bytes=limit * MIB),
        cost_estimate=pl.CostEstimate(flops=flops, bytes_accessed=moved, transcendentals=0),
    )(*arrays)


def low_bits(index, size):
    return jnp.bitwise_and(index, size - 1)


def pair_weight_rows(w_pair, head_count, cols):
    rows = head_count * cols
    shift = cols.bit_length() - 1
    head = lax.shift_right_logical(
        lax.broadcasted_iota(jnp.int32, (rows, head_count), 0), jnp.int32(shift)
    )
    pick = (head == lax.broadcasted_iota(jnp.int32, (rows, head_count), 1)).astype(f32)
    spread = mm(pick.astype(bf16), w_pair)
    row_col = low_bits(lax.broadcasted_iota(jnp.int32, spread.shape, 0), cols)
    return spread, row_col


def own_slice(weight, t, own_width):
    if weight.shape[1] == own_width:
        return weight
    return weight.at[:, pl.ds(pl.multiple_of(t * own_width, own_width), own_width)]


def enter_kernel(toks, cols, ids, *rest):
    noisy, single, restype, table, gain, pair, pair_gain, w_pair, chain, keymask = rest[:10]
    chain_weight, x_out, columns, facts_out, chain_out, bias_out, rounded, bias = rest[10:]
    t = ids[0]
    rows = noisy.shape[0]
    pair_scaled, _, _ = layer_forward(pair[...].astype(f32), pair_gain[...])
    rounded[...] = pair_scaled.astype(bf16).astype(f32)
    head_count = w_pair.shape[0]
    spread, row_col = pair_weight_rows(w_pair[...], head_count, cols)
    total = jnp.zeros((head_count * cols, rows), f32)
    for j in range(cols):
        column = rounded[pl.ds(j, rows, stride=cols), :].astype(bf16)
        columns[j] = column
        total = total + mm(jnp.where(row_col == j, spread, 0.0).astype(bf16), column, NT)
    bias[...] = total
    part = bias_out.shape[1]
    for r in range(toks):
        start = pl.multiple_of(jnp.bitwise_xor(t, r) * part, part)
        bias_out[r] = bias[pl.ds(start, part), :].astype(bf16)
    normed_scaled, _, _ = layer_forward(noisy[...].astype(f32), gain[...])
    types = table.shape[0]
    onehot = (lax.broadcasted_iota(jnp.int32, (types, rows), 0) == restype[...]).astype(f32)
    condition = single[...].astype(f32) + mm(onehot.astype(bf16), table[...], TN)
    x_out[...] = (normed_scaled + condition).astype(bf16)
    chain_row = chain[...]
    tokens = chain_row.shape[1]
    own_heads = head_count // toks
    keep_row = keymask[...].astype(f32)
    line = lax.broadcasted_iota(jnp.int32, (128, tokens), 0)
    facts = jnp.where(line == 0, chain_row.astype(f32), 0.0) + jnp.where(line == 1, keep_row, 0.0)
    for h in range(own_heads):
        weight_row = jnp.zeros((1, tokens), f32)
        for m in range(chain_weight.shape[0]):
            weight_row = jnp.where(chain_row == m, chain_weight[m, t * own_heads + h], weight_row)
        facts = jnp.where(line == 2 + h, weight_row, facts)
    facts_out[...] = jnp.transpose(facts)
    chain_out[...] = chain_row.astype(f32)


def stage_kernel(ids, *rest):
    weights, (slices, sem) = rest[:3], rest[3:]
    transfers = []
    for k in range(3):
        transfer = pltpu.make_async_copy(
            own_slice(weights[k], ids[0], slices.shape[2]), slices.at[k], sem.at[k]
        )
        transfer.start()
        transfers.append(transfer)
    for transfer in transfers:
        transfer.wait()


def project_kernel(toks, ids, slices, *rest):
    parts = rest[:toks]
    x_out, outs = rest[toks], rest[toks + 1 :]
    t = ids[0]
    rows = parts[0].shape[0]
    for r in range(toks):
        start = pl.multiple_of(jnp.bitwise_xor(t, r) * rows, rows)
        x_out[pl.ds(start, rows), :] = parts[r][...]
    x = x_out[...]
    for k in range(3):
        outs[k][...] = jnp.transpose(mm(x, slices[k])).astype(bf16)


def split_kernel(count, *refs):
    for n in range(count):
        for r, out in enumerate(refs[count:]):
            out[n] = refs[n][r]


def join_kernel(*refs):
    for n, ref in enumerate(refs[:-1]):
        refs[-1][n] = ref[...]


def attention_kernel(copies, toks, near, cols, head_width, ids, query, key, value, *rest):
    biases, (facts, chain, weights_out, att_out) = rest[:2], rest[2:6]
    pieces, bias = rest[6 : 6 + toks], rest[6 + toks]
    t, low, high = ids[0], low_bits(ids[1], near), ids[1] // near
    for m in range(near):
        for rz in range(copies // near):
            c = jnp.bitwise_xor(high, rz) * near + jnp.bitwise_xor(low, m)
            for r in range(toks):
                bias[c, jnp.bitwise_xor(t, r)] = biases[m % 2][m // 2, r, rz]
    own_heads = weights_out.shape[0]
    tokens = query.shape[1]
    rows = tokens // toks
    same = facts[:, 0:1] == chain[...]
    keep = facts[:, 1:2] > 0.0
    scale = head_width ** (-0.5)
    attended = []
    for h in range(own_heads):
        span = slice(h * head_width, (h + 1) * head_width)
        logits = mm(key[span, :], query[span, :], TN) * scale
        line = slice(h * cols, (h + 1) * cols)
        extra = jnp.concatenate(
            [
                jnp.concatenate(
                    [bias[c, a, line, :] for c in range(copies)], axis=0
                )
                for a in range(toks)
            ],
            axis=1,
        ).astype(f32)
        logits = logits + (extra + jnp.where(same, facts[:, 2 + h : 3 + h], 0.0))
        logits = jnp.where(keep, logits, -1e30)
        exponent = jnp.exp(logits - jnp.max(logits, axis=0, keepdims=True))
        weights = exponent / jnp.sum(exponent, axis=0, keepdims=True)
        weights_b = weights.astype(bf16)
        weights_out[h] = weights_b
        attended.append(mm(value[span, :], weights_b))
    att_out[...] = jnp.transpose(jnp.concatenate(attended, axis=0)).astype(bf16)
    for r in range(toks):
        start = pl.multiple_of(jnp.bitwise_xor(t, r) * rows, rows)
        pieces[r][...] = att_out[pl.ds(start, rows), :]


def down_kernel(upstream, w_down, noisy, gain, d_hidden, upstream_out, noisy_out, gain_out):
    d_hidden[...] = mm(upstream[...], w_down[...], NT)
    upstream_out[...] = upstream[...]
    noisy_out[...] = noisy[...]
    gain_out[...] = gain[...]


def hidden_kernel(toks, chunk, ids, noisy, upstream, d_hidden, gain, *rest):
    parts = rest[:toks]
    held_out, held_gate, held_up = rest[toks : toks + 3]
    d_res_out, d_res_b_out = rest[toks + 3 : toks + 5]
    d_att_outs = rest[toks + 5 :]
    t = ids[0]
    hidden = held_gate.shape[1]
    residual = noisy[...].astype(f32)
    own_width = parts[0].shape[1]
    for r in range(toks):
        start = pl.multiple_of(jnp.bitwise_xor(t, r) * own_width, own_width)
        residual = residual + mm(parts[r][...], held_out[pl.ds(start, own_width), :])
    trans_scaled, trans_hat, trans_inverse = layer_forward(residual, gain[...])
    trans_in = trans_scaled.astype(bf16)
    d_trans = jnp.zeros(residual.shape, f32)
    for k in range(hidden // chunk):
        span = slice(k * chunk, (k + 1) * chunk)
        gate = mm(trans_in, held_gate[:, span])
        up = mm(trans_in, held_up[:, span])
        incoming = d_hidden[:, span]
        sigmoid = jax.nn.sigmoid(gate)
        d_up = (incoming * gate * sigmoid).astype(bf16)
        d_gate = (incoming * up * sigmoid * (1.0 + gate * (1.0 - sigmoid))).astype(bf16)
        d_trans = d_trans + mm(d_gate, held_gate[:, span], NT) + mm(d_up, held_up[:, span], NT)
    d_res = upstream[...].astype(f32) + layer_backward(
        d_trans, gain[...], trans_hat, trans_inverse
    )
    d_res_out[...] = d_res
    d_res_b = d_res.astype(bf16)
    d_res_b_out[...] = d_res_b
    for r in range(toks):
        start = pl.multiple_of(jnp.bitwise_xor(t, r) * own_width, own_width)
        d_att_outs[r][...] = mm(held_out[pl.ds(start, own_width), :], d_res_b, NT).astype(bf16)


def backward_kernel(copies, toks, cols, head_width, ids, query, key, value, weights, *rest):
    parts, d_res_b = rest[:toks], rest[toks]
    d_query, d_key, d_value, bias_kept, bias_sent, d_res_out = rest[toks + 1 : toks + 7]
    blocks, d_logits = rest[toks + 7 :]
    d_res_out[...] = d_res_b[...]
    t = ids[0]
    bit = low_bits(ids[1] // 2, 2)
    heads = weights.shape[0]
    for r in range(toks):
        blocks[jnp.bitwise_xor(t, r)] = parts[r][...]
    d_att = jnp.concatenate([blocks[a] for a in range(toks)], axis=1)
    count = tile_count(cols, query.shape[1])
    scale = head_width ** (-0.5)
    for h in range(weights.shape[0]):
        span = slice(h * head_width, (h + 1) * head_width)
        d_att_h = d_att[span, :]
        weights_b = weights[h]
        d_weights = mm(value[span, :], d_att_h, TN)
        weights_f = weights_b.astype(f32)
        delta = jnp.sum(weights_f * d_weights, axis=0, keepdims=True)
        d_logits_b = (weights_f * (d_weights - delta)).astype(bf16)
        d_logits[...] = d_logits_b
        for k in range(copies // 2):
            for side, out in ((bit, bias_kept), (1 - bit, bias_sent)):
                start = pl.multiple_of((k // 2 * 4 + side * 2 + k % 2) * cols, cols)
                put(out, (k * heads + h) * count, d_logits[pl.ds(start, cols), :])
        d_query[span, :] = (mm(key[span, :], d_logits_b) * scale).astype(bf16)
        d_key[span, :] = (mm(query[span, :], d_logits_b, NT) * scale).astype(bf16)
        d_value[span, :] = mm(d_att_h, weights_b, NT).astype(bf16)


def tile_count(rows, lanes):
    return -(-rows // 16) * -(-lanes // 128)


def put(out, base, value):
    rows, lanes = value.shape
    for i in range(0, rows, 16):
        for j in range(0, lanes, 128):
            part = value[i : i + 16, j : j + 128]
            if part.shape != (16, 128):
                out[base] = jnp.zeros((16, 128), out.dtype)
            out[base, : part.shape[0], : part.shape[1]] = part
            base += 1


def take(tiles, base, rows, lanes):
    across = -(-lanes // 128)
    lines = []
    for i in range(-(-rows // 16)):
        line = [tiles[base + i * across + j] for j in range(across)]
        lines.append(jnp.concatenate(line, axis=1) if across > 1 else line[0])
    whole = jnp.concatenate(lines, axis=0) if len(lines) > 1 else lines[0]
    return whole[:rows, :lanes]


def cut_wide(copies, toks, core, base, stride, grad, kept, sent):
    group = copies // toks
    cut, depth = grad.shape[1] // copies, grad.shape[1] // toks
    for side, out in ((core, kept), (1 - core, sent)):
        for q in range(copies // 2):
            h = 2 * q // group
            first = pl.multiple_of((2 * q - h * group + side) * cut, 8)
            part = grad[pl.ds(first, cut), h * depth : (h + 1) * depth]
            put(out, q * stride + base, part.astype(bf16))


def first_kernel(copies, toks, ids, slices, x, d_query, d_key, d_value, *rest):
    kept, sent, d_own, single_all = rest[:4]
    d_others, (wide, d_inputs) = rest[4 : 3 + toks], rest[3 + toks :]
    t, core = ids[0], low_bits(ids[1], 2)
    rows = d_own.shape[1]
    cut = x.shape[1] // copies
    count = tile_count(cut, d_query.shape[0])
    stride = 3 * count
    for k, part in enumerate((d_query, d_key, d_value)):
        wide[...] = mm(part[...], x[...])
        cut_wide(copies, toks, core, k * count, stride, wide, kept, sent)
    total = mm(slices[0], d_query[...]) + mm(slices[1], d_key[...])
    total = total + mm(slices[2], d_value[...])
    single_all[...] = total
    for a in range(toks):
        d_inputs[a] = total[:, a * rows : (a + 1) * rows]
    d_own[...] = d_inputs[t]
    for r in range(1, toks):
        d_others[r - 1][...] = d_inputs[jnp.bitwise_xor(t, r)].astype(bf16)


def second_kernel(copies, toks, ids, att, single_all, bias_kept, bias_got, *rest):
    d_res_parts, (kept, sent, d_res, narrow) = rest[:toks], rest[toks:]
    t, core = ids[0], low_bits(ids[1], 2)
    rows = d_res_parts[0].shape[0]
    cut = narrow.shape[0] // copies
    count = tile_count(cut, narrow.shape[1])
    for r in range(toks):
        start = pl.multiple_of(jnp.bitwise_xor(t, r) * rows, rows)
        d_res[pl.ds(start, rows), :] = d_res_parts[r][...]
    narrow[...] = mm(d_res[...], att[...], TN)
    stride = count + tile_count(cut, rows * toks)
    base = copies // 2 * stride
    bias_count = bias_kept.shape[0] // (copies // 2)
    for side, out in ((core, kept), (1 - core, sent)):
        for q in range(copies // 2):
            first = pl.multiple_of((2 * q + side) * cut, 8)
            put(out, q * stride, narrow[pl.ds(first, cut), :].astype(bf16))
            put(out, q * stride + count, single_all[pl.ds(first, cut), :].astype(bf16))
        for z in range(copies // 4):
            span = pl.ds((2 * z + side) * bias_count, bias_count)
            out[base + z * bias_count : base + (z + 1) * bias_count] = (
                bias_kept[span].astype(f32) + bias_got[span].astype(f32)
            ).astype(bf16)


def step_kernel(segments, ids, *refs):
    count = 1 + max(segment[0] for segment in segments)
    ins, outs = refs[: 2 * count], refs[2 * count :]
    for source, base, parts, tiles, mask, inner, target, start in segments:
        kept, got = ins[2 * source : 2 * source + 2]
        bit = low_bits(ids[1] // mask, 2)
        for q in range(parts // 2):
            for side, out in ((bit, outs[2 * target]), (1 - bit, outs[2 * target + 1])):
                k = q // inner * 2 * inner + side * inner + q % inner
                span = pl.ds(base + k * tiles, tiles)
                out[start + q * tiles : start + (q + 1) * tiles] = (
                    kept[span].astype(f32) + got[span].astype(f32)
                ).astype(bf16)


def last_bias_kernel(toks, base, count, cols, ids, kept, got, *rest):
    pieces, blocks = rest[:toks], rest[toks]
    span = slice(base, base + count)
    tiles = kept[span].astype(f32) + got[span].astype(f32)
    part_rows, rows = pieces[0].shape
    heads = part_rows // cols
    total = jnp.concatenate(
        [take(tiles, h * (count // heads), cols, rows * toks) for h in range(heads)], axis=0
    )
    for a in range(toks):
        blocks[a] = total[:, a * rows : (a + 1) * rows].astype(bf16)
    for r in range(toks):
        pieces[r][...] = blocks[jnp.bitwise_xor(ids[0], r)]


def across_kernel(segment, ids, kept, got, kept_b, got_b, *outs):
    t = ids[0]
    stride = kept.shape[0] // 2
    step_kernel([(0, 0) + segment], ids, kept_b, got_b, *outs[2:])
    for side, out in ((t, outs[0]), (1 - t, outs[1])):
        span = pl.ds(side * stride, stride)
        out[...] = (kept[span].astype(f32) + got[span].astype(f32)).astype(bf16)


def far_kernel(half, ids, kept, got, kept_b, got_b, kept_out, sent_out, single, other, *scratch):
    groups, blocks = scratch
    t, a = ids[0], ids[1] // half
    groups[t] = kept[...]
    groups[1 - t] = got[...]
    kept_out[...] = groups[a]
    sent_out[...] = groups[1 - a]
    lines = single.shape[0]
    base = kept_b.shape[0] - 2 * lines
    for i in range(lines):
        for j in range(2):
            k = base + 2 * i + j
            blocks[j, i] = (kept_b[k].astype(f32) + got_b[k].astype(f32)).astype(bf16)
    single[...] = blocks[t]
    other[...] = blocks[1 - t]


def close_kernel(kept, got, kept_b, got_b, single, got_single, terms, *outs):
    total = kept[...].astype(f32) + got[...].astype(f32)
    cut, own_width = outs[0].shape
    count = tile_count(cut, own_width)
    for k in range(3):
        outs[k][...] = take(total, k * count, cut, own_width)
    total = kept_b[:count].astype(f32) + got_b[:count].astype(f32)
    outs[3][...] = take(total, 0, cut, own_width)
    total = single[...].astype(f32) + got_single[...].astype(f32)
    outs[4][...] = take(total, 0, cut, outs[4].shape[1])
    outs[5][...] = jnp.sum(terms[...].astype(f32), axis=0)


def last_kernel(toks, ids, kept, got, kept_b, got_b, moved, final, *rest):
    pieces, blocks = rest[:toks], rest[toks]
    first = kept[...].astype(f32) + got[...].astype(f32)
    second = kept_b[...].astype(f32) + got_b[...].astype(f32)
    _, cut, own_width = moved.shape
    count = tile_count(cut, own_width)
    for k in range(3):
        moved[k] = take(first, k * count, cut, own_width).astype(bf16)
    final[...] = take(second, 0, cut, own_width)
    rows = blocks.shape[2]
    single = take(second, count, cut, rows * toks)
    for a in range(toks):
        blocks[a] = single[:, a * rows : (a + 1) * rows]
    for r in range(toks):
        pieces[r][...] = blocks[jnp.bitwise_xor(ids[0], r)].astype(bf16)


def finish_kernel(moved, *rest):
    parts, outs = rest[:-4], rest[-4:]
    for k in range(3):
        outs[k][...] = moved[k].astype(f32)
    total = parts[0][...].astype(f32)
    for part in parts[1:]:
        total = total + part[...].astype(f32)
    outs[3][...] = total


def exit_kernel(toks, noisy, gain, d_res, d_own, columns, *rest):
    others, (grad_noisy, token, columns_out) = rest[: toks - 1], rest[toks - 1 :]
    token[...] = jnp.zeros(token.shape, f32)
    columns_out[...] = columns[...]
    total = d_own[...]
    for part in others:
        total = total + part[...].astype(f32)
    _, noisy_hat, noisy_inverse = layer_forward(noisy[...].astype(f32), gain[...])
    grad_noisy[...] = (
        d_res[...] + layer_backward(jnp.transpose(total), gain[...], noisy_hat, noisy_inverse)
    ).astype(bf16)


def set_heads(toks, ids, parts, grads):
    part_rows = parts[0].shape[0]
    for r in range(toks):
        start = pl.multiple_of(jnp.bitwise_xor(ids[0], r) * part_rows, part_rows)
        grads[pl.ds(start, part_rows), :] = parts[r][...].astype(f32)


def pair_weight_kernel(toks, ids, columns, *rest):
    parts, (weight_grad, grads) = rest[:toks], rest[toks:]
    set_heads(toks, ids, parts, grads)
    cols, rows, channels = columns.shape
    heads = weight_grad.shape[1]
    lines = [grads[pl.ds(j, heads, stride=cols), :].astype(bf16) for j in range(cols)]
    sums = mm(jnp.concatenate(lines, axis=1), columns[...].reshape(cols * rows, channels))
    for n in range(weight_grad.shape[0]):
        weight_grad[n] = sums.astype(weight_grad.dtype)


def pair_kernel(toks, cols, ids, pair, gain, w_pair, *rest):
    parts, (grad_pair, spread_out, grads) = rest[:toks], rest[toks:]
    set_heads(toks, ids, parts, grads)
    rows = parts[0].shape[1]
    _, pair_hat, pair_inverse = layer_forward(pair[...].astype(f32), gain[...])
    spread, row_col = pair_weight_rows(w_pair[...], w_pair.shape[0], cols)
    turned = jnp.transpose(grads[...]).astype(bf16)
    for j in range(cols):
        spread_out[pl.ds(j, rows, stride=cols), :] = mm(
            turned, jnp.where(row_col == j, spread, 0.0).astype(bf16)
        )
    grad_pair[...] = layer_backward(
        spread_out[...], gain[...], pair_hat, pair_inverse
    ).astype(bf16)


def swap_copy(value, mask):
    size = lax.axis_size("copy")
    return lax.ppermute(value, "copy", [(i, i ^ mask) for i in range(size)])


def swap_tok(value, mask):
    size = lax.axis_size("tok")
    return lax.ppermute(value, "tok", [(i, i ^ mask) for i in range(size)])


def exchange(value):
    return lax.all_to_all(value, ("copy", "tok"), 0, 0)


def per_device(
    noisy,
    single,
    pair,
    restype,
    chain,
    keymask,
    restype_table,
    norm_gain,
    pair_gain,
    trans_gain,
    w_query,
    w_key,
    w_value,
    w_out,
    w_pair,
    chain_weight,
    w_hidden_gate,
    w_hidden_up,
    w_down,
    cotangent,
):
    copies = lax.axis_size("copy")
    toks = lax.axis_size("tok")
    _, rows, width = noisy.shape
    cols = pair.shape[1]
    channels = pair.shape[2]
    heads = w_pair.shape[1]
    head_width = width // heads
    own_heads = heads // toks
    own_width = own_heads * head_width
    tokens = rows * toks
    hidden = w_down.shape[0]
    cut = width // copies
    devices = copies * toks
    ids = jnp.stack([lax.axis_index("tok"), lax.axis_index("copy")]).astype(jnp.int32)
    where_am_i = (ids, SMEM)
    noisy2 = noisy.reshape(rows, width)
    pair2 = pair.reshape(rows * cols, channels)
    pair_gain2 = pair_gain.reshape(1, channels)
    norm_gain2 = norm_gain.reshape(1, width)

    weights3 = [w_query, w_key, w_value]
    if own_width % 128:
        weights3 = [
            lax.dynamic_slice_in_dim(w, ids[0] * own_width, own_width, axis=1) for w in weights3
        ]
    small = [noisy2, single, restype.reshape(1, rows), restype_table, norm_gain, pair2, pair_gain2]
    small += [w_pair.T, chain.reshape(1, tokens), keymask.reshape(1, tokens)]
    entered = call(
        functools.partial(enter_kernel, toks, cols),
        "enter",
        [where_am_i]
        + [(array, "fetch") for array in small]
        + [(chain_weight, SMEM)],
        [((rows, width), bf16), ((cols, rows, channels), bf16)]
        + [((tokens, 128), f32), ((1, tokens), f32), ((toks, own_heads * cols, rows), bf16)],
        [VMEM((rows * cols, channels), f32), VMEM((heads * cols, rows), f32)],
        flops=2 * heads * cols * rows * channels * cols,
        limit=60,
    )
    x_own, columns, facts, chain_row, bias_mine = entered
    near = 4
    far = copies // near
    x_parts = [x_own] + [swap_tok(x_own, r) for r in range(1, toks)]
    by_tok = call(
        functools.partial(split_kernel, far),
        "split_far",
        [bias_mine] + [swap_copy(bias_mine, m * near) for m in range(1, far)],
        [((far, own_heads * cols, rows), bf16)] * toks,
        deps=x_parts[1:],
    )
    (slices,) = call(
        stage_kernel,
        "stage",
        [where_am_i] + [(w, ANY) for w in weights3],
        [((3, width, own_width), bf16)],
        [pltpu.SemaphoreType.DMA((3,))],
        deps=[by_tok[0]],
    )
    (lines,) = call(
        join_kernel,
        "join_tok",
        [by_tok[0]] + [swap_tok(by_tok[r], r) for r in range(1, toks)],
        [((toks, far, own_heads * cols, rows), bf16)],
        deps=[slices],
    )
    x, query, key, value = call(
        functools.partial(project_kernel, toks),
        "project",
        [where_am_i, slices] + x_parts,
        [((tokens, width), bf16)] + [((own_width, tokens), bf16)] * 3,
        flops=6 * tokens * width * own_width,
    )
    (lines,) = call(
        join_kernel,
        "join_y",
        [lines, swap_copy(lines, 2)],
        [((2,) + lines.shape, bf16)],
        deps=[value],
    )
    biases = [lines, swap_copy(lines, 1)]
    done = call(
        functools.partial(attention_kernel, copies, toks, near, cols, head_width),
        "attention",
        [where_am_i, query, key, value] + biases + [facts, chain_row],
        [((own_heads, tokens, tokens), bf16), ((tokens, own_width), bf16)]
        + [((rows, own_width), bf16)] * toks,
        [VMEM((copies, toks, own_heads * cols, rows), bf16)],
        flops=4 * tokens * tokens * own_width,
        limit=32,
    )
    weights, att, pieces = done[0], done[1], done[2:]
    att_parts = [pieces[0]] + [swap_tok(pieces[r], r) for r in range(1, toks)]

    d_hidden, upstream, noisy3, trans_gain2 = call(
        down_kernel,
        "down",
        [cotangent.reshape(rows, width), w_down, noisy2, trans_gain.reshape(1, width)],
        [((rows, hidden), f32), ((rows, width), bf16), ((rows, width), bf16), ((1, width), f32)],
        flops=2 * rows * hidden * width,
    )
    chunk = hidden // 3
    results = call(
        functools.partial(hidden_kernel, toks, chunk),
        "hidden",
        [where_am_i, noisy3, upstream, d_hidden, trans_gain2]
        + att_parts
        + [w_out, w_hidden_gate, w_hidden_up],
        [((rows, width), f32), ((rows, width), bf16)] + [((own_width, rows), bf16)] * toks,
        flops=2 * rows * width * (2 * width + 4 * hidden),
    )
    d_res, d_res_b, d_att = results[0], results[1], results[2:]
    d_att_parts = [d_att[0]] + [swap_tok(d_att[r], r) for r in range(1, toks)]
    bias_tiles = own_heads * tile_count(cols, tokens)
    bias_shape = (copies // 2 * bias_tiles, 16, 128)
    d_query, d_key, d_value, bias_kept, bias_sent, d_res_b = call(
        functools.partial(backward_kernel, copies, toks, cols, head_width),
        "backward",
        [where_am_i, query, key, value, weights] + d_att_parts + [d_res_b],
        [((own_width, tokens), bf16)] * 3 + [(bias_shape, bf16)] * 2 + [((rows, width), bf16)],
        [VMEM((toks, own_width, rows), bf16), VMEM((tokens, tokens), bf16)],
        flops=8 * tokens * tokens * own_width,
        limit=32,
    )
    d_res_parts = [d_res_b] + [swap_tok(d_res_b, r) for r in range(1, toks)]
    bias_got = swap_copy(bias_sent, 2)

    wide_tiles = tile_count(cut, own_width)
    single_tiles = tile_count(cut, tokens)
    first_tiles, second_tiles = 3 * wide_tiles, wide_tiles + single_tiles
    found = call(
        functools.partial(first_kernel, copies, toks),
        "first",
        [where_am_i, slices, x, d_query, d_key, d_value],
        [((copies // 2 * first_tiles, 16, 128), bf16)] * 2
        + [((width, rows), f32), ((width, tokens), f32)]
        + [((width, rows), bf16)] * (toks - 1),
        [VMEM((own_width, width), f32), VMEM((toks, width, rows), f32)],
        flops=12 * tokens * width * own_width,
    )
    kept, sent, d_own, single_all = found[:4]
    got = swap_copy(sent, 1)
    d_others = [swap_tok(found[3 + r], r) for r in range(1, toks)]

    def step(name, pairs, segments, deps=()):
        filled, full, masks_of = {}, [], {}
        for source, base, parts, tiles, mask, left, target in segments:
            inner = 1 << sum(1 for other in left if other < mask)
            start = filled.get(target, 0)
            full.append((source, base, parts, tiles, mask, inner, target, start))
            filled[target] = start + parts // 2 * tiles
            masks_of[target] = mask
        outs = []
        for target in range(len(filled)):
            outs += [((filled[target], 16, 128), bf16)] * 2
        results = call(
            functools.partial(step_kernel, full),
            name,
            [where_am_i] + [array for one in pairs for array in one],
            outs,
            deps=deps,
        )
        return [
            (results[2 * n], swap_copy(results[2 * n + 1], masks_of[n]))
            for n in range(len(filled))
        ]

    masks = [1 << b for b in range(1, copies.bit_length() - 1)]
    masks_b = masks[1:] + masks[:1]
    kept_b, sent_b = call(
        functools.partial(second_kernel, copies, toks),
        "second",
        [where_am_i, att, single_all, bias_kept, bias_got] + d_res_parts,
        [((copies // 2 * second_tiles + copies // 4 * bias_tiles, 16, 128), bf16)] * 2,
        [VMEM((tokens, width), bf16), VMEM((width, own_width), f32)],
        flops=20 * tokens * width * own_width,
    )
    got_b = swap_copy(sent_b, 1)

    grad_noisy, exited, columns = call(
        functools.partial(exit_kernel, toks),
        "exit",
        [noisy3, norm_gain2, d_res, d_own, columns] + d_others,
        [((rows, width), bf16), ((8, 128), f32), (columns.shape, bf16)],
    )
    pairs = [(kept, got), (kept_b, got_b)]
    parts = copies // 2
    for n, (mask, mask_b) in enumerate(zip(masks, masks_b)):
        segments = [
            (0, 0, parts, first_tiles, mask, masks[n:], 0),
            (1, 0, parts, second_tiles, mask_b, masks_b[n:], 1),
        ]
        bias_base = parts * second_tiles
        if n + 1 < len(masks):
            segments.append((1, bias_base, parts // 2, bias_tiles, mask_b, masks_b[n:-1], 1))
        else:
            bias_ready = pairs[1]
            if toks == 2:
                break
        pairs = step("step_%d" % n, pairs, segments, deps=[exited] if n == 1 else ())
        parts //= 2
    if toks == 2:
        kept, sent, kept_b, sent_b = call(
            functools.partial(across_kernel, (2, second_tiles, masks_b[-1], 1, 0, 0)),
            "across",
            [where_am_i] + [array for one in pairs for array in one],
            [((first_tiles, 16, 128), bf16)] * 2 + [((second_tiles, 16, 128), bf16)] * 2,
        )
        pairs = [(kept, swap_tok(sent, 1)), (kept_b, swap_copy(sent_b, masks_b[-1]))]
    bias_pieces = call(
        functools.partial(last_bias_kernel, toks, bias_base, bias_tiles, cols),
        "last_bias",
        [where_am_i, *bias_ready],
        [((own_heads * cols, rows), bf16)] * toks,
        [VMEM((toks, own_heads * cols, rows), bf16)],
        deps=[pairs[0][0]],
    )
    bias_pieces = [bias_pieces[0]] + [swap_tok(bias_pieces[r], r) for r in range(1, toks)]
    ready = [pairs[0][1], pairs[1][1]]
    if toks == 2:
        lines = single_tiles // 2
        kept, sent, single_kept, single_sent = call(
            functools.partial(far_kernel, copies // 2),
            "far",
            [where_am_i, *pairs[0], *pairs[1]],
            [((first_tiles, 16, 128), bf16)] * 2 + [((lines, 16, 128), bf16)] * 2,
            [VMEM((2, first_tiles, 16, 128), bf16), VMEM((2, lines, 16, 128), bf16)],
            deps=bias_pieces[1:],
        )
        pairs[0] = (kept, swap_copy(sent, copies // 2))
        single_pair = (single_kept, swap_tok(single_sent, 1))

    group = copies // toks
    swaps = []
    for c in range(copies):
        for t in range(toks):
            swaps.append((c * toks + t, (t * group + c % group) * toks + c // group))

    (weight_grad,) = call(
        functools.partial(pair_weight_kernel, toks),
        "pair_weight",
        [where_am_i, columns] + bias_pieces,
        [((devices, heads, channels), bf16)],
        [VMEM((heads * cols, rows), f32)],
        flops=2 * heads * cols * rows * channels * cols,
        deps=ready,
    )
    (grad_pair,) = call(
        functools.partial(pair_kernel, toks, cols),
        "pair",
        [where_am_i, pair2, pair_gain2, w_pair.T] + bias_pieces,
        [((rows * cols, channels), bf16)],
        [VMEM((rows * cols, channels), f32), VMEM((heads * cols, rows), f32)],
        flops=2 * heads * cols * rows * channels * cols,
    )
    weight_terms = exchange(weight_grad)
    if toks == 2:
        grad_query, grad_key, grad_value, grad_out, grad_single, weight_grad = call(
            close_kernel,
            "close",
            [*pairs[0], *pairs[1], *single_pair, weight_terms],
            [((cut, own_width), f32)] * 4 + [((cut, rows), f32), ((heads, channels), f32)],
        )
    else:
        last = call(
            functools.partial(last_kernel, toks),
            "last",
            [where_am_i, *pairs[0], *pairs[1]],
            [((3, cut, own_width), bf16), ((cut, own_width), f32)] + [((cut, rows), bf16)] * toks,
            [VMEM((toks, cut, rows), f32)],
        )
        weight_grad = jnp.sum(weight_terms.astype(f32), axis=0)
        grad_out, singles = last[1], last[2:]
        singles = [singles[0]] + [swap_tok(singles[r], r) for r in range(1, toks)]
        moved = lax.ppermute(last[0], ("copy", "tok"), swaps)
        grad_query, grad_key, grad_value, grad_single = call(
            finish_kernel,
            "finish",
            [moved] + singles,
            [((cut, own_width), f32)] * 3 + [((cut, rows), f32)],
        )
    return (
        grad_noisy[None],
        grad_single.T,
        grad_pair.reshape(rows, cols, channels),
        grad_query.T,
        grad_key.T,
        grad_value.T,
        grad_out.T,
        weight_grad.T,
    )


def solution(mesh):
    placed = (
        P("copy", "tok", None),
        P("tok", None),
        P("tok", "copy", None),
        P("tok"),
    ) + (P(),) * 15 + (P("copy", "tok", None),)
    return jax.shard_map(
        per_device,
        mesh=mesh,
        in_specs=placed,
        out_specs=(
            P("copy", "tok", None),
            P("tok", "copy"),
            P("tok", "copy", None),
            P("tok", "copy"),
            P("tok", "copy"),
            P("tok", "copy"),
            P("tok", "copy"),
            P(),
        ),
        check_vma=False,
    )
```
